32 devices in a mesh: grp: 8 (over z, x), band: 4 (over y, core).
Axes of the slice: x: 2, y: 2, z: 4, core: 2. Of those that a mesh axis runs over, the one named last changes fastest.
Arguments:
- patches: bfloat16 [16, 32, 32, 1152], P('grp', 'band'), may hold values from -6 to 6
- grad_out: bfloat16 [16, 32, 32, 1152], P('grp', 'band'), may hold values from -6 to 6
- cond_table: float32 [8, 1152], replicated, may hold values from -6 to 6
- group_ids: int32 [16], P('grp'), may hold values from 0 to 7
- live_count: int32 [8], P('grp'), may hold values from 1 to 2, as said below
- band_order: int32 [4], P('band'), may hold values from 0 to 3, each once
- w_ada: bfloat16 [1152, 6912], P('grp'), may hold values from -0.1875 to 0.1875
- b_ada: bfloat16 [6912], P('grp'), may hold values from -2 to 2
- w_qkv: bfloat16 [1152, 3456], P('grp'), may hold values from -0.1875 to 0.1875
- q_gain: float32 [72], replicated, may hold values from 0.25 to 1.75
- k_gain: float32 [72], replicated, may hold values from 0.25 to 1.75
- w_proj: bfloat16 [1152, 1152], P('grp'), may hold values from -0.75 to 0.75
- w_gate: bfloat16 [1152, 3072], P('grp'), may hold values from -0.1875 to 0.1875
- w_up: bfloat16 [1152, 3072], P('grp'), may hold values from -0.1875 to 0.1875
- w_down: bfloat16 [3072, 1152], P('grp'), may hold values from -0.109375 to 0.109375
Outputs:
- patches_out: bfloat16 [16, 32, 32, 1152], P('grp', 'band')
- d_patches: float32 [16, 32, 32, 1152], P('grp', 'band')
- d_cond_table: float32 [8, 1152], replicated
- d_w_ada: float32 [1152, 6912], P('grp')
- d_b_ada: float32 [6912], P('grp')
- d_w_qkv: float32 [1152, 3456], P('grp')
- d_q_gain: float32 [72], replicated
- d_k_gain: float32 [72], replicated
- d_w_proj: float32 [1152, 1152], P('grp')
- d_w_gate: float32 [1152, 3072], P('grp')
- d_w_up: float32 [1152, 3072], P('grp')
- d_w_down: float32 [3072, 1152], P('grp')
The draws below stay inside these ranges and needn't reach their ends.
Inputs may be any that keep to these rules, and one draw needn't show every extreme that they name: `live_count`: live slots come first on each grp index; slots at or above the count are empty; at least one index has all 2 slots live.
All inputs are finite; a program needn't handle non-finite values.
Results may differ from the reference program's by a relative error of at most 0.017.
Values may be sent and summed in bfloat16 or wider, within the bound.
A program may use at most 320 MiB of HBM per device.

```python
import math
import jax
import jax.numpy as jnp
import numpy as np
from jax import lax

D = 1152
HEADS = 16
HDIM = 72
FF = 3072
GRID = 32
IMG_CAP = 2
GROUPS = 8
IMAGES = 16
BAND_ROWS = 8
N_GRP = 8
N_BAND = 4


def draw_live_count(key, part):
    key = jax.random.fold_in(key, 11)
    first_key, second_key = jax.random.split(key)
    counts = jax.random.randint(first_key, (N_GRP,), 1, IMG_CAP + 1)
    busiest = jax.random.randint(second_key, (), 0, N_GRP)
    return jnp.where(jnp.arange(N_GRP) == busiest, IMG_CAP, counts).astype(jnp.int32)


def place_ends(values, key, smallest, largest):
    index_at = [jax.random.randint(jax.random.fold_in(key, axis), (), 0, length) for axis, length in enumerate(values.shape)]
    widest = values.shape.index(max(values.shape))
    neighbour = index_at[:widest] + [(index_at[widest] + 1) % values.shape[widest]] + index_at[widest + 1:]
    return values.at[tuple(index_at)].set(smallest).at[tuple(neighbour)].set(largest)


def with_spikes(values, own_key, source, target, parts, factor):
    owner, partner = [(jnp.arange(values.shape[position]) // (values.shape[position] // parts)).reshape([-1 if axis == position else 1 for axis in range(values.ndim)]) for position in (source, target)]
    chosen = jax.random.permutation(own_key, parts)[partner]
    strong = (owner == chosen) | (owner == (partner + parts // 2) % parts)
    return jnp.where(strong, factor * values, values)


def steps_of(rng, dims, shards, smallest, top_value):
    factor_of, own = 1.0, jax.random.fold_in(rng, 6)
    for position, shards_of in shards:
        draws = jnp.exp(jax.random.uniform(jax.random.fold_in(own, position), (shards_of,), jnp.float32, smallest / len(shards), top_value / len(shards)))
        factor_of = factor_of * jnp.repeat(draws, dims[position] // shards_of).reshape([-1 if axis == position else 1 for axis in range(len(dims))])
    return factor_of


def rank_table(number_of, slope):
    weights = [(1 << 20) // math.isqrt(rank ** slope) + 1 for rank in range(1, number_of + 1)]
    scale = 1 + sum(weights) // (1 << 30)
    return np.cumsum(np.array([max(1, weight // scale) for weight in weights]))


def skewed_ids(own_key, shape, count, slope):
    table = rank_table(count, slope)
    pick = jax.random.randint(jax.random.fold_in(own_key, 1), shape, 0, int(table[count - 1]))
    grade = jnp.searchsorted(jnp.asarray(table, jnp.int32), pick, side="right")
    return jax.random.permutation(jax.random.fold_in(own_key, 2), count)[grade].astype(jnp.int32)


def centred(stream_key, extent, width, bound, cuts=(), kind=jnp.bfloat16):
    array = jax.random.normal(stream_key, extent, jnp.float32) * width
    if len(cuts) > 0:
        array = steps_of(stream_key, extent, cuts, -0.22, 0.18) * array
    return jnp.clip(array, min=-bound, max=bound).astype(kind)


def heavy_noise(stream_key, extent, deviation, reach, cuts, heavy, held_as=jnp.bfloat16):
    array = deviation * jax.random.normal(stream_key, extent, jnp.float32)
    if cuts:
        array = array * steps_of(stream_key, extent, cuts, -0.22, 0.18)
    return jnp.clip(with_spikes(array, jax.random.fold_in(stream_key, 3), *heavy), -reach, reach).astype(held_as)


def setup_inputs(seed: int = 0) -> dict:
    arg_keys = jax.random.split(jax.random.key(seed), 16)
    return {
        "patches": heavy_noise(arg_keys[0], (IMAGES, GRID, GRID, D), 1.0, 6.0, ((0, 8), (1, 4)), (0, 3, 8, 2.0)),
        "grad_out": centred(arg_keys[1], (IMAGES, GRID, GRID, D), 1.0, 6.0, ((0, 8), (1, 4))),
        "cond_table": centred(arg_keys[2], (GROUPS, D), 1.0, 6.0, (), jnp.float32),
        "group_ids": place_ends(skewed_ids(arg_keys[3], (IMAGES,), GROUPS, 2), jax.random.fold_in(arg_keys[3], 3), 0, GROUPS - 1).astype(jnp.int32),
        "live_count": draw_live_count(jax.random.fold_in(arg_keys[15], 71), 0),
        "band_order": jax.random.permutation(arg_keys[5], N_BAND).astype(jnp.int32),
        "w_ada": centred(arg_keys[6], (D, 6 * D), D ** -0.5, 0.1875, ((0, 8),)),
        "b_ada": centred(arg_keys[7], (6 * D,), 0.3, 2.0, ((0, 8),)),
        "w_qkv": centred(arg_keys[8], (D, 3 * D), D ** -0.5, 0.1875, ((0, 8),)),
        "q_gain": jnp.clip(1.0 + 0.15 * jax.random.normal(arg_keys[9], (HDIM,), jnp.float32), 0.25, 1.75),
        "k_gain": jnp.clip(1.0 + 0.15 * jax.random.normal(arg_keys[10], (HDIM,), jnp.float32), 0.25, 1.75),
        "w_proj": centred(arg_keys[11], (D, D), (D // 16) ** -0.5, 0.75, ((0, 8),)),
        "w_gate": centred(arg_keys[12], (D, FF), D ** -0.5, 0.1875, ((0, 8),)),
        "w_up": centred(arg_keys[13], (D, FF), D ** -0.5, 0.1875, ((0, 8),)),
        "w_down": centred(arg_keys[14], (FF, D), FF ** -0.5, 0.109375, ((0, 8),)),
    }


EPS = 1e-06
HIGH = lax.Precision.HIGHEST

@jax.custom_vjp
def low(v):
    return lax.optimization_barrier(v.astype(jnp.bfloat16)).astype(jnp.float32)

@jax.custom_vjp
def low_back(v):
    return v

def low_keep(v):
    return (low(v), None)

def low_pass(kept, grad):
    return (grad,)

def back_keep(v):
    return (v, None)

def back_low(kept, grad):
    return (low(grad),)
low.defvjp(low_keep, low_pass)
low_back.defvjp(back_keep, back_low)

def matmul(left, right):
    return jnp.dot(left, right, precision=HIGH, preferred_element_type=jnp.float32)

def rms_norm(values):
    return values * lax.rsqrt(lax.optimization_barrier(jnp.mean(values * values, axis=-1, keepdims=True)) + EPS)

def rope_tables(row_index, col_index):
    quarter = HDIM // 4
    frequency = 10000.0 ** (-jnp.arange(quarter, dtype=jnp.float32) / quarter)
    row_angle = (row_index[:, None] * frequency[None, :])[:, None, :]
    col_angle = (col_index[:, None] * frequency[None, :])[:, None, :]
    return (jnp.cos(row_angle), jnp.sin(row_angle), jnp.cos(col_angle), jnp.sin(col_angle))

def rotate(tensor, tables):
    quarter = tensor.shape[-1] // 4
    cos_row, sin_row, cos_col, sin_col = tables
    part_a = tensor[..., :quarter]
    part_b = tensor[..., quarter:2 * quarter]
    part_c = tensor[..., 2 * quarter:3 * quarter]
    part_d = tensor[..., 3 * quarter:]
    return jnp.concatenate([part_a * cos_row - part_b * sin_row, part_a * sin_row + part_b * cos_row, part_c * cos_col - part_d * sin_col, part_c * sin_col + part_d * cos_col], axis=-1)

def layer(block, weights, onehot, live_mask, tables):
    cond_table, w_ada, b_ada, w_qkv, q_gain, k_gain, w_proj, w_gate, w_up, w_down = weights
    count = block.shape[0]
    tokens = block.shape[1]
    cond_vec = matmul(onehot, cond_table)
    modulation = low_back(matmul(low(jax.nn.silu(cond_vec)), w_ada) + b_ada)
    shift_one, scale_one, gate_one, shift_two, scale_two, gate_two = jnp.split(modulation, 6, axis=-1)
    normed_one = low(rms_norm(block) * (1.0 + scale_one[:, None, :]) + shift_one[:, None, :])
    qkv = low_back(matmul(normed_one.reshape(-1, D), w_qkv)).reshape(count, tokens, 3, HEADS, HDIM)
    query = low(rotate(rms_norm(qkv[:, :, 0]) * q_gain, tables))
    key_rot = low(rotate(rms_norm(qkv[:, :, 1]) * k_gain, tables))
    value_low = low(qkv[:, :, 2])
    scores = low_back(jnp.einsum('bqhd,bkhd->bhqk', query, key_rot, precision=HIGH) * HDIM ** (-0.5))
    shifted = scores - lax.optimization_barrier(jnp.max(scores, axis=-1, keepdims=True))
    expo_scores = jnp.exp(shifted)
    probs = low(expo_scores / lax.optimization_barrier(jnp.sum(expo_scores, axis=-1, keepdims=True)))
    attended = jnp.einsum('bhqk,bkhd->bqhd', probs, value_low, precision=HIGH).reshape(count, tokens, D)
    attended = low(low_back(attended))
    proj = low_back(matmul(attended.reshape(-1, D), w_proj)).reshape(count, tokens, D)
    middle = block + gate_one[:, None, :] * proj
    normed_two = low(rms_norm(middle) * (1.0 + scale_two[:, None, :]) + shift_two[:, None, :]).reshape(-1, D)
    gate_pre = low_back(matmul(normed_two, w_gate))
    up_pre = low_back(matmul(normed_two, w_up))
    hidden = low(jax.nn.silu(gate_pre) * up_pre)
    mlp = low_back(matmul(hidden, w_down)).reshape(count, tokens, D)
    output = middle + gate_two[:, None, :] * mlp
    return output * live_mask[:, None, None]

def reference(patches, grad_out, cond_table, group_ids, live_count, band_order, w_ada, b_ada, w_qkv, q_gain, k_gain, w_proj, w_gate, w_up, w_down):
    slots = jnp.arange(GRID, dtype=jnp.int32)
    row_pos = jnp.take(band_order, slots // BAND_ROWS) * BAND_ROWS + slots % BAND_ROWS
    row_index = jnp.repeat(row_pos, GRID).astype(jnp.float32)
    col_index = jnp.tile(jnp.arange(GRID, dtype=jnp.int32), GRID).astype(jnp.float32)
    tables = rope_tables(row_index, col_index)
    image_ids = jnp.arange(IMAGES, dtype=jnp.int32)
    live_mask = (image_ids % IMG_CAP < jnp.take(live_count, image_ids // IMG_CAP)).astype(jnp.float32)
    onehot = (group_ids[:, None] == jnp.arange(GROUPS, dtype=jnp.int32)[None, :]).astype(jnp.float32)
    parameters = (cond_table.astype(jnp.float32), w_ada.astype(jnp.float32), b_ada.astype(jnp.float32), w_qkv.astype(jnp.float32), q_gain.astype(jnp.float32), k_gain.astype(jnp.float32), w_proj.astype(jnp.float32), w_gate.astype(jnp.float32), w_up.astype(jnp.float32), w_down.astype(jnp.float32))
    batch_size = math.gcd(IMAGES, max(1, 4096 // (GRID * GRID)))
    rounds = IMAGES // batch_size
    stacked = (patches.astype(jnp.float32).reshape(rounds, batch_size, GRID * GRID, D), grad_out.astype(jnp.float32).reshape(rounds, batch_size, GRID * GRID, D), onehot.reshape(rounds, batch_size, GROUPS), live_mask.reshape(rounds, batch_size))

    def scan_step(totals, item):
        patch_block, grad_block, onehot_block, mask_block = item

        def forward(block, *weights):
            return layer(block, weights, onehot_block, mask_block, tables)
        result, pull = jax.vjp(forward, patch_block, *parameters)
        grads = pull(grad_block)
        summed = tuple((total + fresh for total, fresh in zip(totals, grads[1:])))
        return (summed, (result, grads[0]))
    initial = tuple((jnp.zeros_like(weight) for weight in parameters))
    totals, (outputs, d_blocks) = lax.scan(scan_step, initial, stacked)
    patches_out = outputs.reshape(IMAGES, GRID, GRID, D).astype(jnp.bfloat16)
    d_patches = d_blocks.reshape(IMAGES, GRID, GRID, D)
    d_cond, d_ada, d_bias, d_qkv, d_qgain, d_kgain, d_proj, d_gate, d_up, d_down = totals
    return (patches_out, d_patches, d_cond, d_ada, d_bias, d_qkv, d_qgain, d_kgain, d_proj, d_gate, d_up, d_down)
```

```python
import jax
import jax.numpy as jnp
from jax import lax
from jax.sharding import PartitionSpec as P

HEADS = 16
HDIM = 72
GROUPS = 8


EPS = 1e-06


def rms_norm(values):
    return values * lax.rsqrt(jnp.mean(values * values, axis=-1, keepdims=True) + EPS)


def rope_tables(row_index, col_index):
    quarter = HDIM // 4
    frequency = 10000.0 ** (-jnp.arange(quarter, dtype=jnp.float32) / quarter)
    row_angle = (row_index[:, None] * frequency[None, :])[:, None, :]
    col_angle = (col_index[:, None] * frequency[None, :])[:, None, :]
    return (jnp.cos(row_angle), jnp.sin(row_angle), jnp.cos(col_angle), jnp.sin(col_angle))


def rotate(tensor, tables):
    quarter = tensor.shape[-1] // 4
    cos_row, sin_row, cos_col, sin_col = tables
    part_a = tensor[..., :quarter]
    part_b = tensor[..., quarter : 2 * quarter]
    part_c = tensor[..., 2 * quarter : 3 * quarter]
    part_d = tensor[..., 3 * quarter :]
    return jnp.concatenate(
        [
            part_a * cos_row - part_b * sin_row,
            part_a * sin_row + part_b * cos_row,
            part_c * cos_col - part_d * sin_col,
            part_c * sin_col + part_d * cos_col,
        ],
        axis=-1,
    )


def modulate(values, shift_in, scale_in):
    return rms_norm(values) * (1.0 + scale_in[:, None, :]) + shift_in[:, None, :]


def swiglu(gate_in, up_in):
    return jax.nn.silu(gate_in) * up_in


def split_heads(tensor, per_block):
    count, span, heads_all, size = tensor.shape
    groups = heads_all // per_block
    shaped = tensor.reshape(count, span, groups, per_block, size)
    return jnp.transpose(shaped, (0, 2, 1, 3, 4)).reshape(count * groups, span, per_block, size)


def join_heads(tensor, count):
    blocks, span, per_block, size = tensor.shape
    groups = blocks // count
    shaped = tensor.reshape(count, groups, span, per_block, size)
    return jnp.transpose(shaped, (0, 2, 1, 3, 4)).reshape(count, span, groups * per_block, size)


def body(
    patches,
    grad_out,
    cond_table,
    group_ids,
    live_count,
    band_order,
    w_ada,
    b_ada,
    w_qkv,
    q_gain,
    k_gain,
    w_proj,
    w_gate,
    w_up,
    w_down,
):
    images, rows, cols, width = patches.shape
    length = rows * cols
    score_scale = HDIM ** (-0.5)
    per_block = 4
    grp = lax.axis_index("grp")
    ada_rows = w_ada.shape[0]
    bias_cols = b_ada.shape[0]
    qkv_all = lax.all_gather(w_qkv, "grp", axis=0, tiled=True)
    proj_all = lax.all_gather(w_proj, "grp", axis=0, tiled=True)
    gate_all = lax.all_gather(w_gate, "grp", axis=0, tiled=True)
    up_all = lax.all_gather(w_up, "grp", axis=0, tiled=True)
    down_all = lax.all_gather(w_down, "grp", axis=0, tiled=True)
    onehot = (group_ids[:, None] == jnp.arange(GROUPS, dtype=jnp.int32)[None, :]).astype(
        jnp.float32
    )
    cond_rows = lax.dynamic_slice_in_dim(cond_table, grp * ada_rows, ada_rows, axis=1)
    silu_rows, silu_pull = jax.vjp(jax.nn.silu, cond_rows)
    silu_rows = silu_rows.astype(jnp.bfloat16)
    mod_part = jnp.dot(silu_rows, w_ada, preferred_element_type=jnp.float32)
    bias_part = lax.dynamic_update_slice_in_dim(
        jnp.zeros((mod_part.shape[1],), jnp.float32),
        b_ada.astype(jnp.float32),
        grp * bias_cols,
        axis=0,
    )
    mod_table = lax.psum(mod_part + bias_part[None, :], "grp")
    modulation = jnp.take(mod_table, group_ids, axis=0)
    shift_one, scale_one, gate_one, shift_two, scale_two, gate_two = jnp.split(
        modulation, 6, axis=-1
    )
    live_mask = (jnp.arange(images, dtype=jnp.int32) < live_count[0]).astype(jnp.float32)
    row_index = jnp.repeat(band_order[0] * rows + jnp.arange(rows, dtype=jnp.int32), cols).astype(
        jnp.float32
    )
    col_index = jnp.tile(jnp.arange(cols, dtype=jnp.int32), rows).astype(jnp.float32)
    tables = rope_tables(row_index, col_index)
    x_flat = patches.reshape(images, length, width).astype(jnp.float32)
    normed_one, norm_one_pull = jax.vjp(modulate, x_flat, shift_one, scale_one)
    normed_one_low = normed_one.astype(jnp.bfloat16).reshape(images * length, width)
    qkv = jnp.dot(normed_one_low, qkv_all, preferred_element_type=jnp.float32).reshape(
        images, length, 3, HEADS, HDIM
    )

    def query_key(query_raw, key_raw, query_gain, key_gain):
        return (
            rotate(rms_norm(query_raw) * query_gain, tables),
            rotate(rms_norm(key_raw) * key_gain, tables),
        )

    (query_rot, key_rot), qk_pull = jax.vjp(query_key, qkv[:, :, 0], qkv[:, :, 1], q_gain, k_gain)
    query_low = query_rot.astype(jnp.bfloat16)
    key_low = key_rot.astype(jnp.bfloat16).reshape(images, length, width)
    value_low = qkv[:, :, 2].astype(jnp.bfloat16).reshape(images, length, width)
    kv_local = jnp.concatenate([key_low, value_low], axis=-1)
    kv_rows = lax.all_gather(kv_local, "band", axis=1, tiled=True)
    query_blocks = split_heads(query_low, per_block)
    keys_all = kv_rows[..., :width].reshape(images, -1, HEADS, HDIM)
    values_all = kv_rows[..., width:].reshape(images, -1, HEADS, HDIM)
    key_blocks = split_heads(keys_all, per_block)
    value_blocks = split_heads(values_all, per_block)

    def forward_block(item):
        query_part, key_part, value_part = item
        scores = (
            jnp.einsum("qhd,khd->hqk", query_part, key_part, preferred_element_type=jnp.float32)
            * score_scale
        )
        top_score = jnp.max(scores, axis=-1, keepdims=True)
        expo_scores = jnp.exp(scores - top_score)
        total_weight = jnp.sum(expo_scores, axis=-1, keepdims=True)
        probs_low = (expo_scores / total_weight).astype(jnp.bfloat16)
        attended_part = jnp.einsum(
            "hqk,khd->qhd", probs_low, value_part, preferred_element_type=jnp.float32
        )
        return (attended_part.astype(jnp.bfloat16), top_score + jnp.log(total_weight))

    attended_blocks, log_blocks = lax.map(forward_block, (query_blocks, key_blocks, value_blocks))
    attended_low = join_heads(attended_blocks, images).reshape(images * length, width)
    proj = jnp.dot(attended_low, proj_all, preferred_element_type=jnp.float32).reshape(
        images, length, width
    )
    middle = x_flat + gate_one[:, None, :] * proj
    normed_two, norm_two_pull = jax.vjp(modulate, middle, shift_two, scale_two)
    normed_two_low = normed_two.astype(jnp.bfloat16).reshape(images * length, width)
    gate_pre = jnp.dot(normed_two_low, gate_all, preferred_element_type=jnp.float32)
    up_pre = jnp.dot(normed_two_low, up_all, preferred_element_type=jnp.float32)
    hidden, swiglu_pull = jax.vjp(swiglu, gate_pre, up_pre)
    hidden_low = hidden.astype(jnp.bfloat16)
    mlp = jnp.dot(hidden_low, down_all, preferred_element_type=jnp.float32).reshape(
        images, length, width
    )
    output = (middle + gate_two[:, None, :] * mlp) * live_mask[:, None, None]
    patches_out = output.astype(jnp.bfloat16).reshape(images, rows, cols, width)
    grad_y = grad_out.reshape(images, length, width).astype(jnp.float32) * live_mask[:, None, None]
    d_gate_two = jnp.sum(grad_y * mlp, axis=1)
    d_mlp = (grad_y * gate_two[:, None, :]).astype(jnp.bfloat16).reshape(images * length, width)
    d_w_down = jnp.einsum("tf,td->fd", hidden_low, d_mlp, preferred_element_type=jnp.float32)
    d_hidden = jnp.einsum("td,fd->tf", d_mlp, down_all, preferred_element_type=jnp.float32)
    d_gate_pre, d_up_pre = swiglu_pull(d_hidden)
    d_gate_low = d_gate_pre.astype(jnp.bfloat16)
    d_up_low = d_up_pre.astype(jnp.bfloat16)
    d_w_gate = jnp.einsum(
        "td,tf->df", normed_two_low, d_gate_low, preferred_element_type=jnp.float32
    )
    d_w_up = jnp.einsum("td,tf->df", normed_two_low, d_up_low, preferred_element_type=jnp.float32)
    d_normed_two = jnp.einsum("tf,df->td", d_gate_low, gate_all, preferred_element_type=jnp.float32)
    d_normed_two = d_normed_two + jnp.einsum(
        "tf,df->td", d_up_low, up_all, preferred_element_type=jnp.float32
    )
    d_middle_norm, d_shift_two, d_scale_two = norm_two_pull(
        d_normed_two.reshape(images, length, width)
    )
    d_middle = grad_y + d_middle_norm
    d_gate_one = jnp.sum(d_middle * proj, axis=1)
    d_proj = (d_middle * gate_one[:, None, :]).astype(jnp.bfloat16).reshape(images * length, width)
    d_w_proj = jnp.einsum("td,te->de", attended_low, d_proj, preferred_element_type=jnp.float32)
    d_attended = jnp.einsum("te,de->td", d_proj, proj_all, preferred_element_type=jnp.float32)
    d_attended = d_attended.astype(jnp.bfloat16).reshape(images, length, HEADS, HDIM)
    d_att_blocks = split_heads(d_attended, per_block)

    def backward_block(item):
        query_part, key_part, value_part, d_att_part, log_part = item
        scores = (
            jnp.einsum("qhd,khd->hqk", query_part, key_part, preferred_element_type=jnp.float32)
            * score_scale
        )
        probs = jnp.exp(scores - log_part)
        probs_low = probs.astype(jnp.bfloat16)
        d_probs = jnp.einsum(
            "qhd,khd->hqk", d_att_part, value_part, preferred_element_type=jnp.float32
        )
        row_delta = jnp.sum(probs * d_probs, axis=-1, keepdims=True)
        d_scores = (probs * (d_probs - row_delta)).astype(jnp.bfloat16)
        d_query_part = (
            jnp.einsum("hqk,khd->qhd", d_scores, key_part, preferred_element_type=jnp.float32)
            * score_scale
        )
        key_grad = (
            jnp.einsum("hqk,qhd->khd", d_scores, query_part, preferred_element_type=jnp.float32)
            * score_scale
        )
        value_grad = jnp.einsum(
            "hqk,qhd->khd", probs_low, d_att_part, preferred_element_type=jnp.float32
        )
        return (d_query_part, key_grad, value_grad)

    query_grads, key_grads, value_grads = lax.map(
        backward_block, (query_blocks, key_blocks, value_blocks, d_att_blocks, log_blocks)
    )
    d_query = join_heads(query_grads, images)
    key_terms = join_heads(key_grads, images).reshape(images, -1, width)
    value_terms = join_heads(value_grads, images).reshape(images, -1, width)
    kv_terms = jnp.concatenate([key_terms, value_terms], axis=-1)
    kv_grad = lax.psum_scatter(
        kv_terms.astype(jnp.bfloat16), "band", scatter_dimension=1, tiled=True
    ).astype(jnp.float32)
    d_key = kv_grad[..., :width].reshape(images, length, HEADS, HDIM)
    d_value = kv_grad[..., width:]
    d_query_raw, d_key_raw, d_q_gain, d_k_gain = qk_pull((d_query, d_key))
    d_qkv = jnp.concatenate(
        [
            d_query_raw.reshape(images, length, width),
            d_key_raw.reshape(images, length, width),
            d_value,
        ],
        axis=-1,
    )
    d_qkv = d_qkv.astype(jnp.bfloat16).reshape(images * length, 3 * width)
    d_w_qkv = jnp.einsum("td,te->de", normed_one_low, d_qkv, preferred_element_type=jnp.float32)
    d_normed_one = jnp.einsum("te,de->td", d_qkv, qkv_all, preferred_element_type=jnp.float32)
    d_x_norm, d_shift_one, d_scale_one = norm_one_pull(d_normed_one.reshape(images, length, width))
    d_patches = (d_middle + d_x_norm).reshape(images, rows, cols, width)
    d_mod_part = jnp.concatenate(
        [d_shift_one, d_scale_one, d_gate_one, d_shift_two, d_scale_two, d_gate_two], axis=-1
    )
    d_modulation = lax.psum(d_mod_part, "band").astype(jnp.bfloat16)
    payload = jnp.concatenate([d_modulation, onehot.astype(jnp.bfloat16)], axis=-1)
    payload = lax.all_gather(payload, "grp", axis=0, tiled=True)
    d_mod_all = payload[:, : d_modulation.shape[1]]
    onehot_all = payload[:, d_modulation.shape[1] :]
    silu_all = jnp.dot(onehot_all, silu_rows, preferred_element_type=jnp.float32).astype(
        jnp.bfloat16
    )
    d_w_ada = jnp.einsum("bd,be->de", silu_all, d_mod_all, preferred_element_type=jnp.float32)
    d_b_ada = lax.dynamic_slice_in_dim(
        jnp.sum(d_mod_all.astype(jnp.float32), axis=0), grp * bias_cols, bias_cols, axis=0
    )
    d_silu = jnp.einsum("be,de->bd", d_mod_all, w_ada, preferred_element_type=jnp.float32)
    d_silu = jnp.dot(
        onehot_all.astype(jnp.float32).T,
        d_silu,
        precision=lax.Precision.HIGHEST,
        preferred_element_type=jnp.float32,
    )
    d_cond_rows = silu_pull(d_silu)[0]
    d_cond = lax.all_gather(d_cond_rows, "grp", axis=1, tiled=True)
    d_q_gain, d_k_gain = lax.psum((d_q_gain, d_k_gain), ("grp", "band"))

    def spread(grad):
        shard = lax.psum_scatter(
            grad.astype(jnp.bfloat16), "grp", scatter_dimension=0, tiled=True
        )
        return lax.psum(shard, "band").astype(jnp.float32)

    return (
        patches_out,
        d_patches,
        d_cond,
        d_w_ada,
        d_b_ada,
        spread(d_w_qkv),
        d_q_gain,
        d_k_gain,
        spread(d_w_proj),
        spread(d_w_gate),
        spread(d_w_up),
        spread(d_w_down),
    )


def solution(mesh):
    in_specs = (
        P("grp", "band", None, None),
        P("grp", "band", None, None),
        P(),
        P("grp"),
        P("grp"),
        P("band"),
        P("grp", None),
        P("grp"),
        P("grp", None),
        P(),
        P(),
        P("grp", None),
        P("grp", None),
        P("grp", None),
        P("grp", None),
    )
    out_specs = (
        P("grp", "band", None, None),
        P("grp", "band", None, None),
        P(),
        P("grp", None),
        P("grp"),
        P("grp", None),
        P(),
        P(),
        P("grp", None),
        P("grp", None),
        P("grp", None),
        P("grp", None),
    )
    return jax.shard_map(body, mesh=mesh, in_specs=in_specs, out_specs=out_specs, check_vma=False)
```

```python
import functools

import jax
import jax.numpy as jnp
from jax import lax
from jax.experimental import pallas as pl
from jax.experimental.pallas import tpu as pltpu
from jax.sharding import PartitionSpec as P

MESH = pl.DeviceIdType.MESH

def gather_kernel(cuts, when_own, *refs):
    n = len(cuts)
    ins, outs = refs[:n], refs[n:2*n]
    lsem, zs, zr, xs, xr, ys, yr, cs, cr, ds, dr = refs[2*n:]
    g = lax.axis_index("grp"); band = lax.axis_index("band")
    z = g // 2; x = g % 2; y = band // 2; c = band % 2
    far = [z, z + 1 - 2 * (z % 2), 2 - z // 2, 3 - 3 * (z // 2)]
    ypeer = (g, (1 - y) * 2 + c); cpeer = (g, y * 2 + 1 - c); xpeer = (z * 2 + 1 - x, band)
    bar = pltpu.get_barrier_semaphore()
    for d in [xpeer, ypeer, cpeer] + [(zz * 2 + x, band) for zz in far[1:]]:
        pl.semaphore_signal(bar, inc=1, device_id=d, device_id_type=MESH)
    pl.semaphore_wait(bar, 6)
    def at(ref, shard, axis, start, size):
        ref = ref if shard is None else ref.at[shard]
        if axis == 0:
            return ref.at[pl.ds(pl.multiple_of(start, 16), size), :]
        return ref.at[:, pl.ds(pl.multiple_of(start, 128), size)]
    def piece(i, ref, shard, yy, cc):
        axis, half, a, b = cuts[i]
        return at(ref, shard, axis, cc * half + yy * b, a + b)
    def bpart(i, ref, shard, yy, cc):
        axis, half, a, b = cuts[i]
        return at(ref, shard, axis, cc * half + yy * (a + b), b)
    tail = []
    def send(src, dst, ssem, rsem, dev, cond=None):
        d = pltpu.make_async_remote_copy(src_ref=src, dst_ref=dst, send_sem=ssem, recv_sem=rsem, device_id=dev, device_id_type=MESH)
        if cond is None:
            d.start(); tail.append(d.wait_send)
        else:
            pl.when(cond)(d.start); tail.append(lambda: pl.when(cond)(d.wait_send))
    def arrived(ref, rsem):
        pltpu.make_async_remote_copy(src_ref=ref, dst_ref=ref, send_sem=lsem.at[0], recv_sem=rsem, device_id=xpeer, device_id_type=MESH).wait_recv()
    def own(i):
        src, dst = piece(i, ins[i], None, y, c), piece(i, outs[i], g, y, c)
        send(src, dst, zs.at[i, 0], zr.at[i, z], (g + 2, band), z < 3)
        send(src, dst, ds.at[i], zr.at[i, z], (g - 2, band), z > 0)
        send(src, dst, xs.at[i, 0], xr.at[i, 0], xpeer)
        d = pltpu.make_async_copy(ins[i], outs[i].at[g], lsem.at[i]); d.start(); tail.append(d.wait)
    def down(i, slot, shard):
        p = bpart(i, outs[i], shard, y, c)
        send(p, p, ys.at[i, slot], yr.at[i, slot], ypeer)
        p = piece(i, outs[i], shard, y, c)
        send(p, p, cs.at[i, slot], cr.at[i, slot], cpeer)
    def zarr(i, t):
        zz = far[t]
        s = zz * 2 + x
        p = piece(i, outs[i], s, y, c)
        arrived(p, zr.at[i, zz])
        nxt = jnp.where(zz < z, z + 1, z - 1)
        send(p, p, zs.at[i, t], zr.at[i, zz], (jnp.clip(nxt, 0, 3) * 2 + x, band), (nxt >= 0) & (nxt <= 3))
        send(p, p, xs.at[i, t], xr.at[i, t], xpeer)
        down(i, t - 1, s)
    def xarr(i, t):
        s = far[t] * 2 + 1 - x
        arrived(piece(i, outs[i], s, y, c), xr.at[i, t])
        down(i, 3 + t, s)
    def slots():
        return [(t - 1, far[t] * 2 + x) for t in (1, 2, 3)] + [(3 + t, far[t] * 2 + 1 - x) for t in range(4)]
    def yarr(i, slot, s):
        p = bpart(i, outs[i], s, 1 - y, c)
        arrived(p, yr.at[i, slot])
        send(p, p, cs.at[i, 7 + slot], cr.at[i, 7 + slot], cpeer)
    acts = []
    order = [3, 0, 4, 1, 5, 2, 6]
    for i in range(n):
        if i == 0:
            acts.append(lambda: own(0))
        seq = [lambda i=i: zarr(i, 1), lambda i=i: xarr(i, 0), lambda i=i: zarr(i, 2), lambda i=i: xarr(i, 1), lambda i=i: zarr(i, 3), lambda i=i: xarr(i, 2), lambda i=i: xarr(i, 3)]
        if i + 1 < n:
            seq.insert(when_own, lambda i=i: own(i + 1))
        sl = slots()
        if i > 0:
            for q in range(7):
                seq.insert(2 * q + 1, lambda i=i, q=q: yarr(i - 1, *sl[order[q]]))
        acts += seq
    sl = slots()
    acts += [lambda q=q: yarr(n - 1, *sl[order[q]]) for q in range(7)]
    for a in acts:
        a()
    for i in range(n):
        for slot, s in sl:
            arrived(piece(i, outs[i], s, y, 1 - c), cr.at[i, slot])
            arrived(bpart(i, outs[i], s, 1 - y, 1 - c), cr.at[i, 7 + slot])
    for w in tail:
        w()

def gather(ws, cuts, cid=0, when_own=3):
    n = len(ws)
    S = pltpu.SemaphoreType.DMA
    return pl.pallas_call(
        functools.partial(gather_kernel, cuts, when_own),
        out_shape=[jax.ShapeDtypeStruct((8,) + w.shape, w.dtype) for w in ws],
        in_specs=[pl.BlockSpec(memory_space=pl.ANY)] * n,
        out_specs=[pl.BlockSpec(memory_space=pl.ANY)] * n,
        scratch_shapes=[S((n,)), S((n, 4)), S((n, 4)), S((n, 4)), S((n, 4)), S((n, 7)), S((n, 7)), S((n, 14)), S((n, 14)), S((n,)), S((n,))],
        compiler_params=pltpu.CompilerParams(collective_id=cid, has_side_effects=True),
        name="weight_gather",
    )(*ws)

HEADS = 16
HDIM = 72
GROUPS = 8


EPS = 1e-06


def rms_norm(values):
    return values * lax.rsqrt(jnp.mean(values * values, axis=-1, keepdims=True) + EPS)


def rope_tables(row_index, col_index):
    quarter = HDIM // 4
    frequency = 10000.0 ** (-jnp.arange(quarter, dtype=jnp.float32) / quarter)
    row_angle = (row_index[:, None] * frequency[None, :])[:, None, :]
    col_angle = (col_index[:, None] * frequency[None, :])[:, None, :]
    return (jnp.cos(row_angle), jnp.sin(row_angle), jnp.cos(col_angle), jnp.sin(col_angle))


def rotate(tensor, tables):
    quarter = tensor.shape[-1] // 4
    cos_row, sin_row, cos_col, sin_col = tables
    part_a = tensor[..., :quarter]
    part_b = tensor[..., quarter : 2 * quarter]
    part_c = tensor[..., 2 * quarter : 3 * quarter]
    part_d = tensor[..., 3 * quarter :]
    return jnp.concatenate(
        [
            part_a * cos_row - part_b * sin_row,
            part_a * sin_row + part_b * cos_row,
            part_c * cos_col - part_d * sin_col,
            part_c * sin_col + part_d * cos_col,
        ],
        axis=-1,
    )


def modulate(values, shift_in, scale_in):
    return rms_norm(values) * (1.0 + scale_in[:, None, :]) + shift_in[:, None, :]


def swiglu(gate_in, up_in):
    return jax.nn.silu(gate_in) * up_in


def split_heads(tensor, per_block):
    count, span, heads_all, size = tensor.shape
    groups = heads_all // per_block
    shaped = tensor.reshape(count, span, groups, per_block, size)
    return jnp.transpose(shaped, (0, 2, 1, 3, 4)).reshape(count * groups, span, per_block, size)


def join_heads(tensor, count):
    blocks, span, per_block, size = tensor.shape
    groups = blocks // count
    shaped = tensor.reshape(count, groups, span, per_block, size)
    return jnp.transpose(shaped, (0, 2, 1, 3, 4)).reshape(count, span, groups * per_block, size)


def half_cuts(axis, size, own_parts, shared_parts):
    unit = size // 2 // (own_parts + 2 * shared_parts)
    return (axis, size // 2, own_parts * unit, shared_parts * unit)


def gather_weights(shards):
    rows, wide = shards[0].shape
    fits = (
        lax.axis_size("grp") == 8
        and lax.axis_size("band") == 4
        and rows % 16 == 0
        and shards[2].shape[0] % 96 == 0
        and wide % 768 == 0
        and shards[1].shape[1] % 768 == 0
    )
    if not fits:
        return [lax.all_gather(w, "grp", axis=0, tiled=True) for w in shards]
    cuts = (
        half_cuts(1, wide, 1, 1),
        half_cuts(1, shards[1].shape[1], 1, 1),
        half_cuts(0, shards[2].shape[0], 1, 1),
    )
    full = gather(shards, cuts)
    return [w.reshape(-1, w.shape[-1]) for w in full]


def body(
    patches,
    grad_out,
    cond_table,
    group_ids,
    live_count,
    band_order,
    w_ada,
    b_ada,
    w_qkv,
    q_gain,
    k_gain,
    w_proj,
    w_gate,
    w_up,
    w_down,
):
    images, rows, cols, width = patches.shape
    length = rows * cols
    score_scale = HDIM ** (-0.5)
    per_block = 4
    grp = lax.axis_index("grp")
    ada_rows = w_ada.shape[0]
    bias_cols = b_ada.shape[0]
    shards = (
        jnp.concatenate([w_qkv, w_proj], axis=1),
        jnp.concatenate([w_gate, w_up], axis=1),
        w_down,
    )
    qp_all, gu_all, down_all = gather_weights(shards)
    qkv_all, proj_all = qp_all[:, : w_qkv.shape[1]], qp_all[:, w_qkv.shape[1] :]
    gate_all, up_all = gu_all[:, : w_gate.shape[1]], gu_all[:, w_gate.shape[1] :]
    onehot = (group_ids[:, None] == jnp.arange(GROUPS, dtype=jnp.int32)[None, :]).astype(
        jnp.float32
    )
    cond_rows = lax.dynamic_slice_in_dim(cond_table, grp * ada_rows, ada_rows, axis=1)
    silu_rows, silu_pull = jax.vjp(jax.nn.silu, cond_rows)
    silu_rows = silu_rows.astype(jnp.bfloat16)
    mod_part = jnp.dot(silu_rows, w_ada, preferred_element_type=jnp.float32)
    bias_part = lax.dynamic_update_slice_in_dim(
        jnp.zeros((mod_part.shape[1],), jnp.float32),
        b_ada.astype(jnp.float32),
        grp * bias_cols,
        axis=0,
    )
    mod_table = lax.psum(mod_part + bias_part[None, :], "grp")
    modulation = jnp.take(mod_table, group_ids, axis=0)
    shift_one, scale_one, gate_one, shift_two, scale_two, gate_two = jnp.split(
        modulation, 6, axis=-1
    )
    live_mask = (jnp.arange(images, dtype=jnp.int32) < live_count[0]).astype(jnp.float32)
    row_index = jnp.repeat(band_order[0] * rows + jnp.arange(rows, dtype=jnp.int32), cols).astype(
        jnp.float32
    )
    col_index = jnp.tile(jnp.arange(cols, dtype=jnp.int32), rows).astype(jnp.float32)
    tables = rope_tables(row_index, col_index)
    x_flat = patches.reshape(images, length, width).astype(jnp.float32)
    normed_one, norm_one_pull = jax.vjp(modulate, x_flat, shift_one, scale_one)
    normed_one_low = normed_one.astype(jnp.bfloat16).reshape(images * length, width)
    qkv = jnp.dot(normed_one_low, qkv_all, preferred_element_type=jnp.float32).reshape(
        images, length, 3, HEADS, HDIM
    )

    def query_key(query_raw, key_raw, query_gain, key_gain):
        return (
            rotate(rms_norm(query_raw) * query_gain, tables),
            rotate(rms_norm(key_raw) * key_gain, tables),
        )

    (query_rot, key_rot), qk_pull = jax.vjp(query_key, qkv[:, :, 0], qkv[:, :, 1], q_gain, k_gain)
    query_low = query_rot.astype(jnp.bfloat16)
    key_low = key_rot.astype(jnp.bfloat16).reshape(images, length, width)
    value_low = qkv[:, :, 2].astype(jnp.bfloat16).reshape(images, length, width)
    kv_local = jnp.concatenate([key_low, value_low], axis=-1)
    kv_rows = lax.all_gather(kv_local, "band", axis=1, tiled=True)
    query_blocks = split_heads(query_low, per_block)
    keys_all = kv_rows[..., :width].reshape(images, -1, HEADS, HDIM)
    values_all = kv_rows[..., width:].reshape(images, -1, HEADS, HDIM)
    key_blocks = split_heads(keys_all, per_block)
    value_blocks = split_heads(values_all, per_block)

    def forward_block(item):
        query_part, key_part, value_part = item
        scores = (
            jnp.einsum("qhd,khd->hqk", query_part, key_part, preferred_element_type=jnp.float32)
            * score_scale
        )
        top_score = jnp.max(scores, axis=-1, keepdims=True)
        expo_scores = jnp.exp(scores - top_score)
        total_weight = jnp.sum(expo_scores, axis=-1, keepdims=True)
        probs_low = (expo_scores / total_weight).astype(jnp.bfloat16)
        attended_part = jnp.einsum(
            "hqk,khd->qhd", probs_low, value_part, preferred_element_type=jnp.float32
        )
        return (attended_part.astype(jnp.bfloat16), top_score + jnp.log(total_weight))

    attended_blocks, log_blocks = lax.map(forward_block, (query_blocks, key_blocks, value_blocks))
    attended_low = join_heads(attended_blocks, images).reshape(images * length, width)
    proj = jnp.dot(attended_low, proj_all, preferred_element_type=jnp.float32).reshape(
        images, length, width
    )
    middle = x_flat + gate_one[:, None, :] * proj
    normed_two, norm_two_pull = jax.vjp(modulate, middle, shift_two, scale_two)
    normed_two_low = normed_two.astype(jnp.bfloat16).reshape(images * length, width)
    gate_pre = jnp.dot(normed_two_low, gate_all, preferred_element_type=jnp.float32)
    up_pre = jnp.dot(normed_two_low, up_all, preferred_element_type=jnp.float32)
    hidden, swiglu_pull = jax.vjp(swiglu, gate_pre, up_pre)
    hidden_low = hidden.astype(jnp.bfloat16)
    mlp = jnp.dot(hidden_low, down_all, preferred_element_type=jnp.float32).reshape(
        images, length, width
    )
    output = (middle + gate_two[:, None, :] * mlp) * live_mask[:, None, None]
    patches_out = output.astype(jnp.bfloat16).reshape(images, rows, cols, width)
    grad_y = grad_out.reshape(images, length, width).astype(jnp.float32) * live_mask[:, None, None]
    d_gate_two = jnp.sum(grad_y * mlp, axis=1)
    d_mlp = (grad_y * gate_two[:, None, :]).astype(jnp.bfloat16).reshape(images * length, width)
    d_w_down = jnp.einsum("tf,td->fd", hidden_low, d_mlp, preferred_element_type=jnp.float32)
    d_hidden = jnp.einsum("td,fd->tf", d_mlp, down_all, preferred_element_type=jnp.float32)
    d_gate_pre, d_up_pre = swiglu_pull(d_hidden)
    d_gate_low = d_gate_pre.astype(jnp.bfloat16)
    d_up_low = d_up_pre.astype(jnp.bfloat16)
    d_w_gate = jnp.einsum(
        "td,tf->df", normed_two_low, d_gate_low, preferred_element_type=jnp.float32
    )
    d_w_up = jnp.einsum("td,tf->df", normed_two_low, d_up_low, preferred_element_type=jnp.float32)
    d_normed_two = jnp.einsum("tf,df->td", d_gate_low, gate_all, preferred_element_type=jnp.float32)
    d_normed_two = d_normed_two + jnp.einsum(
        "tf,df->td", d_up_low, up_all, preferred_element_type=jnp.float32
    )
    d_middle_norm, d_shift_two, d_scale_two = norm_two_pull(
        d_normed_two.reshape(images, length, width)
    )
    d_middle = grad_y + d_middle_norm
    d_gate_one = jnp.sum(d_middle * proj, axis=1)
    d_proj = (d_middle * gate_one[:, None, :]).astype(jnp.bfloat16).reshape(images * length, width)
    d_w_proj = jnp.einsum("td,te->de", attended_low, d_proj, preferred_element_type=jnp.float32)
    d_attended = jnp.einsum("te,de->td", d_proj, proj_all, preferred_element_type=jnp.float32)
    d_attended = d_attended.astype(jnp.bfloat16).reshape(images, length, HEADS, HDIM)
    d_att_blocks = split_heads(d_attended, per_block)

    def backward_block(item):
        query_part, key_part, value_part, d_att_part, log_part = item
        scores = (
            jnp.einsum("qhd,khd->hqk", query_part, key_part, preferred_element_type=jnp.float32)
            * score_scale
        )
        probs = jnp.exp(scores - log_part)
        probs_low = probs.astype(jnp.bfloat16)
        d_probs = jnp.einsum(
            "qhd,khd->hqk", d_att_part, value_part, preferred_element_type=jnp.float32
        )
        row_delta = jnp.sum(probs * d_probs, axis=-1, keepdims=True)
        d_scores = (probs * (d_probs - row_delta)).astype(jnp.bfloat16)
        d_query_part = (
            jnp.einsum("hqk,khd->qhd", d_scores, key_part, preferred_element_type=jnp.float32)
            * score_scale
        )
        key_grad = (
            jnp.einsum("hqk,qhd->khd", d_scores, query_part, preferred_element_type=jnp.float32)
            * score_scale
        )
        value_grad = jnp.einsum(
            "hqk,qhd->khd", probs_low, d_att_part, preferred_element_type=jnp.float32
        )
        return (d_query_part, key_grad, value_grad)

    query_grads, key_grads, value_grads = lax.map(
        backward_block, (query_blocks, key_blocks, value_blocks, d_att_blocks, log_blocks)
    )
    d_query = join_heads(query_grads, images)
    key_terms = join_heads(key_grads, images).reshape(images, -1, width)
    value_terms = join_heads(value_grads, images).reshape(images, -1, width)
    kv_terms = jnp.concatenate([key_terms, value_terms], axis=-1)
    kv_grad = lax.psum_scatter(
        kv_terms.astype(jnp.bfloat16), "band", scatter_dimension=1, tiled=True
    ).astype(jnp.float32)
    d_key = kv_grad[..., :width].reshape(images, length, HEADS, HDIM)
    d_value = kv_grad[..., width:]
    d_query_raw, d_key_raw, d_q_gain, d_k_gain = qk_pull((d_query, d_key))
    d_qkv = jnp.concatenate(
        [
            d_query_raw.reshape(images, length, width),
            d_key_raw.reshape(images, length, width),
            d_value,
        ],
        axis=-1,
    )
    d_qkv = d_qkv.astype(jnp.bfloat16).reshape(images * length, 3 * width)
    d_w_qkv = jnp.einsum("td,te->de", normed_one_low, d_qkv, preferred_element_type=jnp.float32)
    d_normed_one = jnp.einsum("te,de->td", d_qkv, qkv_all, preferred_element_type=jnp.float32)
    d_x_norm, d_shift_one, d_scale_one = norm_one_pull(d_normed_one.reshape(images, length, width))
    d_patches = (d_middle + d_x_norm).reshape(images, rows, cols, width)
    d_mod_part = jnp.concatenate(
        [d_shift_one, d_scale_one, d_gate_one, d_shift_two, d_scale_two, d_gate_two], axis=-1
    )
    d_modulation = lax.psum(d_mod_part, "band").astype(jnp.bfloat16)
    payload = jnp.concatenate([d_modulation, onehot.astype(jnp.bfloat16)], axis=-1)
    payload = lax.all_gather(payload, "grp", axis=0, tiled=True)
    d_mod_all = payload[:, : d_modulation.shape[1]]
    onehot_all = payload[:, d_modulation.shape[1] :]
    silu_all = jnp.dot(onehot_all, silu_rows, preferred_element_type=jnp.float32).astype(
        jnp.bfloat16
    )
    d_w_ada = jnp.einsum("bd,be->de", silu_all, d_mod_all, preferred_element_type=jnp.float32)
    d_b_ada = lax.dynamic_slice_in_dim(
        jnp.sum(d_mod_all.astype(jnp.float32), axis=0), grp * bias_cols, bias_cols, axis=0
    )
    d_silu = jnp.einsum("be,de->bd", d_mod_all, w_ada, preferred_element_type=jnp.float32)
    d_silu = jnp.dot(
        onehot_all.astype(jnp.float32).T,
        d_silu,
        precision=lax.Precision.HIGHEST,
        preferred_element_type=jnp.float32,
    )
    d_cond_rows = silu_pull(d_silu)[0]
    d_cond = lax.all_gather(d_cond_rows, "grp", axis=1, tiled=True)
    d_q_gain, d_k_gain = lax.psum((d_q_gain, d_k_gain), ("grp", "band"))

    def spread(grad):
        shard = lax.psum_scatter(
            grad.astype(jnp.bfloat16), "grp", scatter_dimension=0, tiled=True
        )
        return lax.psum(shard, "band").astype(jnp.float32)

    return (
        patches_out,
        d_patches,
        d_cond,
        d_w_ada,
        d_b_ada,
        spread(d_w_qkv),
        d_q_gain,
        d_k_gain,
        spread(d_w_proj),
        spread(d_w_gate),
        spread(d_w_up),
        spread(d_w_down),
    )


def solution(mesh):
    in_specs = (
        P("grp", "band", None, None),
        P("grp", "band", None, None),
        P(),
        P("grp"),
        P("grp"),
        P("band"),
        P("grp", None),
        P("grp"),
        P("grp", None),
        P(),
        P(),
        P("grp", None),
        P("grp", None),
        P("grp", None),
        P("grp", None),
    )
    out_specs = (
        P("grp", "band", None, None),
        P("grp", "band", None, None),
        P(),
        P("grp", None),
        P("grp"),
        P("grp", None),
        P(),
        P(),
        P("grp", None),
        P("grp", None),
        P("grp", None),
        P("grp", None),
    )
    return jax.shard_map(body, mesh=mesh, in_specs=in_specs, out_specs=out_specs, check_vma=False)
```

```python
import functools

import jax
import jax.numpy as jnp
from jax import lax
from jax.experimental import pallas as pl
from jax.experimental.pallas import tpu as pltpu
from jax.sharding import PartitionSpec as P

MESH = pl.DeviceIdType.MESH

def gather_kernel(cuts, when_own, *refs):
    n = len(cuts)
    ins, outs = refs[:n], refs[n:2*n]
    lsem, zs, zr, xs, xr, ys, yr, cs, cr, ds, dr = refs[2*n:]
    g = lax.axis_index("grp"); band = lax.axis_index("band")
    z = g // 2; x = g % 2; y = band // 2; c = band % 2
    far = [z, z + 1 - 2 * (z % 2), 2 - z // 2, 3 - 3 * (z // 2)]
    ypeer = (g, (1 - y) * 2 + c); cpeer = (g, y * 2 + 1 - c); xpeer = (z * 2 + 1 - x, band)
    bar = pltpu.get_barrier_semaphore()
    for d in [xpeer, ypeer, cpeer] + [(zz * 2 + x, band) for zz in far[1:]]:
        pl.semaphore_signal(bar, inc=1, device_id=d, device_id_type=MESH)
    pl.semaphore_wait(bar, 6)
    def at(ref, shard, axis, start, size):
        ref = ref if shard is None else ref.at[shard]
        if axis == 0:
            return ref.at[pl.ds(pl.multiple_of(start, 16), size), :]
        return ref.at[:, pl.ds(pl.multiple_of(start, 128), size)]
    def piece(i, ref, shard, yy, cc):
        axis, half, a, b = cuts[i]
        return at(ref, shard, axis, cc * half + yy * b, a + b)
    def bpart(i, ref, shard, yy, cc):
        axis, half, a, b = cuts[i]
        return at(ref, shard, axis, cc * half + yy * (a + b), b)
    tail = []
    def send(src, dst, ssem, rsem, dev, cond=None):
        d = pltpu.make_async_remote_copy(src_ref=src, dst_ref=dst, send_sem=ssem, recv_sem=rsem, device_id=dev, device_id_type=MESH)
        if cond is None:
            d.start(); tail.append(d.wait_send)
        else:
            pl.when(cond)(d.start); tail.append(lambda: pl.when(cond)(d.wait_send))
    def arrived(ref, rsem):
        pltpu.make_async_remote_copy(src_ref=ref, dst_ref=ref, send_sem=lsem.at[0], recv_sem=rsem, device_id=xpeer, device_id_type=MESH).wait_recv()
    def own(i):
        src, dst = piece(i, ins[i], None, y, c), piece(i, outs[i], g, y, c)
        send(src, dst, zs.at[i, 0], zr.at[i, z], (g + 2, band), z < 3)
        send(src, dst, ds.at[i], zr.at[i, z], (g - 2, band), z > 0)
        send(src, dst, xs.at[i, 0], xr.at[i, 0], xpeer)
        d = pltpu.make_async_copy(ins[i], outs[i].at[g], lsem.at[i]); d.start(); tail.append(d.wait)
    def down(i, slot, shard):
        p = bpart(i, outs[i], shard, y, c)
        send(p, p, ys.at[i, slot], yr.at[i, slot], ypeer)
        p = piece(i, outs[i], shard, y, c)
        send(p, p, cs.at[i, slot], cr.at[i, slot], cpeer)
    def zarr(i, t):
        zz = far[t]
        s = zz * 2 + x
        p = piece(i, outs[i], s, y, c)
        arrived(p, zr.at[i, zz])
        nxt = jnp.where(zz < z, z + 1, z - 1)
        send(p, p, zs.at[i, t], zr.at[i, zz], (jnp.clip(nxt, 0, 3) * 2 + x, band), (nxt >= 0) & (nxt <= 3))
        send(p, p, xs.at[i, t], xr.at[i, t], xpeer)
        down(i, t - 1, s)
    def xarr(i, t):
        s = far[t] * 2 + 1 - x
        arrived(piece(i, outs[i], s, y, c), xr.at[i, t])
        down(i, 3 + t, s)
    def slots():
        return [(t - 1, far[t] * 2 + x) for t in (1, 2, 3)] + [(3 + t, far[t] * 2 + 1 - x) for t in range(4)]
    def yarr(i, slot, s):
        p = bpart(i, outs[i], s, 1 - y, c)
        arrived(p, yr.at[i, slot])
        send(p, p, cs.at[i, 7 + slot], cr.at[i, 7 + slot], cpeer)
    acts = []
    order = [3, 0, 4, 1, 5, 2, 6]
    for i in range(n):
        if i == 0:
            acts.append(lambda: own(0))
        seq = [lambda i=i: zarr(i, 1), lambda i=i: xarr(i, 0), lambda i=i: zarr(i, 2), lambda i=i: xarr(i, 1), lambda i=i: zarr(i, 3), lambda i=i: xarr(i, 2), lambda i=i: xarr(i, 3)]
        if i + 1 < n:
            seq.insert(when_own, lambda i=i: own(i + 1))
        sl = slots()
        if i > 0:
            for q in range(7):
                seq.insert(2 * q + 1, lambda i=i, q=q: yarr(i - 1, *sl[order[q]]))
        acts += seq
    sl = slots()
    acts += [lambda q=q: yarr(n - 1, *sl[order[q]]) for q in range(7)]
    for a in acts:
        a()
    for i in range(n):
        for slot, s in sl:
            arrived(piece(i, outs[i], s, y, 1 - c), cr.at[i, slot])
            arrived(bpart(i, outs[i], s, 1 - y, 1 - c), cr.at[i, 7 + slot])
    for w in tail:
        w()

def gather(ws, cuts, cid=0, when_own=3):
    n = len(ws)
    S = pltpu.SemaphoreType.DMA
    return pl.pallas_call(
        functools.partial(gather_kernel, cuts, when_own),
        out_shape=[jax.ShapeDtypeStruct((8,) + w.shape, w.dtype) for w in ws],
        in_specs=[pl.BlockSpec(memory_space=pl.ANY)] * n,
        out_specs=[pl.BlockSpec(memory_space=pl.ANY)] * n,
        scratch_shapes=[S((n,)), S((n, 4)), S((n, 4)), S((n, 4)), S((n, 4)), S((n, 7)), S((n, 7)), S((n, 14)), S((n, 14)), S((n,)), S((n,))],
        compiler_params=pltpu.CompilerParams(collective_id=cid, has_side_effects=True),
        name="weight_gather",
    )(*ws)

HEADS = 16
HDIM = 72
GROUPS = 8


EPS = 1e-06


def rms_norm(values):
    return values * lax.rsqrt(jnp.mean(values * values, axis=-1, keepdims=True) + EPS)


def rope_tables(row_index, col_index):
    quarter = HDIM // 4
    frequency = 10000.0 ** (-jnp.arange(quarter, dtype=jnp.float32) / quarter)
    row_angle = (row_index[:, None] * frequency[None, :])[:, None, :]
    col_angle = (col_index[:, None] * frequency[None, :])[:, None, :]
    return (jnp.cos(row_angle), jnp.sin(row_angle), jnp.cos(col_angle), jnp.sin(col_angle))


def rotate(tensor, tables):
    quarter = tensor.shape[-1] // 4
    cos_row, sin_row, cos_col, sin_col = tables
    part_a = tensor[..., :quarter]
    part_b = tensor[..., quarter : 2 * quarter]
    part_c = tensor[..., 2 * quarter : 3 * quarter]
    part_d = tensor[..., 3 * quarter :]
    return jnp.concatenate(
        [
            part_a * cos_row - part_b * sin_row,
            part_a * sin_row + part_b * cos_row,
            part_c * cos_col - part_d * sin_col,
            part_c * sin_col + part_d * cos_col,
        ],
        axis=-1,
    )


def modulate(values, shift_in, scale_in):
    return rms_norm(values) * (1.0 + scale_in[:, None, :]) + shift_in[:, None, :]


def swiglu(gate_in, up_in):
    return jax.nn.silu(gate_in) * up_in


def split_heads(tensor, per_block):
    count, span, heads_all, size = tensor.shape
    groups = heads_all // per_block
    shaped = tensor.reshape(count, span, groups, per_block, size)
    return jnp.transpose(shaped, (0, 2, 1, 3, 4)).reshape(count * groups, span, per_block, size)


def join_heads(tensor, count):
    blocks, span, per_block, size = tensor.shape
    groups = blocks // count
    shaped = tensor.reshape(count, groups, span, per_block, size)
    return jnp.transpose(shaped, (0, 2, 1, 3, 4)).reshape(count, span, groups * per_block, size)


def scatter_kernel(cuts, lags, *refs):
    n = len(cuts)
    ins, outs = refs[:n], refs[n:2*n]
    O, C, Y, X, Z, F = (refs[2*n + k*n: 2*n + (k+1)*n] for k in range(6))
    ls, cs, cr, ys, yr, xs, xr, zs, zr, fs, fr, es, er, ws = refs[8*n:]
    g = lax.axis_index("grp"); band = lax.axis_index("band")
    z = g // 2; x = g % 2; y = band // 2; c = band % 2
    far = [z, z + 1 - 2 * (z % 2), 2 - z // 2, 3 - 3 * (z // 2)]
    ypeer = (g, (1 - y) * 2 + c); cpeer = (g, y * 2 + 1 - c); xpeer = (z * 2 + 1 - x, band)
    bar = pltpu.get_barrier_semaphore()
    for d in [xpeer, ypeer, cpeer] + [(zz * 2 + x, band) for zz in far[1:]]:
        pl.semaphore_signal(bar, inc=1, device_id=d, device_id_type=MESH)
    pl.semaphore_wait(bar, 6)
    def at(ref, axis, start, size):
        if axis == 0:
            return ref.at[pl.ds(pl.multiple_of(start, 16), size), :]
        return ref.at[:, pl.ds(pl.multiple_of(start, 128), size)]
    def piece(i, ref):
        axis, half, a, b = cuts[i]
        return at(ref, axis, y * b, a + b)
    def bpart(i, ref, yy):
        axis, half, a, b = cuts[i]
        return at(ref, axis, yy * (a + b), b)
    tail = []
    def send(src, dst, ssem, rsem, dev, cond=None):
        d = pltpu.make_async_remote_copy(src_ref=src, dst_ref=dst, send_sem=ssem, recv_sem=rsem, device_id=dev, device_id_type=MESH)
        if cond is None:
            d.start(); tail.append(d.wait_send)
            return d.wait_send
        else:
            pl.when(cond)(d.start); tail.append(lambda: pl.when(cond)(d.wait_send))
    def arrived(ref, rsem):
        pltpu.make_async_remote_copy(src_ref=ref, dst_ref=ref, send_sem=ls.at[0, 0], recv_sem=rsem, device_id=xpeer, device_id_type=MESH).wait_recv()
    def add(dst, src):
        rows = src.shape[0]
        def step(r, _):
            w = pl.ds(pl.multiple_of(r * 16, 16), 16)
            dst[w, :] = dst[w, :] + src[w, :]
            return 0
        lax.fori_loop(0, rows // 16, step, 0)
    order = [(t, j) for t in (3, 2, 1, 0) for j in (1, 0)]
    def shard(t, j):
        return far[t] * 2 + (1 - x if j else x)
    seq = [(i, t, j) for i in range(n) for (t, j) in order]
    loads, sent = {}, {}
    for i, t, j in seq:
        axis, half, a, b = cuts[i]
        s = shard(t, j)
        q = order.index((t, j))
        send(at(ins[i].at[s], axis, (1 - c) * half, half), C[i].at[s], cs.at[i, q], cr.at[i, s], cpeer)
        d = pltpu.make_async_copy(at(ins[i].at[s], axis, c * half, half), O[i].at[s], ls.at[i, q])
        d.start(); loads[(i, t, j)] = d
    def cadd(i, t, j):
        s = shard(t, j)
        loads[(i, t, j)].wait()
        arrived(C[i].at[s], cr.at[i, s])
        add(O[i].at[s], C[i].at[s])
        sent[i, t, j] = send(bpart(i, O[i].at[s], 1 - y), Y[i].at[s], ys.at[i, order.index((t, j))], yr.at[i, s], ypeer)
    def yadd(i, t, j):
        s = shard(t, j)
        arrived(Y[i].at[s], yr.at[i, s])
        add(bpart(i, O[i].at[s], y), Y[i].at[s])
        if j:
            send(piece(i, O[i].at[s]), X[i].at[far[t]], xs.at[i, t], xr.at[i, far[t]], xpeer)
    def xadd(i, t):
        zz = far[t]
        arrived(X[i].at[zz], xr.at[i, zz])
        add(piece(i, O[i].at[shard(t, 0)]), X[i].at[zz])
    def zadd(i, t):
        zz = far[t]
        p = piece(i, O[i].at[shard(t, 0)])
        if t > 0:
            inc = jnp.where(zz < z, z + 1, z - 1)
            @pl.when((inc >= 0) & (inc <= 3))
            def _():
                arrived(Z[i].at[zz], zr.at[i, zz])
                add(p, Z[i].at[zz])
            nxt = jnp.where(zz < z, z - 1, z + 1)
            slot = jnp.where((zz < z) & (nxt == zz), 4, zz)
            send(p, Z[i].at[slot], zs.at[i, t - 1], zr.at[i, slot], (nxt * 2 + x, band))
        else:
            @pl.when(z > 0)
            def _():
                arrived(Z[i].at[z], zr.at[i, z])
                add(p, Z[i].at[z])
            @pl.when(z < 3)
            def _():
                arrived(Z[i].at[4], zr.at[i, 4])
                add(p, Z[i].at[4])
            sent[i] = send(p, F[i], fs.at[i], fr.at[i], ypeer)
    def fin2(i):
        axis, half, a, b = cuts[i]
        own = O[i].at[g]
        arrived(F[i], fr.at[i])
        for done in (sent[i], sent[i, 0, 0]):
            done(); tail.remove(done)
        for yy in (0, 1):
            @pl.when(y == 1 - yy)
            def _():
                add(at(own, axis, b, a), at(F[i], axis, b if yy == 0 else 0, a))
                dst = at(own, axis, yy * (a + b), b); src = at(F[i], axis, 0 if yy == 0 else a, b)
                def step(r, _):
                    w = pl.ds(pl.multiple_of(r * 16, 16), 16)
                    dst[w, :] = src[w, :]
                    return 0
                lax.fori_loop(0, src.shape[0] // 16, step, 0)
        o = at(outs[i], axis, c * half, half)
        send(own, o, es.at[i], er.at[i], cpeer)
        d = pltpu.make_async_copy(own, o, ws.at[i]); d.start(); tail.append(d.wait)
    ly, lx, lz, lf = lags
    N = len(seq)
    todo = {}
    for q, (i, t, j) in enumerate(seq):
        todo.setdefault(q, []).append((0, lambda a=(i, t, j): cadd(*a)))
        todo.setdefault(q + ly, []).append((1, lambda a=(i, t, j): yadd(*a)))
        if j == 0:
            todo.setdefault(q + ly + lx, []).append((2, lambda a=(i, t): xadd(*a)))
            todo.setdefault(q + ly + lx + lz, []).append((3, lambda a=(i, t): zadd(*a)))
            if t == 0:
                todo.setdefault(q + ly + lx + lz + lf, []).append((4, lambda i=i: fin2(i)))
    for q in sorted(todo):
        for _, f in sorted(todo[q], key=lambda p: p[0]):
            f()
    for i in range(n):
        axis, half, a, b = cuts[i]
        arrived(at(outs[i], axis, (1 - c) * half, half), er.at[i])
    for w in tail:
        w()

def scatter(gs, cuts, cid=1, lags=(2, 2, 1, 2)):
    n = len(gs)
    S = pltpu.SemaphoreType.DMA
    bf = jnp.bfloat16
    def buf(lead, cut, w, size):
        shape = (w.shape[1], size) if cut[0] == 1 else (size, w.shape[2])
        return pltpu.VMEM(lead + shape, bf)
    scr = [buf((8,), c, w, c[1]) for c, w in zip(cuts, gs)]
    scr += [buf((8,), c, w, c[1]) for c, w in zip(cuts, gs)]
    scr += [buf((8,), c, w, c[3]) for c, w in zip(cuts, gs)]
    scr += [buf((4,), c, w, c[2] + c[3]) for c, w in zip(cuts, gs)]
    scr += [buf((5,), c, w, c[2] + c[3]) for c, w in zip(cuts, gs)]
    scr += [buf((), c, w, c[2] + c[3]) for c, w in zip(cuts, gs)]
    return pl.pallas_call(
        functools.partial(scatter_kernel, cuts, lags),
        out_shape=[jax.ShapeDtypeStruct(w.shape[1:], bf) for w in gs],
        in_specs=[pl.BlockSpec(memory_space=pl.ANY)] * n,
        out_specs=[pl.BlockSpec(memory_space=pl.ANY)] * n,
        scratch_shapes=scr + [S((n, 8)), S((n, 8)), S((n, 8)), S((n, 8)), S((n, 8)), S((n, 4)), S((n, 4)), S((n, 3)), S((n, 5)), S((n,)), S((n,)), S((n,)), S((n,)), S((n,))],
        compiler_params=pltpu.CompilerParams(collective_id=cid, has_side_effects=True, vmem_limit_bytes=60 * 2**20),
        name="gradient_scatter",
    )(*gs)


def half_cuts(axis, size, own_parts, shared_parts):
    unit = size // 2 // (own_parts + 2 * shared_parts)
    return (axis, size // 2, own_parts * unit, shared_parts * unit)


def fits(rows, wide, widest, deep):
    return (
        lax.axis_size("grp") == 8
        and lax.axis_size("band") == 4
        and rows % 16 == 0
        and wide % 4608 == 0
        and widest % 1024 == 0
        and deep % 384 == 0
    )


def gather_weights(shards):
    rows, wide = shards[0].shape
    widest, deep = shards[1].shape[1], shards[2].shape[0]
    if not fits(rows, wide, widest, deep):
        return [lax.all_gather(w, "grp", axis=0, tiled=True) for w in shards]
    cuts = (
        half_cuts(1, wide, 1, 1),
        half_cuts(1, widest, 1, 1),
        half_cuts(0, deep, 1, 1),
    )
    full = gather(shards, cuts)
    return [w.reshape(-1, w.shape[-1]) for w in full]


def scatter_grads(grads):
    parts = lax.axis_size("grp")
    split = [w.reshape(parts, w.shape[0] // parts, w.shape[1]) for w in grads]
    rows, wide = split[0].shape[1:]
    widest, deep = split[1].shape[2], split[2].shape[1]
    if not fits(rows, wide, widest, deep):
        shards = [lax.psum_scatter(w, "grp", scatter_dimension=0, tiled=True) for w in grads]
        return [lax.psum(w, "band") for w in shards]
    cuts = (
        half_cuts(1, wide, 8, 5),
        half_cuts(1, widest, 2, 1),
        half_cuts(0, deep, 2, 1),
    )
    return scatter([split[k] for k in (2, 1, 0)], [cuts[k] for k in (2, 1, 0)])[::-1]


def body(
    patches,
    grad_out,
    cond_table,
    group_ids,
    live_count,
    band_order,
    w_ada,
    b_ada,
    w_qkv,
    q_gain,
    k_gain,
    w_proj,
    w_gate,
    w_up,
    w_down,
):
    images, rows, cols, width = patches.shape
    length = rows * cols
    score_scale = HDIM ** (-0.5)
    per_block = 4
    grp = lax.axis_index("grp")
    ada_rows = w_ada.shape[0]
    bias_cols = b_ada.shape[0]
    shards = (
        jnp.concatenate([w_qkv, w_proj], axis=1),
        jnp.concatenate([w_gate, w_up], axis=1),
        w_down,
    )
    qp_all, gu_all, down_all = gather_weights(shards)
    qkv_all, proj_all = qp_all[:, : w_qkv.shape[1]], qp_all[:, w_qkv.shape[1] :]
    ff = w_gate.shape[1]
    onehot = (group_ids[:, None] == jnp.arange(GROUPS, dtype=jnp.int32)[None, :]).astype(
        jnp.float32
    )
    cond_rows = lax.dynamic_slice_in_dim(cond_table, grp * ada_rows, ada_rows, axis=1)
    silu_rows, silu_pull = jax.vjp(jax.nn.silu, cond_rows)
    silu_rows = silu_rows.astype(jnp.bfloat16)
    mod_part = jnp.dot(silu_rows, w_ada, preferred_element_type=jnp.float32)
    bias_part = lax.dynamic_update_slice_in_dim(
        jnp.zeros((mod_part.shape[1],), jnp.float32),
        b_ada.astype(jnp.float32),
        grp * bias_cols,
        axis=0,
    )
    mod_table = lax.psum(mod_part + bias_part[None, :], "grp")
    modulation = jnp.take(mod_table, group_ids, axis=0)
    shift_one, scale_one, gate_one, shift_two, scale_two, gate_two = jnp.split(
        modulation, 6, axis=-1
    )
    live_mask = (jnp.arange(images, dtype=jnp.int32) < live_count[0]).astype(jnp.float32)
    row_index = jnp.repeat(band_order[0] * rows + jnp.arange(rows, dtype=jnp.int32), cols).astype(
        jnp.float32
    )
    col_index = jnp.tile(jnp.arange(cols, dtype=jnp.int32), rows).astype(jnp.float32)
    tables = rope_tables(row_index, col_index)
    x_flat = patches.reshape(images, length, width).astype(jnp.float32)
    normed_one, norm_one_pull = jax.vjp(modulate, x_flat, shift_one, scale_one)
    normed_one_low = normed_one.astype(jnp.bfloat16).reshape(images * length, width)
    qkv = jnp.dot(normed_one_low, qkv_all, preferred_element_type=jnp.float32).reshape(
        images, length, 3, HEADS, HDIM
    )

    def query_key(query_raw, key_raw, query_gain, key_gain):
        return (
            rotate(rms_norm(query_raw) * query_gain, tables),
            rotate(rms_norm(key_raw) * key_gain, tables),
        )

    (query_rot, key_rot), qk_pull = jax.vjp(query_key, qkv[:, :, 0], qkv[:, :, 1], q_gain, k_gain)
    query_low = query_rot.astype(jnp.bfloat16)
    key_low = key_rot.astype(jnp.bfloat16).reshape(images, length, width)
    value_low = qkv[:, :, 2].astype(jnp.bfloat16).reshape(images, length, width)
    kv_local = jnp.concatenate([key_low, value_low], axis=-1)
    kv_rows = lax.all_gather(kv_local, "band", axis=1, tiled=True)
    query_blocks = split_heads(query_low, per_block)
    keys_all = kv_rows[..., :width].reshape(images, -1, HEADS, HDIM)
    values_all = kv_rows[..., width:].reshape(images, -1, HEADS, HDIM)
    key_blocks = split_heads(keys_all, per_block)
    value_blocks = split_heads(values_all, per_block)

    def forward_block(item):
        query_part, key_part, value_part = item
        scores = (
            jnp.einsum("qhd,khd->hqk", query_part, key_part, preferred_element_type=jnp.float32)
            * score_scale
        )
        top_score = jnp.max(scores, axis=-1, keepdims=True)
        expo_scores = jnp.exp(scores - top_score)
        total_weight = jnp.sum(expo_scores, axis=-1, keepdims=True)
        probs_low = (expo_scores / total_weight).astype(jnp.bfloat16)
        attended_part = jnp.einsum(
            "hqk,khd->qhd", probs_low, value_part, preferred_element_type=jnp.float32
        )
        return (attended_part.astype(jnp.bfloat16), top_score + jnp.log(total_weight))

    attended_blocks, log_blocks = lax.map(forward_block, (query_blocks, key_blocks, value_blocks))
    attended_low = join_heads(attended_blocks, images).reshape(images * length, width)
    proj = jnp.dot(attended_low, proj_all, preferred_element_type=jnp.float32).reshape(
        images, length, width
    )
    middle = x_flat + gate_one[:, None, :] * proj
    normed_two, norm_two_pull = jax.vjp(modulate, middle, shift_two, scale_two)
    normed_two_low = normed_two.astype(jnp.bfloat16).reshape(images * length, width)
    pre = jnp.dot(normed_two_low, gu_all, preferred_element_type=jnp.float32)
    gate_pre, up_pre = pre[:, :ff], pre[:, ff:]
    hidden, swiglu_pull = jax.vjp(swiglu, gate_pre, up_pre)
    hidden_low = hidden.astype(jnp.bfloat16)
    mlp = jnp.dot(hidden_low, down_all, preferred_element_type=jnp.float32).reshape(
        images, length, width
    )
    output = (middle + gate_two[:, None, :] * mlp) * live_mask[:, None, None]
    patches_out = output.astype(jnp.bfloat16).reshape(images, rows, cols, width)
    grad_y = grad_out.reshape(images, length, width).astype(jnp.float32) * live_mask[:, None, None]
    d_gate_two = jnp.sum(grad_y * mlp, axis=1)
    d_mlp = (grad_y * gate_two[:, None, :]).astype(jnp.bfloat16).reshape(images * length, width)
    d_w_down = jnp.einsum("tf,td->fd", hidden_low, d_mlp, preferred_element_type=jnp.float32)
    d_hidden = jnp.einsum("td,fd->tf", d_mlp, down_all, preferred_element_type=jnp.float32)
    d_gate_pre, d_up_pre = swiglu_pull(d_hidden)
    d_pre_low = jnp.concatenate(
        [d_gate_pre.astype(jnp.bfloat16), d_up_pre.astype(jnp.bfloat16)], axis=1
    )
    d_w_gu = jnp.einsum("td,tf->df", normed_two_low, d_pre_low, preferred_element_type=jnp.float32)
    d_normed_two = jnp.einsum("tf,df->td", d_pre_low, gu_all, preferred_element_type=jnp.float32)
    d_middle_norm, d_shift_two, d_scale_two = norm_two_pull(
        d_normed_two.reshape(images, length, width)
    )
    d_middle = grad_y + d_middle_norm
    d_gate_one = jnp.sum(d_middle * proj, axis=1)
    d_proj = (d_middle * gate_one[:, None, :]).astype(jnp.bfloat16).reshape(images * length, width)
    d_w_proj = jnp.einsum("td,te->de", attended_low, d_proj, preferred_element_type=jnp.float32)
    d_attended = jnp.einsum("te,de->td", d_proj, proj_all, preferred_element_type=jnp.float32)
    d_attended = d_attended.astype(jnp.bfloat16).reshape(images, length, HEADS, HDIM)
    d_att_blocks = split_heads(d_attended, per_block)

    def backward_block(item):
        query_part, key_part, value_part, d_att_part, log_part = item
        scores = (
            jnp.einsum("qhd,khd->hqk", query_part, key_part, preferred_element_type=jnp.float32)
            * score_scale
        )
        probs = jnp.exp(scores - log_part)
        probs_low = probs.astype(jnp.bfloat16)
        d_probs = jnp.einsum(
            "qhd,khd->hqk", d_att_part, value_part, preferred_element_type=jnp.float32
        )
        row_delta = jnp.sum(probs * d_probs, axis=-1, keepdims=True)
        d_scores = (probs * (d_probs - row_delta)).astype(jnp.bfloat16)
        d_query_part = (
            jnp.einsum("hqk,khd->qhd", d_scores, key_part, preferred_element_type=jnp.float32)
            * score_scale
        )
        key_grad = (
            jnp.einsum("hqk,qhd->khd", d_scores, query_part, preferred_element_type=jnp.float32)
            * score_scale
        )
        value_grad = jnp.einsum(
            "hqk,qhd->khd", probs_low, d_att_part, preferred_element_type=jnp.float32
        )
        return (d_query_part, key_grad, value_grad)

    query_grads, key_grads, value_grads = lax.map(
        backward_block, (query_blocks, key_blocks, value_blocks, d_att_blocks, log_blocks)
    )
    d_query = join_heads(query_grads, images)
    key_terms = join_heads(key_grads, images).reshape(images, -1, width)
    value_terms = join_heads(value_grads, images).reshape(images, -1, width)
    kv_terms = jnp.concatenate([key_terms, value_terms], axis=-1)
    kv_grad = lax.psum_scatter(
        kv_terms.astype(jnp.bfloat16), "band", scatter_dimension=1, tiled=True
    ).astype(jnp.float32)
    d_key = kv_grad[..., :width].reshape(images, length, HEADS, HDIM)
    d_value = kv_grad[..., width:]
    d_query_raw, d_key_raw, d_q_gain, d_k_gain = qk_pull((d_query, d_key))
    d_qkv = jnp.concatenate(
        [
            d_query_raw.reshape(images, length, width),
            d_key_raw.reshape(images, length, width),
            d_value,
        ],
        axis=-1,
    )
    d_qkv = d_qkv.astype(jnp.bfloat16).reshape(images * length, 3 * width)
    d_w_qkv = jnp.einsum("td,te->de", normed_one_low, d_qkv, preferred_element_type=jnp.float32)
    d_normed_one = jnp.einsum("te,de->td", d_qkv, qkv_all, preferred_element_type=jnp.float32)
    d_x_norm, d_shift_one, d_scale_one = norm_one_pull(d_normed_one.reshape(images, length, width))
    d_patches = (d_middle + d_x_norm).reshape(images, rows, cols, width)
    d_mod_part = jnp.concatenate(
        [d_shift_one, d_scale_one, d_gate_one, d_shift_two, d_scale_two, d_gate_two], axis=-1
    )
    d_modulation = lax.psum(d_mod_part, "band").astype(jnp.bfloat16)
    payload = jnp.concatenate([d_modulation, onehot.astype(jnp.bfloat16)], axis=-1)
    payload = lax.all_gather(payload, "grp", axis=0, tiled=True)
    d_mod_all = payload[:, : d_modulation.shape[1]]
    onehot_all = payload[:, d_modulation.shape[1] :]
    silu_all = jnp.dot(onehot_all, silu_rows, preferred_element_type=jnp.float32).astype(
        jnp.bfloat16
    )
    d_w_ada = jnp.einsum("bd,be->de", silu_all, d_mod_all, preferred_element_type=jnp.float32)
    d_b_ada = lax.dynamic_slice_in_dim(
        jnp.sum(d_mod_all.astype(jnp.float32), axis=0), grp * bias_cols, bias_cols, axis=0
    )
    d_silu = jnp.einsum("be,de->bd", d_mod_all, w_ada, preferred_element_type=jnp.float32)
    d_silu = jnp.dot(
        onehot_all.astype(jnp.float32).T,
        d_silu,
        precision=lax.Precision.HIGHEST,
        preferred_element_type=jnp.float32,
    )
    d_cond_rows = silu_pull(d_silu)[0]
    d_cond = lax.all_gather(d_cond_rows, "grp", axis=1, tiled=True)
    d_q_gain, d_k_gain = lax.psum((d_q_gain, d_k_gain), ("grp", "band"))

    d_w_qp = jnp.concatenate(
        [d_w_qkv.astype(jnp.bfloat16), d_w_proj.astype(jnp.bfloat16)], axis=1
    )
    d_qp, d_gu, d_down = (
        w.astype(jnp.float32)
        for w in scatter_grads(
            (d_w_qp, d_w_gu.astype(jnp.bfloat16), d_w_down.astype(jnp.bfloat16))
        )
    )
    return (
        patches_out,
        d_patches,
        d_cond,
        d_w_ada,
        d_b_ada,
        d_qp[:, : w_qkv.shape[1]],
        d_q_gain,
        d_k_gain,
        d_qp[:, w_qkv.shape[1] :],
        d_gu[:, :ff],
        d_gu[:, ff:],
        d_down,
    )


def solution(mesh):
    in_specs = (
        P("grp", "band", None, None),
        P("grp", "band", None, None),
        P(),
        P("grp"),
        P("grp"),
        P("band"),
        P("grp", None),
        P("grp"),
        P("grp", None),
        P(),
        P(),
        P("grp", None),
        P("grp", None),
        P("grp", None),
        P("grp", None),
    )
    out_specs = (
        P("grp", "band", None, None),
        P("grp", "band", None, None),
        P(),
        P("grp", None),
        P("grp"),
        P("grp", None),
        P(),
        P(),
        P("grp", None),
        P("grp", None),
        P("grp", None),
        P("grp", None),
    )
    return jax.shard_map(body, mesh=mesh, in_specs=in_specs, out_specs=out_specs, check_vma=False)
```

```python
import functools

import jax
import jax.numpy as jnp
from jax import lax
from jax.experimental import pallas as pl
from jax.experimental.pallas import tpu as pltpu
from jax.sharding import PartitionSpec as P

HEADS = 16
HDIM = 72
GROUPS = 8
LANES = 128
EPS = 1e-06
LOG2E = 1.4426950408889634

MESH = pl.DeviceIdType.MESH


class Place:
    def __init__(self):
        self.g, self.band = lax.axis_index("grp"), lax.axis_index("band")
        self.z, self.x = self.g // 2, self.g % 2
        self.y, self.c = self.band // 2, self.band % 2
        z = self.z
        self.far = [z, z + 1 - 2 * (z % 2), 2 - z // 2, 3 - 3 * (z // 2)]
        self.ypeer = (self.g, (1 - self.y) * 2 + self.c)
        self.cpeer = (self.g, self.y * 2 + 1 - self.c)
        self.xpeer = (z * 2 + 1 - self.x, self.band)
        self.draining = False

    def line(self, zz):
        return (zz * 2 + self.x, self.band)

    def greet(self, peers):
        bar = pltpu.get_barrier_semaphore()
        for d in peers:
            pl.semaphore_signal(bar, inc=1, device_id=d, device_id_type=MESH)
        pl.semaphore_wait(bar, len(peers))

    def greet_band(self):
        self.greet([self.ypeer, self.cpeer])

    def greet_all(self):
        self.greet([self.xpeer, self.ypeer, self.cpeer] + [self.line(zz) for zz in self.far[1:]])

    def copy(self, src, dst, ssem, rsem, dev):
        return pltpu.make_async_remote_copy(
            src_ref=src, dst_ref=dst, send_sem=ssem, recv_sem=rsem, device_id=dev, device_id_type=MESH
        )

    def send(self, src, dst, ssem, rsem, dev, cond=None):
        d = self.copy(src, dst, ssem, rsem, dev)
        act = d.wait_send if self.draining else d.start
        if cond is None:
            act()
        else:
            pl.when(cond)(act)

    def keep(self, src, dst, sem):
        d = pltpu.make_async_copy(src, dst, sem)
        d.wait() if self.draining else d.start()

    def arrived(self, ref, rsem):
        if not self.draining:
            self.copy(ref, ref, rsem, rsem, self.ypeer).wait_recv()

    def drain(self, steps):
        self.draining = True
        for step in steps:
            step()
        self.draining = False


def span(ref, axis, start, size):
    if axis == 0:
        return ref.at[pl.ds(pl.multiple_of(start, 16), size), :]
    return ref.at[:, pl.ds(pl.multiple_of(start, LANES), size)]


def gather_sems(n):
    s = pltpu.SemaphoreType.DMA
    return [s((n,)), s((n, 4)), s((n, 4)), s((n, 4)), s((n, 4)), s((n, 7)), s((n, 7)), s((n, 14)), s((n, 14)), s((n,))]


def gather_steps(at, cuts, ins, outs, sems):
    n = len(cuts)
    lsem, zs, zr, xs, xr, ys, yr, cs, cr, ds = sems
    x, y, z, c, far = at.x, at.y, at.z, at.c, at.far

    def piece(i, ref, yy, cc):
        axis, half, a, b = cuts[i]
        return span(ref, axis, cc * half + yy * b, a + b)

    def bpart(i, ref, yy, cc):
        axis, half, a, b = cuts[i]
        return span(ref, axis, cc * half + yy * (a + b), b)

    def own(i):
        src, dst = piece(i, ins[i], y, c), piece(i, outs[i].at[at.g], y, c)
        at.send(src, dst, zs.at[i, 0], zr.at[i, z], (at.g + 2, at.band), z < 3)
        at.send(src, dst, ds.at[i], zr.at[i, z], (at.g - 2, at.band), z > 0)
        at.send(src, dst, xs.at[i, 0], xr.at[i, 0], at.xpeer)
        at.keep(ins[i], outs[i].at[at.g], lsem.at[i])

    def down(i, slot, shard):
        p = bpart(i, outs[i].at[shard], y, c)
        at.send(p, p, ys.at[i, slot], yr.at[i, slot], at.ypeer)
        p = piece(i, outs[i].at[shard], y, c)
        at.send(p, p, cs.at[i, slot], cr.at[i, slot], at.cpeer)

    def zarr(i, t):
        zz = far[t]
        s = zz * 2 + x
        p = piece(i, outs[i].at[s], y, c)
        at.arrived(p, zr.at[i, zz])
        nxt = jnp.where(zz < z, z + 1, z - 1)
        at.send(p, p, zs.at[i, t], zr.at[i, zz], at.line(jnp.clip(nxt, 0, 3)), (nxt >= 0) & (nxt <= 3))
        at.send(p, p, xs.at[i, t], xr.at[i, t], at.xpeer)
        down(i, t - 1, s)

    def xarr(i, t):
        s = far[t] * 2 + 1 - x
        at.arrived(piece(i, outs[i].at[s], y, c), xr.at[i, t])
        down(i, 3 + t, s)

    def yarr(i, slot, s):
        p = bpart(i, outs[i].at[s], 1 - y, c)
        at.arrived(p, yr.at[i, slot])
        at.send(p, p, cs.at[i, 7 + slot], cr.at[i, 7 + slot], at.cpeer)

    slots = [(t - 1, far[t] * 2 + x) for t in (1, 2, 3)]
    slots += [(3 + t, far[t] * 2 + 1 - x) for t in range(4)]
    order = [slots[k] for k in (3, 0, 4, 1, 5, 2, 6)]
    steps = [lambda: own(0)]
    for i in range(n):
        steps.append(lambda i=i: zarr(i, 1))
        if i + 1 < n:
            steps.append(lambda i=i: own(i + 1))
        rest = [lambda i=i: xarr(i, 0)]
        for t in (2, 3):
            rest += [lambda i=i, t=t: zarr(i, t), lambda i=i, t=t: xarr(i, t - 1)]
        rest.append(lambda i=i: xarr(i, 3))
        for k, step in enumerate(rest):
            if i > 0:
                steps.append(lambda i=i, k=k: yarr(i - 1, *order[k]))
            steps.append(step)
        if i > 0:
            steps.append(lambda i=i: yarr(i - 1, *order[6]))
    steps += [lambda k=k: yarr(n - 1, *order[k]) for k in range(7)]

    def last():
        for i in range(n):
            for slot, s in slots:
                at.arrived(piece(i, outs[i].at[s], y, 1 - c), cr.at[i, slot])
                at.arrived(bpart(i, outs[i].at[s], 1 - y, 1 - c), cr.at[i, 7 + slot])

    return steps, last


def gather_kernel(cuts, *refs):
    n = len(cuts)
    at = Place()
    at.greet_all()
    steps, last = gather_steps(at, cuts, refs[:n], refs[n : 2 * n], refs[2 * n :])
    for step in steps:
        step()
    last()
    at.drain(steps)


def gather(ws, cuts):
    n = len(ws)
    return pl.pallas_call(
        functools.partial(gather_kernel, cuts),
        out_shape=[jax.ShapeDtypeStruct((8,) + w.shape, w.dtype) for w in ws],
        in_specs=[pl.BlockSpec(memory_space=pl.ANY)] * n,
        out_specs=[pl.BlockSpec(memory_space=pl.ANY)] * n,
        scratch_shapes=gather_sems(n),
        compiler_params=pltpu.CompilerParams(collective_id=0, has_side_effects=True),
        name="weight_gather",
    )(*ws)
def add_into(dst, src):
    def step(r, _):
        rows = pl.ds(pl.multiple_of(r * 16, 16), 16)
        dst[rows, :] = dst[rows, :] + src[rows, :]
        return 0

    lax.fori_loop(0, src.shape[0] // 16, step, 0)


def move_into(dst, src):
    def step(r, _):
        rows = pl.ds(pl.multiple_of(r * 16, 16), 16)
        dst[rows, :] = src[rows, :]
        return 0

    lax.fori_loop(0, src.shape[0] // 16, step, 0)


def scatter_scratch(grads, cuts):
    n = len(cuts)
    s = pltpu.SemaphoreType.DMA

    def buf(lead, k, size):
        shape = (grads[k].shape[1], size) if cuts[k][0] == 1 else (size, grads[k].shape[2])
        return pltpu.VMEM(lead + shape, jnp.bfloat16)

    out = []
    for lead, pick in (
        ((8,), lambda c: c[1]),
        ((8,), lambda c: c[1]),
        ((8,), lambda c: c[3]),
        ((4,), lambda c: c[2] + c[3]),
        ((5,), lambda c: c[2] + c[3]),
        ((), lambda c: c[2] + c[3]),
    ):
        out += [buf(lead, k, pick(cuts[k])) for k in range(n)]
    out += [s((n, 8))] * 5 + [s((n, 4))] * 2 + [s((n, 3)), s((n, 5))] + [s((n,))] * 5
    return out


def scatter_steps(at, cuts, ins, outs, scratch, lags):
    n = len(cuts)
    own_half, core_buf, y_buf, x_buf, z_buf, fin_buf = (scratch[k * n : (k + 1) * n] for k in range(6))
    ls, cs, cr, ys, yr, xs, xr, zs, zr, fs, fr, es, er, ws = scratch[6 * n :]
    x, y, z, c, far = at.x, at.y, at.z, at.c, at.far

    def piece(i, ref):
        _, _, a, b = cuts[i]
        return span(ref, cuts[i][0], y * b, a + b)

    def bpart(i, ref, yy):
        _, _, a, b = cuts[i]
        return span(ref, cuts[i][0], yy * (a + b), b)

    order = [(t, j) for t in (3, 2, 1, 0) for j in (1, 0)]

    def shard(t, j):
        return far[t] * 2 + (1 - x if j else x)

    def load(i, t, j):
        axis, half, _, _ = cuts[i]
        s, q = shard(t, j), order.index((t, j))
        return pltpu.make_async_copy(span(ins[i].at[s], axis, c * half, half), own_half[i].at[s], ls.at[i, q])

    def give(i, t, j):
        axis, half, _, _ = cuts[i]
        s, q = shard(t, j), order.index((t, j))
        src = span(ins[i].at[s], axis, (1 - c) * half, half)
        at.send(src, core_buf[i].at[s], cs.at[i, q], cr.at[i, s], at.cpeer)
        if not at.draining:
            load(i, t, j).start()

    def to_y(i, t, j):
        s = shard(t, j)
        src = bpart(i, own_half[i].at[s], 1 - y)
        return at.copy(src, y_buf[i].at[s], ys.at[i, order.index((t, j))], yr.at[i, s], at.ypeer)

    def to_fin(i):
        return at.copy(piece(i, own_half[i].at[at.g]), fin_buf[i], fs.at[i], fr.at[i], at.ypeer)

    def cadd(i, t, j):
        s = shard(t, j)
        if at.draining:
            if (t, j) != (0, 0):
                to_y(i, t, j).wait_send()
            return
        load(i, t, j).wait()
        at.arrived(core_buf[i].at[s], cr.at[i, s])
        add_into(own_half[i].at[s], core_buf[i].at[s])
        to_y(i, t, j).start()

    def yadd(i, t, j):
        s = shard(t, j)
        at.arrived(y_buf[i].at[s], yr.at[i, s])
        if not at.draining:
            add_into(bpart(i, own_half[i].at[s], y), y_buf[i].at[s])
        if j:
            at.send(piece(i, own_half[i].at[s]), x_buf[i].at[far[t]], xs.at[i, t], xr.at[i, far[t]], at.xpeer)

    def xadd(i, t):
        if at.draining:
            return
        at.arrived(x_buf[i].at[far[t]], xr.at[i, far[t]])
        add_into(piece(i, own_half[i].at[shard(t, 0)]), x_buf[i].at[far[t]])

    def zadd(i, t):
        zz = far[t]
        p = piece(i, own_half[i].at[shard(t, 0)])

        def join(cond, slot):
            def do():
                at.arrived(z_buf[i].at[slot], zr.at[i, slot])
                add_into(p, z_buf[i].at[slot])

            if not at.draining:
                pl.when(cond)(do)

        if t > 0:
            inc = jnp.where(zz < z, z + 1, z - 1)
            join((inc >= 0) & (inc <= 3), zz)
            nxt = jnp.where(zz < z, z - 1, z + 1)
            slot = jnp.where((zz < z) & (nxt == zz), 4, zz)
            at.send(p, z_buf[i].at[slot], zs.at[i, t - 1], zr.at[i, slot], at.line(nxt))
        else:
            join(z > 0, z)
            join(z < 3, 4)
            if not at.draining:
                to_fin(i).start()

    def fin(i):
        axis, half, a, b = cuts[i]
        own = own_half[i].at[at.g]
        if not at.draining:
            at.arrived(fin_buf[i], fr.at[i])
            to_fin(i).wait_send()
            to_y(i, 0, 0).wait_send()
            for yy in (0, 1):

                @pl.when(y == 1 - yy)
                def _():
                    add_into(span(own, axis, b, a), span(fin_buf[i], axis, b if yy == 0 else 0, a))
                    move_into(span(own, axis, yy * (a + b), b), span(fin_buf[i], axis, 0 if yy == 0 else a, b))

        o = span(outs[i], axis, c * half, half)
        at.send(own, o, es.at[i], er.at[i], at.cpeer)
        at.keep(own, o, ws.at[i])

    seq = [(i, t, j) for i in range(n) for (t, j) in order]
    opening = [functools.partial(give, *p) for p in seq]
    ly, lx, lz, lf = lags
    todo = []
    for q, (i, t, j) in enumerate(seq):
        todo.append((q, 0, functools.partial(cadd, i, t, j)))
        todo.append((q + ly, 1, functools.partial(yadd, i, t, j)))
        if j == 0:
            todo.append((q + ly + lx, 2, functools.partial(xadd, i, t)))
            todo.append((q + ly + lx + lz, 3, functools.partial(zadd, i, t)))
            if t == 0:
                todo.append((q + ly + lx + lz + lf, 4, functools.partial(fin, i)))
    todo.sort(key=lambda p: p[:2])

    def last():
        for i in range(n):
            axis, half, _, _ = cuts[i]
            at.arrived(span(outs[i], axis, (1 - c) * half, half), er.at[i])

    return opening, [f for _, _, f in todo], last


def scatter_kernel(cuts, lags, *refs):
    n = len(cuts)
    at = Place()
    at.greet_all()
    opening, steps, last = scatter_steps(at, cuts, refs[:n], refs[n : 2 * n], refs[2 * n :], lags)
    for step in opening + steps:
        step()
    last()
    at.drain(opening + steps)


def scatter(grads, cuts, lags):
    n = len(grads)
    return pl.pallas_call(
        functools.partial(scatter_kernel, cuts, lags),
        out_shape=[jax.ShapeDtypeStruct(w.shape[1:], jnp.bfloat16) for w in grads],
        in_specs=[pl.BlockSpec(memory_space=pl.ANY)] * n,
        out_specs=[pl.BlockSpec(memory_space=pl.ANY)] * n,
        scratch_shapes=scatter_scratch(grads, cuts),
        compiler_params=pltpu.CompilerParams(
            collective_id=1, has_side_effects=True, vmem_limit_bytes=60 * 2**20
        ),
        name="gradient_scatter",
    )(*grads)
def head_window(h):
    first = jnp.minimum(h * HDIM // LANES, HEADS * HDIM // LANES - 2) * LANES
    lane = lax.broadcasted_iota(jnp.int32, (1, 2 * LANES), 1) + first
    inside = (lane >= h * HDIM) & (lane < h * HDIM + HDIM)
    return pl.ds(pl.multiple_of(first, LANES), 2 * LANES), inside


def dot_t(left, right):
    return lax.dot_general(left, right, (((1,), (1,)), ((), ())), preferred_element_type=jnp.float32)


def first_dot(left, right):
    return lax.dot_general(left, right, (((0,), (0,)), ((), ())), preferred_element_type=jnp.float32)


def exact_dot(left, right):
    return jnp.dot(
        left, right, precision=lax.Precision.HIGHEST, preferred_element_type=jnp.float32
    )


def turn(values, cos, sin_next, sin_prev):
    width = values.shape[-1]
    after = pltpu.roll(values, width - HDIM // 4, 1)
    before = pltpu.roll(values, HDIM // 4, 1)
    return values * cos + after * sin_next + before * sin_prev


def turn_back(values, cos, sin_next, sin_prev):
    width = values.shape[-1]
    after = pltpu.roll(values, width - HDIM // 4, 1)
    before = pltpu.roll(values, HDIM // 4, 1)
    return values * cos - after * sin_next - before * sin_prev


def qkv_kernel(
    x_ref, mod_ref, w_ref, gains_ref, cos_ref, next_ref, prev_ref, pick_ref, spread_ref,
    normed_ref, q_ref, k_ref, v_ref, nq_ref, nk_ref, rq_ref, rk_ref,
):
    width = x_ref.shape[-1]
    x = x_ref[0].astype(jnp.float32)
    root = lax.rsqrt(jnp.mean(x * x, axis=-1, keepdims=True) + EPS)
    shift, scale = mod_ref[0, 0:1, :], mod_ref[0, 1:2, :]
    normed = (x * root * (1.0 + scale) + shift).astype(jnp.bfloat16)
    normed_ref[0] = normed
    tables = (cos_ref[...], next_ref[...], prev_ref[...])
    outs = ((q_ref, nq_ref, rq_ref), (k_ref, nk_ref, rk_ref))
    for part, (low_ref, n_ref, r_ref) in enumerate(outs):
        raw = jnp.dot(
            normed, w_ref[:, part * width : (part + 1) * width], preferred_element_type=jnp.float32
        )
        inv = lax.rsqrt(exact_dot(raw * raw, pick_ref[...]) * (1.0 / HDIM) + EPS)
        r_ref[0] = inv
        unit = raw * exact_dot(inv, spread_ref[...])
        n_ref[0] = unit
        low_ref[0] = turn(unit * gains_ref[part : part + 1, :], *tables).astype(jnp.bfloat16)
    v_ref[0] = jnp.dot(
        normed, w_ref[:, 2 * width : 3 * width], preferred_element_type=jnp.float32
    ).astype(jnp.bfloat16)


def qkv_forward(x, mod, qp_all, gains, tables, pick, spread):
    images, length, width = x.shape
    row = lambda w, d: (jax.ShapeDtypeStruct((images, length, w), d), pl.BlockSpec((1, length, w), lambda i: (i, 0, 0)))
    whole = lambda a: pl.BlockSpec(a.shape, lambda i: (0,) * a.ndim)
    outs = [row(width, jnp.bfloat16)] * 4 + [row(width, jnp.float32)] * 2 + [row(LANES, jnp.float32)] * 2
    return pl.pallas_call(
        qkv_kernel,
        grid=(images,),
        in_specs=[
            pl.BlockSpec((1, length, width), lambda i: (i, 0, 0)),
            pl.BlockSpec((1, 6, width), lambda i: (i, 0, 0)),
            pl.BlockSpec((width, 3 * width), lambda i: (0, 0)),
            whole(gains),
        ]
        + [whole(t) for t in tables]
        + [whole(pick), whole(spread)],
        out_shape=[s for s, _ in outs],
        out_specs=[b for _, b in outs],
        compiler_params=pltpu.CompilerParams(vmem_limit_bytes=60 * 2**20),
        name="qkv_forward",
    )(x, mod, qp_all, gains, *tables, pick, spread)


def qkv_back_kernel(
    x_ref, mod_ref, mid_ref, dq_ref, dk_ref, dv_ref, nq_ref, nk_ref, rq_ref, rk_ref, w_ref,
    gains_ref, cos_ref, next_ref, prev_ref, pick_ref, spread_ref,
    dqkv_ref, dx_ref, sums_ref,
):
    width = x_ref.shape[-1]
    tables = (cos_ref[...], next_ref[...], prev_ref[...])
    ins = ((dq_ref, nq_ref, rq_ref), (dk_ref, nk_ref, rk_ref))
    for part, (d_ref, n_ref, r_ref) in enumerate(ins):
        back = turn_back(d_ref[0].astype(jnp.float32) * HDIM ** (-0.5), *tables)
        unit = n_ref[0]
        sums_ref[0, 2 + part : 3 + part, :] = jnp.sum(back * unit, axis=0, keepdims=True)
        inner = back * gains_ref[part : part + 1, :]
        mean = exact_dot(inner * unit, pick_ref[...]) * (1.0 / HDIM)
        grad = (inner - unit * exact_dot(mean, spread_ref[...])) * exact_dot(r_ref[0], spread_ref[...])
        dqkv_ref[0, :, part * width : (part + 1) * width] = grad.astype(jnp.bfloat16)
    dqkv_ref[0, :, 2 * width : 3 * width] = dv_ref[0]
    d_normed = dot_t(dqkv_ref[0], w_ref[...])
    x = x_ref[0].astype(jnp.float32)
    root = lax.rsqrt(jnp.mean(x * x, axis=-1, keepdims=True) + EPS)
    unit = x * root
    sums_ref[0, 0:1, :] = jnp.sum(d_normed, axis=0, keepdims=True)
    sums_ref[0, 1:2, :] = jnp.sum(d_normed * unit, axis=0, keepdims=True)
    inner = d_normed * (1.0 + mod_ref[0, 1:2, :])
    dx_ref[0] = mid_ref[0] + root * (inner - unit * jnp.mean(inner * unit, axis=-1, keepdims=True))


def qkv_backward(x, mod, d_mid, dq, dk, dv, nq, nk, rq, rk, qp_all, gains, tables, pick, spread):
    images, length, width = x.shape
    row = lambda w: pl.BlockSpec((1, length, w), lambda i: (i, 0, 0))
    whole = lambda a: pl.BlockSpec(a.shape, lambda i: (0,) * a.ndim)
    return pl.pallas_call(
        qkv_back_kernel,
        grid=(images,),
        in_specs=[row(width), pl.BlockSpec((1, 6, width), lambda i: (i, 0, 0))]
        + [row(width)] * 6
        + [row(LANES)] * 2
        + [pl.BlockSpec((width, 3 * width), lambda i: (0, 0)), whole(gains)]
        + [whole(t) for t in tables]
        + [whole(pick), whole(spread)],
        out_shape=[
            jax.ShapeDtypeStruct((images, length, 3 * width), jnp.bfloat16),
            jax.ShapeDtypeStruct((images, length, width), jnp.float32),
            jax.ShapeDtypeStruct((images, 4, width), jnp.float32),
        ],
        out_specs=[row(3 * width), row(width), pl.BlockSpec((1, 4, width), lambda i: (i, 0, 0))],
        compiler_params=pltpu.CompilerParams(vmem_limit_bytes=60 * 2**20),
        name="qkv_backward",
    )(x, mod, d_mid, dq, dk, dv, nq, nk, rq, rk, qp_all, gains, *tables, pick, spread)
def attention_kernel(cuts, q_ref, k_ref, v_ref, *refs):
    n = len(cuts)
    ins, (o_ref, inv_ref, kv_out), outs = refs[:n], refs[n : n + 3], refs[n + 3 : 2 * n + 3]
    kv, own_sem, ks, kr, os = refs[2 * n + 3 : 2 * n + 8]
    images, length, width = q_ref.shape
    at = Place()
    at.greet_all() if n else at.greet_band()
    parts = [(i, s) for i in range(images) for s in (0, 1)]

    def rows(s, i, band):
        return kv.at[s, i, pl.ds(pl.multiple_of(band * length, 16), length), :]

    here, over = at.band, (1 - at.y) * 2 + at.c
    beside, across = at.y * 2 + 1 - at.c, (1 - at.y) * 2 + 1 - at.c
    def give(i, s):
        src, dst = (k_ref, v_ref)[s].at[i], rows(s, i, here)
        at.send(src, dst, ks.at[i, s, 0], kr.at[i, s, 0], at.ypeer)
        at.send(src, dst, ks.at[i, s, 1], kr.at[i, s, 1], at.cpeer)
        if not at.draining:
            at.keep(src, dst, own_sem.at[i, s])

    for i, s in parts:
        give(i, s)
    steps, last = gather_steps(at, cuts, ins, outs, refs[2 * n + 8 :]) if n else ([], lambda: None)

    def pass_on(i, s):
        p = rows(s, i, over)
        at.arrived(p, kr.at[i, s, 0])
        at.send(p, p, ks.at[i, s, 2], kr.at[i, s, 2], at.cpeer)

    def ready(i):
        for s in (0, 1):
            if not at.draining:
                src, dst = (k_ref, v_ref)[s].at[i], rows(s, i, here)
                pltpu.make_async_copy(src, dst, own_sem.at[i, s]).wait()
            at.arrived(rows(s, i, beside), kr.at[i, s, 1])
            at.arrived(rows(s, i, across), kr.at[i, s, 2])
            at.keep(kv.at[s, i], kv_out.at[s, i], os.at[i, s])

    def head(i, h):
        win, inside = head_window(h)
        query = q_ref[i, :, win]
        query = jnp.where(inside, query, jnp.zeros_like(query))
        power = jnp.exp2(dot_t(query, kv[0, i, :, win]) * (HDIM ** (-0.5) * LOG2E))
        inv = 1.0 / jnp.sum(power, axis=-1, keepdims=True)
        out = jnp.dot(
            (power * inv).astype(jnp.bfloat16), kv[1, i, :, win], preferred_element_type=jnp.float32
        )
        o_ref[i, :, win] = jnp.where(inside, out.astype(jnp.bfloat16), o_ref[i, :, win])
        lane = lax.broadcasted_iota(jnp.int32, (1, LANES), 1)
        inv_ref[i] = jnp.where(lane == h, inv, inv_ref[i])

    o_ref[...] = jnp.zeros_like(o_ref)
    inv_ref[...] = jnp.zeros_like(inv_ref)
    early = steps[:5]
    for step in early:
        step()
    pass_on(0, 0)
    pass_on(0, 1)
    ready(0)
    todo = steps[5:]
    for i in range(images):
        if i > 0:
            pass_on(i, 0)
            pass_on(i, 1)
            ready(i)
        mine, todo = (todo[:HEADS], todo[HEADS:])

        def body(h, _, i=i, mine=mine):
            for k, step in enumerate(mine):
                pl.when(h == k)(step)
            head(i, h)
            return 0

        lax.fori_loop(0, HEADS, body, 0)
    for step in todo:
        step()
    last()
    at.drain(steps)
    for i, s in parts:
        at.drain([functools.partial(give, i, s), functools.partial(pass_on, i, s)])
    for i in range(images):
        at.drain([functools.partial(ready, i)])


def attention_forward(q, k, v, shards, cuts):
    n = len(shards)
    images, length, width = q.shape
    bands = lax.axis_size("band")
    keys = (2, images, bands * length, width)
    s = pltpu.SemaphoreType.DMA
    any_ref = pl.BlockSpec(memory_space=pl.ANY)
    vmem = pl.BlockSpec(memory_space=pltpu.VMEM)
    return pl.pallas_call(
        functools.partial(attention_kernel, cuts),
        out_shape=[
            jax.ShapeDtypeStruct(q.shape, jnp.bfloat16),
            jax.ShapeDtypeStruct((images, length, LANES), jnp.float32),
            jax.ShapeDtypeStruct(keys, jnp.bfloat16),
        ]
        + [jax.ShapeDtypeStruct((8,) + w.shape, w.dtype) for w in shards],
        in_specs=[vmem, any_ref, any_ref] + [any_ref] * n,
        out_specs=[vmem, vmem, any_ref] + [any_ref] * n,
        scratch_shapes=[
            pltpu.VMEM(keys, jnp.bfloat16),
            s((images, 2)),
            s((images, 2, 3)),
            s((images, 2, 3)),
            s((images, 2)),
        ]
        + (gather_sems(n) if n else []),
        compiler_params=pltpu.CompilerParams(
            collective_id=2, has_side_effects=True, vmem_limit_bytes=60 * 2**20
        ),
        name="attention_forward",
    )(q, k, v, *shards)
def attention_back_kernel(cuts, lags, q_ref, do_ref, inv_ref, kv_ref, *refs):
    n = len(cuts)
    ins, (dq_ref, d_out), outs = refs[:n], refs[n : n + 2], refs[n + 2 : 2 * n + 2]
    kv, dkv, core_buf, y_buf, load_sem, ks, kr, ys, yr, ws = refs[2 * n + 2 : 2 * n + 12]
    images, length, width = q_ref.shape
    at = Place()
    loads = [pltpu.make_async_copy(kv_ref.at[:, i], kv.at[i], load_sem.at[i]) for i in range(images)]
    for d in loads:
        d.start()
    at.greet_all() if n else at.greet_band()
    opening, todo, last = [], [], lambda: None
    if n:
        opening, todo, last = scatter_steps(at, cuts, ins, outs, refs[2 * n + 12 :], lags)
    for step in opening:
        step()
    steps = opening + todo

    def rows(s, i, band):
        return dkv.at[s, i, pl.ds(pl.multiple_of(band * length, 16), length), :]

    def to_core(i):
        for s in (0, 1):
            for yy in (0, 1):
                at.send(rows(s, i, yy * 2 + 1 - at.c), core_buf.at[i, s, yy], ks.at[i, s, yy], kr.at[i, s, yy], at.cpeer)

    def core_add(i):
        for s in (0, 1):
            p = rows(s, i, (1 - at.y) * 2 + at.c)
            at.arrived(core_buf.at[i, s, 1 - at.y], kr.at[i, s, 1 - at.y])
            if not at.draining:
                add_into(p, core_buf.at[i, s, 1 - at.y])
            at.send(p, y_buf.at[i, s], ys.at[i, s], yr.at[i, s], at.ypeer)
        for s in (0, 1):
            at.arrived(core_buf.at[i, s, at.y], kr.at[i, s, at.y])
            if not at.draining:
                add_into(rows(s, i, at.band), core_buf.at[i, s, at.y])

    def y_add(i):
        for s in (0, 1):
            p = rows(s, i, at.band)
            at.arrived(y_buf.at[i, s], yr.at[i, s])
            if not at.draining:
                add_into(p, y_buf.at[i, s])
            at.keep(p, d_out.at[s, i], ws.at[i, s])

    def head(i, h):
        win, inside = head_window(h)
        query, grad = q_ref[i, :, win], do_ref[i, :, win]
        query = jnp.where(inside, query, jnp.zeros_like(query))
        grad = jnp.where(inside, grad, jnp.zeros_like(grad))
        keys, values = kv[i, 0, :, win], kv[i, 1, :, win]
        inv = inv_ref[i, pl.ds(h, 1), :]
        probs = jnp.exp2(dot_t(keys, query) * (HDIM ** (-0.5) * LOG2E)) * inv
        d_probs = dot_t(values, grad)
        delta = jnp.sum(probs * d_probs, axis=0, keepdims=True)
        d_scores = (probs * (d_probs - delta)).astype(jnp.bfloat16)
        d_key = jnp.dot(d_scores, query, preferred_element_type=jnp.float32).astype(jnp.bfloat16)
        d_value = jnp.dot(
            probs.astype(jnp.bfloat16), grad, preferred_element_type=jnp.float32
        ).astype(jnp.bfloat16)
        dkv[0, i, :, win] = jnp.where(inside, d_key, dkv[0, i, :, win])
        dkv[1, i, :, win] = jnp.where(inside, d_value, dkv[1, i, :, win])
        dq_ref[i, :, win] = jnp.where(inside, first_dot(d_scores, keys), dq_ref[i, :, win])

    dq_ref[...] = jnp.zeros_like(dq_ref)
    for s in (0, 1):
        for i in range(images):

            def clear(r, _, s=s, i=i):
                dkv[s, i, pl.ds(pl.multiple_of(r * 16, 16), 16), :] = jnp.zeros((16, width), jnp.bfloat16)
                return 0

            lax.fori_loop(0, kv.shape[2] // 16, clear, 0)
    exchange = []
    for i in range(images):
        loads[i].wait()
        mine, todo = (todo[:HEADS], todo[HEADS:])
        due = exchange
        exchange = [functools.partial(f, i) for f in (core_add, y_add)]

        def body(h, _, i=i, mine=mine, due=due):
            for k, step in enumerate(due):
                pl.when(h == 1 + 12 * k)(step)
            for k, step in enumerate(mine):
                pl.when(h == k)(step)
            head(i, h)
            return 0

        lax.fori_loop(0, HEADS, body, 0)
        to_core(i)
        steps += [functools.partial(to_core, i)] + exchange
    exchange[0]()
    part = min(6, len(todo))
    for step in todo[:part] + [exchange[1]] + todo[part:]:
        step()
    last()
    at.drain(steps)


def attention_backward(q, d_att, inv_rows, kv_all, grads, cuts, lags):
    n = len(grads)
    images, length, width = q.shape
    s = pltpu.SemaphoreType.DMA
    any_ref = pl.BlockSpec(memory_space=pl.ANY)
    vmem = pl.BlockSpec(memory_space=pltpu.VMEM)
    bf = jnp.bfloat16
    return pl.pallas_call(
        functools.partial(attention_back_kernel, cuts, lags),
        out_shape=[
            jax.ShapeDtypeStruct(q.shape, jnp.float32),
            jax.ShapeDtypeStruct((2, images, length, width), bf),
        ]
        + [jax.ShapeDtypeStruct(w.shape[1:], bf) for w in grads],
        in_specs=[vmem, vmem, vmem, any_ref] + [any_ref] * n,
        out_specs=[vmem, any_ref] + [any_ref] * n,
        scratch_shapes=[
            pltpu.VMEM((images, 2) + kv_all.shape[2:], bf),
            pltpu.VMEM(kv_all.shape, bf),
            pltpu.VMEM((images, 2, 2, length, width), bf),
            pltpu.VMEM((images, 2, length, width), bf),
            s((images,)),
            s((images, 2, 2)),
            s((images, 2, 2)),
            s((images, 2)),
            s((images, 2)),
            s((images, 2)),
        ]
        + (scatter_scratch(grads, cuts) if n else []),
        compiler_params=pltpu.CompilerParams(
            collective_id=3, has_side_effects=True, vmem_limit_bytes=63 * 2**20
        ),
        name="attention_backward",
    )(q, d_att, inv_rows, kv_all, *grads)
def modulate(values, shift_in, scale_in):
    root = lax.rsqrt(jnp.mean(values * values, axis=-1, keepdims=True) + EPS)
    return values * root * (1.0 + scale_in[:, None, :]) + shift_in[:, None, :]


def swiglu(gate_in, up_in):
    return jax.nn.silu(gate_in) * up_in


def rope_tables(band, rows, cols):
    quarter = HDIM // 4
    lane = jnp.arange(HDIM, dtype=jnp.int32)
    part = lane // quarter
    frequency = 10000.0 ** (-(lane % quarter).astype(jnp.float32) / quarter)
    row_index = jnp.repeat(band * rows + jnp.arange(rows, dtype=jnp.int32), cols)
    col_index = jnp.tile(jnp.arange(cols, dtype=jnp.int32), rows)
    index = jnp.where(part[None, :] < 2, row_index[:, None], col_index[:, None])
    angle = index.astype(jnp.float32) * frequency[None, :]
    sine = jnp.sin(angle)
    low = (part % 2 == 0)[None, :]
    tables = (jnp.cos(angle), jnp.where(low, -sine, 0.0), jnp.where(low, 0.0, sine))
    return [jnp.tile(t, (1, HEADS)) for t in tables]


def half_cuts(axis, size, own_parts, shared_parts):
    unit = size // 2 // (own_parts + 2 * shared_parts)
    return (axis, size // 2, own_parts * unit, shared_parts * unit)


def by_shard(grad):
    parts = lax.axis_size("grp")
    return grad.reshape(parts, grad.shape[0] // parts, grad.shape[1])


def body(
    patches,
    grad_out,
    cond_table,
    group_ids,
    live_count,
    band_order,
    w_ada,
    b_ada,
    w_qkv,
    q_gain,
    k_gain,
    w_proj,
    w_gate,
    w_up,
    w_down,
):
    images, rows, cols, width = patches.shape
    length = rows * cols
    ff = w_gate.shape[1]
    bf = jnp.bfloat16
    grp = lax.axis_index("grp")
    ada_rows, ada_cols, bias_cols = w_ada.shape[0], w_ada.shape[1], b_ada.shape[0]
    fits = (
        lax.axis_size("grp") == 8
        and w_qkv.shape[0] % 16 == 0
        and 4 * width % 4608 == 0
        and 2 * ff % 1024 == 0
        and w_down.shape[0] % 128 == 0
    )
    qp_cut = half_cuts(1, 4 * width, 8, 5)
    gu_cut = half_cuts(1, 2 * ff, 2, 1)
    down_cut = half_cuts(0, w_down.shape[0], 2, 1)

    w_qp = jnp.concatenate([w_qkv, w_proj], axis=1)
    w_gu = jnp.concatenate([w_gate, w_up], axis=1)
    full = lambda w: w.reshape(-1, w.shape[-1])
    if fits:
        qp_all = full(gather([w_qp], (qp_cut,))[0])
    else:
        qp_all, gu_all, down_all = (lax.all_gather(w, "grp", axis=0, tiled=True) for w in (w_qp, w_gu, w_down))

    onehot = (group_ids[:, None] == jnp.arange(GROUPS, dtype=jnp.int32)[None, :]).astype(jnp.float32)
    cond_rows = lax.dynamic_slice_in_dim(cond_table, grp * ada_rows, ada_rows, axis=1)
    silu_rows, silu_pull = jax.vjp(jax.nn.silu, cond_rows)
    silu_rows = silu_rows.astype(bf)
    mod_part = jnp.dot(silu_rows, w_ada, preferred_element_type=jnp.float32)
    bias_part = lax.dynamic_update_slice_in_dim(
        jnp.zeros((ada_cols,), jnp.float32), b_ada.astype(jnp.float32), grp * bias_cols, axis=0
    )
    mod_table = lax.psum(mod_part + bias_part[None, :], "grp")
    mod = jnp.take(mod_table, group_ids, axis=0).reshape(images, 6, width)
    gate_one, shift_two, scale_two, gate_two = (mod[:, k] for k in (2, 3, 4, 5))
    live_mask = (jnp.arange(images, dtype=jnp.int32) < live_count[0]).astype(jnp.float32)

    tables = rope_tables(band_order[0], rows, cols)
    gains = jnp.stack([jnp.tile(q_gain, HEADS), jnp.tile(k_gain, HEADS)])
    head_of = jnp.arange(width, dtype=jnp.int32) // HDIM
    pick = (head_of[:, None] == jnp.arange(LANES, dtype=jnp.int32)[None, :]).astype(jnp.float32)
    spread = pick.T
    x = patches.reshape(images, length, width)
    normed_one, query, key, value, nq, nk, rq, rk = qkv_forward(x, mod, qp_all, gains, tables, pick, spread)
    attended, inv, kv_all, *rest = attention_forward(
        query, key, value, [w_gu, w_down] if fits else [], (gu_cut, down_cut) if fits else ()
    )
    if fits:
        gu_all, down_all = full(rest[0]), full(rest[1])
    proj_all = qp_all[:, 3 * width :]
    flat = lambda a: a.reshape(images * length, a.shape[-1])
    attended_low = flat(attended)
    proj = jnp.dot(attended_low, proj_all, preferred_element_type=jnp.float32).reshape(images, length, width)
    middle = x.astype(jnp.float32) + gate_one[:, None, :] * proj
    normed_two, norm_two_pull = jax.vjp(modulate, middle, shift_two, scale_two)
    normed_two_low = flat(normed_two.astype(bf))
    pre = jnp.dot(normed_two_low, gu_all, preferred_element_type=jnp.float32)
    hidden, swiglu_pull = jax.vjp(swiglu, pre[:, :ff], pre[:, ff:])
    hidden_low = hidden.astype(bf)
    mlp = jnp.dot(hidden_low, down_all, preferred_element_type=jnp.float32).reshape(images, length, width)
    output = (middle + gate_two[:, None, :] * mlp) * live_mask[:, None, None]
    patches_out = output.astype(bf).reshape(images, rows, cols, width)

    grad_y = grad_out.reshape(images, length, width).astype(jnp.float32) * live_mask[:, None, None]
    d_gate_two = jnp.sum(grad_y * mlp, axis=1)
    d_mlp = flat((grad_y * gate_two[:, None, :]).astype(bf))
    d_w_down = jnp.einsum("tf,td->fd", hidden_low, d_mlp, preferred_element_type=jnp.float32).astype(bf)
    d_hidden = jnp.einsum("td,fd->tf", d_mlp, down_all, preferred_element_type=jnp.float32)
    d_pre = jnp.concatenate([d.astype(bf) for d in swiglu_pull(d_hidden)], axis=1)
    d_w_gu = jnp.einsum("td,tf->df", normed_two_low, d_pre, preferred_element_type=jnp.float32).astype(bf)
    d_normed_two = jnp.einsum("tf,df->td", d_pre, gu_all, preferred_element_type=jnp.float32)
    d_middle_norm, d_shift_two, d_scale_two = norm_two_pull(d_normed_two.reshape(images, length, width))
    d_middle = grad_y + d_middle_norm
    d_gate_one = jnp.sum(d_middle * proj, axis=1)
    d_proj = flat((d_middle * gate_one[:, None, :]).astype(bf))
    d_w_proj = jnp.einsum("td,te->de", attended_low, d_proj, preferred_element_type=jnp.float32).astype(bf)
    d_attended = jnp.einsum("te,de->td", d_proj, proj_all, preferred_element_type=jnp.float32).astype(bf)
    d_query, d_kv, *rest = attention_backward(
        query,
        d_attended.reshape(images, length, width),
        jnp.swapaxes(inv, 1, 2),
        kv_all,
        [by_shard(d_w_gu)] if fits else [],
        (gu_cut,) if fits else (),
        (2, 2, 1, 2),
    )
    d_qkv, d_x, sums = qkv_backward(
        x, mod, d_middle, d_query, d_kv[0], d_kv[1], nq, nk, rq, rk, qp_all, gains, tables, pick, spread
    )
    d_patches = d_x.reshape(images, rows, cols, width)
    d_w_qkv = jnp.einsum("td,te->de", flat(normed_one), flat(d_qkv), preferred_element_type=jnp.float32).astype(bf)
    d_w_qp = jnp.concatenate([d_w_qkv, d_w_proj], axis=1)

    d_mod_part = jnp.concatenate(
        [sums[:, 0], sums[:, 1], d_gate_one, d_shift_two, d_scale_two, d_gate_two], axis=-1
    )
    gain_part = jnp.sum(sums[:, 2:4].reshape(images, 2, HEADS, HDIM), axis=(0, 2))
    summed = lax.psum(jnp.concatenate([d_mod_part.reshape(-1), gain_part.reshape(-1)]), "band")
    d_modulation = summed[: images * ada_cols].reshape(images, ada_cols).astype(bf)
    gain_sum = summed[images * ada_cols :]
    high = lax.reduce_precision(gain_sum, 8, 7)
    middle_part = lax.reduce_precision(gain_sum - high, 8, 7)
    pieces = jnp.stack([high, middle_part, gain_sum - high - middle_part]).astype(bf)
    payload = jnp.concatenate([d_modulation.reshape(-1), onehot.astype(bf).reshape(-1), pieces.reshape(-1)])
    payload = lax.all_gather(payload, "grp", axis=0)
    parts = payload.shape[0]
    at_onehot = images * ada_cols
    at_gain = at_onehot + images * GROUPS
    d_mod_all = payload[:, :at_onehot].reshape(parts * images, ada_cols)
    onehot_all = payload[:, at_onehot:at_gain].reshape(parts * images, GROUPS)
    gain_all = jnp.sum(payload[:, at_gain:].astype(jnp.float32).reshape(parts * 3, 2, HDIM), axis=0)
    silu_all = jnp.dot(onehot_all, silu_rows, preferred_element_type=jnp.float32).astype(bf)
    d_w_ada = jnp.einsum("bd,be->de", silu_all, d_mod_all, preferred_element_type=jnp.float32)
    d_b_ada = lax.dynamic_slice_in_dim(
        jnp.sum(d_mod_all.astype(jnp.float32), axis=0), grp * bias_cols, bias_cols, axis=0
    )
    d_silu = jnp.einsum("be,de->bd", d_mod_all, w_ada, preferred_element_type=jnp.float32)
    d_silu = jnp.dot(
        onehot_all.astype(jnp.float32).T,
        d_silu,
        precision=lax.Precision.HIGHEST,
        preferred_element_type=jnp.float32,
    )
    d_cond = lax.all_gather(silu_pull(d_silu)[0], "grp", axis=1, tiled=True)

    if fits:
        d_gu = rest[0]
        d_down, d_qp = scatter([by_shard(d_w_down), by_shard(d_w_qp)], (down_cut, qp_cut), (2, 2, 1, 2))
    else:
        d_gu, d_down, d_qp = (
            lax.psum(lax.psum_scatter(w, "grp", scatter_dimension=0, tiled=True), "band")
            for w in (d_w_gu, d_w_down, d_w_qp)
        )
    wide = lambda a: a.astype(jnp.float32)
    return (
        patches_out,
        d_patches,
        d_cond,
        d_w_ada,
        d_b_ada,
        wide(d_qp[:, : 3 * width]),
        gain_all[0],
        gain_all[1],
        wide(d_qp[:, 3 * width :]),
        wide(d_gu[:, :ff]),
        wide(d_gu[:, ff:]),
        wide(d_down),
    )


def solution(mesh):
    in_specs = (
        P("grp", "band", None, None),
        P("grp", "band", None, None),
        P(),
        P("grp"),
        P("grp"),
        P("band"),
        P("grp", None),
        P("grp"),
        P("grp", None),
        P(),
        P(),
        P("grp", None),
        P("grp", None),
        P("grp", None),
        P("grp", None),
    )
    out_specs = (
        P("grp", "band", None, None),
        P("grp", "band", None, None),
        P(),
        P("grp", None),
        P("grp"),
        P("grp", None),
        P(),
        P(),
        P("grp", None),
        P("grp", None),
        P("grp", None),
        P("grp", None),
    )
    return jax.shard_map(body, mesh=mesh, in_specs=in_specs, out_specs=out_specs, check_vma=False)
```

```python
import functools

import jax
import jax.numpy as jnp
from jax import lax
from jax.experimental import pallas as pl
from jax.experimental.pallas import tpu as pltpu
from jax.sharding import PartitionSpec as P

HEADS = 16
HDIM = 72
GROUPS = 8
LANES = 128
EPS = 1e-06
LOG2E = 1.4426950408889634

MESH = pl.DeviceIdType.MESH


class Place:
    def __init__(self):
        self.g, self.band = lax.axis_index("grp"), lax.axis_index("band")
        self.z, self.x = self.g // 2, self.g % 2
        self.y, self.c = self.band // 2, self.band % 2
        z = self.z
        self.far = [z, z + 1 - 2 * (z % 2), 2 - z // 2, 3 - 3 * (z // 2)]
        self.ypeer = (self.g, (1 - self.y) * 2 + self.c)
        self.cpeer = (self.g, self.y * 2 + 1 - self.c)
        self.xpeer = (z * 2 + 1 - self.x, self.band)
        self.draining = False

    def line(self, zz):
        return (zz * 2 + self.x, self.band)

    def greet(self, peers):
        bar = pltpu.get_barrier_semaphore()
        for d in peers:
            pl.semaphore_signal(bar, inc=1, device_id=d, device_id_type=MESH)
        pl.semaphore_wait(bar, len(peers))

    def greet_band(self):
        self.greet([self.ypeer, self.cpeer])

    def greet_all(self):
        self.greet([self.xpeer, self.ypeer, self.cpeer] + [self.line(zz) for zz in self.far[1:]])

    def copy(self, src, dst, ssem, rsem, dev):
        return pltpu.make_async_remote_copy(
            src_ref=src, dst_ref=dst, send_sem=ssem, recv_sem=rsem, device_id=dev, device_id_type=MESH
        )

    def send(self, src, dst, ssem, rsem, dev, cond=None):
        d = self.copy(src, dst, ssem, rsem, dev)
        act = d.wait_send if self.draining else d.start
        if cond is None:
            act()
        else:
            pl.when(cond)(act)

    def keep(self, src, dst, sem):
        d = pltpu.make_async_copy(src, dst, sem)
        d.wait() if self.draining else d.start()

    def arrived(self, ref, rsem):
        if not self.draining:
            self.copy(ref, ref, rsem, rsem, self.ypeer).wait_recv()

    def drain(self, steps):
        self.draining = True
        for step in steps:
            step()
        self.draining = False


def span(ref, axis, start, size):
    if axis == 0:
        return ref.at[pl.ds(pl.multiple_of(start, 16), size), :]
    return ref.at[:, pl.ds(pl.multiple_of(start, LANES), size)]


def gather_sems(n):
    s = pltpu.SemaphoreType.DMA
    return [s((n,)), s((n, 4)), s((n, 4)), s((n, 4)), s((n, 4)), s((n, 7)), s((n, 7)), s((n, 14)), s((n, 14)), s((n,))]


def gather_steps(at, cuts, ins, outs, sems):
    n = len(cuts)
    lsem, zs, zr, xs, xr, ys, yr, cs, cr, ds = sems
    ins, outs = ([refs[cut[5]] for cut in cuts] for refs in (ins, outs))
    soon = sum(cut[5] == 0 for cut in cuts)
    x, y, z, c, far = at.x, at.y, at.z, at.c, at.far

    def piece(i, ref, yy, cc):
        axis, half, a, b, base, _ = cuts[i]
        return span(ref, axis, base + cc * half + yy * b, a + b)

    def bpart(i, ref, yy, cc):
        axis, half, a, b, base, _ = cuts[i]
        return span(ref, axis, base + cc * half + yy * (a + b), b)

    def own(i):
        src, dst = piece(i, ins[i], y, c), piece(i, outs[i].at[at.g], y, c)
        at.send(src, dst, zs.at[i, 0], zr.at[i, z], (at.g + 2, at.band), z < 3)
        at.send(src, dst, ds.at[i], zr.at[i, z], (at.g - 2, at.band), z > 0)
        at.send(src, dst, xs.at[i, 0], xr.at[i, 0], at.xpeer)
        if cuts[i][4] == 0 and not (at.draining and cuts[i][5] == 0):
            at.keep(ins[i], outs[i].at[at.g], lsem.at[i])

    def down(i, slot, shard):
        p = bpart(i, outs[i].at[shard], y, c)
        at.send(p, p, ys.at[i, slot], yr.at[i, slot], at.ypeer)
        p = piece(i, outs[i].at[shard], y, c)
        at.send(p, p, cs.at[i, slot], cr.at[i, slot], at.cpeer)

    def zarr(i, t):
        zz = far[t]
        s = zz * 2 + x
        p = piece(i, outs[i].at[s], y, c)
        at.arrived(p, zr.at[i, zz])
        nxt = jnp.where(zz < z, z + 1, z - 1)
        at.send(p, p, zs.at[i, t], zr.at[i, zz], at.line(jnp.clip(nxt, 0, 3)), (nxt >= 0) & (nxt <= 3))
        at.send(p, p, xs.at[i, t], xr.at[i, t], at.xpeer)
        down(i, t - 1, s)

    def xarr(i, t):
        s = far[t] * 2 + 1 - x
        at.arrived(piece(i, outs[i].at[s], y, c), xr.at[i, t])
        down(i, 3 + t, s)

    def yarr(i, slot, s):
        p = bpart(i, outs[i].at[s], 1 - y, c)
        at.arrived(p, yr.at[i, slot])
        at.send(p, p, cs.at[i, 7 + slot], cr.at[i, 7 + slot], at.cpeer)

    slots = [(t - 1, far[t] * 2 + x) for t in (1, 2, 3)]
    slots += [(3 + t, far[t] * 2 + 1 - x) for t in range(4)]
    order = [slots[k] for k in (3, 0, 4, 1, 5, 2, 6)]
    steps = [lambda: own(0)]
    for i in range(n):
        mine = [lambda i=i: zarr(i, 1)]
        if i + 1 < n:
            mine.append(lambda i=i: own(i + 1))
        mine.append(lambda i=i: xarr(i, 0))
        for t in (2, 3):
            mine += [lambda i=i, t=t: zarr(i, t), lambda i=i, t=t: xarr(i, t - 1)]
        mine.append(lambda i=i: xarr(i, 3))
        if i > 0:
            late = [lambda i=i, k=k: yarr(i - 1, *order[k]) for k in range(7)]
            pace, held = 3 if i == soon else 1, list(late)
            merged = []
            while late or mine:
                merged += late[:pace] + mine[:1]
                late, mine = late[pace:], mine[1:]
            mine = merged
        if i == soon:
            first = len(steps) + max(k for k, step in enumerate(mine) if step in held) + 1
        steps += mine
    steps += [lambda k=k: yarr(n - 1, *order[k]) for k in range(7)]

    def last(i):
        for slot, s in slots:
            at.arrived(piece(i, outs[i].at[s], y, 1 - c), cr.at[i, slot])
            at.arrived(bpart(i, outs[i].at[s], 1 - y, 1 - c), cr.at[i, 7 + slot])

    return steps, first, last


def add_into(dst, src):
    def step(r, _):
        rows = pl.ds(pl.multiple_of(r * 16, 16), 16)
        dst[rows, :] = dst[rows, :] + src[rows, :]
        return 0

    lax.fori_loop(0, src.shape[0] // 16, step, 0)


def move_into(dst, src):
    def step(r, _):
        rows = pl.ds(pl.multiple_of(r * 16, 16), 16)
        dst[rows, :] = src[rows, :]
        return 0

    lax.fori_loop(0, src.shape[0] // 16, step, 0)


def scatter_scratch(grads, cuts):
    n = len(cuts)
    s = pltpu.SemaphoreType.DMA

    def buf(lead, k, size):
        grad = grads[cuts[k][5]]
        shape = (grad.shape[1], size) if cuts[k][0] == 1 else (size, grad.shape[2])
        return pltpu.VMEM(lead + shape, jnp.bfloat16)

    out = []
    for lead, pick in (
        ((8,), lambda c: c[1]),
        ((8,), lambda c: c[1]),
        ((8,), lambda c: c[3]),
        ((4,), lambda c: c[2] + c[3]),
        ((5,), lambda c: c[2] + c[3]),
        ((), lambda c: c[2] + c[3]),
    ):
        out += [buf(lead, k, pick(cuts[k])) for k in range(n)]
    out += [s((n, 8))] * 5 + [s((n, 4))] * 2 + [s((n, 3)), s((n, 5))] + [s((n,))] * 5
    return out


def scatter_steps(at, cuts, ins, outs, scratch, lags):
    n = len(cuts)
    own_half, core_buf, y_buf, x_buf, z_buf, fin_buf = (scratch[k * n : (k + 1) * n] for k in range(6))
    ls, cs, cr, ys, yr, xs, xr, zs, zr, fs, fr, es, er, ws = scratch[6 * n :]
    x, y, z, c, far = at.x, at.y, at.z, at.c, at.far
    ins, outs = ([refs[cut[5]] for cut in cuts] for refs in (ins, outs))

    def piece(i, ref):
        _, _, a, b = cuts[i][:4]
        return span(ref, cuts[i][0], y * b, a + b)

    def bpart(i, ref, yy):
        _, _, a, b = cuts[i][:4]
        return span(ref, cuts[i][0], yy * (a + b), b)

    order = [(t, j) for t in (3, 2, 1, 0) for j in (1, 0)]

    def shard(t, j):
        return far[t] * 2 + (1 - x if j else x)

    def load(i, t, j):
        axis, half, _, _, base, _ = cuts[i]
        s, q = shard(t, j), order.index((t, j))
        return pltpu.make_async_copy(span(ins[i].at[s], axis, base + c * half, half), own_half[i].at[s], ls.at[i, q])

    def give(i, t, j):
        axis, half, _, _, base, _ = cuts[i]
        s, q = shard(t, j), order.index((t, j))
        src = span(ins[i].at[s], axis, base + (1 - c) * half, half)
        at.send(src, core_buf[i].at[s], cs.at[i, q], cr.at[i, s], at.cpeer)
        if not at.draining:
            load(i, t, j).start()

    def to_y(i, t, j):
        s = shard(t, j)
        src = bpart(i, own_half[i].at[s], 1 - y)
        return at.copy(src, y_buf[i].at[s], ys.at[i, order.index((t, j))], yr.at[i, s], at.ypeer)

    def to_fin(i):
        return at.copy(piece(i, own_half[i].at[at.g]), fin_buf[i], fs.at[i], fr.at[i], at.ypeer)

    def cadd(i, t, j):
        s = shard(t, j)
        if at.draining:
            if (t, j) != (0, 0):
                to_y(i, t, j).wait_send()
            return
        load(i, t, j).wait()
        at.arrived(core_buf[i].at[s], cr.at[i, s])
        add_into(own_half[i].at[s], core_buf[i].at[s])
        to_y(i, t, j).start()

    def yadd(i, t, j):
        s = shard(t, j)
        at.arrived(y_buf[i].at[s], yr.at[i, s])
        if not at.draining:
            add_into(bpart(i, own_half[i].at[s], y), y_buf[i].at[s])
        if j:
            at.send(piece(i, own_half[i].at[s]), x_buf[i].at[far[t]], xs.at[i, t], xr.at[i, far[t]], at.xpeer)

    def xadd(i, t):
        if at.draining:
            return
        at.arrived(x_buf[i].at[far[t]], xr.at[i, far[t]])
        add_into(piece(i, own_half[i].at[shard(t, 0)]), x_buf[i].at[far[t]])

    def zadd(i, t):
        zz = far[t]
        p = piece(i, own_half[i].at[shard(t, 0)])

        def join(cond, slot):
            def do():
                at.arrived(z_buf[i].at[slot], zr.at[i, slot])
                add_into(p, z_buf[i].at[slot])

            if not at.draining:
                pl.when(cond)(do)

        if t > 0:
            inc = jnp.where(zz < z, z + 1, z - 1)
            join((inc >= 0) & (inc <= 3), zz)
            nxt = jnp.where(zz < z, z - 1, z + 1)
            slot = jnp.where((zz < z) & (nxt == zz), 4, zz)
            at.send(p, z_buf[i].at[slot], zs.at[i, t - 1], zr.at[i, slot], at.line(nxt))
        else:
            join(z > 0, z)
            join(z < 3, 4)
            if not at.draining:
                to_fin(i).start()

    def fin(i):
        axis, half, a, b, base, _ = cuts[i]
        own = own_half[i].at[at.g]
        if not at.draining:
            at.arrived(fin_buf[i], fr.at[i])
            to_fin(i).wait_send()
            to_y(i, 0, 0).wait_send()
            for yy in (0, 1):

                @pl.when(y == 1 - yy)
                def _():
                    add_into(span(own, axis, b, a), span(fin_buf[i], axis, b if yy == 0 else 0, a))
                    move_into(span(own, axis, yy * (a + b), b), span(fin_buf[i], axis, 0 if yy == 0 else a, b))

        o = span(outs[i], axis, base + c * half, half)
        at.send(own, o, es.at[i], er.at[i], at.cpeer)
        at.keep(own, o, ws.at[i])

    seq = [(i, t, j) for i in range(n) for (t, j) in order]
    opening = [functools.partial(give, *p) for p in seq]
    ly, lx, lz, lf = lags
    todo = []
    for q, (i, t, j) in enumerate(seq):
        todo.append((q, 0, functools.partial(cadd, i, t, j)))
        todo.append((q + ly, 1, functools.partial(yadd, i, t, j)))
        if j == 0:
            todo.append((q + ly + lx, 2, functools.partial(xadd, i, t)))
            todo.append((q + ly + lx + lz, 3, functools.partial(zadd, i, t)))
            if t == 0:
                todo.append((q + ly + lx + lz + lf, 4, functools.partial(fin, i)))
    todo.sort(key=lambda p: p[:2])

    def last():
        for i in range(n):
            axis, half, _, _, base, _ = cuts[i]
            at.arrived(span(outs[i], axis, base + (1 - c) * half, half), er.at[i])

    return opening, [f for _, _, f in todo], last


def scatter_kernel(n, cuts, lags, *refs):
    at = Place()
    at.greet_all()
    opening, steps, last = scatter_steps(at, cuts, refs[:n], refs[n : 2 * n], refs[2 * n :], lags)
    for step in opening + steps:
        step()
    last()
    at.drain(opening + steps)


def scatter(grads, cuts, lags):
    n = len(grads)
    return pl.pallas_call(
        functools.partial(scatter_kernel, n, cuts, lags),
        out_shape=[jax.ShapeDtypeStruct(w.shape[1:], jnp.bfloat16) for w in grads],
        in_specs=[pl.BlockSpec(memory_space=pl.ANY)] * n,
        out_specs=[pl.BlockSpec(memory_space=pl.ANY)] * n,
        scratch_shapes=scatter_scratch(grads, cuts),
        compiler_params=pltpu.CompilerParams(
            collective_id=1, has_side_effects=True, vmem_limit_bytes=60 * 2**20
        ),
        name="gradient_scatter",
    )(*grads)
def head_window(h):
    first = jnp.minimum(h * HDIM // LANES, HEADS * HDIM // LANES - 2) * LANES
    lane = lax.broadcasted_iota(jnp.int32, (1, 2 * LANES), 1) + first
    inside = (lane >= h * HDIM) & (lane < h * HDIM + HDIM)
    return pl.ds(pl.multiple_of(first, LANES), 2 * LANES), inside


def dot_t(left, right):
    return lax.dot_general(left, right, (((1,), (1,)), ((), ())), preferred_element_type=jnp.float32)


def first_dot(left, right):
    return lax.dot_general(left, right, (((0,), (0,)), ((), ())), preferred_element_type=jnp.float32)


def pick_dot(values, chosen):
    high = values.astype(jnp.bfloat16)
    low = (values - high.astype(jnp.float32)).astype(jnp.bfloat16)
    return jnp.dot(high, chosen, preferred_element_type=jnp.float32) + jnp.dot(
        low, chosen, preferred_element_type=jnp.float32
    )


def turn(values, cos, sin_next, sin_prev):
    width = values.shape[-1]
    after = pltpu.roll(values, width - HDIM // 4, 1)
    before = pltpu.roll(values, HDIM // 4, 1)
    return values * cos + after * sin_next + before * sin_prev


def turn_back(values, cos, sin_next, sin_prev):
    width = values.shape[-1]
    after = pltpu.roll(values, width - HDIM // 4, 1)
    before = pltpu.roll(values, HDIM // 4, 1)
    return values * cos - after * sin_next - before * sin_prev


def qkv_back_kernel(
    x_ref, mod_ref, mid_ref, dq_ref, dk_ref, dv_ref, nq_ref, nk_ref, rq_ref, rk_ref, w_ref,
    gains_ref, cos_ref, next_ref, prev_ref, pick_ref, spread_ref,
    dqkv_ref, dx_ref, sums_ref,
):
    width = x_ref.shape[-1]
    tables = (cos_ref[...], next_ref[...], prev_ref[...])
    ins = ((dq_ref, nq_ref, rq_ref), (dk_ref, nk_ref, rk_ref))
    for part, (d_ref, n_ref, r_ref) in enumerate(ins):
        back = turn_back(d_ref[0].astype(jnp.float32) * HDIM ** (-0.5), *tables)
        unit = n_ref[0]
        sums_ref[0, 2 + part : 3 + part, :] = jnp.sum(back * unit, axis=0, keepdims=True)
        inner = back * gains_ref[part : part + 1, :]
        mean = pick_dot(inner * unit, pick_ref[...]) * (1.0 / HDIM)
        grad = (inner - unit * pick_dot(mean, spread_ref[...])) * pick_dot(r_ref[0], spread_ref[...])
        dqkv_ref[0, :, part * width : (part + 1) * width] = grad.astype(jnp.bfloat16)
    dqkv_ref[0, :, 2 * width : 3 * width] = dv_ref[0]
    d_normed = dot_t(dqkv_ref[0], w_ref[...])
    x = x_ref[0].astype(jnp.float32)
    root = lax.rsqrt(jnp.mean(x * x, axis=-1, keepdims=True) + EPS)
    unit = x * root
    sums_ref[0, 0:1, :] = jnp.sum(d_normed, axis=0, keepdims=True)
    sums_ref[0, 1:2, :] = jnp.sum(d_normed * unit, axis=0, keepdims=True)
    inner = d_normed * (1.0 + mod_ref[0, 1:2, :])
    dx_ref[0] = mid_ref[0] + root * (inner - unit * jnp.mean(inner * unit, axis=-1, keepdims=True))


def qkv_backward(x, mod, d_mid, dq, dk, dv, nq, nk, rq, rk, qp_all, gains, tables, pick, spread):
    images, length, width = x.shape
    row = lambda w: pl.BlockSpec((1, length, w), lambda i: (i, 0, 0))
    whole = lambda a: pl.BlockSpec(a.shape, lambda i: (0,) * a.ndim)
    return pl.pallas_call(
        qkv_back_kernel,
        grid=(images,),
        in_specs=[row(width), pl.BlockSpec((1, 6, width), lambda i: (i, 0, 0))]
        + [row(width)] * 6
        + [row(LANES)] * 2
        + [pl.BlockSpec((width, 3 * width), lambda i: (0, 0)), whole(gains)]
        + [whole(t) for t in tables]
        + [whole(pick), whole(spread)],
        out_shape=[
            jax.ShapeDtypeStruct((images, length, 3 * width), jnp.bfloat16),
            jax.ShapeDtypeStruct((images, length, width), jnp.float32),
            jax.ShapeDtypeStruct((images, 4, width), jnp.float32),
        ],
        out_specs=[row(3 * width), row(width), pl.BlockSpec((1, 4, width), lambda i: (i, 0, 0))],
        compiler_params=pltpu.CompilerParams(vmem_limit_bytes=60 * 2**20),
        name="qkv_backward",
    )(x, mod, d_mid, dq, dk, dv, nq, nk, rq, rk, qp_all, gains, *tables, pick, spread)
def forward_kernel(cuts, refs):
    n = len(cuts)
    soon = sum(cut[5] == 0 for cut in cuts)
    at = Place()
    x_ref, part_ref, group_ref, gains_ref, cos_ref, next_ref, prev_ref, pick_ref, spread_ref = refs["in"]
    normed_ref, q_ref, nq_ref, nk_ref, rq_ref, rk_ref, o_ref, inv_ref, mod_ref, kv_out = refs["out"]
    kv, w_buf, mod_buf, mod_in, w_sem, ms, mr, ks, kr, os = refs["scratch"]
    ins, outs = refs["shards"], refs["full"]
    images, length, width = x_ref.shape
    parts = [(i, s) for i in range(images) for s in (0, 1)]
    if n:
        at.greet_all()
        steps, first, last = gather_steps(at, cuts, ins, outs, refs["sems"])
    else:
        at.greet_band()
        steps, first, last = [], 0, None

    mod_buf[...] = part_ref[...]

    def mod_copy(r):
        peer = (at.xpeer, at.line(at.far[1]), at.line((at.z + 2) % 4))[r]
        return at.copy(mod_buf, mod_in.at[r], ms.at[r], mr.at[r], peer)

    def mod_step(r):
        if at.draining:
            return
        if r > 0:
            mod_copy(r - 1).wait()
            mod_buf[...] = mod_buf[...] + mod_in[r - 1]
        if r < 3:
            mod_copy(r).start()

    def rows(s, i, band):
        return kv.at[s, i, pl.ds(pl.multiple_of(band * length, 16), length), :]

    here, over = at.band, (1 - at.y) * 2 + at.c
    beside, across = at.y * 2 + 1 - at.c, (1 - at.y) * 2 + 1 - at.c

    def give(i, s):
        p = rows(s, i, here)
        at.send(p, p, ks.at[i, s, 0], kr.at[i, s, 0], at.ypeer)
        at.send(p, p, ks.at[i, s, 1], kr.at[i, s, 1], at.cpeer)

    def pass_on(i, s):
        p = rows(s, i, over)
        at.arrived(p, kr.at[i, s, 0])
        at.send(p, p, ks.at[i, s, 2], kr.at[i, s, 2], at.cpeer)

    def ready(i):
        for s in (0, 1):
            at.arrived(rows(s, i, beside), kr.at[i, s, 1])
            at.arrived(rows(s, i, across), kr.at[i, s, 2])
            at.keep(kv.at[s, i], kv_out.at[s, i], os.at[i, s])

    def norm(i):
        value = x_ref[i].astype(jnp.float32)
        root = lax.rsqrt(jnp.mean(value * value, axis=-1, keepdims=True) + EPS)
        chosen = jnp.sum(group_ref[:, i : i + 1] * mod_buf[...], axis=0, keepdims=True)
        mod_ref[i : i + 1, :] = chosen
        shift, scale = chosen[:, :width], chosen[:, width : 2 * width]
        normed_ref[i] = (value * root * (1.0 + scale) + shift).astype(jnp.bfloat16)

    def raw(i, part):
        return jnp.dot(
            normed_ref[i], w_buf[:, part * width : (part + 1) * width], preferred_element_type=jnp.float32
        )

    def project(i, part, n_ref, r_ref):
        values = raw(i, part)
        inv = lax.rsqrt(pick_dot(values * values, pick_ref[...]) * (1.0 / HDIM) + EPS)
        r_ref[i] = inv
        unit = values * pick_dot(inv, spread_ref[...])
        n_ref[i] = unit
        scaled = unit * gains_ref[part : part + 1, :]
        return turn(scaled, cos_ref[...], next_ref[...], prev_ref[...]).astype(jnp.bfloat16)

    def key_part(i):
        norm(i)
        kv[0, i, pl.ds(pl.multiple_of(here * length, 16), length), :] = project(i, 1, nk_ref, rk_ref)
        give(i, 0)

    def value_part(i):
        kv[1, i, pl.ds(pl.multiple_of(here * length, 16), length), :] = raw(i, 2).astype(jnp.bfloat16)
        give(i, 1)

    def query_part(i):
        q_ref[i] = project(i, 0, nq_ref, rq_ref)

    def head(i, h):
        win, inside = head_window(h)
        query = q_ref[i, :, win]
        query = jnp.where(inside, query, jnp.zeros_like(query))
        power = jnp.exp2(dot_t(query, kv[0, i, :, win]) * (HDIM ** (-0.5) * LOG2E))
        inv = 1.0 / jnp.sum(power, axis=-1, keepdims=True)
        out = jnp.dot(
            (power * inv).astype(jnp.bfloat16), kv[1, i, :, win], preferred_element_type=jnp.float32
        )
        o_ref[i, :, win] = jnp.where(inside, out.astype(jnp.bfloat16), o_ref[i, :, win])
        lane = lax.broadcasted_iota(jnp.int32, (1, LANES), 1)
        inv_ref[i] = jnp.where(lane == h, inv, inv_ref[i])

    if n:
        for k in range(3):
            mod_step(k)
            for step in steps[2 * k : 2 * k + 2]:
                step()
        mod_step(3)
        for step in steps[6:first]:
            step()
        for i in range(soon):
            last(i)
        pltpu.make_async_copy(ins[0], outs[0].at[at.g], refs["sems"][0].at[0]).wait()
        loads = [
            pltpu.make_async_copy(
                outs[0].at[k, :, pl.ds(0, 3 * width)],
                w_buf.at[pl.ds(k * (width // 8), width // 8), :],
                w_sem.at[k],
            )
            for k in range(8)
        ]
    else:
        loads = [pltpu.make_async_copy(ins[0].at[:, pl.ds(0, 3 * width)], w_buf, w_sem.at[0])]
    for d in loads:
        d.start()
    o_ref[...] = jnp.zeros_like(o_ref)
    inv_ref[...] = jnp.zeros_like(inv_ref)
    for d in loads:
        d.wait()
    todo = steps[first:]
    for i in range(images):
        for work in (key_part, value_part):
            work(i)
            for step in todo[:2]:
                step()
            todo = todo[2:]
    for i in range(images):
        query_part(i)
        for step in todo[:2]:
            step()
        todo = todo[2:]
    for i in range(images):
        pass_on(i, 0)
        pass_on(i, 1)
        ready(i)
        mine, todo = (todo[: HEADS // 2], todo[HEADS // 2 :])

        def body(h, _, i=i, mine=mine):
            for k, step in enumerate(mine):
                pl.when(h == 2 * k)(step)
            head(i, h)
            return 0

        lax.fori_loop(0, HEADS, body, 0)
    for step in todo:
        step()
    for i in range(soon, n):
        last(i)
    at.drain(steps)
    for i, s in parts:
        at.drain([functools.partial(give, i, s), functools.partial(pass_on, i, s)])
    for i in range(images):
        at.drain([functools.partial(ready, i)])


def forward(x, mod_part, groups, gains, tables, pick, spread, shards, cuts):
    n = len(cuts)
    images, length, width = x.shape
    bands = lax.axis_size("band")
    keys = (2, images, bands * length, width)
    s = pltpu.SemaphoreType.DMA
    bf = jnp.bfloat16
    any_ref = pl.BlockSpec(memory_space=pl.ANY)
    vmem = pl.BlockSpec(memory_space=pltpu.VMEM)
    args = [x, mod_part, groups, gains, *tables, pick, spread]
    rows = lambda w, d: jax.ShapeDtypeStruct((images, length, w), d)
    outs = [rows(width, bf)] * 2 + [rows(width, jnp.float32)] * 2 + [rows(LANES, jnp.float32)] * 2
    outs += [rows(width, bf), rows(LANES, jnp.float32), jax.ShapeDtypeStruct((images, mod_part.shape[1]), jnp.float32)]
    scratch = [
        pltpu.VMEM(keys, bf),
        pltpu.VMEM((width, 3 * width), bf),
        pltpu.VMEM(mod_part.shape, jnp.float32),
        pltpu.VMEM((3,) + mod_part.shape, jnp.float32),
        s((8,)),
        s((3,)),
        s((3,)),
        s((images, 2, 3)),
        s((images, 2, 3)),
        s((images, 2)),
    ]
    whole = len(shards) if n else 0
    sizes = [len(args), len(shards), len(outs) + 1, whole, len(scratch), 10 if n else 0]

    def kernel(*refs):
        groups_of, start = [], 0
        for size in sizes:
            groups_of.append(refs[start : start + size])
            start += size
        names = ("in", "shards", "out", "full", "scratch", "sems")
        forward_kernel(cuts, dict(zip(names, groups_of)))

    return pl.pallas_call(
        kernel,
        out_shape=outs
        + [jax.ShapeDtypeStruct(keys, bf)]
        + [jax.ShapeDtypeStruct((8,) + w.shape, w.dtype) for w in shards[:whole]],
        in_specs=[vmem] * len(args) + [any_ref] * len(shards),
        out_specs=[vmem] * len(outs) + [any_ref] * (1 + whole),
        scratch_shapes=scratch + (gather_sems(n) if n else []),
        compiler_params=pltpu.CompilerParams(
            collective_id=2, has_side_effects=True, vmem_limit_bytes=60 * 2**20
        ),
        name="forward",
    )(*args, *shards)


EACH = 9


def attention_back_kernel(n, cuts, lags, q_ref, do_ref, inv_ref, kv_ref, *refs):
    ins, (dq_ref, d_out), outs = refs[:n], refs[n : n + 2], refs[n + 2 : 2 * n + 2]
    kv, dkv, core_buf, y_buf, load_sem, ks, kr, ys, yr, ws = refs[2 * n + 2 : 2 * n + 12]
    images, length, width = q_ref.shape
    at = Place()
    loads = [pltpu.make_async_copy(kv_ref.at[:, i], kv.at[i], load_sem.at[i]) for i in range(images)]
    for d in loads:
        d.start()
    at.greet_all() if n else at.greet_band()
    opening, todo, last = [], [], lambda: None
    if n:
        opening, todo, last = scatter_steps(at, cuts, ins, outs, refs[2 * n + 12 :], lags)
    for step in opening:
        step()
    steps = opening + todo

    def rows(s, i, band):
        return dkv.at[s, i, pl.ds(pl.multiple_of(band * length, 16), length), :]

    def to_core(i):
        for s in (0, 1):
            for yy in (0, 1):
                at.send(rows(s, i, yy * 2 + 1 - at.c), core_buf.at[i, s, yy], ks.at[i, s, yy], kr.at[i, s, yy], at.cpeer)

    def core_add(i):
        for s in (0, 1):
            p = rows(s, i, (1 - at.y) * 2 + at.c)
            at.arrived(core_buf.at[i, s, 1 - at.y], kr.at[i, s, 1 - at.y])
            if not at.draining:
                add_into(p, core_buf.at[i, s, 1 - at.y])
            at.send(p, y_buf.at[i, s], ys.at[i, s], yr.at[i, s], at.ypeer)
        for s in (0, 1):
            at.arrived(core_buf.at[i, s, at.y], kr.at[i, s, at.y])
            if not at.draining:
                add_into(rows(s, i, at.band), core_buf.at[i, s, at.y])

    def y_add(i):
        for s in (0, 1):
            p = rows(s, i, at.band)
            at.arrived(y_buf.at[i, s], yr.at[i, s])
            if not at.draining:
                add_into(p, y_buf.at[i, s])
            at.keep(p, d_out.at[s, i], ws.at[i, s])

    def head(i, h):
        win, inside = head_window(h)
        query, grad = q_ref[i, :, win], do_ref[i, :, win]
        query = jnp.where(inside, query, jnp.zeros_like(query))
        grad = jnp.where(inside, grad, jnp.zeros_like(grad))
        keys, values = kv[i, 0, :, win], kv[i, 1, :, win]
        inv = inv_ref[i, pl.ds(h, 1), :]
        probs = jnp.exp2(dot_t(keys, query) * (HDIM ** (-0.5) * LOG2E)) * inv
        d_probs = dot_t(values, grad)
        delta = jnp.sum(probs * d_probs, axis=0, keepdims=True)
        d_scores = (probs * (d_probs - delta)).astype(jnp.bfloat16)
        d_key = jnp.dot(d_scores, query, preferred_element_type=jnp.float32).astype(jnp.bfloat16)
        d_value = jnp.dot(
            probs.astype(jnp.bfloat16), grad, preferred_element_type=jnp.float32
        ).astype(jnp.bfloat16)
        dkv[0, i, :, win] = jnp.where(inside, d_key, dkv[0, i, :, win])
        dkv[1, i, :, win] = jnp.where(inside, d_value, dkv[1, i, :, win])
        dq_ref[i, :, win] = jnp.where(inside, first_dot(d_scores, keys), dq_ref[i, :, win])

    dq_ref[...] = jnp.zeros_like(dq_ref)
    for s in (0, 1):
        for i in range(images):

            def clear(r, _, s=s, i=i):
                dkv[s, i, pl.ds(pl.multiple_of(r * 16, 16), 16), :] = jnp.zeros((16, width), jnp.bfloat16)
                return 0

            lax.fori_loop(0, kv.shape[2] // 16, clear, 0)
    exchange = []
    for i in range(images):
        loads[i].wait()
        mine, todo = (todo[:EACH], todo[EACH:])
        due = exchange
        exchange = [functools.partial(f, i) for f in (core_add, y_add)]

        def body(h, _, i=i, mine=mine, due=due):
            for k, step in enumerate(due):
                pl.when(h == 1 + 12 * k)(step)
            for k, step in enumerate(mine):
                pl.when(h == k * HEADS // EACH)(step)
            head(i, h)
            return 0

        lax.fori_loop(0, HEADS, body, 0)
        to_core(i)
        steps += [functools.partial(to_core, i)] + exchange
    exchange[0]()
    part = min(6, len(todo))
    for step in todo[:part] + [exchange[1]] + todo[part:]:
        step()
    last()
    at.drain(steps)


def attention_backward(q, d_att, inv_rows, kv_all, grads, cuts, lags):
    n = len(grads)
    images, length, width = q.shape
    s = pltpu.SemaphoreType.DMA
    any_ref = pl.BlockSpec(memory_space=pl.ANY)
    vmem = pl.BlockSpec(memory_space=pltpu.VMEM)
    bf = jnp.bfloat16
    return pl.pallas_call(
        functools.partial(attention_back_kernel, n, cuts, lags),
        out_shape=[
            jax.ShapeDtypeStruct(q.shape, jnp.float32),
            jax.ShapeDtypeStruct((2, images, length, width), bf),
        ]
        + [jax.ShapeDtypeStruct(w.shape[1:], bf) for w in grads],
        in_specs=[vmem, vmem, vmem, any_ref] + [any_ref] * n,
        out_specs=[vmem, any_ref] + [any_ref] * n,
        scratch_shapes=[
            pltpu.VMEM((images, 2) + kv_all.shape[2:], bf),
            pltpu.VMEM(kv_all.shape, bf),
            pltpu.VMEM((images, 2, 2, length, width), bf),
            pltpu.VMEM((images, 2, length, width), bf),
            s((images,)),
            s((images, 2, 2)),
            s((images, 2, 2)),
            s((images, 2)),
            s((images, 2)),
            s((images, 2)),
        ]
        + (scatter_scratch(grads, cuts) if n else []),
        compiler_params=pltpu.CompilerParams(
            collective_id=3, has_side_effects=True, vmem_limit_bytes=63 * 2**20
        ),
        name="attention_backward",
    )(q, d_att, inv_rows, kv_all, *grads)
def modulate(values, shift_in, scale_in):
    root = lax.rsqrt(jnp.mean(values * values, axis=-1, keepdims=True) + EPS)
    return values * root * (1.0 + scale_in[:, None, :]) + shift_in[:, None, :]


def swiglu(gate_in, up_in):
    return jax.nn.silu(gate_in) * up_in


def rope_tables(band, rows, cols):
    quarter = HDIM // 4
    lane = jnp.arange(HDIM, dtype=jnp.int32)
    part = lane // quarter
    frequency = 10000.0 ** (-(lane % quarter).astype(jnp.float32) / quarter)
    row_index = jnp.repeat(band * rows + jnp.arange(rows, dtype=jnp.int32), cols)
    col_index = jnp.tile(jnp.arange(cols, dtype=jnp.int32), rows)
    index = jnp.where(part[None, :] < 2, row_index[:, None], col_index[:, None])
    angle = index.astype(jnp.float32) * frequency[None, :]
    sine = jnp.sin(angle)
    low = (part % 2 == 0)[None, :]
    tables = (jnp.cos(angle), jnp.where(low, -sine, 0.0), jnp.where(low, 0.0, sine))
    return [jnp.tile(t, (1, HEADS)) for t in tables]


def half_cuts(ref, axis, base, size, own_parts, shared_parts):
    unit = size // 2 // (own_parts + 2 * shared_parts)
    return (axis, size // 2, own_parts * unit, shared_parts * unit, base, ref)


def by_shard(grad):
    parts = lax.axis_size("grp")
    return grad.reshape(parts, grad.shape[0] // parts, grad.shape[1])


def body(
    patches,
    grad_out,
    cond_table,
    group_ids,
    live_count,
    band_order,
    w_ada,
    b_ada,
    w_qkv,
    q_gain,
    k_gain,
    w_proj,
    w_gate,
    w_up,
    w_down,
):
    images, rows, cols, width = patches.shape
    length = rows * cols
    ff = w_gate.shape[1]
    bf = jnp.bfloat16
    grp = lax.axis_index("grp")
    ada_rows, ada_cols, bias_cols = w_ada.shape[0], w_ada.shape[1], b_ada.shape[0]
    fits = (
        lax.axis_size("grp") == 8
        and w_qkv.shape[0] % 16 == 0
        and 4 * width % 4608 == 0
        and 2 * ff % 3072 == 0
        and w_down.shape[0] % 384 == 0
    )
    w_qp = jnp.concatenate([w_qkv, w_proj], axis=1)
    w_gu = jnp.concatenate([w_gate, w_up], axis=1)
    full = lambda w: w.reshape(-1, w.shape[-1])
    onehot = (group_ids[:, None] == jnp.arange(GROUPS, dtype=jnp.int32)[None, :]).astype(jnp.float32)
    cond_rows = lax.dynamic_slice_in_dim(cond_table, grp * ada_rows, ada_rows, axis=1)
    silu_rows, silu_pull = jax.vjp(jax.nn.silu, cond_rows)
    silu_rows = silu_rows.astype(bf)
    mod_part = jnp.dot(silu_rows, w_ada, preferred_element_type=jnp.float32)
    bias_part = lax.dynamic_update_slice_in_dim(
        jnp.zeros((ada_cols,), jnp.float32), b_ada.astype(jnp.float32), grp * bias_cols, axis=0
    )
    mod_part = mod_part + bias_part[None, :]
    live_mask = (jnp.arange(images, dtype=jnp.int32) < live_count[0]).astype(jnp.float32)

    tables = rope_tables(band_order[0], rows, cols)
    gains = jnp.stack([jnp.tile(q_gain, HEADS), jnp.tile(k_gain, HEADS)])
    head_of = jnp.arange(width, dtype=jnp.int32) // HDIM
    pick = (head_of[:, None] == jnp.arange(LANES, dtype=jnp.int32)[None, :]).astype(jnp.float32)
    spread = pick.T
    pick, spread = pick.astype(bf), spread.astype(bf)
    x = patches.reshape(images, length, width)
    groups = jnp.pad(onehot.T, ((0, 0), (0, LANES - images)))
    common = (groups, gains, tables, pick, spread)
    if fits:
        shards = [w_qp, w_gu, w_down]
        cuts = [half_cuts(0, 1, 0, 4 * width, 1, 1), half_cuts(1, 1, 0, 2 * ff, 4, 1)]
        cuts += [half_cuts(2, 0, 0, w_down.shape[0], 4, 1)]
    else:
        qp_all, gu_all, down_all = (lax.all_gather(w, "grp", axis=0, tiled=True) for w in (w_qp, w_gu, w_down))
        mod_part = lax.psum(mod_part, "grp")
        shards, cuts = [qp_all], []
    normed_one, query, nq, nk, rq, rk, attended, inv, mod, kv_all, *rest = forward(x, mod_part, *common, shards, cuts)
    if fits:
        qp_all, gu_all, down_all = (full(w) for w in rest)
    mod = mod.reshape(images, 6, width)
    gate_one, shift_two, scale_two, gate_two = (mod[:, k] for k in (2, 3, 4, 5))
    proj_all = qp_all[:, 3 * width :]
    flat = lambda a: a.reshape(images * length, a.shape[-1])
    attended_low = flat(attended)
    proj = jnp.dot(attended_low, proj_all, preferred_element_type=jnp.float32).reshape(images, length, width)
    middle = x.astype(jnp.float32) + gate_one[:, None, :] * proj
    normed_two, norm_two_pull = jax.vjp(modulate, middle, shift_two, scale_two)
    normed_two_low = flat(normed_two.astype(bf))
    pre = jnp.dot(normed_two_low, gu_all, preferred_element_type=jnp.float32)
    hidden, swiglu_pull = jax.vjp(swiglu, pre[:, :ff], pre[:, ff:])
    hidden_low = hidden.astype(bf)
    mlp = jnp.dot(hidden_low, down_all, preferred_element_type=jnp.float32).reshape(images, length, width)
    output = (middle + gate_two[:, None, :] * mlp) * live_mask[:, None, None]
    patches_out = output.astype(bf).reshape(images, rows, cols, width)

    grad_y = grad_out.reshape(images, length, width).astype(jnp.float32) * live_mask[:, None, None]
    d_gate_two = jnp.sum(grad_y * mlp, axis=1)
    d_mlp = flat((grad_y * gate_two[:, None, :]).astype(bf))
    d_w_down = jnp.einsum("tf,td->fd", hidden_low, d_mlp, preferred_element_type=jnp.float32).astype(bf)
    d_hidden = jnp.einsum("td,fd->tf", d_mlp, down_all, preferred_element_type=jnp.float32)
    d_pre = jnp.concatenate([d.astype(bf) for d in swiglu_pull(d_hidden)], axis=1)
    d_w_gu = jnp.einsum("td,tf->df", normed_two_low, d_pre, preferred_element_type=jnp.float32).astype(bf)
    d_normed_two = jnp.einsum("tf,df->td", d_pre, gu_all, preferred_element_type=jnp.float32)
    d_middle_norm, d_shift_two, d_scale_two = norm_two_pull(d_normed_two.reshape(images, length, width))
    d_middle = grad_y + d_middle_norm
    d_gate_one = jnp.sum(d_middle * proj, axis=1)
    d_proj = flat((d_middle * gate_one[:, None, :]).astype(bf))
    d_w_proj = jnp.einsum("td,te->de", attended_low, d_proj, preferred_element_type=jnp.float32).astype(bf)
    d_attended = jnp.einsum("te,de->td", d_proj, proj_all, preferred_element_type=jnp.float32).astype(bf)
    d_query, d_kv, *rest = attention_backward(
        query,
        d_attended.reshape(images, length, width),
        jnp.swapaxes(inv, 1, 2),
        kv_all,
        [by_shard(d_w_gu)] if fits else [],
        [half_cuts(0, 1, 0, 2 * ff, 4, 1)] if fits else [],
        (2, 2, 1, 2),
    )
    d_qkv, d_x, sums = qkv_backward(
        x, mod, d_middle, d_query, d_kv[0], d_kv[1], nq, nk, rq, rk, qp_all, gains, tables, pick, spread
    )
    d_patches = d_x.reshape(images, rows, cols, width)
    d_w_qkv = jnp.einsum("td,te->de", flat(normed_one), flat(d_qkv), preferred_element_type=jnp.float32).astype(bf)
    d_w_qp = jnp.concatenate([d_w_qkv, d_w_proj], axis=1)

    d_mod_part = jnp.concatenate(
        [sums[:, 0], sums[:, 1], d_gate_one, d_shift_two, d_scale_two, d_gate_two], axis=-1
    )
    gain_part = jnp.sum(sums[:, 2:4].reshape(images, 2, HEADS, HDIM), axis=(0, 2))
    summed = lax.psum(jnp.concatenate([d_mod_part.reshape(-1), gain_part.reshape(-1)]), "band")
    d_modulation = summed[: images * ada_cols].reshape(images, ada_cols).astype(bf)
    gain_sum = summed[images * ada_cols :]
    high = lax.reduce_precision(gain_sum, 8, 7)
    middle_part = lax.reduce_precision(gain_sum - high, 8, 7)
    pieces = jnp.stack([high, middle_part, gain_sum - high - middle_part]).astype(bf)
    payload = jnp.concatenate([d_modulation.reshape(-1), onehot.astype(bf).reshape(-1), pieces.reshape(-1)])
    payload = lax.all_gather(payload, "grp", axis=0)
    parts = payload.shape[0]
    at_onehot = images * ada_cols
    at_gain = at_onehot + images * GROUPS
    d_mod_all = payload[:, :at_onehot].reshape(parts * images, ada_cols)
    onehot_all = payload[:, at_onehot:at_gain].reshape(parts * images, GROUPS)
    gain_all = jnp.sum(payload[:, at_gain:].astype(jnp.float32).reshape(parts * 3, 2, HDIM), axis=0)
    silu_all = jnp.dot(onehot_all, silu_rows, preferred_element_type=jnp.float32).astype(bf)
    d_w_ada = jnp.einsum("bd,be->de", silu_all, d_mod_all, preferred_element_type=jnp.float32)
    d_b_ada = lax.dynamic_slice_in_dim(
        jnp.sum(d_mod_all.astype(jnp.float32), axis=0), grp * bias_cols, bias_cols, axis=0
    )
    d_silu = jnp.einsum("be,de->bd", d_mod_all, w_ada, preferred_element_type=jnp.float32)
    d_silu = jnp.dot(
        onehot_all.astype(jnp.float32).T,
        d_silu,
        precision=lax.Precision.HIGHEST,
        preferred_element_type=jnp.float32,
    )
    d_cond = lax.all_gather(silu_pull(d_silu)[0], "grp", axis=1, tiled=True)

    if fits:
        d_gu = rest[0]
        cuts = [half_cuts(0, 0, 0, w_down.shape[0], 2, 1)]
        cuts += [half_cuts(1, 1, 0, 4 * width, 8, 5)]
        d_down, d_qp = scatter([by_shard(d_w_down), by_shard(d_w_qp)], cuts, (2, 2, 1, 2))
    else:
        d_gu, d_down, d_qp = (
            lax.psum(lax.psum_scatter(w, "grp", scatter_dimension=0, tiled=True), "band")
            for w in (d_w_gu, d_w_down, d_w_qp)
        )
    wide = lambda a: a.astype(jnp.float32)
    return (
        patches_out,
        d_patches,
        d_cond,
        d_w_ada,
        d_b_ada,
        wide(d_qp[:, : 3 * width]),
        gain_all[0],
        gain_all[1],
        wide(d_qp[:, 3 * width :]),
        wide(d_gu[:, :ff]),
        wide(d_gu[:, ff:]),
        wide(d_down),
    )


def solution(mesh):
    in_specs = (
        P("grp", "band", None, None),
        P("grp", "band", None, None),
        P(),
        P("grp"),
        P("grp"),
        P("band"),
        P("grp", None),
        P("grp"),
        P("grp", None),
        P(),
        P(),
        P("grp", None),
        P("grp", None),
        P("grp", None),
        P("grp", None),
    )
    out_specs = (
        P("grp", "band", None, None),
        P("grp", "band", None, None),
        P(),
        P("grp", None),
        P("grp"),
        P("grp", None),
        P(),
        P(),
        P("grp", None),
        P("grp", None),
        P("grp", None),
        P("grp", None),
    )
    return jax.shard_map(body, mesh=mesh, in_specs=in_specs, out_specs=out_specs, check_vma=False)
```

```python
import functools
import math

import jax
import jax.numpy as jnp
from jax import lax
from jax.experimental import pallas as pl
from jax.experimental.pallas import tpu as pltpu
from jax.sharding import PartitionSpec as P

HEADS = 16
HDIM = 72
GROUPS = 8
LANES = 128
EPS = 1e-06
LOG2E = 1.4426950408889634

MESH = pl.DeviceIdType.MESH


class Place:
    def __init__(self):
        self.g, self.band = lax.axis_index("grp"), lax.axis_index("band")
        self.z, self.x = self.g // 2, self.g % 2
        self.y, self.c = self.band // 2, self.band % 2
        z = self.z
        self.far = [z, z + 1 - 2 * (z % 2), 2 - z // 2, 3 - 3 * (z // 2)]
        self.ypeer = (self.g, (1 - self.y) * 2 + self.c)
        self.cpeer = (self.g, self.y * 2 + 1 - self.c)
        self.xpeer = (z * 2 + 1 - self.x, self.band)
        self.draining = False

    def line(self, zz):
        return (zz * 2 + self.x, self.band)

    def greet(self, peers):
        bar = pltpu.get_barrier_semaphore()
        for d in peers:
            pl.semaphore_signal(bar, inc=1, device_id=d, device_id_type=MESH)
        pl.semaphore_wait(bar, len(peers))

    def greet_band(self):
        self.greet([self.ypeer, self.cpeer])

    def greet_all(self):
        self.greet([self.xpeer, self.ypeer, self.cpeer] + [self.line(zz) for zz in self.far[1:]])

    def copy(self, src, dst, ssem, rsem, dev):
        return pltpu.make_async_remote_copy(
            src_ref=src, dst_ref=dst, send_sem=ssem, recv_sem=rsem, device_id=dev, device_id_type=MESH
        )

    def send(self, src, dst, ssem, rsem, dev, cond=None):
        d = self.copy(src, dst, ssem, rsem, dev)
        act = d.wait_send if self.draining else d.start
        if cond is None:
            act()
        else:
            pl.when(cond)(act)

    def keep(self, src, dst, sem):
        d = pltpu.make_async_copy(src, dst, sem)
        d.wait() if self.draining else d.start()

    def arrived(self, ref, rsem):
        if not self.draining:
            self.copy(ref, ref, rsem, rsem, self.ypeer).wait_recv()

    def drain(self, steps):
        self.draining = True
        for step in steps:
            step()
        self.draining = False


def span(ref, axis, start, size):
    if axis == 0:
        return ref.at[pl.ds(pl.multiple_of(start, 16), size), :]
    return ref.at[:, pl.ds(pl.multiple_of(start, LANES), size)]


def gather_sems(n):
    s = pltpu.SemaphoreType.DMA
    return [s((n,)), s((n, 4)), s((n, 4)), s((n, 4)), s((n, 4)), s((n, 7)), s((n, 7)), s((n, 14)), s((n, 14)), s((n,))]


def gather_steps(at, cuts, ins, outs, sems):
    n = len(cuts)
    lsem, zs, zr, xs, xr, ys, yr, cs, cr, ds = sems
    ins, outs = ([refs[cut[5]] for cut in cuts] for refs in (ins, outs))
    soon = sum(cut[5] == 0 for cut in cuts)
    x, y, z, c, far = at.x, at.y, at.z, at.c, at.far

    def piece(i, ref, yy, cc):
        axis, half, a, b, base, _ = cuts[i]
        return span(ref, axis, base + cc * half + yy * b, a + b)

    def bpart(i, ref, yy, cc):
        axis, half, a, b, base, _ = cuts[i]
        return span(ref, axis, base + cc * half + yy * (a + b), b)

    def own(i):
        src, dst = piece(i, ins[i], y, c), piece(i, outs[i].at[at.g], y, c)
        at.send(src, dst, zs.at[i, 0], zr.at[i, z], (at.g + 2, at.band), z < 3)
        at.send(src, dst, ds.at[i], zr.at[i, z], (at.g - 2, at.band), z > 0)
        at.send(src, dst, xs.at[i, 0], xr.at[i, 0], at.xpeer)
        if cuts[i][4] == 0 and not (at.draining and cuts[i][5] == 0):
            at.keep(ins[i], outs[i].at[at.g], lsem.at[i])

    def down(i, slot, shard):
        p = bpart(i, outs[i].at[shard], y, c)
        at.send(p, p, ys.at[i, slot], yr.at[i, slot], at.ypeer)
        p = piece(i, outs[i].at[shard], y, c)
        at.send(p, p, cs.at[i, slot], cr.at[i, slot], at.cpeer)

    def zarr(i, t):
        zz = far[t]
        s = zz * 2 + x
        p = piece(i, outs[i].at[s], y, c)
        at.arrived(p, zr.at[i, zz])
        nxt = jnp.where(zz < z, z + 1, z - 1)
        at.send(p, p, zs.at[i, t], zr.at[i, zz], at.line(jnp.clip(nxt, 0, 3)), (nxt >= 0) & (nxt <= 3))
        at.send(p, p, xs.at[i, t], xr.at[i, t], at.xpeer)
        down(i, t - 1, s)

    def xarr(i, t):
        s = far[t] * 2 + 1 - x
        at.arrived(piece(i, outs[i].at[s], y, c), xr.at[i, t])
        down(i, 3 + t, s)

    def yarr(i, slot, s):
        p = bpart(i, outs[i].at[s], 1 - y, c)
        at.arrived(p, yr.at[i, slot])
        at.send(p, p, cs.at[i, 7 + slot], cr.at[i, 7 + slot], at.cpeer)

    slots = [(t - 1, far[t] * 2 + x) for t in (1, 2, 3)]
    slots += [(3 + t, far[t] * 2 + 1 - x) for t in range(4)]
    order = [slots[k] for k in (3, 0, 4, 1, 5, 2, 6)]
    steps = [lambda: own(0)]
    for i in range(n):
        mine = [lambda i=i: zarr(i, 1)]
        if i + 1 < n:
            mine.append(lambda i=i: own(i + 1))
        mine.append(lambda i=i: xarr(i, 0))
        for t in (2, 3):
            mine += [lambda i=i, t=t: zarr(i, t), lambda i=i, t=t: xarr(i, t - 1)]
        mine.append(lambda i=i: xarr(i, 3))
        if i > 0:
            late = [lambda i=i, k=k: yarr(i - 1, *order[k]) for k in range(7)]
            pace, held = 3 if i == soon else 1, list(late)
            merged = []
            while late or mine:
                merged += late[:pace] + mine[:1]
                late, mine = late[pace:], mine[1:]
            mine = merged
        if i == soon:
            first = len(steps) + max(k for k, step in enumerate(mine) if step in held) + 1
        steps += mine
    steps += [lambda k=k: yarr(n - 1, *order[k]) for k in range(7)]

    def last(i):
        for slot, s in slots:
            at.arrived(piece(i, outs[i].at[s], y, 1 - c), cr.at[i, slot])
            at.arrived(bpart(i, outs[i].at[s], 1 - y, 1 - c), cr.at[i, 7 + slot])

    return steps, first, last


def add_into(dst, src):
    def step(r, _):
        rows = pl.ds(pl.multiple_of(r * 16, 16), 16)
        dst[rows, :] = dst[rows, :] + src[rows, :]
        return 0

    lax.fori_loop(0, src.shape[0] // 16, step, 0)


def move_into(dst, src):
    def step(r, _):
        rows = pl.ds(pl.multiple_of(r * 16, 16), 16)
        dst[rows, :] = src[rows, :]
        return 0

    lax.fori_loop(0, src.shape[0] // 16, step, 0)


def scatter_scratch(grads, cuts):
    n = len(cuts)
    s = pltpu.SemaphoreType.DMA

    def buf(lead, k, size):
        grad = grads[cuts[k][5]]
        shape = (grad.shape[1], size) if cuts[k][0] == 1 else (size, grad.shape[2])
        return pltpu.VMEM(lead + shape, jnp.bfloat16)

    out = []
    for lead, pick in (
        ((8,), lambda c: c[1]),
        ((8,), lambda c: c[1]),
        ((8,), lambda c: c[3]),
        ((4,), lambda c: c[2] + c[3]),
        ((5,), lambda c: c[2] + c[3]),
        ((), lambda c: c[2] + c[3]),
    ):
        out += [buf(lead, k, pick(cuts[k])) for k in range(n)]
    out += [s((n, 8))] * 5 + [s((n, 4))] * 2 + [s((n, 3)), s((n, 5))] + [s((n,))] * 5
    return out


def scatter_steps(at, cuts, ins, outs, scratch, lags):
    n = len(cuts)
    own_half, core_buf, y_buf, x_buf, z_buf, fin_buf = (scratch[k * n : (k + 1) * n] for k in range(6))
    ls, cs, cr, ys, yr, xs, xr, zs, zr, fs, fr, es, er, ws = scratch[6 * n :]
    x, y, z, c, far = at.x, at.y, at.z, at.c, at.far
    ins, outs = ([refs[cut[5]] for cut in cuts] for refs in (ins, outs))

    def piece(i, ref):
        _, _, a, b = cuts[i][:4]
        return span(ref, cuts[i][0], y * b, a + b)

    def bpart(i, ref, yy):
        _, _, a, b = cuts[i][:4]
        return span(ref, cuts[i][0], yy * (a + b), b)

    order = [(t, j) for t in (3, 2, 1, 0) for j in (1, 0)]

    def shard(t, j):
        return far[t] * 2 + (1 - x if j else x)

    def load(i, t, j):
        axis, half, _, _, base, _ = cuts[i]
        s, q = shard(t, j), order.index((t, j))
        return pltpu.make_async_copy(span(ins[i].at[s], axis, base + c * half, half), own_half[i].at[s], ls.at[i, q])

    def give(i, t, j):
        axis, half, _, _, base, _ = cuts[i]
        s, q = shard(t, j), order.index((t, j))
        src = span(ins[i].at[s], axis, base + (1 - c) * half, half)
        at.send(src, core_buf[i].at[s], cs.at[i, q], cr.at[i, s], at.cpeer)
        if not at.draining:
            load(i, t, j).start()

    def to_y(i, t, j):
        s = shard(t, j)
        src = bpart(i, own_half[i].at[s], 1 - y)
        return at.copy(src, y_buf[i].at[s], ys.at[i, order.index((t, j))], yr.at[i, s], at.ypeer)

    def to_fin(i):
        return at.copy(piece(i, own_half[i].at[at.g]), fin_buf[i], fs.at[i], fr.at[i], at.ypeer)

    def cadd(i, t, j):
        s = shard(t, j)
        if at.draining:
            if (t, j) != (0, 0):
                to_y(i, t, j).wait_send()
            return
        load(i, t, j).wait()
        at.arrived(core_buf[i].at[s], cr.at[i, s])
        add_into(own_half[i].at[s], core_buf[i].at[s])
        to_y(i, t, j).start()

    def yadd(i, t, j):
        s = shard(t, j)
        at.arrived(y_buf[i].at[s], yr.at[i, s])
        if not at.draining:
            add_into(bpart(i, own_half[i].at[s], y), y_buf[i].at[s])
        if j:
            at.send(piece(i, own_half[i].at[s]), x_buf[i].at[far[t]], xs.at[i, t], xr.at[i, far[t]], at.xpeer)

    def xadd(i, t):
        if at.draining:
            return
        at.arrived(x_buf[i].at[far[t]], xr.at[i, far[t]])
        add_into(piece(i, own_half[i].at[shard(t, 0)]), x_buf[i].at[far[t]])

    def zadd(i, t):
        zz = far[t]
        p = piece(i, own_half[i].at[shard(t, 0)])

        def join(cond, slot):
            def do():
                at.arrived(z_buf[i].at[slot], zr.at[i, slot])
                add_into(p, z_buf[i].at[slot])

            if not at.draining:
                pl.when(cond)(do)

        if t > 0:
            inc = jnp.where(zz < z, z + 1, z - 1)
            join((inc >= 0) & (inc <= 3), zz)
            nxt = jnp.where(zz < z, z - 1, z + 1)
            slot = jnp.where((zz < z) & (nxt == zz), 4, zz)
            at.send(p, z_buf[i].at[slot], zs.at[i, t - 1], zr.at[i, slot], at.line(nxt))
        else:
            join(z > 0, z)
            join(z < 3, 4)
            if not at.draining:
                to_fin(i).start()

    def fin(i):
        axis, half, a, b, base, _ = cuts[i]
        own = own_half[i].at[at.g]
        if not at.draining:
            at.arrived(fin_buf[i], fr.at[i])
            to_fin(i).wait_send()
            to_y(i, 0, 0).wait_send()
            for yy in (0, 1):

                @pl.when(y == 1 - yy)
                def _():
                    add_into(span(own, axis, b, a), span(fin_buf[i], axis, b if yy == 0 else 0, a))
                    move_into(span(own, axis, yy * (a + b), b), span(fin_buf[i], axis, 0 if yy == 0 else a, b))

        o = span(outs[i], axis, base + c * half, half)
        at.send(own, o, es.at[i], er.at[i], at.cpeer)
        at.keep(own, o, ws.at[i])

    seq = [(i, t, j) for i in range(n) for (t, j) in order]
    opening = [functools.partial(give, *p) for p in seq]
    ly, lx, lz, lf = lags
    todo = []
    for q, (i, t, j) in enumerate(seq):
        todo.append((q, 0, functools.partial(cadd, i, t, j)))
        todo.append((q + ly, 1, functools.partial(yadd, i, t, j)))
        if j == 0:
            todo.append((q + ly + lx, 2, functools.partial(xadd, i, t)))
            todo.append((q + ly + lx + lz, 3, functools.partial(zadd, i, t)))
            if t == 0:
                todo.append((q + ly + lx + lz + lf, 4, functools.partial(fin, i)))
    todo.sort(key=lambda p: p[:2])

    def last():
        for i in range(n):
            axis, half, _, _, base, _ = cuts[i]
            at.arrived(span(outs[i], axis, base + (1 - c) * half, half), er.at[i])

    return opening, [f for _, _, f in todo], last


def head_window(h):
    first = jnp.minimum(h * HDIM // LANES, HEADS * HDIM // LANES - 2) * LANES
    lane = lax.broadcasted_iota(jnp.int32, (1, 2 * LANES), 1) + first
    inside = (lane >= h * HDIM) & (lane < h * HDIM + HDIM)
    return pl.ds(pl.multiple_of(first, LANES), 2 * LANES), inside


def dot_t(left, right):
    return lax.dot_general(left, right, (((1,), (1,)), ((), ())), preferred_element_type=jnp.float32)


def first_dot(left, right):
    return lax.dot_general(left, right, (((0,), (0,)), ((), ())), preferred_element_type=jnp.float32)


def pick_dot(values, chosen):
    high = values.astype(jnp.bfloat16)
    low = (values - high.astype(jnp.float32)).astype(jnp.bfloat16)
    return jnp.dot(high, chosen, preferred_element_type=jnp.float32) + jnp.dot(
        low, chosen, preferred_element_type=jnp.float32
    )


def head_pick(width):
    row = lax.broadcasted_iota(jnp.int32, (width, LANES), 0)
    first = lax.broadcasted_iota(jnp.int32, (width, LANES), 1) * HDIM
    return ((row >= first) & (row < first + HDIM)).astype(jnp.float32).astype(jnp.bfloat16)


def head_spread(width):
    lane = lax.broadcasted_iota(jnp.int32, (LANES, width), 1)
    first = lax.broadcasted_iota(jnp.int32, (LANES, width), 0) * HDIM
    return ((lane >= first) & (lane < first + HDIM)).astype(jnp.float32).astype(jnp.bfloat16)


def rope_tables(band, rows, cols, width):
    quarter = HDIM // 4
    shape = (rows * cols, width)
    token = lax.broadcasted_iota(jnp.int32, shape, 0)
    lane = lax.broadcasted_iota(jnp.int32, shape, 1) % HDIM
    power = (lane % quarter).astype(jnp.float32) * (-math.log(10000.0) / quarter)
    by_row = band * rows + (token // cols).astype(jnp.float32)
    index = jnp.where(lane < 2 * quarter, by_row, (token % cols).astype(jnp.float32))
    angle = index * jnp.exp(power)
    sine = jnp.sin(angle)
    low = (lane // quarter) % 2 == 0
    return jnp.cos(angle), jnp.where(low, -sine, 0.0), jnp.where(low, 0.0, sine)


def turn(values, cos, sin_next, sin_prev):
    width = values.shape[-1]
    after = pltpu.roll(values, width - HDIM // 4, 1)
    before = pltpu.roll(values, HDIM // 4, 1)
    return values * cos + after * sin_next + before * sin_prev


def turn_back(values, cos, sin_next, sin_prev):
    width = values.shape[-1]
    after = pltpu.roll(values, width - HDIM // 4, 1)
    before = pltpu.roll(values, HDIM // 4, 1)
    return values * cos - after * sin_next - before * sin_prev


def qkv_back_kernel(
    x_ref, mod_ref, mid_ref, dq_ref, dk_ref, dv_ref, nq_ref, nk_ref, rq_ref, rk_ref, w_ref,
    gains_ref, cos_ref, next_ref, prev_ref,
    dqkv_ref, dx_ref, sums_ref,
):
    width = x_ref.shape[-1]
    tables = (cos_ref[...], next_ref[...], prev_ref[...])
    pick, spread = head_pick(width), head_spread(width)
    ins = ((dq_ref, nq_ref, rq_ref), (dk_ref, nk_ref, rk_ref))
    for part, (d_ref, n_ref, r_ref) in enumerate(ins):
        back = turn_back(d_ref[0].astype(jnp.float32) * HDIM ** (-0.5), *tables)
        unit = n_ref[0]
        sums_ref[0, 2 + part : 3 + part, :] = jnp.sum(back * unit, axis=0, keepdims=True)
        inner = back * gains_ref[part : part + 1, :]
        mean = pick_dot(inner * unit, pick) * (1.0 / HDIM)
        grad = (inner - unit * pick_dot(mean, spread)) * pick_dot(r_ref[0], spread)
        dqkv_ref[0, :, part * width : (part + 1) * width] = grad.astype(jnp.bfloat16)
    dqkv_ref[0, :, 2 * width : 3 * width] = dv_ref[0]
    d_normed = dot_t(dqkv_ref[0], w_ref[...])
    x = x_ref[0].astype(jnp.float32)
    root = lax.rsqrt(jnp.mean(x * x, axis=-1, keepdims=True) + EPS)
    unit = x * root
    sums_ref[0, 0:1, :] = jnp.sum(d_normed, axis=0, keepdims=True)
    sums_ref[0, 1:2, :] = jnp.sum(d_normed * unit, axis=0, keepdims=True)
    inner = d_normed * (1.0 + mod_ref[0, 1:2, :])
    dx_ref[0] = mid_ref[0] + root * (inner - unit * jnp.mean(inner * unit, axis=-1, keepdims=True))


def qkv_backward(x, mod, d_mid, dq, dk, dv, nq, nk, rq, rk, qp_all, gains, tables):
    images, length, width = x.shape
    row = lambda w: pl.BlockSpec((1, length, w), lambda i: (i, 0, 0))
    whole = lambda a: pl.BlockSpec(a.shape, lambda i: (0,) * a.ndim)
    return pl.pallas_call(
        qkv_back_kernel,
        grid=(images,),
        in_specs=[row(width), pl.BlockSpec((1, 6, width), lambda i: (i, 0, 0))]
        + [row(width)] * 6
        + [row(LANES)] * 2
        + [pl.BlockSpec((width, 3 * width), lambda i: (0, 0)), whole(gains)]
        + [whole(t) for t in tables],
        out_shape=[
            jax.ShapeDtypeStruct((images, length, 3 * width), jnp.bfloat16),
            jax.ShapeDtypeStruct((images, length, width), jnp.float32),
            jax.ShapeDtypeStruct((images, 4, width), jnp.float32),
        ],
        out_specs=[row(3 * width), row(width), pl.BlockSpec((1, 4, width), lambda i: (i, 0, 0))],
        compiler_params=pltpu.CompilerParams(vmem_limit_bytes=60 * 2**20),
        name="qkv_backward",
    )(x, mod, d_mid, dq, dk, dv, nq, nk, rq, rk, qp_all, gains, *tables)
def tail_scratch():
    s = pltpu.SemaphoreType.DMA
    wide = SMALL_COLS
    return [
        pltpu.VMEM((SMALL_ROWS, wide), jnp.float32),
        pltpu.VMEM((2, SMALL_ROWS, wide), jnp.float32),
        pltpu.VMEM((8, SMALL_ROWS, wide), jnp.bfloat16),
        pltpu.VMEM((8, GROUPS, 2 * LANES), jnp.float32),
        s((8,)),
        s((8,)),
    ]


def tail_steps(at, ins, outs, scratch):
    part_ref, ada_ref, slope_ref = ins
    all_ref, cond_ref = outs
    acc, inbox, blocks, cond, ss, rs = scratch
    width = HEADS * HDIM
    z = at.z
    line = (at.xpeer, at.line(at.far[1]), at.line((z + 2) % 4))

    def copy(r):
        if r < 2:
            return at.copy(acc, inbox.at[r], ss.at[r], rs.at[r], (at.cpeer, at.ypeer)[r])
        ref, k = (blocks, r - 2) if r < 5 else (cond, r - 5)
        start, size = ((at.g, 1), (2 * z, 2), (4 * (z // 2), 4))[k]
        src = ref.at[pl.ds(start, size)]
        return at.copy(src, src, ss.at[r], rs.at[r], line[k])

    def pack():
        row = lax.broadcasted_iota(jnp.int32, (SMALL_ROWS, 1), 0)
        value = acc[...]
        rest = value - value.astype(jnp.bfloat16).astype(jnp.float32)
        last = rest - rest.astype(jnp.bfloat16).astype(jnp.float32)
        value = jnp.where(row == GAIN_ROW + 1, rest, jnp.where(row == GAIN_ROW + 2, last, value))
        blocks[at.g] = value.astype(jnp.bfloat16)

    def cond_rows():
        flat = blocks[...].reshape(8 * SMALL_ROWS, SMALL_COLS)
        row = lax.broadcasted_iota(jnp.int32, (8 * SMALL_ROWS, 1), 0) % SMALL_ROWS
        silu = jnp.zeros((8 * SMALL_ROWS, ada_ref.shape[0]), jnp.float32)
        for k in range(6):
            product = dot_t(flat[:, :width], ada_ref[:, k * width : (k + 1) * width])
            silu = jnp.where((row % 6 == k) & (row < GAIN_ROW), product, silu)
        by_group = lax.dot_general(
            flat[:, width:].astype(jnp.float32),
            silu,
            (((0,), (0,)), ((), ())),
            precision=lax.Precision.HIGHEST,
            preferred_element_type=jnp.float32,
        )
        cond[at.g] = jnp.zeros((GROUPS, 2 * LANES), jnp.float32)
        cond[at.g, :, : ada_ref.shape[0]] = by_group[:GROUPS] * slope_ref[...]

    def step(r):
        if at.draining:
            return
        if r > 0:
            copy(r - 1).wait()
        if r == 0:
            acc[...] = part_ref[...]
        elif r <= 2:
            acc[...] = acc[...] + inbox[r - 1]
        if r == 2:
            pack()
        if r == 5:
            cond_rows()
        if r < 8:
            copy(r).start()
        else:
            all_ref[...] = blocks[...]
            cond_ref[...] = cond[...]

    return [functools.partial(step, r) for r in range(9)]


SMALL_ROWS, SMALL_COLS, GAIN_ROW = 16, HEADS * HDIM + LANES, 12


def scatter_kernel(n, cuts, lags, *refs):
    at = Place()
    at.greet_all()
    ins, small_in = refs[:n], refs[n : n + 3]
    outs, small_out = refs[n + 3 : 2 * n + 3], refs[2 * n + 3 : 2 * n + 5]
    small = tail_steps(at, small_in, small_out, refs[2 * n + 5 : 2 * n + 11])
    opening, steps, last = scatter_steps(at, cuts, ins, outs, refs[2 * n + 11 :], lags)
    small[0]()
    for step in opening:
        step()
    small = small[1:]
    for k, step in enumerate(steps):
        step()
        if k % 3 == 2 and small:
            small[0]()
            small = small[1:]
    for step in small:
        step()
    last()
    at.drain(opening + steps)


def scatter(grads, cuts, lags, part, w_ada, slope):
    n = len(grads)
    any_ref = pl.BlockSpec(memory_space=pl.ANY)
    vmem = pl.BlockSpec(memory_space=pltpu.VMEM)
    return pl.pallas_call(
        functools.partial(scatter_kernel, n, cuts, lags),
        out_shape=[jax.ShapeDtypeStruct(w.shape[1:], jnp.bfloat16) for w in grads]
        + [
            jax.ShapeDtypeStruct((8, SMALL_ROWS, SMALL_COLS), jnp.bfloat16),
            jax.ShapeDtypeStruct((8, GROUPS, 2 * LANES), jnp.float32),
        ],
        in_specs=[any_ref] * n + [vmem] * 3,
        out_specs=[any_ref] * n + [vmem] * 2,
        scratch_shapes=tail_scratch() + scatter_scratch(grads, cuts),
        compiler_params=pltpu.CompilerParams(
            collective_id=1, has_side_effects=True, vmem_limit_bytes=60 * 2**20
        ),
        name="gradient_scatter",
    )(*grads, part, w_ada, slope)


def forward_kernel(cuts, cols, refs):
    n = len(cuts)
    soon = sum(cut[5] == 0 for cut in cuts)
    at = Place()
    x_ref, part_ref, group_ref, gains_ref, band_ref = refs["in"]
    normed_ref, q_ref, nq_ref, nk_ref, rq_ref, rk_ref, o_ref, inv_ref, mod_ref, *table_refs, kv_out = refs["out"]
    kv, w_buf, pick_ref, spread_ref, mod_buf, mod_in, w_sem, ms, mr, ks, kr, os = refs["scratch"]
    ins, outs = refs["shards"], refs["full"]
    images, length, width = x_ref.shape
    parts = [(i, s) for i in range(images) for s in (0, 1)]
    if n:
        at.greet_all()
        steps, first, last = gather_steps(at, cuts, ins, outs, refs["sems"])
    else:
        at.greet_band()
        steps, first, last = [], 0, None

    mod_buf[...] = part_ref[...]

    def mod_copy(r):
        peer = (at.xpeer, at.line(at.far[1]), at.line((at.z + 2) % 4))[r]
        return at.copy(mod_buf, mod_in.at[r], ms.at[r], mr.at[r], peer)

    def mod_step(r):
        if at.draining:
            return
        if r > 0:
            mod_copy(r - 1).wait()
            mod_buf[...] = mod_buf[...] + mod_in[r - 1]
        if r < 3:
            mod_copy(r).start()

    def rows(s, i, band):
        return kv.at[s, i, pl.ds(pl.multiple_of(band * length, 16), length), :]

    here, over = at.band, (1 - at.y) * 2 + at.c
    beside, across = at.y * 2 + 1 - at.c, (1 - at.y) * 2 + 1 - at.c

    def give(i, s):
        p = rows(s, i, here)
        at.send(p, p, ks.at[i, s, 0], kr.at[i, s, 0], at.ypeer)
        at.send(p, p, ks.at[i, s, 1], kr.at[i, s, 1], at.cpeer)

    def pass_on(i, s):
        p = rows(s, i, over)
        at.arrived(p, kr.at[i, s, 0])
        at.send(p, p, ks.at[i, s, 2], kr.at[i, s, 2], at.cpeer)

    def ready(i):
        for s in (0, 1):
            at.arrived(rows(s, i, beside), kr.at[i, s, 1])
            at.arrived(rows(s, i, across), kr.at[i, s, 2])
            at.keep(kv.at[s, i], kv_out.at[s, i], os.at[i, s])

    def norm(i):
        value = x_ref[i].astype(jnp.float32)
        root = lax.rsqrt(jnp.mean(value * value, axis=-1, keepdims=True) + EPS)
        chosen = jnp.sum(group_ref[:, i : i + 1] * mod_buf[...], axis=0, keepdims=True)
        mod_ref[i : i + 1, :] = chosen
        shift, scale = chosen[:, :width], chosen[:, width : 2 * width]
        normed_ref[i] = (value * root * (1.0 + scale) + shift).astype(jnp.bfloat16)

    def raw(i, part):
        return jnp.dot(
            normed_ref[i], w_buf[:, part * width : (part + 1) * width], preferred_element_type=jnp.float32
        )

    def project(i, part, n_ref, r_ref):
        values = raw(i, part)
        inv = lax.rsqrt(pick_dot(values * values, pick_ref[...]) * (1.0 / HDIM) + EPS)
        r_ref[i] = inv
        unit = values * pick_dot(inv, spread_ref[...])
        n_ref[i] = unit
        scaled = unit * gains_ref[part : part + 1, :]
        return turn(scaled, *(t[...] for t in table_refs)).astype(jnp.bfloat16)

    def key_part(i):
        norm(i)
        kv[0, i, pl.ds(pl.multiple_of(here * length, 16), length), :] = project(i, 1, nk_ref, rk_ref)
        give(i, 0)

    def value_part(i):
        kv[1, i, pl.ds(pl.multiple_of(here * length, 16), length), :] = raw(i, 2).astype(jnp.bfloat16)
        give(i, 1)

    def query_part(i):
        q_ref[i] = project(i, 0, nq_ref, rq_ref)

    def head(i, h):
        win, inside = head_window(h)
        query = q_ref[i, :, win]
        query = jnp.where(inside, query, jnp.zeros_like(query))
        power = jnp.exp2(dot_t(query, kv[0, i, :, win]) * (HDIM ** (-0.5) * LOG2E))
        inv = 1.0 / jnp.sum(power, axis=-1, keepdims=True)
        out = jnp.dot(
            (power * inv).astype(jnp.bfloat16), kv[1, i, :, win], preferred_element_type=jnp.float32
        )
        o_ref[i, :, win] = jnp.where(inside, out.astype(jnp.bfloat16), o_ref[i, :, win])
        lane = lax.broadcasted_iota(jnp.int32, (1, LANES), 1)
        inv_ref[i] = jnp.where(lane == h, inv, inv_ref[i])

    def prepare():
        pick_ref[...] = head_pick(width)
        spread_ref[...] = head_spread(width)

        def block(r, _):
            rows_of = pl.ds(pl.multiple_of(r * cols, cols), cols)
            row = band_ref[0:1, 0:1] * (length // cols) + r.astype(jnp.float32)
            for ref, value in zip(table_refs, rope_tables(row, 1, cols, width)):
                ref[rows_of, :] = value
            return 0

        lax.fori_loop(0, length // cols, block, 0)

    if not n:
        prepare()
    if n:
        for k in range(3):
            mod_step(k)
            for step in steps[2 * k : 2 * k + 2]:
                step()
                if k == 0 and step is steps[0]:
                    prepare()
        mod_step(3)
        for step in steps[6:first]:
            step()
        for i in range(soon):
            last(i)
        pltpu.make_async_copy(ins[0], outs[0].at[at.g], refs["sems"][0].at[0]).wait()
        loads = [
            pltpu.make_async_copy(
                outs[0].at[k, :, pl.ds(0, 3 * width)],
                w_buf.at[pl.ds(k * (width // 8), width // 8), :],
                w_sem.at[k],
            )
            for k in range(8)
        ]
    else:
        loads = [pltpu.make_async_copy(ins[0].at[:, pl.ds(0, 3 * width)], w_buf, w_sem.at[0])]
    for d in loads:
        d.start()
    o_ref[...] = jnp.zeros_like(o_ref)
    inv_ref[...] = jnp.zeros_like(inv_ref)
    for d in loads:
        d.wait()
    todo = steps[first:]
    for i in range(images):
        for work in (key_part, value_part):
            work(i)
            for step in todo[:2]:
                step()
            todo = todo[2:]
    for i in range(images):
        query_part(i)
        for step in todo[:2]:
            step()
        todo = todo[2:]
    for i in range(images):
        pass_on(i, 0)
        pass_on(i, 1)
        ready(i)
        mine, todo = (todo[: HEADS // 2], todo[HEADS // 2 :])

        def body(h, _, i=i, mine=mine):
            for k, step in enumerate(mine):
                pl.when(h == 2 * k)(step)
            head(i, h)
            return 0

        lax.fori_loop(0, HEADS, body, 0)
    for step in todo:
        step()
    for i in range(soon, n):
        last(i)
    at.drain(steps)
    for i, s in parts:
        at.drain([functools.partial(give, i, s), functools.partial(pass_on, i, s)])
    for i in range(images):
        at.drain([functools.partial(ready, i)])


def forward(x, mod_part, groups, gains, band, cols, shards, cuts):
    n = len(cuts)
    images, length, width = x.shape
    bands = lax.axis_size("band")
    keys = (2, images, bands * length, width)
    s = pltpu.SemaphoreType.DMA
    bf = jnp.bfloat16
    any_ref = pl.BlockSpec(memory_space=pl.ANY)
    vmem = pl.BlockSpec(memory_space=pltpu.VMEM)
    args = [x, mod_part, groups, gains, band]
    rows = lambda w, d: jax.ShapeDtypeStruct((images, length, w), d)
    outs = [rows(width, bf)] * 2 + [rows(width, jnp.float32)] * 2 + [rows(LANES, jnp.float32)] * 2
    outs += [rows(width, bf), rows(LANES, jnp.float32), jax.ShapeDtypeStruct((images, mod_part.shape[1]), jnp.float32)]
    outs += [jax.ShapeDtypeStruct((length, width), jnp.float32)] * 3
    scratch = [
        pltpu.VMEM(keys, bf),
        pltpu.VMEM((width, 3 * width), bf),
        pltpu.VMEM((width, LANES), bf),
        pltpu.VMEM((LANES, width), bf),
        pltpu.VMEM(mod_part.shape, jnp.float32),
        pltpu.VMEM((3,) + mod_part.shape, jnp.float32),
        s((8,)),
        s((3,)),
        s((3,)),
        s((images, 2, 3)),
        s((images, 2, 3)),
        s((images, 2)),
    ]
    whole = len(shards) if n else 0
    sizes = [len(args), len(shards), len(outs) + 1, whole, len(scratch), 10 if n else 0]

    def kernel(*refs):
        groups_of, start = [], 0
        for size in sizes:
            groups_of.append(refs[start : start + size])
            start += size
        names = ("in", "shards", "out", "full", "scratch", "sems")
        forward_kernel(cuts, cols, dict(zip(names, groups_of)))

    return pl.pallas_call(
        kernel,
        out_shape=outs
        + [jax.ShapeDtypeStruct(keys, bf)]
        + [jax.ShapeDtypeStruct((8,) + w.shape, w.dtype) for w in shards[:whole]],
        in_specs=[vmem] * len(args) + [any_ref] * len(shards),
        out_specs=[vmem] * len(outs) + [any_ref] * (1 + whole),
        scratch_shapes=scratch + (gather_sems(n) if n else []),
        compiler_params=pltpu.CompilerParams(
            collective_id=2, has_side_effects=True, vmem_limit_bytes=60 * 2**20
        ),
        name="forward",
    )(*args, *shards)


EACH = 9


def attention_back_kernel(n, cuts, lags, q_ref, do_ref, inv_ref, kv_ref, *refs):
    ins, (dq_ref, d_out), outs = refs[:n], refs[n : n + 2], refs[n + 2 : 2 * n + 2]
    kv, dkv, core_buf, y_buf, load_sem, ks, kr, ys, yr, ws = refs[2 * n + 2 : 2 * n + 12]
    images, length, width = q_ref.shape
    at = Place()
    loads = [pltpu.make_async_copy(kv_ref.at[:, i], kv.at[i], load_sem.at[i]) for i in range(images)]
    for d in loads:
        d.start()
    at.greet_all() if n else at.greet_band()
    opening, todo, last = [], [], lambda: None
    if n:
        opening, todo, last = scatter_steps(at, cuts, ins, outs, refs[2 * n + 12 :], lags)
    for step in opening:
        step()
    steps = opening + todo

    def rows(s, i, band):
        return dkv.at[s, i, pl.ds(pl.multiple_of(band * length, 16), length), :]

    def to_core(i):
        for s in (0, 1):
            for yy in (0, 1):
                at.send(rows(s, i, yy * 2 + 1 - at.c), core_buf.at[i, s, yy], ks.at[i, s, yy], kr.at[i, s, yy], at.cpeer)

    def core_add(i):
        for s in (0, 1):
            p = rows(s, i, (1 - at.y) * 2 + at.c)
            at.arrived(core_buf.at[i, s, 1 - at.y], kr.at[i, s, 1 - at.y])
            if not at.draining:
                add_into(p, core_buf.at[i, s, 1 - at.y])
            at.send(p, y_buf.at[i, s], ys.at[i, s], yr.at[i, s], at.ypeer)
        for s in (0, 1):
            at.arrived(core_buf.at[i, s, at.y], kr.at[i, s, at.y])
            if not at.draining:
                add_into(rows(s, i, at.band), core_buf.at[i, s, at.y])

    def y_add(i):
        for s in (0, 1):
            p = rows(s, i, at.band)
            at.arrived(y_buf.at[i, s], yr.at[i, s])
            if not at.draining:
                add_into(p, y_buf.at[i, s])
            at.keep(p, d_out.at[s, i], ws.at[i, s])

    def head(i, h):
        win, inside = head_window(h)
        query, grad = q_ref[i, :, win], do_ref[i, :, win]
        query = jnp.where(inside, query, jnp.zeros_like(query))
        grad = jnp.where(inside, grad, jnp.zeros_like(grad))
        keys, values = kv[i, 0, :, win], kv[i, 1, :, win]
        inv = inv_ref[i, pl.ds(h, 1), :]
        probs = jnp.exp2(dot_t(keys, query) * (HDIM ** (-0.5) * LOG2E)) * inv
        d_probs = dot_t(values, grad)
        delta = jnp.sum(probs * d_probs, axis=0, keepdims=True)
        d_scores = (probs * (d_probs - delta)).astype(jnp.bfloat16)
        d_key = jnp.dot(d_scores, query, preferred_element_type=jnp.float32).astype(jnp.bfloat16)
        d_value = jnp.dot(
            probs.astype(jnp.bfloat16), grad, preferred_element_type=jnp.float32
        ).astype(jnp.bfloat16)
        dkv[0, i, :, win] = jnp.where(inside, d_key, dkv[0, i, :, win])
        dkv[1, i, :, win] = jnp.where(inside, d_value, dkv[1, i, :, win])
        dq_ref[i, :, win] = jnp.where(inside, first_dot(d_scores, keys), dq_ref[i, :, win])

    dq_ref[...] = jnp.zeros_like(dq_ref)
    for s in (0, 1):
        for i in range(images):

            def clear(r, _, s=s, i=i):
                dkv[s, i, pl.ds(pl.multiple_of(r * 16, 16), 16), :] = jnp.zeros((16, width), jnp.bfloat16)
                return 0

            lax.fori_loop(0, kv.shape[2] // 16, clear, 0)
    exchange = []
    for i in range(images):
        loads[i].wait()
        mine, todo = (todo[:EACH], todo[EACH:])
        due = exchange
        exchange = [functools.partial(f, i) for f in (core_add, y_add)]

        def body(h, _, i=i, mine=mine, due=due):
            for k, step in enumerate(due):
                pl.when(h == 1 + 12 * k)(step)
            for k, step in enumerate(mine):
                pl.when(h == k * HEADS // EACH)(step)
            head(i, h)
            return 0

        lax.fori_loop(0, HEADS, body, 0)
        to_core(i)
        steps += [functools.partial(to_core, i)] + exchange
    exchange[0]()
    part = min(6, len(todo))
    for step in todo[:part] + [exchange[1]] + todo[part:]:
        step()
    last()
    at.drain(steps)


def attention_backward(q, d_att, inv_rows, kv_all, grads, cuts, lags):
    n = len(grads)
    images, length, width = q.shape
    s = pltpu.SemaphoreType.DMA
    any_ref = pl.BlockSpec(memory_space=pl.ANY)
    vmem = pl.BlockSpec(memory_space=pltpu.VMEM)
    bf = jnp.bfloat16
    return pl.pallas_call(
        functools.partial(attention_back_kernel, n, cuts, lags),
        out_shape=[
            jax.ShapeDtypeStruct(q.shape, jnp.float32),
            jax.ShapeDtypeStruct((2, images, length, width), bf),
        ]
        + [jax.ShapeDtypeStruct(w.shape[1:], bf) for w in grads],
        in_specs=[vmem, vmem, vmem, any_ref] + [any_ref] * n,
        out_specs=[vmem, any_ref] + [any_ref] * n,
        scratch_shapes=[
            pltpu.VMEM((images, 2) + kv_all.shape[2:], bf),
            pltpu.VMEM(kv_all.shape, bf),
            pltpu.VMEM((images, 2, 2, length, width), bf),
            pltpu.VMEM((images, 2, length, width), bf),
            s((images,)),
            s((images, 2, 2)),
            s((images, 2, 2)),
            s((images, 2)),
            s((images, 2)),
            s((images, 2)),
        ]
        + (scatter_scratch(grads, cuts) if n else []),
        compiler_params=pltpu.CompilerParams(
            collective_id=3, has_side_effects=True, vmem_limit_bytes=63 * 2**20
        ),
        name="attention_backward",
    )(q, d_att, inv_rows, kv_all, *grads)
def modulate(values, shift_in, scale_in):
    root = lax.rsqrt(jnp.mean(values * values, axis=-1, keepdims=True) + EPS)
    return values * root * (1.0 + scale_in[:, None, :]) + shift_in[:, None, :]


def swiglu(gate_in, up_in):
    return jax.nn.silu(gate_in) * up_in


def half_cuts(ref, axis, base, size, own_parts, shared_parts):
    unit = size // 2 // (own_parts + 2 * shared_parts)
    return (axis, size // 2, own_parts * unit, shared_parts * unit, base, ref)


def by_shard(grad):
    parts = lax.axis_size("grp")
    return grad.reshape(parts, grad.shape[0] // parts, grad.shape[1])


def body(
    patches,
    grad_out,
    cond_table,
    group_ids,
    live_count,
    band_order,
    w_ada,
    b_ada,
    w_qkv,
    q_gain,
    k_gain,
    w_proj,
    w_gate,
    w_up,
    w_down,
):
    images, rows, cols, width = patches.shape
    length = rows * cols
    ff = w_gate.shape[1]
    bf = jnp.bfloat16
    grp = lax.axis_index("grp")
    ada_rows, ada_cols, bias_cols = w_ada.shape[0], w_ada.shape[1], b_ada.shape[0]
    fits = (
        lax.axis_size("grp") == 8
        and images == 2
        and width == HEADS * HDIM
        and w_qkv.shape[0] % 16 == 0
        and 4 * width % 4608 == 0
        and 2 * ff % 3072 == 0
        and w_down.shape[0] % 384 == 0
    )
    w_qp = jnp.concatenate([w_qkv, w_proj], axis=1)
    w_gu = jnp.concatenate([w_gate, w_up], axis=1)
    full = lambda w: w.reshape(-1, w.shape[-1])
    onehot = (group_ids[:, None] == jnp.arange(GROUPS, dtype=jnp.int32)[None, :]).astype(jnp.float32)
    cond_rows = lax.dynamic_slice_in_dim(cond_table, grp * ada_rows, ada_rows, axis=1)
    sigmoid = jax.nn.sigmoid(cond_rows)
    silu_rows = (cond_rows * sigmoid).astype(bf)
    silu_slope = sigmoid * (1.0 + cond_rows * (1.0 - sigmoid))
    mod_part = jnp.dot(silu_rows, w_ada, preferred_element_type=jnp.float32)
    bias_part = lax.dynamic_update_slice_in_dim(
        jnp.zeros((ada_cols,), jnp.float32), b_ada.astype(jnp.float32), grp * bias_cols, axis=0
    )
    mod_part = mod_part + bias_part[None, :]
    live_mask = (jnp.arange(images, dtype=jnp.int32) < live_count[0]).astype(jnp.float32)

    gains = jnp.stack([jnp.tile(q_gain, HEADS), jnp.tile(k_gain, HEADS)])
    x = patches.reshape(images, length, width)
    groups = jnp.pad(onehot.T, ((0, 0), (0, LANES - images)))
    band = jnp.broadcast_to(band_order.astype(jnp.float32)[:, None], (1, LANES))
    common = (groups, gains, band, cols)
    if fits:
        shards = [w_qp, w_gu, w_down]
        cuts = [half_cuts(0, 1, 0, 4 * width, 1, 1), half_cuts(1, 1, 0, 2 * ff, 4, 1)]
        cuts += [half_cuts(2, 0, 0, w_down.shape[0], 4, 1)]
    else:
        qp_all, gu_all, down_all = (lax.all_gather(w, "grp", axis=0, tiled=True) for w in (w_qp, w_gu, w_down))
        mod_part = lax.psum(mod_part, "grp")
        shards, cuts = [qp_all], []
    outs = forward(x, mod_part, *common, shards, cuts)
    normed_one, query, nq, nk, rq, rk, attended, inv, mod = outs[:9]
    tables, kv_all, rest = outs[9:12], outs[12], outs[13:]
    if fits:
        qp_all, gu_all, down_all = (full(w) for w in rest)
    mod = mod.reshape(images, 6, width)
    gate_one, shift_two, scale_two, gate_two = (mod[:, k] for k in (2, 3, 4, 5))
    proj_all = qp_all[:, 3 * width :]
    flat = lambda a: a.reshape(images * length, a.shape[-1])
    attended_low = flat(attended)
    proj = jnp.dot(attended_low, proj_all, preferred_element_type=jnp.float32).reshape(images, length, width)
    middle = x.astype(jnp.float32) + gate_one[:, None, :] * proj
    normed_two, norm_two_pull = jax.vjp(modulate, middle, shift_two, scale_two)
    normed_two_low = flat(normed_two.astype(bf))
    pre = jnp.dot(normed_two_low, gu_all, preferred_element_type=jnp.float32)
    hidden, swiglu_pull = jax.vjp(swiglu, pre[:, :ff], pre[:, ff:])
    hidden_low = hidden.astype(bf)
    mlp = jnp.dot(hidden_low, down_all, preferred_element_type=jnp.float32).reshape(images, length, width)
    output = (middle + gate_two[:, None, :] * mlp) * live_mask[:, None, None]
    patches_out = output.astype(bf).reshape(images, rows, cols, width)

    grad_y = grad_out.reshape(images, length, width).astype(jnp.float32) * live_mask[:, None, None]
    d_gate_two = jnp.sum(grad_y * mlp, axis=1)
    d_mlp = flat((grad_y * gate_two[:, None, :]).astype(bf))
    d_w_down = jnp.einsum("tf,td->fd", hidden_low, d_mlp, preferred_element_type=jnp.float32).astype(bf)
    d_hidden = jnp.einsum("td,fd->tf", d_mlp, down_all, preferred_element_type=jnp.float32)
    d_pre = jnp.concatenate([d.astype(bf) for d in swiglu_pull(d_hidden)], axis=1)
    d_w_gu = jnp.einsum("td,tf->df", normed_two_low, d_pre, preferred_element_type=jnp.float32).astype(bf)
    d_normed_two = jnp.einsum("tf,df->td", d_pre, gu_all, preferred_element_type=jnp.float32)
    d_middle_norm, d_shift_two, d_scale_two = norm_two_pull(d_normed_two.reshape(images, length, width))
    d_middle = grad_y + d_middle_norm
    d_gate_one = jnp.sum(d_middle * proj, axis=1)
    d_proj = flat((d_middle * gate_one[:, None, :]).astype(bf))
    d_w_proj = jnp.einsum("td,te->de", attended_low, d_proj, preferred_element_type=jnp.float32).astype(bf)
    d_attended = jnp.einsum("te,de->td", d_proj, proj_all, preferred_element_type=jnp.float32).astype(bf)
    d_query, d_kv, *rest = attention_backward(
        query,
        d_attended.reshape(images, length, width),
        jnp.swapaxes(inv, 1, 2),
        kv_all,
        [by_shard(d_w_gu)] if fits else [],
        [half_cuts(0, 1, 0, 2 * ff, 4, 1)] if fits else [],
        (2, 2, 1, 2),
    )
    d_qkv, d_x, sums = qkv_backward(
        x, mod, d_middle, d_query, d_kv[0], d_kv[1], nq, nk, rq, rk, qp_all, gains, tables
    )
    d_patches = d_x.reshape(images, rows, cols, width)
    d_w_qkv = jnp.einsum("td,te->de", flat(normed_one), flat(d_qkv), preferred_element_type=jnp.float32).astype(bf)
    d_w_qp = jnp.concatenate([d_w_qkv, d_w_proj], axis=1)

    d_mod_part = jnp.stack([sums[:, 0], sums[:, 1], d_gate_one, d_shift_two, d_scale_two, d_gate_two], axis=1)
    gain_part = jnp.sum(sums[:, 2:4].reshape(images, 2, HEADS, HDIM), axis=(0, 2))
    if fits:
        tags = jnp.pad(jnp.repeat(onehot * (1.0 / lax.axis_size("band")), 6, axis=0), ((0, 0), (0, LANES - GROUPS)))
        small = jnp.concatenate([d_mod_part.reshape(images * 6, width), tags], axis=1)
        gain_row = jnp.pad(gain_part.reshape(1, -1), ((0, 0), (0, SMALL_COLS - 2 * HDIM)))
        small = jnp.concatenate([small, gain_row, gain_row, gain_row, jnp.zeros_like(gain_row)])
        cuts = [half_cuts(0, 0, 0, w_down.shape[0], 2, 1), half_cuts(1, 1, 0, 4 * width, 8, 5)]
        d_gu = rest[0]
        d_down, d_qp, gathered, cond_blocks = scatter(
            [by_shard(d_w_down), by_shard(d_w_qp)], cuts, (2, 2, 1, 2), small, w_ada, silu_slope
        )
        d_mod_all = gathered[:, :GAIN_ROW, :width].reshape(-1, ada_cols)
        onehot_all = gathered[:, 0:GAIN_ROW:6, width : width + GROUPS].reshape(-1, GROUPS)
        gain_all = gathered[:, GAIN_ROW : GAIN_ROW + 3, : 2 * HDIM].astype(jnp.float32)
        gain_all = jnp.sum(gain_all, axis=(0, 1)).reshape(2, HDIM)
        d_cond = jnp.swapaxes(cond_blocks[:, :, :ada_rows], 0, 1).reshape(GROUPS, -1)
    else:
        d_gu, d_down, d_qp = (
            lax.psum(lax.psum_scatter(w, "grp", scatter_dimension=0, tiled=True), "band")
            for w in (d_w_gu, d_w_down, d_w_qp)
        )
        d_modulation = lax.psum(d_mod_part.reshape(images, ada_cols), "band").astype(bf)
        gain_all = lax.psum(gain_part, ("grp", "band"))
        payload = jnp.concatenate([d_modulation, onehot.astype(bf)], axis=1)
        payload = lax.all_gather(payload, "grp", axis=0, tiled=True)
        d_mod_all, onehot_all = payload[:, :ada_cols], payload[:, ada_cols:]
        d_silu = jnp.einsum("be,de->bd", d_mod_all, w_ada, preferred_element_type=jnp.float32)
        d_silu = jnp.dot(
            onehot_all.astype(jnp.float32).T,
            d_silu,
            precision=lax.Precision.HIGHEST,
            preferred_element_type=jnp.float32,
        )
        d_cond = lax.all_gather(d_silu * silu_slope, "grp", axis=1, tiled=True)
    silu_all = jnp.dot(onehot_all, silu_rows, preferred_element_type=jnp.float32).astype(bf)
    d_w_ada = jnp.einsum("bd,be->de", silu_all, d_mod_all, preferred_element_type=jnp.float32)
    d_b_ada = lax.dynamic_slice_in_dim(
        jnp.sum(d_mod_all.astype(jnp.float32), axis=0), grp * bias_cols, bias_cols, axis=0
    )
    wide = lambda a: a.astype(jnp.float32)
    return (
        patches_out,
        d_patches,
        d_cond,
        d_w_ada,
        d_b_ada,
        wide(d_qp[:, : 3 * width]),
        gain_all[0],
        gain_all[1],
        wide(d_qp[:, 3 * width :]),
        wide(d_gu[:, :ff]),
        wide(d_gu[:, ff:]),
        wide(d_down),
    )


def solution(mesh):
    in_specs = (
        P("grp", "band", None, None),
        P("grp", "band", None, None),
        P(),
        P("grp"),
        P("grp"),
        P("band"),
        P("grp", None),
        P("grp"),
        P("grp", None),
        P(),
        P(),
        P("grp", None),
        P("grp", None),
        P("grp", None),
        P("grp", None),
    )
    out_specs = (
        P("grp", "band", None, None),
        P("grp", "band", None, None),
        P(),
        P("grp", None),
        P("grp"),
        P("grp", None),
        P(),
        P(),
        P("grp", None),
        P("grp", None),
        P("grp", None),
        P("grp", None),
    )
    return jax.shard_map(body, mesh=mesh, in_specs=in_specs, out_specs=out_specs, check_vma=False)
```

```python
import functools
import math

import jax
import jax.numpy as jnp
from jax import lax
from jax.experimental import pallas as pl
from jax.experimental.pallas import tpu as pltpu
from jax.sharding import PartitionSpec as P

HEADS = 16
HDIM = 72
GROUPS = 8
LANES = 128
EPS = 1e-06
LOG2E = 1.4426950408889634

MESH = pl.DeviceIdType.MESH


class Place:
    def __init__(self):
        self.g, self.band = lax.axis_index("grp"), lax.axis_index("band")
        self.z, self.x = self.g // 2, self.g % 2
        self.y, self.c = self.band // 2, self.band % 2
        z = self.z
        self.far = [z, z + 1 - 2 * (z % 2), 2 - z // 2, 3 - 3 * (z // 2)]
        self.ypeer = (self.g, (1 - self.y) * 2 + self.c)
        self.cpeer = (self.g, self.y * 2 + 1 - self.c)
        self.xpeer = (z * 2 + 1 - self.x, self.band)
        self.draining = False

    def line(self, zz):
        return (zz * 2 + self.x, self.band)

    def greet(self, peers):
        bar = pltpu.get_barrier_semaphore()
        for d in peers:
            pl.semaphore_signal(bar, inc=1, device_id=d, device_id_type=MESH)
        pl.semaphore_wait(bar, len(peers))

    def greet_band(self):
        self.greet([self.ypeer, self.cpeer])

    def greet_all(self):
        self.greet([self.xpeer, self.ypeer, self.cpeer] + [self.line(zz) for zz in self.far[1:]])

    def copy(self, src, dst, ssem, rsem, dev):
        return pltpu.make_async_remote_copy(
            src_ref=src, dst_ref=dst, send_sem=ssem, recv_sem=rsem, device_id=dev, device_id_type=MESH
        )

    def send(self, src, dst, ssem, rsem, dev, cond=None):
        d = self.copy(src, dst, ssem, rsem, dev)
        act = d.wait_send if self.draining else d.start
        if cond is None:
            act()
        else:
            pl.when(cond)(act)

    def keep(self, src, dst, sem):
        d = pltpu.make_async_copy(src, dst, sem)
        d.wait() if self.draining else d.start()

    def arrived(self, ref, rsem):
        if not self.draining:
            self.copy(ref, ref, rsem, rsem, self.ypeer).wait_recv()

    def drain(self, steps):
        self.draining = True
        for step in steps:
            step()
        self.draining = False


def span(ref, axis, start, size):
    if axis == 0:
        return ref.at[pl.ds(pl.multiple_of(start, 16), size), :]
    return ref.at[:, pl.ds(pl.multiple_of(start, LANES), size)]


def gather_sems(n):
    s = pltpu.SemaphoreType.DMA
    return [s((n,)), s((n, 4)), s((n, 4)), s((n, 4)), s((n, 4)), s((n, 7)), s((n, 7)), s((n, 14)), s((n, 14)), s((n,))]


def gather_steps(at, cuts, ins, outs, sems):
    n = len(cuts)
    lsem, zs, zr, xs, xr, ys, yr, cs, cr, ds = sems
    ins, outs = ([refs[cut[5]] for cut in cuts] for refs in (ins, outs))
    soon = sum(cut[5] == 0 for cut in cuts)
    x, y, z, c, far = at.x, at.y, at.z, at.c, at.far

    def piece(i, ref, yy, cc):
        axis, half, a, b, base, _ = cuts[i]
        return span(ref, axis, base + cc * half + yy * b, a + b)

    def bpart(i, ref, yy, cc):
        axis, half, a, b, base, _ = cuts[i]
        return span(ref, axis, base + cc * half + yy * (a + b), b)

    def own(i):
        src, dst = piece(i, ins[i], y, c), piece(i, outs[i].at[at.g], y, c)
        at.send(src, dst, zs.at[i, 0], zr.at[i, z], (at.g + 2, at.band), z < 3)
        at.send(src, dst, ds.at[i], zr.at[i, z], (at.g - 2, at.band), z > 0)
        at.send(src, dst, xs.at[i, 0], xr.at[i, 0], at.xpeer)
        if cuts[i][4] == 0 and not (at.draining and cuts[i][5] == 0):
            at.keep(ins[i], outs[i].at[at.g], lsem.at[i])

    def down(i, slot, shard):
        p = bpart(i, outs[i].at[shard], y, c)
        at.send(p, p, ys.at[i, slot], yr.at[i, slot], at.ypeer)
        p = piece(i, outs[i].at[shard], y, c)
        at.send(p, p, cs.at[i, slot], cr.at[i, slot], at.cpeer)

    def zarr(i, t):
        zz = far[t]
        s = zz * 2 + x
        p = piece(i, outs[i].at[s], y, c)
        at.arrived(p, zr.at[i, zz])
        nxt = jnp.where(zz < z, z + 1, z - 1)
        at.send(p, p, zs.at[i, t], zr.at[i, zz], at.line(jnp.clip(nxt, 0, 3)), (nxt >= 0) & (nxt <= 3))
        at.send(p, p, xs.at[i, t], xr.at[i, t], at.xpeer)
        down(i, t - 1, s)

    def xarr(i, t):
        s = far[t] * 2 + 1 - x
        at.arrived(piece(i, outs[i].at[s], y, c), xr.at[i, t])
        down(i, 3 + t, s)

    def yarr(i, slot, s):
        p = bpart(i, outs[i].at[s], 1 - y, c)
        at.arrived(p, yr.at[i, slot])
        at.send(p, p, cs.at[i, 7 + slot], cr.at[i, 7 + slot], at.cpeer)

    slots = [(t - 1, far[t] * 2 + x) for t in (1, 2, 3)]
    slots += [(3 + t, far[t] * 2 + 1 - x) for t in range(4)]
    order = [slots[k] for k in (3, 0, 4, 1, 5, 2, 6)]
    steps = [lambda: own(0)]
    for i in range(n):
        mine = [lambda i=i: zarr(i, 1)]
        if i + 1 < n:
            mine.append(lambda i=i: own(i + 1))
        mine.append(lambda i=i: xarr(i, 0))
        for t in (2, 3):
            mine += [lambda i=i, t=t: zarr(i, t), lambda i=i, t=t: xarr(i, t - 1)]
        mine.append(lambda i=i: xarr(i, 3))
        if i > 0:
            late = [lambda i=i, k=k: yarr(i - 1, *order[k]) for k in range(7)]
            pace, held = 3 if i == soon else 1, list(late)
            merged = []
            while late or mine:
                merged += late[:pace] + mine[:1]
                late, mine = late[pace:], mine[1:]
            mine = merged
        if i == soon:
            first = len(steps) + max(k for k, step in enumerate(mine) if step in held) + 1
        steps += mine
    steps += [lambda k=k: yarr(n - 1, *order[k]) for k in range(7)]

    def last(i):
        for slot, s in slots:
            at.arrived(piece(i, outs[i].at[s], y, 1 - c), cr.at[i, slot])
            at.arrived(bpart(i, outs[i].at[s], 1 - y, 1 - c), cr.at[i, 7 + slot])

    return steps, first, last


def add_into(dst, src):
    def step(r, _):
        rows = pl.ds(pl.multiple_of(r * 16, 16), 16)
        dst[rows, :] = dst[rows, :] + src[rows, :]
        return 0

    lax.fori_loop(0, src.shape[0] // 16, step, 0)


def move_into(dst, src):
    def step(r, _):
        rows = pl.ds(pl.multiple_of(r * 16, 16), 16)
        dst[rows, :] = src[rows, :]
        return 0

    lax.fori_loop(0, src.shape[0] // 16, step, 0)


def scatter_scratch(grads, cuts):
    n = len(cuts)
    s = pltpu.SemaphoreType.DMA

    def buf(lead, k, size):
        grad = grads[cuts[k][5]]
        shape = (grad.shape[1], size) if cuts[k][0] == 1 else (size, grad.shape[2])
        return pltpu.VMEM(lead + shape, jnp.bfloat16)

    out = []
    for lead, pick in (
        ((8,), lambda c: c[1]),
        ((8,), lambda c: c[1]),
        ((8,), lambda c: c[3]),
        ((4,), lambda c: c[2] + c[3]),
        ((5,), lambda c: c[2] + c[3]),
        ((), lambda c: c[2] + c[3]),
    ):
        out += [buf(lead, k, pick(cuts[k])) for k in range(n)]
    out += [s((n, 8))] * 5 + [s((n, 4))] * 2 + [s((n, 3)), s((n, 5))] + [s((n,))] * 5
    return out


def scatter_steps(at, cuts, ins, outs, scratch, lags):
    n = len(cuts)
    own_half, core_buf, y_buf, x_buf, z_buf, fin_buf = (scratch[k * n : (k + 1) * n] for k in range(6))
    ls, cs, cr, ys, yr, xs, xr, zs, zr, fs, fr, es, er, ws = scratch[6 * n :]
    x, y, z, c, far = at.x, at.y, at.z, at.c, at.far
    ins, outs = ([refs[cut[5]] for cut in cuts] for refs in (ins, outs))

    def piece(i, ref):
        _, _, a, b = cuts[i][:4]
        return span(ref, cuts[i][0], y * b, a + b)

    def bpart(i, ref, yy):
        _, _, a, b = cuts[i][:4]
        return span(ref, cuts[i][0], yy * (a + b), b)

    order = [(t, j) for t in (3, 2, 1, 0) for j in (1, 0)]

    def shard(t, j):
        return far[t] * 2 + (1 - x if j else x)

    def load(i, t, j):
        axis, half, _, _, base, _ = cuts[i]
        s, q = shard(t, j), order.index((t, j))
        return pltpu.make_async_copy(span(ins[i].at[s], axis, base + c * half, half), own_half[i].at[s], ls.at[i, q])

    def give(i, t, j):
        axis, half, _, _, base, _ = cuts[i]
        s, q = shard(t, j), order.index((t, j))
        src = span(ins[i].at[s], axis, base + (1 - c) * half, half)
        at.send(src, core_buf[i].at[s], cs.at[i, q], cr.at[i, s], at.cpeer)
        if not at.draining:
            load(i, t, j).start()

    def to_y(i, t, j):
        s = shard(t, j)
        src = bpart(i, own_half[i].at[s], 1 - y)
        return at.copy(src, y_buf[i].at[s], ys.at[i, order.index((t, j))], yr.at[i, s], at.ypeer)

    def to_fin(i):
        return at.copy(piece(i, own_half[i].at[at.g]), fin_buf[i], fs.at[i], fr.at[i], at.ypeer)

    def cadd(i, t, j):
        s = shard(t, j)
        if at.draining:
            if (t, j) != (0, 0):
                to_y(i, t, j).wait_send()
            return
        load(i, t, j).wait()
        at.arrived(core_buf[i].at[s], cr.at[i, s])
        add_into(own_half[i].at[s], core_buf[i].at[s])
        to_y(i, t, j).start()

    def yadd(i, t, j):
        s = shard(t, j)
        at.arrived(y_buf[i].at[s], yr.at[i, s])
        if not at.draining:
            add_into(bpart(i, own_half[i].at[s], y), y_buf[i].at[s])
        if j:
            at.send(piece(i, own_half[i].at[s]), x_buf[i].at[far[t]], xs.at[i, t], xr.at[i, far[t]], at.xpeer)

    def xadd(i, t):
        if at.draining:
            return
        at.arrived(x_buf[i].at[far[t]], xr.at[i, far[t]])
        add_into(piece(i, own_half[i].at[shard(t, 0)]), x_buf[i].at[far[t]])

    def zadd(i, t):
        zz = far[t]
        p = piece(i, own_half[i].at[shard(t, 0)])

        def join(cond, slot):
            def do():
                at.arrived(z_buf[i].at[slot], zr.at[i, slot])
                add_into(p, z_buf[i].at[slot])

            if not at.draining:
                pl.when(cond)(do)

        if t > 0:
            inc = jnp.where(zz < z, z + 1, z - 1)
            join((inc >= 0) & (inc <= 3), zz)
            nxt = jnp.where(zz < z, z - 1, z + 1)
            slot = jnp.where((zz < z) & (nxt == zz), 4, zz)
            at.send(p, z_buf[i].at[slot], zs.at[i, t - 1], zr.at[i, slot], at.line(nxt))
        else:
            join(z > 0, z)
            join(z < 3, 4)
            if not at.draining:
                to_fin(i).start()

    def fin(i):
        axis, half, a, b, base, _ = cuts[i]
        own = own_half[i].at[at.g]
        if not at.draining:
            at.arrived(fin_buf[i], fr.at[i])
            to_fin(i).wait_send()
            to_y(i, 0, 0).wait_send()
            for yy in (0, 1):

                @pl.when(y == 1 - yy)
                def _():
                    add_into(span(own, axis, b, a), span(fin_buf[i], axis, b if yy == 0 else 0, a))
                    move_into(span(own, axis, yy * (a + b), b), span(fin_buf[i], axis, 0 if yy == 0 else a, b))

        o = span(outs[i], axis, base + c * half, half)
        at.send(own, o, es.at[i], er.at[i], at.cpeer)
        at.keep(own, o, ws.at[i])

    seq = [(i, t, j) for i in range(n) for (t, j) in order]
    opening = [functools.partial(give, *p) for p in seq]
    ly, lx, lz, lf = lags
    todo = []
    for q, (i, t, j) in enumerate(seq):
        todo.append((q, 0, functools.partial(cadd, i, t, j)))
        todo.append((q + ly, 1, functools.partial(yadd, i, t, j)))
        if j == 0:
            todo.append((q + ly + lx, 2, functools.partial(xadd, i, t)))
            todo.append((q + ly + lx + lz, 3, functools.partial(zadd, i, t)))
            if t == 0:
                todo.append((q + ly + lx + lz + lf, 4, functools.partial(fin, i)))
    todo.sort(key=lambda p: p[:2])

    def last():
        for i in range(n):
            axis, half, _, _, base, _ = cuts[i]
            at.arrived(span(outs[i], axis, base + (1 - c) * half, half), er.at[i])

    return opening, [f for _, _, f in todo], last


def head_window(h):
    first = jnp.minimum(h * HDIM // LANES, HEADS * HDIM // LANES - 2) * LANES
    lane = lax.broadcasted_iota(jnp.int32, (1, 2 * LANES), 1) + first
    inside = (lane >= h * HDIM) & (lane < h * HDIM + HDIM)
    return pl.ds(pl.multiple_of(first, LANES), 2 * LANES), inside


def dot_t(left, right):
    return lax.dot_general(left, right, (((1,), (1,)), ((), ())), preferred_element_type=jnp.float32)


def first_dot(left, right):
    return lax.dot_general(left, right, (((0,), (0,)), ((), ())), preferred_element_type=jnp.float32)


def pick_dot(values, chosen):
    high = values.astype(jnp.bfloat16)
    low = (values - high.astype(jnp.float32)).astype(jnp.bfloat16)
    return jnp.dot(high, chosen, preferred_element_type=jnp.float32) + jnp.dot(
        low, chosen, preferred_element_type=jnp.float32
    )


def head_pick(width):
    row = lax.broadcasted_iota(jnp.int32, (width, LANES), 0)
    first = lax.broadcasted_iota(jnp.int32, (width, LANES), 1) * HDIM
    return ((row >= first) & (row < first + HDIM)).astype(jnp.float32).astype(jnp.bfloat16)


def head_spread(width):
    lane = lax.broadcasted_iota(jnp.int32, (LANES, width), 1)
    first = lax.broadcasted_iota(jnp.int32, (LANES, width), 0) * HDIM
    return ((lane >= first) & (lane < first + HDIM)).astype(jnp.float32).astype(jnp.bfloat16)


def rope_tables(band, rows, cols, width):
    quarter = HDIM // 4
    shape = (rows * cols, width)
    token = lax.broadcasted_iota(jnp.int32, shape, 0)
    lane = lax.broadcasted_iota(jnp.int32, shape, 1) % HDIM
    power = (lane % quarter).astype(jnp.float32) * (-math.log(10000.0) / quarter)
    by_row = band * rows + (token // cols).astype(jnp.float32)
    index = jnp.where(lane < 2 * quarter, by_row, (token % cols).astype(jnp.float32))
    angle = index * jnp.exp(power)
    sine = jnp.sin(angle)
    low = (lane // quarter) % 2 == 0
    return jnp.cos(angle), jnp.where(low, -sine, 0.0), jnp.where(low, 0.0, sine)


def turn(values, cos, sin_next, sin_prev):
    width = values.shape[-1]
    after = pltpu.roll(values, width - HDIM // 4, 1)
    before = pltpu.roll(values, HDIM // 4, 1)
    return values * cos + after * sin_next + before * sin_prev


def turn_back(values, cos, sin_next, sin_prev):
    width = values.shape[-1]
    after = pltpu.roll(values, width - HDIM // 4, 1)
    before = pltpu.roll(values, HDIM // 4, 1)
    return values * cos - after * sin_next - before * sin_prev


def qkv_back_kernel(
    x_ref, mod_ref, mid_ref, dq_ref, dk_ref, dv_ref, nq_ref, nk_ref, rq_ref, rk_ref, w_ref,
    gains_ref, cos_ref, next_ref, prev_ref,
    dqkv_ref, dx_ref, sums_ref,
):
    width = x_ref.shape[-1]
    tables = (cos_ref[...], next_ref[...], prev_ref[...])
    pick, spread = head_pick(width), head_spread(width)
    ins = ((dq_ref, nq_ref, rq_ref), (dk_ref, nk_ref, rk_ref))
    for part, (d_ref, n_ref, r_ref) in enumerate(ins):
        back = turn_back(d_ref[0].astype(jnp.float32) * HDIM ** (-0.5), *tables)
        unit = n_ref[0]
        sums_ref[0, 2 + part : 3 + part, :] = jnp.sum(back * unit, axis=0, keepdims=True)
        inner = back * gains_ref[part : part + 1, :]
        mean = pick_dot(inner * unit, pick) * (1.0 / HDIM)
        grad = (inner - unit * pick_dot(mean, spread)) * pick_dot(r_ref[0], spread)
        dqkv_ref[0, :, part * width : (part + 1) * width] = grad.astype(jnp.bfloat16)
    dqkv_ref[0, :, 2 * width : 3 * width] = dv_ref[0]
    d_normed = dot_t(dqkv_ref[0], w_ref[...])
    x = x_ref[0].astype(jnp.float32)
    root = lax.rsqrt(jnp.mean(x * x, axis=-1, keepdims=True) + EPS)
    unit = x * root
    sums_ref[0, 0:1, :] = jnp.sum(d_normed, axis=0, keepdims=True)
    sums_ref[0, 1:2, :] = jnp.sum(d_normed * unit, axis=0, keepdims=True)
    inner = d_normed * (1.0 + mod_ref[0, 1:2, :])
    dx_ref[0] = mid_ref[0] + root * (inner - unit * jnp.mean(inner * unit, axis=-1, keepdims=True))


def qkv_backward(x, mod, d_mid, dq, dk, dv, nq, nk, rq, rk, qp_all, gains, tables):
    images, length, width = x.shape
    row = lambda w: pl.BlockSpec((1, length, w), lambda i: (i, 0, 0))
    whole = lambda a: pl.BlockSpec(a.shape, lambda i: (0,) * a.ndim)
    return pl.pallas_call(
        qkv_back_kernel,
        grid=(images,),
        in_specs=[row(width), pl.BlockSpec((1, 6, width), lambda i: (i, 0, 0))]
        + [row(width)] * 6
        + [row(LANES)] * 2
        + [pl.BlockSpec((width, 3 * width), lambda i: (0, 0)), whole(gains)]
        + [whole(t) for t in tables],
        out_shape=[
            jax.ShapeDtypeStruct((images, length, 3 * width), jnp.bfloat16),
            jax.ShapeDtypeStruct((images, length, width), jnp.float32),
            jax.ShapeDtypeStruct((images, 4, width), jnp.float32),
        ],
        out_specs=[row(3 * width), row(width), pl.BlockSpec((1, 4, width), lambda i: (i, 0, 0))],
        compiler_params=pltpu.CompilerParams(vmem_limit_bytes=60 * 2**20),
        name="qkv_backward",
    )(x, mod, d_mid, dq, dk, dv, nq, nk, rq, rk, qp_all, gains, *tables)
def tail_scratch():
    s = pltpu.SemaphoreType.DMA
    wide = SMALL_COLS
    return [
        pltpu.VMEM((SMALL_ROWS, wide), jnp.float32),
        pltpu.VMEM((2, SMALL_ROWS, wide), jnp.float32),
        pltpu.VMEM((8, SMALL_ROWS, wide), jnp.bfloat16),
        pltpu.VMEM((8, GROUPS, 2 * LANES), jnp.float32),
        s((8,)),
        s((8,)),
    ]


def tail_steps(at, ins, outs, scratch):
    part_ref, ada_ref, slope_ref = ins
    all_ref, cond_ref = outs
    acc, inbox, blocks, cond, ss, rs = scratch
    width = HEADS * HDIM
    z = at.z
    line = (at.xpeer, at.line(at.far[1]), at.line((z + 2) % 4))

    def copy(r):
        if r < 2:
            return at.copy(acc, inbox.at[r], ss.at[r], rs.at[r], (at.cpeer, at.ypeer)[r])
        ref, k = (blocks, r - 2) if r < 5 else (cond, r - 5)
        start, size = ((at.g, 1), (2 * z, 2), (4 * (z // 2), 4))[k]
        src = ref.at[pl.ds(start, size)]
        return at.copy(src, src, ss.at[r], rs.at[r], line[k])

    def pack():
        row = lax.broadcasted_iota(jnp.int32, (SMALL_ROWS, 1), 0)
        value = acc[...]
        rest = value - value.astype(jnp.bfloat16).astype(jnp.float32)
        last = rest - rest.astype(jnp.bfloat16).astype(jnp.float32)
        value = jnp.where(row == GAIN_ROW + 1, rest, jnp.where(row == GAIN_ROW + 2, last, value))
        blocks[at.g] = value.astype(jnp.bfloat16)

    def cond_rows():
        flat = blocks[...].reshape(8 * SMALL_ROWS, SMALL_COLS)
        row = lax.broadcasted_iota(jnp.int32, (8 * SMALL_ROWS, 1), 0) % SMALL_ROWS
        silu = jnp.zeros((8 * SMALL_ROWS, ada_ref.shape[0]), jnp.float32)
        for k in range(6):
            product = dot_t(flat[:, :width], ada_ref[:, k * width : (k + 1) * width])
            silu = jnp.where((row % 6 == k) & (row < GAIN_ROW), product, silu)
        by_group = lax.dot_general(
            flat[:, width:].astype(jnp.float32),
            silu,
            (((0,), (0,)), ((), ())),
            precision=lax.Precision.HIGHEST,
            preferred_element_type=jnp.float32,
        )
        cond[at.g] = jnp.zeros((GROUPS, 2 * LANES), jnp.float32)
        cond[at.g, :, : ada_ref.shape[0]] = by_group[:GROUPS] * slope_ref[...]

    def step(r):
        if at.draining:
            return
        if r > 0:
            copy(r - 1).wait()
        if r == 0:
            acc[...] = part_ref[...]
        elif r <= 2:
            acc[...] = acc[...] + inbox[r - 1]
        if r == 2:
            pack()
        if r == 5:
            cond_rows()
        if r < 8:
            copy(r).start()
        else:
            all_ref[...] = blocks[...]
            cond_ref[...] = cond[...]

    return [functools.partial(step, r) for r in range(9)]


SMALL_ROWS, SMALL_COLS, GAIN_ROW = 16, HEADS * HDIM + LANES, 12


def scatter_kernel(n, cuts, lags, *refs):
    at = Place()
    at.greet_all()
    ins, small_in = refs[:n], refs[n : n + 3]
    outs, small_out = refs[n + 3 : 2 * n + 3], refs[2 * n + 3 : 2 * n + 5]
    small = tail_steps(at, small_in, small_out, refs[2 * n + 5 : 2 * n + 11])
    opening, steps, last = scatter_steps(at, cuts, ins, outs, refs[2 * n + 11 :], lags)
    small[0]()
    for step in opening:
        step()
    small = small[1:]
    for k, step in enumerate(steps):
        step()
        if k % 3 == 2 and small:
            small[0]()
            small = small[1:]
    for step in small:
        step()
    last()
    at.drain(opening + steps)


def scatter(grads, cuts, lags, part, w_ada, slope):
    n = len(grads)
    any_ref = pl.BlockSpec(memory_space=pl.ANY)
    vmem = pl.BlockSpec(memory_space=pltpu.VMEM)
    return pl.pallas_call(
        functools.partial(scatter_kernel, n, cuts, lags),
        out_shape=[jax.ShapeDtypeStruct(w.shape[1:], jnp.bfloat16) for w in grads]
        + [
            jax.ShapeDtypeStruct((8, SMALL_ROWS, SMALL_COLS), jnp.bfloat16),
            jax.ShapeDtypeStruct((8, GROUPS, 2 * LANES), jnp.float32),
        ],
        in_specs=[any_ref] * n + [vmem] * 3,
        out_specs=[any_ref] * n + [vmem] * 2,
        scratch_shapes=tail_scratch() + scatter_scratch(grads, cuts),
        compiler_params=pltpu.CompilerParams(
            collective_id=1, has_side_effects=True, vmem_limit_bytes=60 * 2**20
        ),
        name="gradient_scatter",
    )(*grads, part, w_ada, slope)


def forward_kernel(cuts, cols, refs):
    n = len(cuts)
    soon = sum(cut[5] == 0 for cut in cuts)
    at = Place()
    x_ref, part_ref, group_ref, gains_ref, band_ref = refs["in"]
    normed_ref, q_ref, nq_ref, nk_ref, rq_ref, rk_ref, o_ref, inv_ref, mod_ref, *table_refs, kv_out = refs["out"]
    kv, w_buf, pick_ref, spread_ref, mod_buf, mod_in, w_sem, ms, mr, ks, kr, os = refs["scratch"]
    ins, outs = refs["shards"], refs["full"]
    images, length, width = x_ref.shape
    parts = [(i, s) for i in range(images) for s in (0, 1)]
    if n:
        at.greet_all()
        steps, first, last = gather_steps(at, cuts, ins, outs, refs["sems"])
    else:
        at.greet_band()
        steps, first, last = [], 0, None

    mod_buf[...] = part_ref[...]

    def mod_copy(r):
        peer = (at.xpeer, at.line(at.far[1]), at.line((at.z + 2) % 4))[r]
        return at.copy(mod_buf, mod_in.at[r], ms.at[r], mr.at[r], peer)

    def mod_step(r):
        if at.draining:
            return
        if r > 0:
            mod_copy(r - 1).wait()
            mod_buf[...] = mod_buf[...] + mod_in[r - 1]
        if r < 3:
            mod_copy(r).start()

    def rows(s, i, band):
        return kv.at[s, i, pl.ds(pl.multiple_of(band * length, 16), length), :]

    here, over = at.band, (1 - at.y) * 2 + at.c
    beside, across = at.y * 2 + 1 - at.c, (1 - at.y) * 2 + 1 - at.c

    def give(i, s):
        p = rows(s, i, here)
        at.send(p, p, ks.at[i, s, 0], kr.at[i, s, 0], at.ypeer)
        at.send(p, p, ks.at[i, s, 1], kr.at[i, s, 1], at.cpeer)

    def pass_on(i, s):
        p = rows(s, i, over)
        at.arrived(p, kr.at[i, s, 0])
        at.send(p, p, ks.at[i, s, 2], kr.at[i, s, 2], at.cpeer)

    def ready(i):
        for s in (0, 1):
            at.arrived(rows(s, i, beside), kr.at[i, s, 1])
            at.arrived(rows(s, i, across), kr.at[i, s, 2])
            at.keep(kv.at[s, i], kv_out.at[s, i], os.at[i, s])

    def norm(i):
        value = x_ref[i].astype(jnp.float32)
        root = lax.rsqrt(jnp.mean(value * value, axis=-1, keepdims=True) + EPS)
        chosen = jnp.sum(group_ref[:, i : i + 1] * mod_buf[...], axis=0, keepdims=True)
        mod_ref[i : i + 1, :] = chosen
        shift, scale = chosen[:, :width], chosen[:, width : 2 * width]
        normed_ref[i] = (value * root * (1.0 + scale) + shift).astype(jnp.bfloat16)

    def raw(i, part):
        return jnp.dot(
            normed_ref[i], w_buf[:, part * width : (part + 1) * width], preferred_element_type=jnp.float32
        )

    def project(i, part, n_ref, r_ref):
        values = raw(i, part)
        inv = lax.rsqrt(pick_dot(values * values, pick_ref[...]) * (1.0 / HDIM) + EPS)
        r_ref[i] = inv
        unit = values * pick_dot(inv, spread_ref[...])
        n_ref[i] = unit
        scaled = unit * gains_ref[part : part + 1, :]
        return turn(scaled, *(t[...] for t in table_refs)).astype(jnp.bfloat16)

    def key_part(i):
        norm(i)
        kv[0, i, pl.ds(pl.multiple_of(here * length, 16), length), :] = project(i, 1, nk_ref, rk_ref)
        give(i, 0)

    def value_part(i):
        kv[1, i, pl.ds(pl.multiple_of(here * length, 16), length), :] = raw(i, 2).astype(jnp.bfloat16)
        give(i, 1)

    def query_part(i):
        q_ref[i] = project(i, 0, nq_ref, rq_ref)

    def head(i, h):
        win, inside = head_window(h)
        query = q_ref[i, :, win]
        query = jnp.where(inside, query, jnp.zeros_like(query))
        power = jnp.exp2(dot_t(query, kv[0, i, :, win]) * (HDIM ** (-0.5) * LOG2E))
        inv = 1.0 / jnp.sum(power, axis=-1, keepdims=True)
        out = jnp.dot(
            (power * inv).astype(jnp.bfloat16), kv[1, i, :, win], preferred_element_type=jnp.float32
        )
        o_ref[i, :, win] = jnp.where(inside, out.astype(jnp.bfloat16), o_ref[i, :, win])
        lane = lax.broadcasted_iota(jnp.int32, (1, LANES), 1)
        inv_ref[i] = jnp.where(lane == h, inv, inv_ref[i])

    def prepare():
        pick_ref[...] = head_pick(width)
        spread_ref[...] = head_spread(width)

        def block(r, _):
            rows_of = pl.ds(pl.multiple_of(r * cols, cols), cols)
            row = band_ref[0:1, 0:1] * (length // cols) + r.astype(jnp.float32)
            for ref, value in zip(table_refs, rope_tables(row, 1, cols, width)):
                ref[rows_of, :] = value
            return 0

        lax.fori_loop(0, length // cols, block, 0)

    if not n:
        prepare()
    if n:
        for k in range(3):
            mod_step(k)
            for step in steps[2 * k : 2 * k + 2]:
                step()
                if k == 0 and step is steps[0]:
                    prepare()
        mod_step(3)
        for step in steps[6:first]:
            step()
        for i in range(soon):
            last(i)
        pltpu.make_async_copy(ins[0], outs[0].at[at.g], refs["sems"][0].at[0]).wait()
        loads = [
            pltpu.make_async_copy(
                outs[0].at[k, :, pl.ds(0, 3 * width)],
                w_buf.at[pl.ds(k * (width // 8), width // 8), :],
                w_sem.at[k],
            )
            for k in range(8)
        ]
    else:
        loads = [pltpu.make_async_copy(ins[0].at[:, pl.ds(0, 3 * width)], w_buf, w_sem.at[0])]
    for d in loads:
        d.start()
    o_ref[...] = jnp.zeros_like(o_ref)
    inv_ref[...] = jnp.zeros_like(inv_ref)
    for d in loads:
        d.wait()
    todo = steps[first:]
    for i in range(images):
        for work in (key_part, value_part):
            work(i)
            for step in todo[:2]:
                step()
            todo = todo[2:]
    for i in range(images):
        query_part(i)
        for step in todo[:2]:
            step()
        todo = todo[2:]
    for i in range(images):
        pass_on(i, 0)
        pass_on(i, 1)
        ready(i)
        mine, todo = (todo[: HEADS // 2], todo[HEADS // 2 :])

        def body(h, _, i=i, mine=mine):
            for k, step in enumerate(mine):
                pl.when(h == 2 * k)(step)
            head(i, h)
            return 0

        lax.fori_loop(0, HEADS, body, 0)
    for step in todo:
        step()
    for i in range(soon, n):
        last(i)
    at.drain(steps)
    for i, s in parts:
        at.drain([functools.partial(give, i, s), functools.partial(pass_on, i, s)])
    for i in range(images):
        at.drain([functools.partial(ready, i)])


def forward(x, mod_part, groups, gains, band, cols, shards, cuts):
    n = len(cuts)
    images, length, width = x.shape
    bands = lax.axis_size("band")
    keys = (2, images, bands * length, width)
    s = pltpu.SemaphoreType.DMA
    bf = jnp.bfloat16
    any_ref = pl.BlockSpec(memory_space=pl.ANY)
    vmem = pl.BlockSpec(memory_space=pltpu.VMEM)
    args = [x, mod_part, groups, gains, band]
    rows = lambda w, d: jax.ShapeDtypeStruct((images, length, w), d)
    outs = [rows(width, bf)] * 2 + [rows(width, jnp.float32)] * 2 + [rows(LANES, jnp.float32)] * 2
    outs += [rows(width, bf), rows(LANES, jnp.float32), jax.ShapeDtypeStruct((images, mod_part.shape[1]), jnp.float32)]
    outs += [jax.ShapeDtypeStruct((length, width), jnp.float32)] * 3
    scratch = [
        pltpu.VMEM(keys, bf),
        pltpu.VMEM((width, 3 * width), bf),
        pltpu.VMEM((width, LANES), bf),
        pltpu.VMEM((LANES, width), bf),
        pltpu.VMEM(mod_part.shape, jnp.float32),
        pltpu.VMEM((3,) + mod_part.shape, jnp.float32),
        s((8,)),
        s((3,)),
        s((3,)),
        s((images, 2, 3)),
        s((images, 2, 3)),
        s((images, 2)),
    ]
    whole = len(shards) if n else 0
    sizes = [len(args), len(shards), len(outs) + 1, whole, len(scratch), 10 if n else 0]

    def kernel(*refs):
        groups_of, start = [], 0
        for size in sizes:
            groups_of.append(refs[start : start + size])
            start += size
        names = ("in", "shards", "out", "full", "scratch", "sems")
        forward_kernel(cuts, cols, dict(zip(names, groups_of)))

    return pl.pallas_call(
        kernel,
        out_shape=outs
        + [jax.ShapeDtypeStruct(keys, bf)]
        + [jax.ShapeDtypeStruct((8,) + w.shape, w.dtype) for w in shards[:whole]],
        in_specs=[vmem] * len(args) + [any_ref] * len(shards),
        out_specs=[vmem] * len(outs) + [any_ref] * (1 + whole),
        scratch_shapes=scratch + (gather_sems(n) if n else []),
        compiler_params=pltpu.CompilerParams(
            collective_id=2, has_side_effects=True, vmem_limit_bytes=60 * 2**20
        ),
        name="forward",
    )(*args, *shards)


EACH = 9


def attention_back_kernel(n, cuts, lags, q_ref, do_ref, inv_ref, kv_ref, *refs):
    ins, (dq_ref, d_out), outs = refs[:n], refs[n : n + 2], refs[n + 2 : 2 * n + 2]
    kv, dkv, core_buf, y_buf, load_sem, ks, kr, ys, yr, ws = refs[2 * n + 2 : 2 * n + 12]
    images, length, width = q_ref.shape
    at = Place()
    loads = [pltpu.make_async_copy(kv_ref.at[:, i], kv.at[i], load_sem.at[i]) for i in range(images)]
    for d in loads:
        d.start()
    at.greet_all() if n else at.greet_band()
    opening, todo, last = [], [], lambda: None
    if n:
        opening, todo, last = scatter_steps(at, cuts, ins, outs, refs[2 * n + 12 :], lags)
    for step in opening:
        step()
    steps = opening + todo

    def rows(s, i, band):
        return dkv.at[s, i, pl.ds(pl.multiple_of(band * length, 16), length), :]

    def to_core(i):
        for s in (0, 1):
            for yy in (0, 1):
                at.send(rows(s, i, yy * 2 + 1 - at.c), core_buf.at[i, s, yy], ks.at[i, s, yy], kr.at[i, s, yy], at.cpeer)

    def core_add(i):
        for s in (0, 1):
            p = rows(s, i, (1 - at.y) * 2 + at.c)
            at.arrived(core_buf.at[i, s, 1 - at.y], kr.at[i, s, 1 - at.y])
            if not at.draining:
                add_into(p, core_buf.at[i, s, 1 - at.y])
            at.send(p, y_buf.at[i, s], ys.at[i, s], yr.at[i, s], at.ypeer)
        for s in (0, 1):
            at.arrived(core_buf.at[i, s, at.y], kr.at[i, s, at.y])
            if not at.draining:
                add_into(rows(s, i, at.band), core_buf.at[i, s, at.y])

    def y_add(i):
        for s in (0, 1):
            p = rows(s, i, at.band)
            at.arrived(y_buf.at[i, s], yr.at[i, s])
            if not at.draining:
                add_into(p, y_buf.at[i, s])
            at.keep(p, d_out.at[s, i], ws.at[i, s])

    def head(i, h):
        win, inside = head_window(h)
        query, grad = q_ref[i, :, win], do_ref[i, :, win]
        query = jnp.where(inside, query, jnp.zeros_like(query))
        grad = jnp.where(inside, grad, jnp.zeros_like(grad))
        keys, values = kv[i, 0, :, win], kv[i, 1, :, win]
        inv = inv_ref[i, pl.ds(h, 1), :]
        probs = jnp.exp2(dot_t(keys, query) * (HDIM ** (-0.5) * LOG2E)) * inv
        d_probs = dot_t(values, grad)
        delta = jnp.sum(probs * d_probs, axis=0, keepdims=True)
        d_scores = (probs * (d_probs - delta)).astype(jnp.bfloat16)
        d_key = jnp.dot(d_scores, query, preferred_element_type=jnp.float32).astype(jnp.bfloat16)
        d_value = jnp.dot(
            probs.astype(jnp.bfloat16), grad, preferred_element_type=jnp.float32
        ).astype(jnp.bfloat16)
        dkv[0, i, :, win] = jnp.where(inside, d_key, dkv[0, i, :, win])
        dkv[1, i, :, win] = jnp.where(inside, d_value, dkv[1, i, :, win])
        dq_ref[i, :, win] = jnp.where(inside, first_dot(d_scores, keys), dq_ref[i, :, win])

    dq_ref[...] = jnp.zeros_like(dq_ref)
    for s in (0, 1):
        for i in range(images):

            def clear(r, _, s=s, i=i):
                dkv[s, i, pl.ds(pl.multiple_of(r * 16, 16), 16), :] = jnp.zeros((16, width), jnp.bfloat16)
                return 0

            lax.fori_loop(0, kv.shape[2] // 16, clear, 0)
    exchange = []
    for i in range(images):
        loads[i].wait()
        mine, todo = (todo[:EACH], todo[EACH:])
        due = exchange
        exchange = [functools.partial(f, i) for f in (core_add, y_add)]

        def body(h, _, i=i, mine=mine, due=due):
            for k, step in enumerate(due):
                pl.when(h == 1 + 12 * k)(step)
            for k, step in enumerate(mine):
                pl.when(h == k * HEADS // EACH)(step)
            head(i, h)
            return 0

        lax.fori_loop(0, HEADS, body, 0)
        to_core(i)
        steps += [functools.partial(to_core, i)] + exchange
    exchange[0]()
    part = min(6, len(todo))
    for step in todo[:part] + [exchange[1]] + todo[part:]:
        step()
    last()
    at.drain(steps)


def attention_backward(q, d_att, inv_rows, kv_all, grads, cuts, lags):
    n = len(grads)
    images, length, width = q.shape
    s = pltpu.SemaphoreType.DMA
    any_ref = pl.BlockSpec(memory_space=pl.ANY)
    vmem = pl.BlockSpec(memory_space=pltpu.VMEM)
    bf = jnp.bfloat16
    return pl.pallas_call(
        functools.partial(attention_back_kernel, n, cuts, lags),
        out_shape=[
            jax.ShapeDtypeStruct(q.shape, jnp.float32),
            jax.ShapeDtypeStruct((2, images, length, width), bf),
        ]
        + [jax.ShapeDtypeStruct(w.shape[1:], bf) for w in grads],
        in_specs=[vmem, vmem, vmem, any_ref] + [any_ref] * n,
        out_specs=[vmem, any_ref] + [any_ref] * n,
        scratch_shapes=[
            pltpu.VMEM((images, 2) + kv_all.shape[2:], bf),
            pltpu.VMEM(kv_all.shape, bf),
            pltpu.VMEM((images, 2, 2, length, width), bf),
            pltpu.VMEM((images, 2, length, width), bf),
            s((images,)),
            s((images, 2, 2)),
            s((images, 2, 2)),
            s((images, 2)),
            s((images, 2)),
            s((images, 2)),
        ]
        + (scatter_scratch(grads, cuts) if n else []),
        compiler_params=pltpu.CompilerParams(
            collective_id=3, has_side_effects=True, vmem_limit_bytes=63 * 2**20
        ),
        name="attention_backward",
    )(q, d_att, inv_rows, kv_all, *grads)
def mlp_kernel(
    x_ref, gout_ref, att_ref, mod_ref, live_ref, proj_ref, gate_ref, up_ref, down_ref,
    out_ref, dmid_ref, dproj_ref, datt_ref, sums_ref, dgu_ref, ddown_ref,
    mid, proj, mlp, dnorm, normed, normed_t, dmlp,
):
    step, steps = pl.program_id(0), pl.num_programs(0)
    images, length, width = x_ref.shape
    chunk = gate_ref.shape[1]

    def piece(i, k):
        return mod_ref[i : i + 1, k * width : (k + 1) * width]

    def rows(i):
        return pl.ds(i * length, length)

    def live(i):
        return live_ref[i : i + 1, 0:1]

    def unit(i):
        value = mid[rows(i), :]
        root = lax.rsqrt(jnp.mean(value * value, axis=-1, keepdims=True) + EPS)
        return value * root, root

    @pl.when(step == 0)
    def _():
        for i in range(images):
            proj[rows(i), :] = jnp.dot(att_ref[i], proj_ref[...], preferred_element_type=jnp.float32)
            mid[rows(i), :] = x_ref[i].astype(jnp.float32) + piece(i, 2) * proj[rows(i), :]
            value = (unit(i)[0] * (1.0 + piece(i, 4)) + piece(i, 3)).astype(jnp.bfloat16)
            normed[rows(i), :] = value
            normed_t[:, rows(i)] = value.T
            dmlp[rows(i), :] = (piece(i, 5) * (gout_ref[i].astype(jnp.float32) * live(i))).astype(jnp.bfloat16)
        mlp[...] = jnp.zeros_like(mlp)
        dnorm[...] = jnp.zeros_like(dnorm)

    gate = jnp.dot(normed[...], gate_ref[...], preferred_element_type=jnp.float32)
    up = jnp.dot(normed[...], up_ref[...], preferred_element_type=jnp.float32)
    dhidden = dot_t(dmlp[...], down_ref[...])
    sigmoid = 1.0 / (1.0 + jnp.exp(-gate))
    silu = gate * sigmoid
    hidden = (silu * up).astype(jnp.bfloat16)
    dgate = (dhidden * up * (sigmoid * (1.0 + gate * (1.0 - sigmoid)))).astype(jnp.bfloat16)
    dup = (dhidden * silu).astype(jnp.bfloat16)
    mlp[...] += jnp.dot(hidden, down_ref[...], preferred_element_type=jnp.float32)
    dnorm[...] += dot_t(dgate, gate_ref[...]) + dot_t(dup, up_ref[...])
    ddown_ref[...] = first_dot(hidden, dmlp[...]).astype(jnp.bfloat16)
    dgu_ref[:, :chunk] = jnp.dot(normed_t[...], dgate, preferred_element_type=jnp.float32).astype(jnp.bfloat16)
    dgu_ref[:, chunk:] = jnp.dot(normed_t[...], dup, preferred_element_type=jnp.float32).astype(jnp.bfloat16)

    @pl.when(step == steps - 1)
    def _():
        total = lambda v: jnp.sum(v, axis=0, keepdims=True)
        for i in range(images):
            gy = gout_ref[i].astype(jnp.float32) * live(i)
            value = mlp[rows(i), :]
            out_ref[i] = ((mid[rows(i), :] + piece(i, 5) * value) * live(i)).astype(jnp.bfloat16)
            sums_ref[i, 3:4, :] = total(gy * value)
            n, root = unit(i)
            dn = dnorm[rows(i), :]
            sums_ref[i, 1:2, :] = total(dn)
            sums_ref[i, 2:3, :] = total(dn * n)
            e = dn * (1.0 + piece(i, 4))
            d_mid = gy + root * (e - n * jnp.mean(e * n, axis=-1, keepdims=True))
            dmid_ref[i] = d_mid
            sums_ref[i, 0:1, :] = total(d_mid * proj[rows(i), :])
            d_proj = (piece(i, 2) * d_mid).astype(jnp.bfloat16)
            dproj_ref[i] = d_proj
            datt_ref[i] = dot_t(d_proj, proj_ref[...]).astype(jnp.bfloat16)


def mlp_chunk(ff):
    return 512 if ff % 512 == 0 else 128


def mlp_block(x, grad_out, attended, mod, live, qp_all, gu_all, down_all):
    images, length, width = x.shape
    ff = down_all.shape[0]
    chunk = mlp_chunk(ff)
    steps = ff // chunk
    bf = jnp.bfloat16
    whole = lambda s: pl.BlockSpec(s, lambda k: (0,) * len(s))
    rows = lambda d: jax.ShapeDtypeStruct(x.shape, d)
    tokens = images * length
    return pl.pallas_call(
        mlp_kernel,
        grid=(steps,),
        in_specs=[whole(x.shape)] * 3
        + [whole(mod.shape), whole(live.shape), pl.BlockSpec((width, width), lambda k: (0, 3))]
        + [
            pl.BlockSpec((width, chunk), lambda k: (0, k)),
            pl.BlockSpec((width, chunk), lambda k: (0, steps + k)),
            pl.BlockSpec((chunk, width), lambda k: (k, 0)),
        ],
        out_shape=[rows(bf), rows(jnp.float32), rows(bf), rows(bf)]
        + [
            jax.ShapeDtypeStruct((images, 4, width), jnp.float32),
            jax.ShapeDtypeStruct((width, 2 * ff), bf),
            jax.ShapeDtypeStruct((ff, width), bf),
        ],
        out_specs=[whole(x.shape)] * 4
        + [
            whole((images, 4, width)),
            pl.BlockSpec((width, 2 * chunk), lambda k: (0, k)),
            pl.BlockSpec((chunk, width), lambda k: (k, 0)),
        ],
        scratch_shapes=[pltpu.VMEM((tokens, width), jnp.float32)] * 4
        + [pltpu.VMEM((tokens, width), bf), pltpu.VMEM((width, tokens), bf), pltpu.VMEM((tokens, width), bf)],
        compiler_params=pltpu.CompilerParams(vmem_limit_bytes=60 * 2**20),
        name="mlp_block",
    )(x, grad_out, attended, mod, live, qp_all, gu_all, gu_all, down_all)


def half_cuts(ref, axis, base, size, own_parts, shared_parts):
    unit = size // 2 // (own_parts + 2 * shared_parts)
    return (axis, size // 2, own_parts * unit, shared_parts * unit, base, ref)


def by_shard(grad):
    parts = lax.axis_size("grp")
    return grad.reshape(parts, grad.shape[0] // parts, grad.shape[1])


def body(
    patches,
    grad_out,
    cond_table,
    group_ids,
    live_count,
    band_order,
    w_ada,
    b_ada,
    w_qkv,
    q_gain,
    k_gain,
    w_proj,
    w_gate,
    w_up,
    w_down,
):
    images, rows, cols, width = patches.shape
    length = rows * cols
    ff = w_gate.shape[1]
    bf = jnp.bfloat16
    grp = lax.axis_index("grp")
    ada_rows, ada_cols, bias_cols = w_ada.shape[0], w_ada.shape[1], b_ada.shape[0]
    fits = (
        lax.axis_size("grp") == 8
        and images == 2
        and width == HEADS * HDIM
        and w_qkv.shape[0] % 16 == 0
        and 4 * width % 4608 == 0
        and 2 * ff % 3072 == 0
        and w_down.shape[0] % 384 == 0
    )
    w_qp = jnp.concatenate([w_qkv, w_proj], axis=1)
    w_gu = jnp.concatenate([w_gate, w_up], axis=1)
    full = lambda w: w.reshape(-1, w.shape[-1])
    onehot = (group_ids[:, None] == jnp.arange(GROUPS, dtype=jnp.int32)[None, :]).astype(jnp.float32)
    cond_rows = lax.dynamic_slice_in_dim(cond_table, grp * ada_rows, ada_rows, axis=1)
    sigmoid = jax.nn.sigmoid(cond_rows)
    silu_rows = (cond_rows * sigmoid).astype(bf)
    silu_slope = sigmoid * (1.0 + cond_rows * (1.0 - sigmoid))
    mod_part = jnp.dot(silu_rows, w_ada, preferred_element_type=jnp.float32)
    bias_part = lax.dynamic_update_slice_in_dim(
        jnp.zeros((ada_cols,), jnp.float32), b_ada.astype(jnp.float32), grp * bias_cols, axis=0
    )
    mod_part = mod_part + bias_part[None, :]
    live_mask = (jnp.arange(images, dtype=jnp.int32) < live_count[0]).astype(jnp.float32)

    gains = jnp.stack([jnp.tile(q_gain, HEADS), jnp.tile(k_gain, HEADS)])
    x = patches.reshape(images, length, width)
    groups = jnp.pad(onehot.T, ((0, 0), (0, LANES - images)))
    band = jnp.broadcast_to(band_order.astype(jnp.float32)[:, None], (1, LANES))
    common = (groups, gains, band, cols)
    if fits:
        shards = [w_qp, w_gu, w_down]
        cuts = [half_cuts(0, 1, 0, 4 * width, 1, 1), half_cuts(1, 1, 0, 2 * ff, 4, 1)]
        cuts += [half_cuts(2, 0, 0, w_down.shape[0], 4, 1)]
    else:
        qp_all, gu_all, down_all = (lax.all_gather(w, "grp", axis=0, tiled=True) for w in (w_qp, w_gu, w_down))
        mod_part = lax.psum(mod_part, "grp")
        shards, cuts = [qp_all], []
    outs = forward(x, mod_part, *common, shards, cuts)
    normed_one, query, nq, nk, rq, rk, attended, inv, mod = outs[:9]
    tables, kv_all, rest = outs[9:12], outs[12], outs[13:]
    if fits:
        qp_all, gu_all, down_all = (full(w) for w in rest)
    live = jnp.broadcast_to(live_mask[:, None], (images, LANES))
    flat = lambda a: a.reshape(images * length, a.shape[-1])
    patches_out, d_middle, d_proj, d_attended, mid_sums, d_w_gu, d_w_down = mlp_block(
        x, grad_out.reshape(images, length, width), attended, mod, live, qp_all, gu_all, down_all
    )
    patches_out = patches_out.reshape(images, rows, cols, width)
    mod = mod.reshape(images, 6, width)
    d_w_proj = jnp.einsum("td,te->de", flat(attended), flat(d_proj), preferred_element_type=jnp.float32).astype(bf)
    d_query, d_kv, *rest = attention_backward(
        query,
        d_attended,
        jnp.swapaxes(inv, 1, 2),
        kv_all,
        [by_shard(d_w_gu)] if fits else [],
        [half_cuts(0, 1, 0, 2 * ff, 4, 1)] if fits else [],
        (2, 2, 1, 2),
    )
    d_qkv, d_x, sums = qkv_backward(
        x, mod, d_middle, d_query, d_kv[0], d_kv[1], nq, nk, rq, rk, qp_all, gains, tables
    )
    d_patches = d_x.reshape(images, rows, cols, width)
    d_w_qkv = jnp.einsum("td,te->de", flat(normed_one), flat(d_qkv), preferred_element_type=jnp.float32).astype(bf)
    d_w_qp = jnp.concatenate([d_w_qkv, d_w_proj], axis=1)

    d_mod_part = jnp.concatenate([sums[:, 0:2], mid_sums], axis=1)
    gain_part = jnp.sum(sums[:, 2:4].reshape(images, 2, HEADS, HDIM), axis=(0, 2))
    if fits:
        tags = jnp.pad(jnp.repeat(onehot * (1.0 / lax.axis_size("band")), 6, axis=0), ((0, 0), (0, LANES - GROUPS)))
        small = jnp.concatenate([d_mod_part.reshape(images * 6, width), tags], axis=1)
        gain_row = jnp.pad(gain_part.reshape(1, -1), ((0, 0), (0, SMALL_COLS - 2 * HDIM)))
        small = jnp.concatenate([small, gain_row, gain_row, gain_row, jnp.zeros_like(gain_row)])
        cuts = [half_cuts(0, 0, 0, w_down.shape[0], 2, 1), half_cuts(1, 1, 0, 4 * width, 8, 5)]
        d_gu = rest[0]
        d_down, d_qp, gathered, cond_blocks = scatter(
            [by_shard(d_w_down), by_shard(d_w_qp)], cuts, (2, 2, 1, 2), small, w_ada, silu_slope
        )
        d_mod_all = gathered[:, :GAIN_ROW, :width].reshape(-1, ada_cols)
        onehot_all = gathered[:, 0:GAIN_ROW:6, width : width + GROUPS].reshape(-1, GROUPS)
        gain_all = gathered[:, GAIN_ROW : GAIN_ROW + 3, : 2 * HDIM].astype(jnp.float32)
        gain_all = jnp.sum(gain_all, axis=(0, 1)).reshape(2, HDIM)
        d_cond = jnp.swapaxes(cond_blocks[:, :, :ada_rows], 0, 1).reshape(GROUPS, -1)
    else:
        d_gu, d_down, d_qp = (
            lax.psum(lax.psum_scatter(w, "grp", scatter_dimension=0, tiled=True), "band")
            for w in (d_w_gu, d_w_down, d_w_qp)
        )
        d_modulation = lax.psum(d_mod_part.reshape(images, ada_cols), "band").astype(bf)
        gain_all = lax.psum(gain_part, ("grp", "band"))
        payload = jnp.concatenate([d_modulation, onehot.astype(bf)], axis=1)
        payload = lax.all_gather(payload, "grp", axis=0, tiled=True)
        d_mod_all, onehot_all = payload[:, :ada_cols], payload[:, ada_cols:]
        d_silu = jnp.einsum("be,de->bd", d_mod_all, w_ada, preferred_element_type=jnp.float32)
        d_silu = jnp.dot(
            onehot_all.astype(jnp.float32).T,
            d_silu,
            precision=lax.Precision.HIGHEST,
            preferred_element_type=jnp.float32,
        )
        d_cond = lax.all_gather(d_silu * silu_slope, "grp", axis=1, tiled=True)
    silu_all = jnp.dot(onehot_all, silu_rows, preferred_element_type=jnp.float32).astype(bf)
    d_w_ada = jnp.einsum("bd,be->de", silu_all, d_mod_all, preferred_element_type=jnp.float32)
    d_b_ada = lax.dynamic_slice_in_dim(
        jnp.sum(d_mod_all.astype(jnp.float32), axis=0), grp * bias_cols, bias_cols, axis=0
    )
    wide = lambda a: a.astype(jnp.float32)
    chunk = mlp_chunk(ff)
    d_gu = d_gu.reshape(d_gu.shape[0], ff // chunk, 2, chunk)
    return (
        patches_out,
        d_patches,
        d_cond,
        d_w_ada,
        d_b_ada,
        wide(d_qp[:, : 3 * width]),
        gain_all[0],
        gain_all[1],
        wide(d_qp[:, 3 * width :]),
        wide(d_gu[:, :, 0].reshape(-1, ff)),
        wide(d_gu[:, :, 1].reshape(-1, ff)),
        wide(d_down),
    )


def solution(mesh):
    in_specs = (
        P("grp", "band", None, None),
        P("grp", "band", None, None),
        P(),
        P("grp"),
        P("grp"),
        P("band"),
        P("grp", None),
        P("grp"),
        P("grp", None),
        P(),
        P(),
        P("grp", None),
        P("grp", None),
        P("grp", None),
        P("grp", None),
    )
    out_specs = (
        P("grp", "band", None, None),
        P("grp", "band", None, None),
        P(),
        P("grp", None),
        P("grp"),
        P("grp", None),
        P(),
        P(),
        P("grp", None),
        P("grp", None),
        P("grp", None),
        P("grp", None),
    )
    return jax.shard_map(body, mesh=mesh, in_specs=in_specs, out_specs=out_specs, check_vma=False)
```

```python
import functools
import math

import jax
import jax.numpy as jnp
from jax import lax
from jax.experimental import pallas as pl
from jax.experimental.pallas import tpu as pltpu
from jax.sharding import PartitionSpec as P

HEADS = 16
HDIM = 72
GROUPS = 8
LANES = 128
EPS = 1e-06
LOG2E = 1.4426950408889634

MESH = pl.DeviceIdType.MESH


class Place:
    def __init__(self):
        self.g, self.band = lax.axis_index("grp"), lax.axis_index("band")
        self.z, self.x = self.g // 2, self.g % 2
        self.y, self.c = self.band // 2, self.band % 2
        z = self.z
        self.far = [z, z + 1 - 2 * (z % 2), 2 - z // 2, 3 - 3 * (z // 2)]
        self.ypeer = (self.g, (1 - self.y) * 2 + self.c)
        self.cpeer = (self.g, self.y * 2 + 1 - self.c)
        self.xpeer = (z * 2 + 1 - self.x, self.band)
        self.draining = False

    def line(self, zz):
        return (zz * 2 + self.x, self.band)

    def greet(self, peers):
        bar = pltpu.get_barrier_semaphore()
        for d in peers:
            pl.semaphore_signal(bar, inc=1, device_id=d, device_id_type=MESH)
        pl.semaphore_wait(bar, len(peers))

    def greet_band(self):
        self.greet([self.ypeer, self.cpeer])

    def greet_all(self):
        self.greet([self.xpeer, self.ypeer, self.cpeer] + [self.line(zz) for zz in self.far[1:]])

    def copy(self, src, dst, ssem, rsem, dev):
        return pltpu.make_async_remote_copy(
            src_ref=src, dst_ref=dst, send_sem=ssem, recv_sem=rsem, device_id=dev, device_id_type=MESH
        )

    def send(self, src, dst, ssem, rsem, dev, cond=None):
        d = self.copy(src, dst, ssem, rsem, dev)
        act = d.wait_send if self.draining else d.start
        if cond is None:
            act()
        else:
            pl.when(cond)(act)

    def keep(self, src, dst, sem):
        d = pltpu.make_async_copy(src, dst, sem)
        d.wait() if self.draining else d.start()

    def arrived(self, ref, rsem):
        if not self.draining:
            self.copy(ref, ref, rsem, rsem, self.ypeer).wait_recv()

    def drain(self, steps):
        self.draining = True
        for step in steps:
            step()
        self.draining = False


def span(ref, axis, start, size):
    if axis == 0:
        return ref.at[pl.ds(pl.multiple_of(start, 16), size), :]
    return ref.at[:, pl.ds(pl.multiple_of(start, LANES), size)]


def gather_sems(n):
    s = pltpu.SemaphoreType.DMA
    return [s((n,)), s((n, 4)), s((n, 4)), s((n, 4)), s((n, 4)), s((n, 7)), s((n, 7)), s((n, 14)), s((n, 14)), s((n,))]


def gather_steps(at, cuts, ins, outs, sems):
    n = len(cuts)
    lsem, zs, zr, xs, xr, ys, yr, cs, cr, ds = sems
    ins, outs = ([refs[cut[5]] for cut in cuts] for refs in (ins, outs))
    soon = sum(cut[5] == 0 for cut in cuts)
    x, y, z, c, far = at.x, at.y, at.z, at.c, at.far

    def piece(i, ref, yy, cc):
        axis, half, a, b, base, _ = cuts[i]
        return span(ref, axis, base + cc * half + yy * b, a + b)

    def bpart(i, ref, yy, cc):
        axis, half, a, b, base, _ = cuts[i]
        return span(ref, axis, base + cc * half + yy * (a + b), b)

    def own(i):
        src, dst = piece(i, ins[i], y, c), piece(i, outs[i].at[at.g], y, c)
        at.send(src, dst, zs.at[i, 0], zr.at[i, z], (at.g + 2, at.band), z < 3)
        at.send(src, dst, ds.at[i], zr.at[i, z], (at.g - 2, at.band), z > 0)
        at.send(src, dst, xs.at[i, 0], xr.at[i, 0], at.xpeer)
        if cuts[i][4] == 0 and not (at.draining and cuts[i][5] == 0):
            at.keep(ins[i], outs[i].at[at.g], lsem.at[i])

    def down(i, slot, shard):
        p = bpart(i, outs[i].at[shard], y, c)
        at.send(p, p, ys.at[i, slot], yr.at[i, slot], at.ypeer)
        p = piece(i, outs[i].at[shard], y, c)
        at.send(p, p, cs.at[i, slot], cr.at[i, slot], at.cpeer)

    def zarr(i, t):
        zz = far[t]
        s = zz * 2 + x
        p = piece(i, outs[i].at[s], y, c)
        at.arrived(p, zr.at[i, zz])
        nxt = jnp.where(zz < z, z + 1, z - 1)
        at.send(p, p, zs.at[i, t], zr.at[i, zz], at.line(jnp.clip(nxt, 0, 3)), (nxt >= 0) & (nxt <= 3))
        at.send(p, p, xs.at[i, t], xr.at[i, t], at.xpeer)
        down(i, t - 1, s)

    def xarr(i, t):
        s = far[t] * 2 + 1 - x
        at.arrived(piece(i, outs[i].at[s], y, c), xr.at[i, t])
        down(i, 3 + t, s)

    def yarr(i, slot, s):
        p = bpart(i, outs[i].at[s], 1 - y, c)
        at.arrived(p, yr.at[i, slot])
        at.send(p, p, cs.at[i, 7 + slot], cr.at[i, 7 + slot], at.cpeer)

    slots = [(t - 1, far[t] * 2 + x) for t in (1, 2, 3)]
    slots += [(3 + t, far[t] * 2 + 1 - x) for t in range(4)]
    order = [slots[k] for k in (3, 0, 4, 1, 5, 2, 6)]
    steps = [lambda: own(0)]
    for i in range(n):
        mine = [lambda i=i: zarr(i, 1)]
        if i + 1 < n:
            mine.append(lambda i=i: own(i + 1))
        mine.append(lambda i=i: xarr(i, 0))
        for t in (2, 3):
            mine += [lambda i=i, t=t: zarr(i, t), lambda i=i, t=t: xarr(i, t - 1)]
        mine.append(lambda i=i: xarr(i, 3))
        if i > 0:
            late = [lambda i=i, k=k: yarr(i - 1, *order[k]) for k in range(7)]
            pace, held = 3 if i == soon else 1, list(late)
            merged = []
            while late or mine:
                merged += late[:pace] + mine[:1]
                late, mine = late[pace:], mine[1:]
            mine = merged
        if i == soon:
            first = len(steps) + max(k for k, step in enumerate(mine) if step in held) + 1
        steps += mine
    steps += [lambda k=k: yarr(n - 1, *order[k]) for k in range(7)]

    def last(i):
        for slot, s in slots:
            at.arrived(piece(i, outs[i].at[s], y, 1 - c), cr.at[i, slot])
            at.arrived(bpart(i, outs[i].at[s], 1 - y, 1 - c), cr.at[i, 7 + slot])

    return steps, first, last


def add_into(dst, src):
    def step(r, _):
        rows = pl.ds(pl.multiple_of(r * 16, 16), 16)
        dst[rows, :] = dst[rows, :] + src[rows, :]
        return 0

    lax.fori_loop(0, src.shape[0] // 16, step, 0)


def move_into(dst, src):
    def step(r, _):
        rows = pl.ds(pl.multiple_of(r * 16, 16), 16)
        dst[rows, :] = src[rows, :]
        return 0

    lax.fori_loop(0, src.shape[0] // 16, step, 0)


def scatter_scratch(grads, cuts):
    n = len(cuts)
    s = pltpu.SemaphoreType.DMA

    def buf(lead, k, size):
        rows, cols = grads[cuts[k][5]].shape[-2:]
        shape = (rows, size) if cuts[k][0] == 1 else (size, cols)
        return pltpu.VMEM(lead + shape, jnp.bfloat16)

    out = []
    for lead, pick in (
        ((8,), lambda c: c[1]),
        ((8,), lambda c: c[1]),
        ((8,), lambda c: c[3]),
        ((4,), lambda c: c[2] + c[3]),
        ((5,), lambda c: c[2] + c[3]),
        ((), lambda c: c[2] + c[3]),
    ):
        out += [buf(lead, k, pick(cuts[k])) for k in range(n)]
    out += [s((n, 8))] * 5 + [s((n, 4))] * 2 + [s((n, 3)), s((n, 5))] + [s((n,))] * 5
    return out


def scatter_steps(at, cuts, ins, outs, scratch, lags):
    n = len(cuts)
    own_half, core_buf, y_buf, x_buf, z_buf, fin_buf = (scratch[k * n : (k + 1) * n] for k in range(6))
    ls, cs, cr, ys, yr, xs, xr, zs, zr, fs, fr, es, er, ws = scratch[6 * n :]
    x, y, z, c, far = at.x, at.y, at.z, at.c, at.far
    ins, outs = ([refs[cut[5]] for cut in cuts] for refs in (ins, outs))

    def in_half(i, s, cc):
        axis, half, _, _, base, _ = cuts[i]
        if base is None:
            return ins[i].at[cc, s]
        return span(ins[i].at[s], axis, base + cc * half, half)

    def out_half(i, cc):
        axis, half, _, _, base, _ = cuts[i]
        if base is None:
            return outs[i].at[cc]
        return span(outs[i], axis, base + cc * half, half)

    def piece(i, ref):
        _, _, a, b = cuts[i][:4]
        return span(ref, cuts[i][0], y * b, a + b)

    def bpart(i, ref, yy):
        _, _, a, b = cuts[i][:4]
        return span(ref, cuts[i][0], yy * (a + b), b)

    order = [(t, j) for t in (3, 2, 1, 0) for j in (1, 0)]

    def shard(t, j):
        return far[t] * 2 + (1 - x if j else x)

    def load(i, t, j):
        s, q = shard(t, j), order.index((t, j))
        return pltpu.make_async_copy(in_half(i, s, c), own_half[i].at[s], ls.at[i, q])

    def give(i, t, j):
        s, q = shard(t, j), order.index((t, j))
        src = in_half(i, s, 1 - c)
        at.send(src, core_buf[i].at[s], cs.at[i, q], cr.at[i, s], at.cpeer)
        if not at.draining:
            load(i, t, j).start()

    def to_y(i, t, j):
        s = shard(t, j)
        src = bpart(i, own_half[i].at[s], 1 - y)
        return at.copy(src, y_buf[i].at[s], ys.at[i, order.index((t, j))], yr.at[i, s], at.ypeer)

    def to_fin(i):
        return at.copy(piece(i, own_half[i].at[at.g]), fin_buf[i], fs.at[i], fr.at[i], at.ypeer)

    def cadd(i, t, j):
        s = shard(t, j)
        if at.draining:
            if (t, j) != (0, 0):
                to_y(i, t, j).wait_send()
            return
        load(i, t, j).wait()
        at.arrived(core_buf[i].at[s], cr.at[i, s])
        add_into(own_half[i].at[s], core_buf[i].at[s])
        to_y(i, t, j).start()

    def yadd(i, t, j):
        s = shard(t, j)
        at.arrived(y_buf[i].at[s], yr.at[i, s])
        if not at.draining:
            add_into(bpart(i, own_half[i].at[s], y), y_buf[i].at[s])
        if j:
            at.send(piece(i, own_half[i].at[s]), x_buf[i].at[far[t]], xs.at[i, t], xr.at[i, far[t]], at.xpeer)

    def xadd(i, t):
        if at.draining:
            return
        at.arrived(x_buf[i].at[far[t]], xr.at[i, far[t]])
        add_into(piece(i, own_half[i].at[shard(t, 0)]), x_buf[i].at[far[t]])

    def zadd(i, t):
        zz = far[t]
        p = piece(i, own_half[i].at[shard(t, 0)])

        def join(cond, slot):
            def do():
                at.arrived(z_buf[i].at[slot], zr.at[i, slot])
                add_into(p, z_buf[i].at[slot])

            if not at.draining:
                pl.when(cond)(do)

        if t > 0:
            inc = jnp.where(zz < z, z + 1, z - 1)
            join((inc >= 0) & (inc <= 3), zz)
            nxt = jnp.where(zz < z, z - 1, z + 1)
            slot = jnp.where((zz < z) & (nxt == zz), 4, zz)
            at.send(p, z_buf[i].at[slot], zs.at[i, t - 1], zr.at[i, slot], at.line(nxt))
        else:
            join(z > 0, z)
            join(z < 3, 4)
            if not at.draining:
                to_fin(i).start()

    def fin(i):
        axis, half, a, b, base, _ = cuts[i]
        own = own_half[i].at[at.g]
        if not at.draining:
            at.arrived(fin_buf[i], fr.at[i])
            to_fin(i).wait_send()
            to_y(i, 0, 0).wait_send()
            for yy in (0, 1):

                @pl.when(y == 1 - yy)
                def _():
                    add_into(span(own, axis, b, a), span(fin_buf[i], axis, b if yy == 0 else 0, a))
                    move_into(span(own, axis, yy * (a + b), b), span(fin_buf[i], axis, 0 if yy == 0 else a, b))

        o = out_half(i, c)
        at.send(own, o, es.at[i], er.at[i], at.cpeer)
        at.keep(own, o, ws.at[i])

    seq = [(i, t, j) for i in range(n) for (t, j) in order]
    opening = [functools.partial(give, *p) for p in seq]
    ly, lx, lz, lf = lags
    todo = []
    for q, (i, t, j) in enumerate(seq):
        todo.append((q, 0, functools.partial(cadd, i, t, j)))
        todo.append((q + ly, 1, functools.partial(yadd, i, t, j)))
        if j == 0:
            todo.append((q + ly + lx, 2, functools.partial(xadd, i, t)))
            todo.append((q + ly + lx + lz, 3, functools.partial(zadd, i, t)))
            if t == 0:
                todo.append((q + ly + lx + lz + lf, 4, functools.partial(fin, i)))
    todo.sort(key=lambda p: p[:2])

    def last():
        for i in range(n):
            at.arrived(out_half(i, 1 - c), er.at[i])

    return opening, [f for _, _, f in todo], last


def head_window(h):
    first = jnp.minimum(h * HDIM // LANES, HEADS * HDIM // LANES - 2) * LANES
    lane = lax.broadcasted_iota(jnp.int32, (1, 2 * LANES), 1) + first
    inside = (lane >= h * HDIM) & (lane < h * HDIM + HDIM)
    return pl.ds(pl.multiple_of(first, LANES), 2 * LANES), inside


def dot_t(left, right):
    return lax.dot_general(left, right, (((1,), (1,)), ((), ())), preferred_element_type=jnp.float32)


def first_dot(left, right):
    return lax.dot_general(left, right, (((0,), (0,)), ((), ())), preferred_element_type=jnp.float32)


def pick_dot(values, chosen):
    high = values.astype(jnp.bfloat16)
    low = (values - high.astype(jnp.float32)).astype(jnp.bfloat16)
    return jnp.dot(high, chosen, preferred_element_type=jnp.float32) + jnp.dot(
        low, chosen, preferred_element_type=jnp.float32
    )


def head_pick(width):
    row = lax.broadcasted_iota(jnp.int32, (width, LANES), 0)
    first = lax.broadcasted_iota(jnp.int32, (width, LANES), 1) * HDIM
    return ((row >= first) & (row < first + HDIM)).astype(jnp.float32).astype(jnp.bfloat16)


def head_spread(width):
    lane = lax.broadcasted_iota(jnp.int32, (LANES, width), 1)
    first = lax.broadcasted_iota(jnp.int32, (LANES, width), 0) * HDIM
    return ((lane >= first) & (lane < first + HDIM)).astype(jnp.float32).astype(jnp.bfloat16)


def rope_tables(band, rows, cols, width):
    quarter = HDIM // 4
    shape = (rows * cols, width)
    token = lax.broadcasted_iota(jnp.int32, shape, 0)
    lane = lax.broadcasted_iota(jnp.int32, shape, 1) % HDIM
    power = (lane % quarter).astype(jnp.float32) * (-math.log(10000.0) / quarter)
    by_row = band * rows + (token // cols).astype(jnp.float32)
    index = jnp.where(lane < 2 * quarter, by_row, (token % cols).astype(jnp.float32))
    angle = index * jnp.exp(power)
    sine = jnp.sin(angle)
    low = (lane // quarter) % 2 == 0
    return jnp.cos(angle), jnp.where(low, -sine, 0.0), jnp.where(low, 0.0, sine)


def turn(values, cos, sin_next, sin_prev):
    width = values.shape[-1]
    after = pltpu.roll(values, width - HDIM // 4, 1)
    before = pltpu.roll(values, HDIM // 4, 1)
    return values * cos + after * sin_next + before * sin_prev


def turn_back(values, cos, sin_next, sin_prev):
    width = values.shape[-1]
    after = pltpu.roll(values, width - HDIM // 4, 1)
    before = pltpu.roll(values, HDIM // 4, 1)
    return values * cos - after * sin_next - before * sin_prev


def qkv_back_kernel(
    x_ref, mod_ref, mid_ref, dq_ref, dk_ref, dv_ref, nq_ref, nk_ref, rq_ref, rk_ref, w_ref,
    gains_ref, cos_ref, next_ref, prev_ref,
    dqkv_ref, dx_ref, sums_ref,
):
    width = x_ref.shape[-1]
    tables = (cos_ref[...], next_ref[...], prev_ref[...])
    pick, spread = head_pick(width), head_spread(width)
    ins = ((dq_ref, nq_ref, rq_ref), (dk_ref, nk_ref, rk_ref))
    for part, (d_ref, n_ref, r_ref) in enumerate(ins):
        back = turn_back(d_ref[0].astype(jnp.float32) * HDIM ** (-0.5), *tables)
        unit = n_ref[0]
        sums_ref[0, 2 + part : 3 + part, :] = jnp.sum(back * unit, axis=0, keepdims=True)
        inner = back * gains_ref[part : part + 1, :]
        mean = pick_dot(inner * unit, pick) * (1.0 / HDIM)
        grad = (inner - unit * pick_dot(mean, spread)) * pick_dot(r_ref[0], spread)
        dqkv_ref[0, :, part * width : (part + 1) * width] = grad.astype(jnp.bfloat16)
    dqkv_ref[0, :, 2 * width : 3 * width] = dv_ref[0]
    d_normed = dot_t(dqkv_ref[0], w_ref[...])
    x = x_ref[0].astype(jnp.float32)
    root = lax.rsqrt(jnp.mean(x * x, axis=-1, keepdims=True) + EPS)
    unit = x * root
    sums_ref[0, 0:1, :] = jnp.sum(d_normed, axis=0, keepdims=True)
    sums_ref[0, 1:2, :] = jnp.sum(d_normed * unit, axis=0, keepdims=True)
    inner = d_normed * (1.0 + mod_ref[0, 1:2, :])
    dx_ref[0] = mid_ref[0] + root * (inner - unit * jnp.mean(inner * unit, axis=-1, keepdims=True))


def qkv_backward(x, mod, d_mid, dq, dk, dv, nq, nk, rq, rk, qp_all, gains, tables):
    images, length, width = x.shape
    row = lambda w: pl.BlockSpec((1, length, w), lambda i: (i, 0, 0))
    whole = lambda a: pl.BlockSpec(a.shape, lambda i: (0,) * a.ndim)
    return pl.pallas_call(
        qkv_back_kernel,
        grid=(images,),
        in_specs=[row(width), pl.BlockSpec((1, 6, width), lambda i: (i, 0, 0))]
        + [row(width)] * 6
        + [row(LANES)] * 2
        + [pl.BlockSpec((width, 3 * width), lambda i: (0, 0)), whole(gains)]
        + [whole(t) for t in tables],
        out_shape=[
            jax.ShapeDtypeStruct((images, length, 3 * width), jnp.bfloat16),
            jax.ShapeDtypeStruct((images, length, width), jnp.float32),
            jax.ShapeDtypeStruct((images, 4, width), jnp.float32),
        ],
        out_specs=[row(3 * width), row(width), pl.BlockSpec((1, 4, width), lambda i: (i, 0, 0))],
        compiler_params=pltpu.CompilerParams(vmem_limit_bytes=60 * 2**20),
        name="qkv_backward",
    )(x, mod, d_mid, dq, dk, dv, nq, nk, rq, rk, qp_all, gains, *tables)
def tail_scratch():
    s = pltpu.SemaphoreType.DMA
    wide = SMALL_COLS
    return [
        pltpu.VMEM((SMALL_ROWS, wide), jnp.float32),
        pltpu.VMEM((2, SMALL_ROWS, wide), jnp.float32),
        pltpu.VMEM((8, SMALL_ROWS, wide), jnp.bfloat16),
        pltpu.VMEM((8, GROUPS, 2 * LANES), jnp.float32),
        s((8,)),
        s((8,)),
    ]


def tail_steps(at, ins, outs, scratch):
    part_ref, ada_ref, slope_ref = ins
    all_ref, cond_ref = outs
    acc, inbox, blocks, cond, ss, rs = scratch
    width = HEADS * HDIM
    z = at.z
    line = (at.xpeer, at.line(at.far[1]), at.line((z + 2) % 4))

    def copy(r):
        if r < 2:
            return at.copy(acc, inbox.at[r], ss.at[r], rs.at[r], (at.cpeer, at.ypeer)[r])
        ref, k = (blocks, r - 2) if r < 5 else (cond, r - 5)
        start, size = ((at.g, 1), (2 * z, 2), (4 * (z // 2), 4))[k]
        src = ref.at[pl.ds(start, size)]
        return at.copy(src, src, ss.at[r], rs.at[r], line[k])

    def pack():
        row = lax.broadcasted_iota(jnp.int32, (SMALL_ROWS, 1), 0)
        value = acc[...]
        rest = value - value.astype(jnp.bfloat16).astype(jnp.float32)
        last = rest - rest.astype(jnp.bfloat16).astype(jnp.float32)
        value = jnp.where(row == GAIN_ROW + 1, rest, jnp.where(row == GAIN_ROW + 2, last, value))
        blocks[at.g] = value.astype(jnp.bfloat16)

    def cond_rows():
        flat = blocks[...].reshape(8 * SMALL_ROWS, SMALL_COLS)
        row = lax.broadcasted_iota(jnp.int32, (8 * SMALL_ROWS, 1), 0) % SMALL_ROWS
        silu = jnp.zeros((8 * SMALL_ROWS, ada_ref.shape[0]), jnp.float32)
        for k in range(6):
            product = dot_t(flat[:, :width], ada_ref[:, k * width : (k + 1) * width])
            silu = jnp.where((row % 6 == k) & (row < GAIN_ROW), product, silu)
        by_group = lax.dot_general(
            flat[:, width:].astype(jnp.float32),
            silu,
            (((0,), (0,)), ((), ())),
            precision=lax.Precision.HIGHEST,
            preferred_element_type=jnp.float32,
        )
        cond[at.g] = jnp.zeros((GROUPS, 2 * LANES), jnp.float32)
        cond[at.g, :, : ada_ref.shape[0]] = by_group[:GROUPS] * slope_ref[...]

    def step(r):
        if at.draining:
            return
        if r > 0:
            copy(r - 1).wait()
        if r == 0:
            acc[...] = part_ref[...]
        elif r <= 2:
            acc[...] = acc[...] + inbox[r - 1]
        if r == 2:
            pack()
        if r == 5:
            cond_rows()
        if r < 8:
            copy(r).start()
        else:
            all_ref[...] = blocks[...]
            cond_ref[...] = cond[...]

    return [functools.partial(step, r) for r in range(9)]


SMALL_ROWS, SMALL_COLS, GAIN_ROW = 16, HEADS * HDIM + LANES, 12


def scatter_kernel(n, cuts, lags, *refs):
    at = Place()
    at.greet_all()
    ins, small_in = refs[:n], refs[n : n + 3]
    outs, small_out = refs[n + 3 : 2 * n + 3], refs[2 * n + 3 : 2 * n + 5]
    small = tail_steps(at, small_in, small_out, refs[2 * n + 5 : 2 * n + 11])
    opening, steps, last = scatter_steps(at, cuts, ins, outs, refs[2 * n + 11 :], lags)
    small[0]()
    for step in opening:
        step()
    small = small[1:]
    for k, step in enumerate(steps):
        step()
        if k % 6 == 5 and small:
            small[0]()
            small = small[1:]
    for step in small:
        step()
    last()
    at.drain(opening + steps)


def scatter(grads, cuts, lags, part, w_ada, slope):
    n = len(grads)
    any_ref = pl.BlockSpec(memory_space=pl.ANY)
    vmem = pl.BlockSpec(memory_space=pltpu.VMEM)
    return pl.pallas_call(
        functools.partial(scatter_kernel, n, cuts, lags),
        out_shape=[jax.ShapeDtypeStruct(w.shape[1:], jnp.bfloat16) for w in grads]
        + [
            jax.ShapeDtypeStruct((8, SMALL_ROWS, SMALL_COLS), jnp.bfloat16),
            jax.ShapeDtypeStruct((8, GROUPS, 2 * LANES), jnp.float32),
        ],
        in_specs=[any_ref] * n + [vmem] * 3,
        out_specs=[any_ref] * n + [vmem] * 2,
        scratch_shapes=tail_scratch() + scatter_scratch(grads, cuts),
        compiler_params=pltpu.CompilerParams(
            collective_id=1, has_side_effects=True, vmem_limit_bytes=60 * 2**20
        ),
        name="gradient_scatter",
    )(*grads, part, w_ada, slope)


def forward_kernel(cuts, cols, refs):
    n = len(cuts)
    soon = sum(cut[5] == 0 for cut in cuts)
    at = Place()
    x_ref, part_ref, group_ref, gains_ref, band_ref = refs["in"]
    normed_ref, q_ref, nq_ref, nk_ref, rq_ref, rk_ref, o_ref, inv_ref, mod_ref, *table_refs, kv_out = refs["out"]
    kv, w_buf, pick_ref, spread_ref, mod_buf, mod_in, w_sem, ms, mr, ks, kr, os = refs["scratch"]
    ins, outs = refs["shards"], refs["full"]
    images, length, width = x_ref.shape
    parts = [(i, s) for i in range(images) for s in (0, 1)]
    if n:
        at.greet_all()
        steps, first, last = gather_steps(at, cuts, ins, outs, refs["sems"])
    else:
        at.greet_band()
        steps, first, last = [], 0, None

    mod_buf[...] = part_ref[...]

    def mod_copy(r):
        peer = (at.xpeer, at.line(at.far[1]), at.line((at.z + 2) % 4))[r]
        return at.copy(mod_buf, mod_in.at[r], ms.at[r], mr.at[r], peer)

    def mod_step(r):
        if at.draining:
            return
        if r > 0:
            mod_copy(r - 1).wait()
            mod_buf[...] = mod_buf[...] + mod_in[r - 1]
        if r < 3:
            mod_copy(r).start()

    def rows(s, i, band):
        return kv.at[s, i, pl.ds(pl.multiple_of(band * length, 16), length), :]

    here, over = at.band, (1 - at.y) * 2 + at.c
    beside, across = at.y * 2 + 1 - at.c, (1 - at.y) * 2 + 1 - at.c

    def give(i, s):
        p = rows(s, i, here)
        at.send(p, p, ks.at[i, s, 0], kr.at[i, s, 0], at.ypeer)
        at.send(p, p, ks.at[i, s, 1], kr.at[i, s, 1], at.cpeer)

    def pass_on(i, s):
        p = rows(s, i, over)
        at.arrived(p, kr.at[i, s, 0])
        at.send(p, p, ks.at[i, s, 2], kr.at[i, s, 2], at.cpeer)

    def ready(i):
        for s in (0, 1):
            at.arrived(rows(s, i, beside), kr.at[i, s, 1])
            at.arrived(rows(s, i, across), kr.at[i, s, 2])
            at.keep(kv.at[s, i], kv_out.at[s, i], os.at[i, s])

    def norm(i):
        value = x_ref[i].astype(jnp.float32)
        root = lax.rsqrt(jnp.mean(value * value, axis=-1, keepdims=True) + EPS)
        chosen = jnp.sum(group_ref[:, i : i + 1] * mod_buf[...], axis=0, keepdims=True)
        mod_ref[i : i + 1, :] = chosen
        shift, scale = chosen[:, :width], chosen[:, width : 2 * width]
        normed_ref[i] = (value * root * (1.0 + scale) + shift).astype(jnp.bfloat16)

    def raw(i, part):
        return jnp.dot(
            normed_ref[i], w_buf[:, part * width : (part + 1) * width], preferred_element_type=jnp.float32
        )

    def project(i, part, n_ref, r_ref):
        values = raw(i, part)
        inv = lax.rsqrt(pick_dot(values * values, pick_ref[...]) * (1.0 / HDIM) + EPS)
        r_ref[i] = inv
        unit = values * pick_dot(inv, spread_ref[...])
        n_ref[i] = unit
        scaled = unit * gains_ref[part : part + 1, :]
        return turn(scaled, *(t[...] for t in table_refs)).astype(jnp.bfloat16)

    def key_part(i):
        norm(i)
        kv[0, i, pl.ds(pl.multiple_of(here * length, 16), length), :] = project(i, 1, nk_ref, rk_ref)
        give(i, 0)

    def value_part(i):
        kv[1, i, pl.ds(pl.multiple_of(here * length, 16), length), :] = raw(i, 2).astype(jnp.bfloat16)
        give(i, 1)

    def query_part(i):
        q_ref[i] = project(i, 0, nq_ref, rq_ref)

    def head(i, h):
        win, inside = head_window(h)
        query = q_ref[i, :, win]
        query = jnp.where(inside, query, jnp.zeros_like(query))
        power = jnp.exp2(dot_t(query, kv[0, i, :, win]) * (HDIM ** (-0.5) * LOG2E))
        inv = 1.0 / jnp.sum(power, axis=-1, keepdims=True)
        out = jnp.dot(
            (power * inv).astype(jnp.bfloat16), kv[1, i, :, win], preferred_element_type=jnp.float32
        )
        o_ref[i, :, win] = jnp.where(inside, out.astype(jnp.bfloat16), o_ref[i, :, win])
        lane = lax.broadcasted_iota(jnp.int32, (1, LANES), 1)
        inv_ref[i] = jnp.where(lane == h, inv, inv_ref[i])

    def prepare():
        pick_ref[...] = head_pick(width)
        spread_ref[...] = head_spread(width)

        def block(r, _):
            rows_of = pl.ds(pl.multiple_of(r * cols, cols), cols)
            row = band_ref[0:1, 0:1] * (length // cols) + r.astype(jnp.float32)
            for ref, value in zip(table_refs, rope_tables(row, 1, cols, width)):
                ref[rows_of, :] = value
            return 0

        lax.fori_loop(0, length // cols, block, 0)

    if not n:
        prepare()
    if n:
        for k in range(3):
            mod_step(k)
            for step in steps[2 * k : 2 * k + 2]:
                step()
                if k == 0 and step is steps[0]:
                    prepare()
        mod_step(3)
        for step in steps[6:first]:
            step()
        for i in range(soon):
            last(i)
        pltpu.make_async_copy(ins[0], outs[0].at[at.g], refs["sems"][0].at[0]).wait()
        loads = [
            pltpu.make_async_copy(
                outs[0].at[k, :, pl.ds(0, 3 * width)],
                w_buf.at[pl.ds(k * (width // 8), width // 8), :],
                w_sem.at[k],
            )
            for k in range(8)
        ]
    else:
        loads = [pltpu.make_async_copy(ins[0].at[:, pl.ds(0, 3 * width)], w_buf, w_sem.at[0])]
    for d in loads:
        d.start()
    o_ref[...] = jnp.zeros_like(o_ref)
    inv_ref[...] = jnp.zeros_like(inv_ref)
    for d in loads:
        d.wait()
    todo = steps[first:]
    for i in range(images):
        for work in (key_part, value_part):
            work(i)
            for step in todo[:2]:
                step()
            todo = todo[2:]
    for i in range(images):
        query_part(i)
        for step in todo[:2]:
            step()
        todo = todo[2:]
    for i in range(images):
        pass_on(i, 0)
        pass_on(i, 1)
        ready(i)
        mine, todo = (todo[: HEADS // 2], todo[HEADS // 2 :])

        def body(h, _, i=i, mine=mine):
            for k, step in enumerate(mine):
                pl.when(h == 2 * k)(step)
            head(i, h)
            return 0

        lax.fori_loop(0, HEADS, body, 0)
    for step in todo:
        step()
    for i in range(soon, n):
        last(i)
    at.drain(steps)
    for i, s in parts:
        at.drain([functools.partial(give, i, s), functools.partial(pass_on, i, s)])
    for i in range(images):
        at.drain([functools.partial(ready, i)])


def forward(x, mod_part, groups, gains, band, cols, shards, cuts):
    n = len(cuts)
    images, length, width = x.shape
    bands = lax.axis_size("band")
    keys = (2, images, bands * length, width)
    s = pltpu.SemaphoreType.DMA
    bf = jnp.bfloat16
    any_ref = pl.BlockSpec(memory_space=pl.ANY)
    vmem = pl.BlockSpec(memory_space=pltpu.VMEM)
    args = [x, mod_part, groups, gains, band]
    rows = lambda w, d: jax.ShapeDtypeStruct((images, length, w), d)
    outs = [rows(width, bf)] * 2 + [rows(width, jnp.float32)] * 2 + [rows(LANES, jnp.float32)] * 2
    outs += [rows(width, bf), rows(LANES, jnp.float32), jax.ShapeDtypeStruct((images, mod_part.shape[1]), jnp.float32)]
    outs += [jax.ShapeDtypeStruct((length, width), jnp.float32)] * 3
    scratch = [
        pltpu.VMEM(keys, bf),
        pltpu.VMEM((width, 3 * width), bf),
        pltpu.VMEM((width, LANES), bf),
        pltpu.VMEM((LANES, width), bf),
        pltpu.VMEM(mod_part.shape, jnp.float32),
        pltpu.VMEM((3,) + mod_part.shape, jnp.float32),
        s((8,)),
        s((3,)),
        s((3,)),
        s((images, 2, 3)),
        s((images, 2, 3)),
        s((images, 2)),
    ]
    whole = len(shards) if n else 0
    sizes = [len(args), len(shards), len(outs) + 1, whole, len(scratch), 10 if n else 0]

    def kernel(*refs):
        groups_of, start = [], 0
        for size in sizes:
            groups_of.append(refs[start : start + size])
            start += size
        names = ("in", "shards", "out", "full", "scratch", "sems")
        forward_kernel(cuts, cols, dict(zip(names, groups_of)))

    return pl.pallas_call(
        kernel,
        out_shape=outs
        + [jax.ShapeDtypeStruct(keys, bf)]
        + [jax.ShapeDtypeStruct((8,) + w.shape, w.dtype) for w in shards[:whole]],
        in_specs=[vmem] * len(args) + [any_ref] * len(shards),
        out_specs=[vmem] * len(outs) + [any_ref] * (1 + whole),
        scratch_shapes=scratch + (gather_sems(n) if n else []),
        compiler_params=pltpu.CompilerParams(
            collective_id=2, has_side_effects=True, vmem_limit_bytes=60 * 2**20
        ),
        name="forward",
    )(*args, *shards)


EACH = 9


def attention_back_kernel(n, cuts, lags, q_ref, do_ref, inv_ref, kv_ref, *refs):
    ins, (dq_ref, d_out), outs = refs[:n], refs[n : n + 2], refs[n + 2 : 2 * n + 2]
    kv, dkv, core_buf, y_buf, load_sem, ks, kr, ys, yr, ws = refs[2 * n + 2 : 2 * n + 12]
    images, length, width = q_ref.shape
    at = Place()
    loads = [pltpu.make_async_copy(kv_ref.at[:, i], kv.at[i], load_sem.at[i]) for i in range(images)]
    for d in loads:
        d.start()
    at.greet_all() if n else at.greet_band()
    opening, todo, last = [], [], lambda: None
    if n:
        opening, todo, last = scatter_steps(at, cuts, ins, outs, refs[2 * n + 12 :], lags)
    for step in opening:
        step()
    steps = opening + todo

    def rows(s, i, band):
        return dkv.at[s, i, pl.ds(pl.multiple_of(band * length, 16), length), :]

    def to_core(i):
        for s in (0, 1):
            for yy in (0, 1):
                at.send(rows(s, i, yy * 2 + 1 - at.c), core_buf.at[i, s, yy], ks.at[i, s, yy], kr.at[i, s, yy], at.cpeer)

    def core_add(i):
        for s in (0, 1):
            p = rows(s, i, (1 - at.y) * 2 + at.c)
            at.arrived(core_buf.at[i, s, 1 - at.y], kr.at[i, s, 1 - at.y])
            if not at.draining:
                add_into(p, core_buf.at[i, s, 1 - at.y])
            at.send(p, y_buf.at[i, s], ys.at[i, s], yr.at[i, s], at.ypeer)
        for s in (0, 1):
            at.arrived(core_buf.at[i, s, at.y], kr.at[i, s, at.y])
            if not at.draining:
                add_into(rows(s, i, at.band), core_buf.at[i, s, at.y])

    def y_add(i):
        for s in (0, 1):
            p = rows(s, i, at.band)
            at.arrived(y_buf.at[i, s], yr.at[i, s])
            if not at.draining:
                add_into(p, y_buf.at[i, s])
            at.keep(p, d_out.at[s, i], ws.at[i, s])

    def head(i, h):
        win, inside = head_window(h)
        query, grad = q_ref[i, :, win], do_ref[i, :, win]
        query = jnp.where(inside, query, jnp.zeros_like(query))
        grad = jnp.where(inside, grad, jnp.zeros_like(grad))
        keys, values = kv[i, 0, :, win], kv[i, 1, :, win]
        inv = inv_ref[i, pl.ds(h, 1), :]
        probs = jnp.exp2(dot_t(keys, query) * (HDIM ** (-0.5) * LOG2E)) * inv
        d_probs = dot_t(values, grad)
        delta = jnp.sum(probs * d_probs, axis=0, keepdims=True)
        d_scores = (probs * (d_probs - delta)).astype(jnp.bfloat16)
        d_key = jnp.dot(d_scores, query, preferred_element_type=jnp.float32).astype(jnp.bfloat16)
        d_value = jnp.dot(
            probs.astype(jnp.bfloat16), grad, preferred_element_type=jnp.float32
        ).astype(jnp.bfloat16)
        dkv[0, i, :, win] = jnp.where(inside, d_key, dkv[0, i, :, win])
        dkv[1, i, :, win] = jnp.where(inside, d_value, dkv[1, i, :, win])
        dq_ref[i, :, win] = jnp.where(inside, first_dot(d_scores, keys), dq_ref[i, :, win])

    dq_ref[...] = jnp.zeros_like(dq_ref)
    for s in (0, 1):
        for i in range(images):

            def clear(r, _, s=s, i=i):
                dkv[s, i, pl.ds(pl.multiple_of(r * 16, 16), 16), :] = jnp.zeros((16, width), jnp.bfloat16)
                return 0

            lax.fori_loop(0, kv.shape[2] // 16, clear, 0)
    exchange = []
    for i in range(images):
        loads[i].wait()
        mine, todo = (todo[:EACH], todo[EACH:])
        due = exchange
        exchange = [functools.partial(f, i) for f in (core_add, y_add)]

        def body(h, _, i=i, mine=mine, due=due):
            for k, step in enumerate(due):
                pl.when(h == 1 + 12 * k)(step)
            for k, step in enumerate(mine):
                pl.when(h == k * HEADS // EACH)(step)
            head(i, h)
            return 0

        lax.fori_loop(0, HEADS, body, 0, unroll=2)
        to_core(i)
        steps += [functools.partial(to_core, i)] + exchange
    exchange[0]()
    part = min(6, len(todo))
    for step in todo[:part] + [exchange[1]] + todo[part:]:
        step()
    last()
    at.drain(steps)


def attention_backward(q, d_att, inv_rows, kv_all, grads, cuts, lags):
    n = len(grads)
    images, length, width = q.shape
    s = pltpu.SemaphoreType.DMA
    any_ref = pl.BlockSpec(memory_space=pl.ANY)
    vmem = pl.BlockSpec(memory_space=pltpu.VMEM)
    bf = jnp.bfloat16
    return pl.pallas_call(
        functools.partial(attention_back_kernel, n, cuts, lags),
        out_shape=[
            jax.ShapeDtypeStruct(q.shape, jnp.float32),
            jax.ShapeDtypeStruct((2, images, length, width), bf),
        ]
        + [jax.ShapeDtypeStruct(w.shape[:-3] + w.shape[-2:], bf) for w in grads],
        in_specs=[vmem, vmem, vmem, any_ref] + [any_ref] * n,
        out_specs=[vmem, any_ref] + [any_ref] * n,
        scratch_shapes=[
            pltpu.VMEM((images, 2) + kv_all.shape[2:], bf),
            pltpu.VMEM(kv_all.shape, bf),
            pltpu.VMEM((images, 2, 2, length, width), bf),
            pltpu.VMEM((images, 2, length, width), bf),
            s((images,)),
            s((images, 2, 2)),
            s((images, 2, 2)),
            s((images, 2)),
            s((images, 2)),
            s((images, 2)),
        ]
        + (scatter_scratch(grads, cuts) if n else []),
        compiler_params=pltpu.CompilerParams(
            collective_id=3, has_side_effects=True, vmem_limit_bytes=63 * 2**20
        ),
        name="attention_backward",
    )(q, d_att, inv_rows, kv_all, *grads)
def mlp_kernel(
    x_ref, gout_ref, att_ref, mod_ref, live_ref, proj_ref, gate_ref, up_ref, down_ref,
    out_ref, dmid_ref, dproj_ref, datt_ref, sums_ref, dgu_ref, ddown_ref,
    mid, proj, mlp, dnorm, normed, normed_t, dmlp,
):
    step, steps = pl.program_id(0), pl.num_programs(0)
    images, length, width = x_ref.shape

    def piece(i, k):
        return mod_ref[i : i + 1, k * width : (k + 1) * width]

    def rows(i):
        return pl.ds(i * length, length)

    def live(i):
        return live_ref[i : i + 1, 0:1]

    def unit(i):
        value = mid[rows(i), :]
        root = lax.rsqrt(jnp.mean(value * value, axis=-1, keepdims=True) + EPS)
        return value * root, root

    @pl.when(step == 0)
    def _():
        for i in range(images):
            proj[rows(i), :] = jnp.dot(att_ref[i], proj_ref[...], preferred_element_type=jnp.float32)
            mid[rows(i), :] = x_ref[i].astype(jnp.float32) + piece(i, 2) * proj[rows(i), :]
            value = (unit(i)[0] * (1.0 + piece(i, 4)) + piece(i, 3)).astype(jnp.bfloat16)
            normed[rows(i), :] = value
            normed_t[:, rows(i)] = value.T
            dmlp[rows(i), :] = (piece(i, 5) * (gout_ref[i].astype(jnp.float32) * live(i))).astype(jnp.bfloat16)
        mlp[...] = jnp.zeros_like(mlp)
        dnorm[...] = jnp.zeros_like(dnorm)

    gate = jnp.dot(normed[...], gate_ref[...], preferred_element_type=jnp.float32)
    up = jnp.dot(normed[...], up_ref[...], preferred_element_type=jnp.float32)
    dhidden = dot_t(dmlp[...], down_ref[...])
    sigmoid = 1.0 / (1.0 + jnp.exp(-gate))
    silu = gate * sigmoid
    hidden = (silu * up).astype(jnp.bfloat16)
    dgate = (dhidden * up * (sigmoid * (1.0 + gate * (1.0 - sigmoid)))).astype(jnp.bfloat16)
    dup = (dhidden * silu).astype(jnp.bfloat16)
    mlp[...] += jnp.dot(hidden, down_ref[...], preferred_element_type=jnp.float32)
    dnorm[...] += dot_t(dgate, gate_ref[...]) + dot_t(dup, up_ref[...])
    ddown_ref[...] = first_dot(hidden, dmlp[...]).astype(jnp.bfloat16)
    dgu_ref[0] = jnp.dot(normed_t[...], dgate, preferred_element_type=jnp.float32).astype(jnp.bfloat16)
    dgu_ref[1] = jnp.dot(normed_t[...], dup, preferred_element_type=jnp.float32).astype(jnp.bfloat16)

    @pl.when(step == steps - 1)
    def _():
        total = lambda v: jnp.sum(v, axis=0, keepdims=True)
        for i in range(images):
            gy = gout_ref[i].astype(jnp.float32) * live(i)
            value = mlp[rows(i), :]
            out_ref[i] = ((mid[rows(i), :] + piece(i, 5) * value) * live(i)).astype(jnp.bfloat16)
            sums_ref[i, 3:4, :] = total(gy * value)
            n, root = unit(i)
            dn = dnorm[rows(i), :]
            sums_ref[i, 1:2, :] = total(dn)
            sums_ref[i, 2:3, :] = total(dn * n)
            e = dn * (1.0 + piece(i, 4))
            d_mid = gy + root * (e - n * jnp.mean(e * n, axis=-1, keepdims=True))
            dmid_ref[i] = d_mid
            sums_ref[i, 0:1, :] = total(d_mid * proj[rows(i), :])
            d_proj = (piece(i, 2) * d_mid).astype(jnp.bfloat16)
            dproj_ref[i] = d_proj
            datt_ref[i] = dot_t(d_proj, proj_ref[...]).astype(jnp.bfloat16)


def mlp_block(x, grad_out, attended, mod, live, qp_all, gu_all, down_all):
    images, length, width = x.shape
    ff = down_all.shape[0]
    chunk = 512 if ff % 512 == 0 else LANES
    steps = ff // chunk
    bf = jnp.bfloat16
    whole = lambda s: pl.BlockSpec(s, lambda k: (0,) * len(s))
    rows = lambda d: jax.ShapeDtypeStruct(x.shape, d)
    tokens = images * length
    return pl.pallas_call(
        mlp_kernel,
        grid=(steps,),
        in_specs=[whole(x.shape)] * 3
        + [whole(mod.shape), whole(live.shape), pl.BlockSpec((width, width), lambda k: (0, 3))]
        + [
            pl.BlockSpec((width, chunk), lambda k: (0, k)),
            pl.BlockSpec((width, chunk), lambda k: (0, steps + k)),
            pl.BlockSpec((chunk, width), lambda k: (k, 0)),
        ],
        out_shape=[rows(bf), rows(jnp.float32), rows(bf), rows(bf)]
        + [
            jax.ShapeDtypeStruct((images, 4, width), jnp.float32),
            jax.ShapeDtypeStruct((2, width, ff), bf),
            jax.ShapeDtypeStruct((ff, width), bf),
        ],
        out_specs=[whole(x.shape)] * 4
        + [
            whole((images, 4, width)),
            pl.BlockSpec((2, width, chunk), lambda k: (0, 0, k)),
            pl.BlockSpec((chunk, width), lambda k: (k, 0)),
        ],
        scratch_shapes=[pltpu.VMEM((tokens, width), jnp.float32)] * 4
        + [pltpu.VMEM((tokens, width), bf), pltpu.VMEM((width, tokens), bf), pltpu.VMEM((tokens, width), bf)],
        compiler_params=pltpu.CompilerParams(vmem_limit_bytes=60 * 2**20),
        name="mlp_block",
    )(x, grad_out, attended, mod, live, qp_all, gu_all, gu_all, down_all)


def half_cuts(ref, axis, base, size, own_parts, shared_parts):
    unit = size // 2 // (own_parts + 2 * shared_parts)
    return (axis, size // 2, own_parts * unit, shared_parts * unit, base, ref)


def by_shard(grad):
    parts = lax.axis_size("grp")
    return grad.reshape(parts, grad.shape[0] // parts, grad.shape[1])


def body(
    patches,
    grad_out,
    cond_table,
    group_ids,
    live_count,
    band_order,
    w_ada,
    b_ada,
    w_qkv,
    q_gain,
    k_gain,
    w_proj,
    w_gate,
    w_up,
    w_down,
):
    images, rows, cols, width = patches.shape
    length = rows * cols
    ff = w_gate.shape[1]
    bf = jnp.bfloat16
    grp = lax.axis_index("grp")
    ada_rows, ada_cols, bias_cols = w_ada.shape[0], w_ada.shape[1], b_ada.shape[0]
    fits = (
        lax.axis_size("grp") == 8
        and images == 2
        and width == HEADS * HDIM
        and w_qkv.shape[0] % 16 == 0
        and 4 * width % 4608 == 0
        and 2 * ff % 3072 == 0
        and w_down.shape[0] % 384 == 0
    )
    w_qp = jnp.concatenate([w_qkv, w_proj], axis=1)
    w_gu = jnp.concatenate([w_gate, w_up], axis=1)
    full = lambda w: w.reshape(-1, w.shape[-1])
    onehot = (group_ids[:, None] == jnp.arange(GROUPS, dtype=jnp.int32)[None, :]).astype(jnp.float32)
    cond_rows = lax.dynamic_slice_in_dim(cond_table, grp * ada_rows, ada_rows, axis=1)
    sigmoid = jax.nn.sigmoid(cond_rows)
    silu_rows = (cond_rows * sigmoid).astype(bf)
    silu_slope = sigmoid * (1.0 + cond_rows * (1.0 - sigmoid))
    mod_part = jnp.dot(silu_rows, w_ada, preferred_element_type=jnp.float32)
    bias_part = lax.dynamic_update_slice_in_dim(
        jnp.zeros((ada_cols,), jnp.float32), b_ada.astype(jnp.float32), grp * bias_cols, axis=0
    )
    mod_part = mod_part + bias_part[None, :]
    live_mask = (jnp.arange(images, dtype=jnp.int32) < live_count[0]).astype(jnp.float32)

    gains = jnp.stack([jnp.tile(q_gain, HEADS), jnp.tile(k_gain, HEADS)])
    x = patches.reshape(images, length, width)
    groups = jnp.pad(onehot.T, ((0, 0), (0, LANES - images)))
    band = jnp.broadcast_to(band_order.astype(jnp.float32)[:, None], (1, LANES))
    common = (groups, gains, band, cols)
    if fits:
        shards = [w_qp, w_gu, w_down]
        cuts = [half_cuts(0, 1, 0, 4 * width, 1, 1), half_cuts(1, 1, 0, 2 * ff, 4, 1)]
        cuts += [half_cuts(2, 0, 0, w_down.shape[0], 4, 1)]
    else:
        qp_all, gu_all, down_all = (lax.all_gather(w, "grp", axis=0, tiled=True) for w in (w_qp, w_gu, w_down))
        mod_part = lax.psum(mod_part, "grp")
        shards, cuts = [qp_all], []
    outs = forward(x, mod_part, *common, shards, cuts)
    normed_one, query, nq, nk, rq, rk, attended, inv, mod = outs[:9]
    tables, kv_all, rest = outs[9:12], outs[12], outs[13:]
    if fits:
        qp_all, gu_all, down_all = (full(w) for w in rest)
    live = jnp.broadcast_to(live_mask[:, None], (images, LANES))
    flat = lambda a: a.reshape(images * length, a.shape[-1])
    patches_out, d_middle, d_proj, d_attended, mid_sums, d_w_gu, d_w_down = mlp_block(
        x, grad_out.reshape(images, length, width), attended, mod, live, qp_all, gu_all, down_all
    )
    patches_out = patches_out.reshape(images, rows, cols, width)
    mod = mod.reshape(images, 6, width)
    d_w_proj = jnp.einsum("td,te->de", flat(attended), flat(d_proj), preferred_element_type=jnp.float32).astype(bf)
    d_query, d_kv, *rest = attention_backward(
        query,
        d_attended,
        jnp.swapaxes(inv, 1, 2),
        kv_all,
        [d_w_gu.reshape(2, -1, w_gate.shape[0], ff)] if fits else [],
        [half_cuts(0, 1, None, 2 * ff, 4, 1)] if fits else [],
        (2, 2, 1, 2),
    )
    d_qkv, d_x, sums = qkv_backward(
        x, mod, d_middle, d_query, d_kv[0], d_kv[1], nq, nk, rq, rk, qp_all, gains, tables
    )
    d_patches = d_x.reshape(images, rows, cols, width)
    d_w_qkv = jnp.einsum("td,te->de", flat(normed_one), flat(d_qkv), preferred_element_type=jnp.float32).astype(bf)
    d_w_qp = jnp.concatenate([d_w_qkv, d_w_proj], axis=1)

    d_mod_part = jnp.concatenate([sums[:, 0:2], mid_sums], axis=1)
    gain_part = jnp.sum(sums[:, 2:4].reshape(images, 2, HEADS, HDIM), axis=(0, 2))
    if fits:
        tags = jnp.pad(jnp.repeat(onehot * (1.0 / lax.axis_size("band")), 6, axis=0), ((0, 0), (0, LANES - GROUPS)))
        small = jnp.concatenate([d_mod_part.reshape(images * 6, width), tags], axis=1)
        gain_row = jnp.pad(gain_part.reshape(1, -1), ((0, 0), (0, SMALL_COLS - 2 * HDIM)))
        small = jnp.concatenate([small, gain_row, gain_row, gain_row, jnp.zeros_like(gain_row)])
        cuts = [half_cuts(0, 0, 0, w_down.shape[0], 2, 1), half_cuts(1, 1, 0, 4 * width, 8, 5)]
        d_gu = rest[0]
        d_down, d_qp, gathered, cond_blocks = scatter(
            [by_shard(d_w_down), by_shard(d_w_qp)], cuts, (2, 1, 0, 2), small, w_ada, silu_slope
        )
        d_mod_all = gathered[:, :GAIN_ROW, :width].reshape(-1, ada_cols)
        onehot_all = gathered[:, 0:GAIN_ROW:6, width : width + GROUPS].reshape(-1, GROUPS)
        gain_all = gathered[:, GAIN_ROW : GAIN_ROW + 3, : 2 * HDIM].astype(jnp.float32)
        gain_all = jnp.sum(gain_all, axis=(0, 1)).reshape(2, HDIM)
        d_cond = jnp.swapaxes(cond_blocks[:, :, :ada_rows], 0, 1).reshape(GROUPS, -1)
    else:
        d_gu, d_down, d_qp = (
            lax.psum(lax.psum_scatter(w, "grp", scatter_dimension=w.ndim - 2, tiled=True), "band")
            for w in (d_w_gu, d_w_down, d_w_qp)
        )
        d_modulation = lax.psum(d_mod_part.reshape(images, ada_cols), "band").astype(bf)
        gain_all = lax.psum(gain_part, ("grp", "band"))
        payload = jnp.concatenate([d_modulation, onehot.astype(bf)], axis=1)
        payload = lax.all_gather(payload, "grp", axis=0, tiled=True)
        d_mod_all, onehot_all = payload[:, :ada_cols], payload[:, ada_cols:]
        d_silu = jnp.einsum("be,de->bd", d_mod_all, w_ada, preferred_element_type=jnp.float32)
        d_silu = jnp.dot(
            onehot_all.astype(jnp.float32).T,
            d_silu,
            precision=lax.Precision.HIGHEST,
            preferred_element_type=jnp.float32,
        )
        d_cond = lax.all_gather(d_silu * silu_slope, "grp", axis=1, tiled=True)
    silu_all = jnp.dot(onehot_all, silu_rows, preferred_element_type=jnp.float32).astype(bf)
    d_w_ada = jnp.einsum("bd,be->de", silu_all, d_mod_all, preferred_element_type=jnp.float32)
    d_b_ada = lax.dynamic_slice_in_dim(
        jnp.sum(d_mod_all.astype(jnp.float32), axis=0), grp * bias_cols, bias_cols, axis=0
    )
    wide = lambda a: a.astype(jnp.float32)
    return (
        patches_out,
        d_patches,
        d_cond,
        d_w_ada,
        d_b_ada,
        wide(d_qp[:, : 3 * width]),
        gain_all[0],
        gain_all[1],
        wide(d_qp[:, 3 * width :]),
        wide(d_gu[0]),
        wide(d_gu[1]),
        wide(d_down),
    )


def solution(mesh):
    in_specs = (
        P("grp", "band", None, None),
        P("grp", "band", None, None),
        P(),
        P("grp"),
        P("grp"),
        P("band"),
        P("grp", None),
        P("grp"),
        P("grp", None),
        P(),
        P(),
        P("grp", None),
        P("grp", None),
        P("grp", None),
        P("grp", None),
    )
    out_specs = (
        P("grp", "band", None, None),
        P("grp", "band", None, None),
        P(),
        P("grp", None),
        P("grp"),
        P("grp", None),
        P(),
        P(),
        P("grp", None),
        P("grp", None),
        P("grp", None),
        P("grp", None),
    )
    return jax.shard_map(body, mesh=mesh, in_specs=in_specs, out_specs=out_specs, check_vma=False)
```

```python
import functools
import math

import jax
import jax.numpy as jnp
from jax import lax
from jax.experimental import pallas as pl
from jax.experimental.pallas import tpu as pltpu
from jax.sharding import PartitionSpec as P

HEADS = 16
HDIM = 72
GROUPS = 8
LANES = 128
EPS = 1e-06
LOG2E = 1.4426950408889634

MESH = pl.DeviceIdType.MESH


class Place:
    def __init__(self):
        self.g, self.band = lax.axis_index("grp"), lax.axis_index("band")
        self.z, self.x = self.g // 2, self.g % 2
        self.y, self.c = self.band // 2, self.band % 2
        z = self.z
        self.far = [z, z + 1 - 2 * (z % 2), 2 - z // 2, 3 - 3 * (z // 2)]
        self.ypeer = (self.g, (1 - self.y) * 2 + self.c)
        self.cpeer = (self.g, self.y * 2 + 1 - self.c)
        self.xpeer = (z * 2 + 1 - self.x, self.band)
        self.draining = False

    def line(self, zz):
        return (zz * 2 + self.x, self.band)

    def greet(self, peers):
        bar = pltpu.get_barrier_semaphore()
        for d in peers:
            pl.semaphore_signal(bar, inc=1, device_id=d, device_id_type=MESH)
        pl.semaphore_wait(bar, len(peers))

    def greet_band(self):
        self.greet([self.ypeer, self.cpeer])

    def greet_all(self):
        self.greet([self.xpeer, self.ypeer, self.cpeer] + [self.line(zz) for zz in self.far[1:]])

    def copy(self, src, dst, ssem, rsem, dev):
        return pltpu.make_async_remote_copy(
            src_ref=src, dst_ref=dst, send_sem=ssem, recv_sem=rsem, device_id=dev, device_id_type=MESH
        )

    def send(self, src, dst, ssem, rsem, dev, cond=None):
        d = self.copy(src, dst, ssem, rsem, dev)
        act = d.wait_send if self.draining else d.start
        if cond is None:
            act()
        else:
            pl.when(cond)(act)

    def keep(self, src, dst, sem):
        d = pltpu.make_async_copy(src, dst, sem)
        d.wait() if self.draining else d.start()

    def arrived(self, ref, rsem):
        if not self.draining:
            self.copy(ref, ref, rsem, rsem, self.ypeer).wait_recv()

    def drain(self, steps):
        self.draining = True
        for step in steps:
            step()
        self.draining = False


def span(ref, axis, start, size):
    if axis == 0:
        return ref.at[pl.ds(pl.multiple_of(start, 16), size), :]
    return ref.at[:, pl.ds(pl.multiple_of(start, LANES), size)]


def gather_sems(n):
    s = pltpu.SemaphoreType.DMA
    return [s((n,)), s((n, 4)), s((n, 4)), s((n, 4)), s((n, 4)), s((n, 7)), s((n, 7)), s((n, 14)), s((n, 14)), s((n,))]


def gather_steps(at, cuts, ins, outs, sems):
    n = len(cuts)
    lsem, zs, zr, xs, xr, ys, yr, cs, cr, ds = sems
    ins, outs = ([refs[cut[5]] for cut in cuts] for refs in (ins, outs))
    soon = sum(cut[5] == 0 for cut in cuts)
    x, y, z, c, far = at.x, at.y, at.z, at.c, at.far

    def piece(i, ref, yy, cc):
        axis, half, a, b, base, _ = cuts[i]
        return span(ref, axis, base + cc * half + yy * b, a + b)

    def bpart(i, ref, yy, cc):
        axis, half, a, b, base, _ = cuts[i]
        return span(ref, axis, base + cc * half + yy * (a + b), b)

    def own(i):
        src, dst = piece(i, ins[i], y, c), piece(i, outs[i].at[at.g], y, c)
        at.send(src, dst, zs.at[i, 0], zr.at[i, z], (at.g + 2, at.band), z < 3)
        at.send(src, dst, ds.at[i], zr.at[i, z], (at.g - 2, at.band), z > 0)
        at.send(src, dst, xs.at[i, 0], xr.at[i, 0], at.xpeer)
        if cuts[i][4] == 0 and not (at.draining and cuts[i][5] == 0):
            at.keep(ins[i], outs[i].at[at.g], lsem.at[i])

    def down(i, slot, shard):
        p = bpart(i, outs[i].at[shard], y, c)
        at.send(p, p, ys.at[i, slot], yr.at[i, slot], at.ypeer)
        p = piece(i, outs[i].at[shard], y, c)
        at.send(p, p, cs.at[i, slot], cr.at[i, slot], at.cpeer)

    def zarr(i, t):
        zz = far[t]
        s = zz * 2 + x
        p = piece(i, outs[i].at[s], y, c)
        at.arrived(p, zr.at[i, zz])
        nxt = jnp.where(zz < z, z + 1, z - 1)
        at.send(p, p, zs.at[i, t], zr.at[i, zz], at.line(jnp.clip(nxt, 0, 3)), (nxt >= 0) & (nxt <= 3))
        at.send(p, p, xs.at[i, t], xr.at[i, t], at.xpeer)
        down(i, t - 1, s)

    def xarr(i, t):
        s = far[t] * 2 + 1 - x
        at.arrived(piece(i, outs[i].at[s], y, c), xr.at[i, t])
        down(i, 3 + t, s)

    def yarr(i, slot, s):
        p = bpart(i, outs[i].at[s], 1 - y, c)
        at.arrived(p, yr.at[i, slot])
        at.send(p, p, cs.at[i, 7 + slot], cr.at[i, 7 + slot], at.cpeer)

    slots = [(t - 1, far[t] * 2 + x) for t in (1, 2, 3)]
    slots += [(3 + t, far[t] * 2 + 1 - x) for t in range(4)]
    order = [slots[k] for k in (3, 0, 4, 1, 5, 2, 6)]
    steps = [lambda: own(0)]
    for i in range(n):
        mine = [lambda i=i: zarr(i, 1)]
        if 0 < i and i + 1 < n:
            mine.append(lambda i=i: own(i + 1))
        mine.append(lambda i=i: xarr(i, 0))
        for t in (2, 3):
            mine.append(lambda i=i, t=t: zarr(i, t))
            if i == 0 and t == 3 and n > 1:
                mine.append(lambda: own(1))
            mine.append(lambda i=i, t=t: xarr(i, t - 1))
        mine.append(lambda i=i: xarr(i, 3))
        if i > 0:
            late = [lambda i=i, k=k: yarr(i - 1, *order[k]) for k in range(7)]
            pace, held = 3 if i == soon else 1, list(late)
            merged = []
            while late or mine:
                merged += late[:pace] + mine[:1]
                late, mine = late[pace:], mine[1:]
            mine = merged
        if i == soon:
            first = len(steps) + max(k for k, step in enumerate(mine) if step in held) + 1
        steps += mine
    steps += [lambda k=k: yarr(n - 1, *order[k]) for k in range(7)]

    def last(i):
        for slot, s in slots:
            at.arrived(piece(i, outs[i].at[s], y, 1 - c), cr.at[i, slot])
            at.arrived(bpart(i, outs[i].at[s], 1 - y, 1 - c), cr.at[i, 7 + slot])

    return steps, first, last


def add_into(dst, src):
    def step(r, _):
        rows = pl.ds(pl.multiple_of(r * 16, 16), 16)
        dst[rows, :] = dst[rows, :] + src[rows, :]
        return 0

    lax.fori_loop(0, src.shape[0] // 16, step, 0)


def move_into(dst, src):
    def step(r, _):
        rows = pl.ds(pl.multiple_of(r * 16, 16), 16)
        dst[rows, :] = src[rows, :]
        return 0

    lax.fori_loop(0, src.shape[0] // 16, step, 0)


def scatter_scratch(grads, cuts):
    n = len(cuts)
    s = pltpu.SemaphoreType.DMA

    def buf(lead, k, size):
        rows, cols = grads[cuts[k][5]].shape[-2:]
        shape = (rows, size) if cuts[k][0] == 1 else (size, cols)
        return pltpu.VMEM(lead + shape, jnp.bfloat16)

    out = []
    for lead, pick in (
        ((8,), lambda c: c[1]),
        ((8,), lambda c: c[1]),
        ((8,), lambda c: c[3]),
        ((4,), lambda c: c[2] + c[3]),
        ((5,), lambda c: c[2] + c[3]),
        ((), lambda c: c[2] + c[3]),
    ):
        out += [buf(lead, k, pick(cuts[k])) for k in range(n)]
    out += [s((n, 8))] * 5 + [s((n, 4))] * 2 + [s((n, 3)), s((n, 5))] + [s((n,))] * 5
    return out


def scatter_steps(at, cuts, ins, outs, scratch, lags):
    n = len(cuts)
    own_half, core_buf, y_buf, x_buf, z_buf, fin_buf = (scratch[k * n : (k + 1) * n] for k in range(6))
    ls, cs, cr, ys, yr, xs, xr, zs, zr, fs, fr, es, er, ws = scratch[6 * n :]
    x, y, z, c, far = at.x, at.y, at.z, at.c, at.far
    ins, outs = ([refs[cut[5]] for cut in cuts] for refs in (ins, outs))

    def in_half(i, s, cc):
        axis, half, _, _, base, _ = cuts[i]
        if base is None:
            return ins[i].at[cc, s]
        return span(ins[i].at[s], axis, base + cc * half, half)

    def out_half(i, cc):
        axis, half, _, _, base, _ = cuts[i]
        if base is None:
            return outs[i].at[cc]
        return span(outs[i], axis, base + cc * half, half)

    def piece(i, ref):
        _, _, a, b = cuts[i][:4]
        return span(ref, cuts[i][0], y * b, a + b)

    def bpart(i, ref, yy):
        _, _, a, b = cuts[i][:4]
        return span(ref, cuts[i][0], yy * (a + b), b)

    order = [(t, j) for t in (3, 2, 1, 0) for j in (1, 0)]

    def shard(t, j):
        return far[t] * 2 + (1 - x if j else x)

    def load(i, t, j):
        s, q = shard(t, j), order.index((t, j))
        return pltpu.make_async_copy(in_half(i, s, c), own_half[i].at[s], ls.at[i, q])

    def give(i, t, j):
        s, q = shard(t, j), order.index((t, j))
        src = in_half(i, s, 1 - c)
        at.send(src, core_buf[i].at[s], cs.at[i, q], cr.at[i, s], at.cpeer)
        if not at.draining:
            load(i, t, j).start()

    def to_y(i, t, j):
        s = shard(t, j)
        src = bpart(i, own_half[i].at[s], 1 - y)
        return at.copy(src, y_buf[i].at[s], ys.at[i, order.index((t, j))], yr.at[i, s], at.ypeer)

    def to_fin(i):
        return at.copy(piece(i, own_half[i].at[at.g]), fin_buf[i], fs.at[i], fr.at[i], at.ypeer)

    def cadd(i, t, j):
        s = shard(t, j)
        if at.draining:
            if (t, j) != (0, 0):
                to_y(i, t, j).wait_send()
            return
        load(i, t, j).wait()
        at.arrived(core_buf[i].at[s], cr.at[i, s])
        add_into(own_half[i].at[s], core_buf[i].at[s])
        to_y(i, t, j).start()

    def yadd(i, t, j):
        s = shard(t, j)
        at.arrived(y_buf[i].at[s], yr.at[i, s])
        if not at.draining:
            add_into(bpart(i, own_half[i].at[s], y), y_buf[i].at[s])
        if j:
            at.send(piece(i, own_half[i].at[s]), x_buf[i].at[far[t]], xs.at[i, t], xr.at[i, far[t]], at.xpeer)

    def xadd(i, t):
        if at.draining:
            return
        at.arrived(x_buf[i].at[far[t]], xr.at[i, far[t]])
        add_into(piece(i, own_half[i].at[shard(t, 0)]), x_buf[i].at[far[t]])

    def zadd(i, t):
        zz = far[t]
        p = piece(i, own_half[i].at[shard(t, 0)])

        def join(cond, slot):
            def do():
                at.arrived(z_buf[i].at[slot], zr.at[i, slot])
                add_into(p, z_buf[i].at[slot])

            if not at.draining:
                pl.when(cond)(do)

        if t > 0:
            inc = jnp.where(zz < z, z + 1, z - 1)
            join((inc >= 0) & (inc <= 3), zz)
            nxt = jnp.where(zz < z, z - 1, z + 1)
            slot = jnp.where((zz < z) & (nxt == zz), 4, zz)
            at.send(p, z_buf[i].at[slot], zs.at[i, t - 1], zr.at[i, slot], at.line(nxt))
        else:
            join(z > 0, z)
            join(z < 3, 4)
            if not at.draining:
                to_fin(i).start()

    def fin(i):
        axis, half, a, b, base, _ = cuts[i]
        own = own_half[i].at[at.g]
        if not at.draining:
            at.arrived(fin_buf[i], fr.at[i])
            to_fin(i).wait_send()
            to_y(i, 0, 0).wait_send()
            for yy in (0, 1):

                @pl.when(y == 1 - yy)
                def _():
                    add_into(span(own, axis, b, a), span(fin_buf[i], axis, b if yy == 0 else 0, a))
                    move_into(span(own, axis, yy * (a + b), b), span(fin_buf[i], axis, 0 if yy == 0 else a, b))

        o = out_half(i, c)
        at.send(own, o, es.at[i], er.at[i], at.cpeer)
        at.keep(own, o, ws.at[i])

    seq = [(i, t, j) for i in range(n) for (t, j) in order]
    opening = [functools.partial(give, *p) for p in seq]
    ly, lx, lz, lf = lags
    todo = []
    for q, (i, t, j) in enumerate(seq):
        todo.append((q, 0, functools.partial(cadd, i, t, j)))
        todo.append((q + ly, 1, functools.partial(yadd, i, t, j)))
        if j == 0:
            todo.append((q + ly + lx, 2, functools.partial(xadd, i, t)))
            todo.append((q + ly + lx + lz, 3, functools.partial(zadd, i, t)))
            if t == 0:
                todo.append((q + ly + lx + lz + lf, 4, functools.partial(fin, i)))
    todo.sort(key=lambda p: p[:2])

    def last():
        for i in range(n):
            at.arrived(out_half(i, 1 - c), er.at[i])

    return opening, [f for _, _, f in todo], last


def head_window(h):
    first = jnp.minimum(h * HDIM // LANES, HEADS * HDIM // LANES - 2) * LANES
    lane = lax.broadcasted_iota(jnp.int32, (1, 2 * LANES), 1) + first
    inside = (lane >= h * HDIM) & (lane < h * HDIM + HDIM)
    return pl.ds(pl.multiple_of(first, LANES), 2 * LANES), inside


def dot_t(left, right):
    return lax.dot_general(left, right, (((1,), (1,)), ((), ())), preferred_element_type=jnp.float32)


def first_dot(left, right):
    return lax.dot_general(left, right, (((0,), (0,)), ((), ())), preferred_element_type=jnp.float32)


def pick_dot(values, chosen):
    high = values.astype(jnp.bfloat16)
    low = (values - high.astype(jnp.float32)).astype(jnp.bfloat16)
    return jnp.dot(high, chosen, preferred_element_type=jnp.float32) + jnp.dot(
        low, chosen, preferred_element_type=jnp.float32
    )


def head_pick(width):
    row = lax.broadcasted_iota(jnp.int32, (width, LANES), 0)
    first = lax.broadcasted_iota(jnp.int32, (width, LANES), 1) * HDIM
    return ((row >= first) & (row < first + HDIM)).astype(jnp.float32).astype(jnp.bfloat16)


def head_spread(width):
    lane = lax.broadcasted_iota(jnp.int32, (LANES, width), 1)
    first = lax.broadcasted_iota(jnp.int32, (LANES, width), 0) * HDIM
    return ((lane >= first) & (lane < first + HDIM)).astype(jnp.float32).astype(jnp.bfloat16)


def rope_tables(band, rows, cols, width):
    quarter = HDIM // 4
    shape = (rows * cols, width)
    token = lax.broadcasted_iota(jnp.int32, shape, 0)
    lane = lax.broadcasted_iota(jnp.int32, shape, 1) % HDIM
    power = (lane % quarter).astype(jnp.float32) * (-math.log(10000.0) / quarter)
    by_row = band * rows + (token // cols).astype(jnp.float32)
    index = jnp.where(lane < 2 * quarter, by_row, (token % cols).astype(jnp.float32))
    angle = index * jnp.exp(power)
    sine = jnp.sin(angle)
    low = (lane // quarter) % 2 == 0
    return jnp.cos(angle), jnp.where(low, -sine, 0.0), jnp.where(low, 0.0, sine)


def turn(values, cos, sin_next, sin_prev):
    width = values.shape[-1]
    after = pltpu.roll(values, width - HDIM // 4, 1)
    before = pltpu.roll(values, HDIM // 4, 1)
    return values * cos + after * sin_next + before * sin_prev


def turn_back(values, cos, sin_next, sin_prev):
    width = values.shape[-1]
    after = pltpu.roll(values, width - HDIM // 4, 1)
    before = pltpu.roll(values, HDIM // 4, 1)
    return values * cos - after * sin_next - before * sin_prev


def qkv_back_kernel(
    x_ref, mod_ref, mid_ref, dq_ref, dk_ref, dv_ref, nq_ref, nk_ref, rq_ref, rk_ref, w_ref,
    gains_ref, cos_ref, next_ref, prev_ref,
    dqkv_ref, dx_ref, sums_ref,
):
    width = x_ref.shape[-1]
    tables = (cos_ref[...], next_ref[...], prev_ref[...])
    pick, spread = head_pick(width), head_spread(width)
    ins = ((dq_ref, nq_ref, rq_ref), (dk_ref, nk_ref, rk_ref))
    for part, (d_ref, n_ref, r_ref) in enumerate(ins):
        back = turn_back(d_ref[0].astype(jnp.float32) * HDIM ** (-0.5), *tables)
        unit = n_ref[0]
        sums_ref[0, 2 + part : 3 + part, :] = jnp.sum(back * unit, axis=0, keepdims=True)
        inner = back * gains_ref[part : part + 1, :]
        mean = pick_dot(inner * unit, pick) * (1.0 / HDIM)
        grad = (inner - unit * pick_dot(mean, spread)) * pick_dot(r_ref[0], spread)
        dqkv_ref[0, :, part * width : (part + 1) * width] = grad.astype(jnp.bfloat16)
    dqkv_ref[0, :, 2 * width : 3 * width] = dv_ref[0]
    d_normed = dot_t(dqkv_ref[0], w_ref[...])
    x = x_ref[0].astype(jnp.float32)
    root = lax.rsqrt(jnp.mean(x * x, axis=-1, keepdims=True) + EPS)
    unit = x * root
    sums_ref[0, 0:1, :] = jnp.sum(d_normed, axis=0, keepdims=True)
    sums_ref[0, 1:2, :] = jnp.sum(d_normed * unit, axis=0, keepdims=True)
    inner = d_normed * (1.0 + mod_ref[0, 1:2, :])
    dx_ref[0] = mid_ref[0] + root * (inner - unit * jnp.mean(inner * unit, axis=-1, keepdims=True))


def qkv_backward(x, mod, d_mid, dq, d_kv, nq, nk, rq, rk, qp_all, gains, tables):
    images, length, width = x.shape
    row = lambda w: pl.BlockSpec((1, length, w), lambda i: (i, 0, 0))
    whole = lambda a: pl.BlockSpec(a.shape, lambda i: (0,) * a.ndim)
    return pl.pallas_call(
        qkv_back_kernel,
        grid=(images,),
        in_specs=[row(width), pl.BlockSpec((1, 6, width), lambda i: (i, 0, 0))]
        + [row(width)] * 2
        + [pl.BlockSpec((None, 1, length, width), lambda i, s=s: (s, i, 0, 0)) for s in (0, 1)]
        + [row(width)] * 2
        + [row(LANES)] * 2
        + [pl.BlockSpec((width, 3 * width), lambda i: (0, 0)), whole(gains)]
        + [whole(t) for t in tables],
        out_shape=[
            jax.ShapeDtypeStruct((images, length, 3 * width), jnp.bfloat16),
            jax.ShapeDtypeStruct((images, length, width), jnp.float32),
            jax.ShapeDtypeStruct((images, 4, width), jnp.float32),
        ],
        out_specs=[row(3 * width), row(width), pl.BlockSpec((1, 4, width), lambda i: (i, 0, 0))],
        compiler_params=pltpu.CompilerParams(vmem_limit_bytes=60 * 2**20),
        name="qkv_backward",
    )(x, mod, d_mid, dq, d_kv, d_kv, nq, nk, rq, rk, qp_all, gains, *tables)


def weight_kernel(normed_ref, att_ref, dqkv_ref, dproj_ref, out_ref, turned):
    step = pl.program_id(0)

    @pl.when(step == 0)
    def _():
        turned[...] = normed_ref[...].T

    @pl.when(step == 3)
    def _():
        turned[...] = att_ref[...].T
        out_ref[...] = jnp.dot(turned[...], dproj_ref[...], preferred_element_type=jnp.float32).astype(jnp.bfloat16)

    @pl.when(step < 3)
    def _():
        out_ref[...] = jnp.dot(turned[...], dqkv_ref[...], preferred_element_type=jnp.float32).astype(jnp.bfloat16)


def weight_grads(normed, attended, d_qkv, d_proj):
    tokens, width = normed.shape
    whole = pl.BlockSpec((tokens, width), lambda k: (0, 0))
    return pl.pallas_call(
        weight_kernel,
        grid=(4,),
        in_specs=[whole, whole, pl.BlockSpec((tokens, width), lambda k: (0, jnp.minimum(k, 2))), whole],
        out_shape=jax.ShapeDtypeStruct((width, 4 * width), jnp.bfloat16),
        out_specs=pl.BlockSpec((width, width), lambda k: (0, k)),
        scratch_shapes=[pltpu.VMEM((width, tokens), jnp.bfloat16)],
        compiler_params=pltpu.CompilerParams(vmem_limit_bytes=60 * 2**20),
        name="weight_grads",
    )(normed, attended, d_qkv, d_proj)


def tail_scratch():
    s = pltpu.SemaphoreType.DMA
    wide = SMALL_COLS
    return [
        pltpu.VMEM((SMALL_ROWS, wide), jnp.float32),
        pltpu.VMEM((2, SMALL_ROWS, wide), jnp.float32),
        pltpu.VMEM((8, SMALL_ROWS, wide), jnp.bfloat16),
        pltpu.VMEM((8, GROUPS, 2 * LANES), jnp.float32),
        s((8,)),
        s((8,)),
    ]


def tail_steps(at, ins, outs, scratch):
    sums_ref, mid_ref, tag_ref, ada_ref, slope_ref = ins
    all_ref, cond_ref = outs
    acc, inbox, blocks, cond, ss, rs = scratch
    width = HEADS * HDIM
    z = at.z
    line = (at.xpeer, at.line(at.far[1]), at.line((z + 2) % 4))

    def copy(r):
        if r < 2:
            return at.copy(acc, inbox.at[r], ss.at[r], rs.at[r], (at.cpeer, at.ypeer)[r])
        ref, k = (blocks, r - 2) if r < 5 else (cond, r - 5)
        start, size = ((at.g, 1), (2 * z, 2), (4 * (z // 2), 4))[k]
        src = ref.at[pl.ds(start, size)]
        return at.copy(src, src, ss.at[r], rs.at[r], line[k])

    def collect():
        acc[...] = jnp.zeros_like(acc)
        for i in range(2):
            acc[6 * i : 6 * i + 2, :width] = sums_ref[i, 0:2, :]
            acc[6 * i + 2 : 6 * i + 6, :width] = mid_ref[i]
        acc[:GAIN_ROW, width:] = tag_ref[...]
        gains = sums_ref[0, 2:4, :] + sums_ref[1, 2:4, :]
        acc[GAIN_ROW : GAIN_ROW + 2, :width] = gains
        acc[GAIN_ROW + 2 :, :width] = gains

    def pack():
        row = lax.broadcasted_iota(jnp.int32, (SMALL_ROWS, 1), 0)
        value = acc[...]
        rest = value - value.astype(jnp.bfloat16).astype(jnp.float32)
        blocks[at.g] = jnp.where(row >= GAIN_ROW + 2, rest, value).astype(jnp.bfloat16)

    def cond_rows():
        flat = blocks[...].reshape(8 * SMALL_ROWS, SMALL_COLS)
        row = lax.broadcasted_iota(jnp.int32, (8 * SMALL_ROWS, 1), 0) % SMALL_ROWS
        silu = jnp.zeros((8 * SMALL_ROWS, ada_ref.shape[0]), jnp.float32)
        for k in range(6):
            product = dot_t(flat[:, :width], ada_ref[:, k * width : (k + 1) * width])
            silu = jnp.where((row % 6 == k) & (row < GAIN_ROW), product, silu)
        by_group = lax.dot_general(
            flat[:, width:].astype(jnp.float32),
            silu,
            (((0,), (0,)), ((), ())),
            precision=lax.Precision.HIGHEST,
            preferred_element_type=jnp.float32,
        )
        cond[at.g] = jnp.zeros((GROUPS, 2 * LANES), jnp.float32)
        cond[at.g, :, : ada_ref.shape[0]] = by_group[:GROUPS] * slope_ref[...]

    def step(r):
        if at.draining:
            return
        if r > 0:
            copy(r - 1).wait()
        if r == 0:
            collect()
        elif r <= 2:
            acc[...] = acc[...] + inbox[r - 1]
        if r == 2:
            pack()
        if r == 5:
            cond_rows()
        if r < 8:
            copy(r).start()
        else:
            all_ref[...] = blocks[...]
            cond_ref[...] = cond[...]

    return [functools.partial(step, r) for r in range(9)]


SMALL_ROWS, SMALL_COLS, GAIN_ROW = 16, HEADS * HDIM + LANES, 12


def scatter_kernel(n, cuts, lags, *refs):
    at = Place()
    at.greet_all()
    ins, small_in = refs[:n], refs[n : n + 5]
    outs, small_out = refs[n + 5 : 2 * n + 5], refs[2 * n + 5 : 2 * n + 7]
    small = tail_steps(at, small_in, small_out, refs[2 * n + 7 : 2 * n + 13])
    opening, steps, last = scatter_steps(at, cuts, ins, outs, refs[2 * n + 13 :], lags)
    small[0]()
    for step in opening:
        step()
    small = small[1:]
    for k, step in enumerate(steps):
        step()
        if k % 6 == 5 and small:
            small[0]()
            small = small[1:]
    for step in small:
        step()
    last()
    at.drain(opening + steps)


def scatter(grads, cuts, lags, sums, mid_sums, tags, w_ada, slope):
    n = len(grads)
    any_ref = pl.BlockSpec(memory_space=pl.ANY)
    vmem = pl.BlockSpec(memory_space=pltpu.VMEM)
    return pl.pallas_call(
        functools.partial(scatter_kernel, n, cuts, lags),
        out_shape=[jax.ShapeDtypeStruct(w.shape[1:], jnp.bfloat16) for w in grads]
        + [
            jax.ShapeDtypeStruct((8, SMALL_ROWS, SMALL_COLS), jnp.bfloat16),
            jax.ShapeDtypeStruct((8, GROUPS, 2 * LANES), jnp.float32),
        ],
        in_specs=[any_ref] * n + [vmem] * 5,
        out_specs=[any_ref] * n + [vmem] * 2,
        scratch_shapes=tail_scratch() + scatter_scratch(grads, cuts),
        compiler_params=pltpu.CompilerParams(
            collective_id=1, has_side_effects=True, vmem_limit_bytes=60 * 2**20
        ),
        name="gradient_scatter",
    )(*grads, sums, mid_sums, tags, w_ada, slope)


def forward_kernel(cuts, cols, refs):
    n = len(cuts)
    soon = sum(cut[5] == 0 for cut in cuts)
    at = Place()
    x_ref, part_ref, group_ref, gains_ref, band_ref = refs["in"]
    normed_ref, q_ref, nq_ref, nk_ref, rq_ref, rk_ref, o_ref, inv_ref, mod_ref, *table_refs, kv_out = refs["out"]
    kv, w_buf, pick_ref, spread_ref, mod_buf, mod_in, w_sem, ms, mr, ks, kr, os = refs["scratch"]
    ins, outs = refs["shards"], refs["full"]
    images, length, width = x_ref.shape
    parts = [(i, s) for i in range(images) for s in (0, 1)]
    if n:
        at.greet_all()
        steps, first, last = gather_steps(at, cuts, ins, outs, refs["sems"])
    else:
        at.greet_band()
        steps, first, last = [], 0, None

    mod_buf[...] = part_ref[...]

    def mod_copy(r):
        peer = (at.xpeer, at.line(at.far[1]), at.line((at.z + 2) % 4))[r]
        return at.copy(mod_buf, mod_in.at[r], ms.at[r], mr.at[r], peer)

    def mod_step(r):
        if at.draining:
            return
        if r > 0:
            mod_copy(r - 1).wait()
            mod_buf[...] = mod_buf[...] + mod_in[r - 1]
        if r < 3:
            mod_copy(r).start()

    def rows(s, i, band):
        return kv.at[s, i, pl.ds(pl.multiple_of(band * length, 16), length), :]

    here, over = at.band, (1 - at.y) * 2 + at.c
    beside, across = at.y * 2 + 1 - at.c, (1 - at.y) * 2 + 1 - at.c

    def give(i, s):
        p = rows(s, i, here)
        at.send(p, p, ks.at[i, s, 0], kr.at[i, s, 0], at.ypeer)
        at.send(p, p, ks.at[i, s, 1], kr.at[i, s, 1], at.cpeer)

    def pass_on(i, s):
        p = rows(s, i, over)
        at.arrived(p, kr.at[i, s, 0])
        at.send(p, p, ks.at[i, s, 2], kr.at[i, s, 2], at.cpeer)

    def ready(i):
        for s in (0, 1):
            at.arrived(rows(s, i, beside), kr.at[i, s, 1])
            at.arrived(rows(s, i, across), kr.at[i, s, 2])
            at.keep(kv.at[s, i], kv_out.at[s, i], os.at[i, s])

    def norm(i):
        value = x_ref[i].astype(jnp.float32)
        root = lax.rsqrt(jnp.mean(value * value, axis=-1, keepdims=True) + EPS)
        chosen = jnp.sum(group_ref[:, i : i + 1] * mod_buf[...], axis=0, keepdims=True)
        mod_ref[i : i + 1, :] = chosen
        shift, scale = chosen[:, :width], chosen[:, width : 2 * width]
        normed_ref[i] = (value * root * (1.0 + scale) + shift).astype(jnp.bfloat16)

    def raw(i, part):
        return jnp.dot(
            normed_ref[i], w_buf[:, part * width : (part + 1) * width], preferred_element_type=jnp.float32
        )

    def project(i, part, n_ref, r_ref):
        values = raw(i, part)
        inv = lax.rsqrt(pick_dot(values * values, pick_ref[...]) * (1.0 / HDIM) + EPS)
        r_ref[i] = inv
        unit = values * pick_dot(inv, spread_ref[...])
        n_ref[i] = unit
        scaled = unit * gains_ref[part : part + 1, :]
        return turn(scaled, *(t[...] for t in table_refs)).astype(jnp.bfloat16)

    def key_part(i):
        norm(i)
        kv[0, i, pl.ds(pl.multiple_of(here * length, 16), length), :] = project(i, 1, nk_ref, rk_ref)
        give(i, 0)

    def value_part(i):
        kv[1, i, pl.ds(pl.multiple_of(here * length, 16), length), :] = raw(i, 2).astype(jnp.bfloat16)
        give(i, 1)

    def query_part(i):
        q_ref[i] = project(i, 0, nq_ref, rq_ref)

    def head(i, h):
        win, inside = head_window(h)
        query = q_ref[i, :, win]
        query = jnp.where(inside, query, jnp.zeros_like(query))
        power = jnp.exp2(dot_t(query, kv[0, i, :, win]) * (HDIM ** (-0.5) * LOG2E))
        inv = 1.0 / jnp.sum(power, axis=-1, keepdims=True)
        out = jnp.dot(
            (power * inv).astype(jnp.bfloat16), kv[1, i, :, win], preferred_element_type=jnp.float32
        )
        o_ref[i, :, win] = jnp.where(inside, out.astype(jnp.bfloat16), o_ref[i, :, win])
        lane = lax.broadcasted_iota(jnp.int32, (1, LANES), 1)
        inv_ref[i] = jnp.where(lane == h, inv, inv_ref[i])

    def prepare():
        pick_ref[...] = head_pick(width)
        spread_ref[...] = head_spread(width)

        def block(r, _):
            rows_of = pl.ds(pl.multiple_of(r * cols, cols), cols)
            row = band_ref[0:1, 0:1] * (length // cols) + r.astype(jnp.float32)
            for ref, value in zip(table_refs, rope_tables(row, 1, cols, width)):
                ref[rows_of, :] = value
            return 0

        lax.fori_loop(0, length // cols, block, 0)

    if not n:
        prepare()
    if n:
        for k in range(3):
            mod_step(k)
            for step in steps[2 * k : 2 * k + 2]:
                step()
                if k == 0 and step is steps[0]:
                    prepare()
        mod_step(3)
        for step in steps[6:first]:
            step()
        for i in range(soon):
            last(i)
        pltpu.make_async_copy(ins[0], outs[0].at[at.g], refs["sems"][0].at[0]).wait()
        loads = [
            pltpu.make_async_copy(
                outs[0].at[k, :, pl.ds(0, 3 * width)],
                w_buf.at[pl.ds(k * (width // 8), width // 8), :],
                w_sem.at[k],
            )
            for k in range(8)
        ]
    else:
        loads = [pltpu.make_async_copy(ins[0].at[:, pl.ds(0, 3 * width)], w_buf, w_sem.at[0])]
    for d in loads:
        d.start()
    o_ref[...] = jnp.zeros_like(o_ref)
    inv_ref[...] = jnp.zeros_like(inv_ref)
    for d in loads:
        d.wait()
    todo = steps[first:]
    for i in range(images):
        for work in (key_part, value_part):
            work(i)
            for step in todo[:2]:
                step()
            todo = todo[2:]
    for i in range(images):
        query_part(i)
        for step in todo[:2]:
            step()
        todo = todo[2:]
    for i in range(images):
        pass_on(i, 0)
        pass_on(i, 1)
        ready(i)
        mine, todo = (todo[: HEADS // 2], todo[HEADS // 2 :])

        def body(h, _, i=i, mine=mine):
            for k, step in enumerate(mine):
                pl.when(h == 2 * k)(step)
            head(i, h)
            return 0

        lax.fori_loop(0, HEADS, body, 0)
    for step in todo:
        step()
    for i in range(soon, n):
        last(i)
    at.drain(steps)
    for i, s in parts:
        at.drain([functools.partial(give, i, s), functools.partial(pass_on, i, s)])
    for i in range(images):
        at.drain([functools.partial(ready, i)])


def forward(x, mod_part, groups, gains, band, cols, shards, cuts):
    n = len(cuts)
    images, length, width = x.shape
    bands = lax.axis_size("band")
    keys = (2, images, bands * length, width)
    s = pltpu.SemaphoreType.DMA
    bf = jnp.bfloat16
    any_ref = pl.BlockSpec(memory_space=pl.ANY)
    vmem = pl.BlockSpec(memory_space=pltpu.VMEM)
    args = [x, mod_part, groups, gains, band]
    rows = lambda w, d: jax.ShapeDtypeStruct((images, length, w), d)
    outs = [rows(width, bf)] * 2 + [rows(width, jnp.float32)] * 2 + [rows(LANES, jnp.float32)] * 2
    outs += [rows(width, bf), rows(LANES, jnp.float32), jax.ShapeDtypeStruct((images, mod_part.shape[1]), jnp.float32)]
    outs += [jax.ShapeDtypeStruct((length, width), jnp.float32)] * 3
    scratch = [
        pltpu.VMEM(keys, bf),
        pltpu.VMEM((width, 3 * width), bf),
        pltpu.VMEM((width, LANES), bf),
        pltpu.VMEM((LANES, width), bf),
        pltpu.VMEM(mod_part.shape, jnp.float32),
        pltpu.VMEM((3,) + mod_part.shape, jnp.float32),
        s((8,)),
        s((3,)),
        s((3,)),
        s((images, 2, 3)),
        s((images, 2, 3)),
        s((images, 2)),
    ]
    whole = len(shards) if n else 0
    sizes = [len(args), len(shards), len(outs) + 1, whole, len(scratch), 10 if n else 0]

    def kernel(*refs):
        groups_of, start = [], 0
        for size in sizes:
            groups_of.append(refs[start : start + size])
            start += size
        names = ("in", "shards", "out", "full", "scratch", "sems")
        forward_kernel(cuts, cols, dict(zip(names, groups_of)))

    return pl.pallas_call(
        kernel,
        out_shape=outs
        + [jax.ShapeDtypeStruct(keys, bf)]
        + [jax.ShapeDtypeStruct((8,) + w.shape, w.dtype) for w in shards[:whole]],
        in_specs=[vmem] * len(args) + [any_ref] * len(shards),
        out_specs=[vmem] * len(outs) + [any_ref] * (1 + whole),
        scratch_shapes=scratch + (gather_sems(n) if n else []),
        compiler_params=pltpu.CompilerParams(
            collective_id=2, has_side_effects=True, vmem_limit_bytes=60 * 2**20
        ),
        name="forward",
    )(*args, *shards)


EACH = 9


def attention_back_kernel(n, cuts, lags, q_ref, do_ref, inv_ref, kv_ref, *refs):
    ins, (dq_ref, d_out), outs = refs[:n], refs[n : n + 2], refs[n + 2 : 2 * n + 2]
    kv, dkv, core_buf, y_buf, load_sem, ks, kr, ys, yr, ws = refs[2 * n + 2 : 2 * n + 12]
    images, length, width = q_ref.shape
    at = Place()
    loads = [pltpu.make_async_copy(kv_ref.at[:, i], kv.at[i], load_sem.at[i]) for i in range(images)]
    for d in loads:
        d.start()
    at.greet_all() if n else at.greet_band()
    opening, todo, last = [], [], lambda: None
    if n:
        opening, todo, last = scatter_steps(at, cuts, ins, outs, refs[2 * n + 12 :], lags)
    for step in opening:
        step()
    steps = opening + todo

    def rows(s, i, band):
        return dkv.at[s, i, pl.ds(pl.multiple_of(band * length, 16), length), :]

    def to_core(i):
        for s in (0, 1):
            for yy in (0, 1):
                at.send(rows(s, i, yy * 2 + 1 - at.c), core_buf.at[i, s, yy], ks.at[i, s, yy], kr.at[i, s, yy], at.cpeer)

    def core_add(i):
        for s in (0, 1):
            p = rows(s, i, (1 - at.y) * 2 + at.c)
            at.arrived(core_buf.at[i, s, 1 - at.y], kr.at[i, s, 1 - at.y])
            if not at.draining:
                add_into(p, core_buf.at[i, s, 1 - at.y])
            at.send(p, y_buf.at[i, s], ys.at[i, s], yr.at[i, s], at.ypeer)
        for s in (0, 1):
            at.arrived(core_buf.at[i, s, at.y], kr.at[i, s, at.y])
            if not at.draining:
                add_into(rows(s, i, at.band), core_buf.at[i, s, at.y])

    def y_add(i):
        for s in (0, 1):
            p = rows(s, i, at.band)
            at.arrived(y_buf.at[i, s], yr.at[i, s])
            if not at.draining:
                add_into(p, y_buf.at[i, s])
            at.keep(p, d_out.at[s, i], ws.at[i, s])

    def head(i, h):
        win, inside = head_window(h)
        query, grad = q_ref[i, :, win], do_ref[i, :, win]
        query = jnp.where(inside, query, jnp.zeros_like(query))
        grad = jnp.where(inside, grad, jnp.zeros_like(grad))
        keys, values = kv[i, 0, :, win], kv[i, 1, :, win]
        inv = inv_ref[i, pl.ds(h, 1), :]
        probs = jnp.exp2(dot_t(keys, query) * (HDIM ** (-0.5) * LOG2E)) * inv
        d_probs = dot_t(values, grad)
        delta = jnp.sum(probs * d_probs, axis=0, keepdims=True)
        d_scores = (probs * (d_probs - delta)).astype(jnp.bfloat16)
        d_key = jnp.dot(d_scores, query, preferred_element_type=jnp.float32).astype(jnp.bfloat16)
        d_value = jnp.dot(
            probs.astype(jnp.bfloat16), grad, preferred_element_type=jnp.float32
        ).astype(jnp.bfloat16)
        dkv[0, i, :, win] = jnp.where(inside, d_key, dkv[0, i, :, win])
        dkv[1, i, :, win] = jnp.where(inside, d_value, dkv[1, i, :, win])
        dq_ref[i, :, win] = jnp.where(inside, first_dot(d_scores, keys), dq_ref[i, :, win])

    dq_ref[...] = jnp.zeros_like(dq_ref)
    for s in (0, 1):
        for i in range(images):

            def clear(r, _, s=s, i=i):
                dkv[s, i, pl.ds(pl.multiple_of(r * 16, 16), 16), :] = jnp.zeros((16, width), jnp.bfloat16)
                return 0

            lax.fori_loop(0, kv.shape[2] // 16, clear, 0)
    exchange = []
    for i in range(images):
        loads[i].wait()
        mine, todo = (todo[:EACH], todo[EACH:])
        due = exchange
        exchange = [functools.partial(f, i) for f in (core_add, y_add)]

        def body(h, _, i=i, mine=mine, due=due):
            for k, step in enumerate(due):
                pl.when(h == 1 + 12 * k)(step)
            for k, step in enumerate(mine):
                pl.when(h == k * HEADS // EACH)(step)
            head(i, h)
            return 0

        lax.fori_loop(0, HEADS, body, 0, unroll=2)
        to_core(i)
        steps += [functools.partial(to_core, i)] + exchange
    exchange[0]()
    part = min(6, len(todo))
    for step in todo[:part] + [exchange[1]] + todo[part:]:
        step()
    last()
    at.drain(steps)


def attention_backward(q, d_att, inv_rows, kv_all, grads, cuts, lags):
    n = len(grads)
    images, length, width = q.shape
    s = pltpu.SemaphoreType.DMA
    any_ref = pl.BlockSpec(memory_space=pl.ANY)
    vmem = pl.BlockSpec(memory_space=pltpu.VMEM)
    bf = jnp.bfloat16
    return pl.pallas_call(
        functools.partial(attention_back_kernel, n, cuts, lags),
        out_shape=[
            jax.ShapeDtypeStruct(q.shape, jnp.float32),
            jax.ShapeDtypeStruct((2, images, length, width), bf),
        ]
        + [jax.ShapeDtypeStruct(w.shape[:-3] + w.shape[-2:], bf) for w in grads],
        in_specs=[vmem, vmem, vmem, any_ref] + [any_ref] * n,
        out_specs=[vmem, any_ref] + [any_ref] * n,
        scratch_shapes=[
            pltpu.VMEM((images, 2) + kv_all.shape[2:], bf),
            pltpu.VMEM(kv_all.shape, bf),
            pltpu.VMEM((images, 2, 2, length, width), bf),
            pltpu.VMEM((images, 2, length, width), bf),
            s((images,)),
            s((images, 2, 2)),
            s((images, 2, 2)),
            s((images, 2)),
            s((images, 2)),
            s((images, 2)),
        ]
        + (scatter_scratch(grads, cuts) if n else []),
        compiler_params=pltpu.CompilerParams(
            collective_id=3, has_side_effects=True, vmem_limit_bytes=63 * 2**20
        ),
        name="attention_backward",
    )(q, d_att, inv_rows, kv_all, *grads)
def mlp_kernel(
    x_ref, gout_ref, att_ref, mod_ref, live_ref, proj_ref, gate_ref, up_ref, down_ref,
    out_ref, dmid_ref, dproj_ref, datt_ref, sums_ref, dgu_ref, ddown_ref,
    mid, proj, mlp, dnorm, normed, normed_t, dmlp,
):
    step, steps = pl.program_id(0), pl.num_programs(0)
    images, length, width = x_ref.shape

    def piece(i, k):
        return mod_ref[i : i + 1, k * width : (k + 1) * width]

    def rows(i):
        return pl.ds(i * length, length)

    def live(i):
        return live_ref[i : i + 1, 0:1]

    def unit(i):
        value = mid[rows(i), :]
        root = lax.rsqrt(jnp.mean(value * value, axis=-1, keepdims=True) + EPS)
        return value * root, root

    @pl.when(step == 0)
    def _():
        for i in range(images):
            proj[rows(i), :] = jnp.dot(att_ref[i], proj_ref[...], preferred_element_type=jnp.float32)
            mid[rows(i), :] = x_ref[i].astype(jnp.float32) + piece(i, 2) * proj[rows(i), :]
            value = (unit(i)[0] * (1.0 + piece(i, 4)) + piece(i, 3)).astype(jnp.bfloat16)
            normed[rows(i), :] = value
            normed_t[:, rows(i)] = value.T
            dmlp[rows(i), :] = (piece(i, 5) * (gout_ref[i].astype(jnp.float32) * live(i))).astype(jnp.bfloat16)
        mlp[...] = jnp.zeros_like(mlp)
        dnorm[...] = jnp.zeros_like(dnorm)

    gate = jnp.dot(normed[...], gate_ref[...], preferred_element_type=jnp.float32)
    up = jnp.dot(normed[...], up_ref[...], preferred_element_type=jnp.float32)
    dhidden = dot_t(dmlp[...], down_ref[...])
    sigmoid = 1.0 / (1.0 + jnp.exp(-gate))
    silu = gate * sigmoid
    hidden = (silu * up).astype(jnp.bfloat16)
    dgate = (dhidden * up * (sigmoid * (1.0 + gate * (1.0 - sigmoid)))).astype(jnp.bfloat16)
    dup = (dhidden * silu).astype(jnp.bfloat16)
    mlp[...] += jnp.dot(hidden, down_ref[...], preferred_element_type=jnp.float32)
    dnorm[...] += dot_t(dgate, gate_ref[...]) + dot_t(dup, up_ref[...])
    ddown_ref[...] = first_dot(hidden, dmlp[...]).astype(jnp.bfloat16)
    dgu_ref[0] = jnp.dot(normed_t[...], dgate, preferred_element_type=jnp.float32).astype(jnp.bfloat16)
    dgu_ref[1] = jnp.dot(normed_t[...], dup, preferred_element_type=jnp.float32).astype(jnp.bfloat16)

    @pl.when(step == steps - 1)
    def _():
        total = lambda v: jnp.sum(v, axis=0, keepdims=True)
        for i in range(images):
            gy = gout_ref[i].astype(jnp.float32) * live(i)
            value = mlp[rows(i), :]
            out_ref[i] = ((mid[rows(i), :] + piece(i, 5) * value) * live(i)).astype(jnp.bfloat16)
            sums_ref[i, 3:4, :] = total(gy * value)
            n, root = unit(i)
            dn = dnorm[rows(i), :]
            sums_ref[i, 1:2, :] = total(dn)
            sums_ref[i, 2:3, :] = total(dn * n)
            e = dn * (1.0 + piece(i, 4))
            d_mid = gy + root * (e - n * jnp.mean(e * n, axis=-1, keepdims=True))
            dmid_ref[i] = d_mid
            sums_ref[i, 0:1, :] = total(d_mid * proj[rows(i), :])
            d_proj = (piece(i, 2) * d_mid).astype(jnp.bfloat16)
            dproj_ref[i] = d_proj
            datt_ref[i] = dot_t(d_proj, proj_ref[...]).astype(jnp.bfloat16)


def mlp_block(x, grad_out, attended, mod, live, qp_all, gu_all, down_all):
    images, length, width = x.shape
    ff = down_all.shape[0]
    chunk = 512 if ff % 512 == 0 else LANES
    steps = ff // chunk
    bf = jnp.bfloat16
    whole = lambda s: pl.BlockSpec(s, lambda k: (0,) * len(s))
    rows = lambda d: jax.ShapeDtypeStruct(x.shape, d)
    tokens = images * length
    return pl.pallas_call(
        mlp_kernel,
        grid=(steps,),
        in_specs=[whole(x.shape)] * 3
        + [whole(mod.shape), whole(live.shape), pl.BlockSpec((width, width), lambda k: (0, 3))]
        + [
            pl.BlockSpec((width, chunk), lambda k: (0, k)),
            pl.BlockSpec((width, chunk), lambda k: (0, steps + k)),
            pl.BlockSpec((chunk, width), lambda k: (k, 0)),
        ],
        out_shape=[rows(bf), rows(jnp.float32), rows(bf), rows(bf)]
        + [
            jax.ShapeDtypeStruct((images, 4, width), jnp.float32),
            jax.ShapeDtypeStruct((2, width, ff), bf),
            jax.ShapeDtypeStruct((ff, width), bf),
        ],
        out_specs=[whole(x.shape)] * 4
        + [
            whole((images, 4, width)),
            pl.BlockSpec((2, width, chunk), lambda k: (0, 0, k)),
            pl.BlockSpec((chunk, width), lambda k: (k, 0)),
        ],
        scratch_shapes=[pltpu.VMEM((tokens, width), jnp.float32)] * 4
        + [pltpu.VMEM((tokens, width), bf), pltpu.VMEM((width, tokens), bf), pltpu.VMEM((tokens, width), bf)],
        compiler_params=pltpu.CompilerParams(vmem_limit_bytes=60 * 2**20),
        name="mlp_block",
    )(x, grad_out, attended, mod, live, qp_all, gu_all, gu_all, down_all)


def half_cuts(ref, axis, base, size, own_parts, shared_parts):
    unit = size // 2 // (own_parts + 2 * shared_parts)
    return (axis, size // 2, own_parts * unit, shared_parts * unit, base, ref)


def by_shard(grad):
    parts = lax.axis_size("grp")
    return grad.reshape(parts, grad.shape[0] // parts, grad.shape[1])


def body(
    patches,
    grad_out,
    cond_table,
    group_ids,
    live_count,
    band_order,
    w_ada,
    b_ada,
    w_qkv,
    q_gain,
    k_gain,
    w_proj,
    w_gate,
    w_up,
    w_down,
):
    images, rows, cols, width = patches.shape
    length = rows * cols
    ff = w_gate.shape[1]
    bf = jnp.bfloat16
    grp = lax.axis_index("grp")
    ada_rows, ada_cols, bias_cols = w_ada.shape[0], w_ada.shape[1], b_ada.shape[0]
    fits = (
        lax.axis_size("grp") == 8
        and images == 2
        and width == HEADS * HDIM
        and w_qkv.shape[0] % 16 == 0
        and 4 * width % 4608 == 0
        and 2 * ff % 3072 == 0
        and w_down.shape[0] % 384 == 0
    )
    w_qp = jnp.concatenate([w_qkv, w_proj], axis=1)
    w_gu = jnp.concatenate([w_gate, w_up], axis=1)
    full = lambda w: w.reshape(-1, w.shape[-1])
    onehot = (group_ids[:, None] == jnp.arange(GROUPS, dtype=jnp.int32)[None, :]).astype(jnp.float32)
    cond_rows = lax.dynamic_slice_in_dim(cond_table, grp * ada_rows, ada_rows, axis=1)
    sigmoid = jax.nn.sigmoid(cond_rows)
    silu_rows = (cond_rows * sigmoid).astype(bf)
    silu_slope = sigmoid * (1.0 + cond_rows * (1.0 - sigmoid))
    mod_part = jnp.dot(silu_rows, w_ada, preferred_element_type=jnp.float32)
    bias_part = lax.dynamic_update_slice_in_dim(
        jnp.zeros((ada_cols,), jnp.float32), b_ada.astype(jnp.float32), grp * bias_cols, axis=0
    )
    mod_part = mod_part + bias_part[None, :]
    live_mask = (jnp.arange(images, dtype=jnp.int32) < live_count[0]).astype(jnp.float32)

    gains = jnp.stack([jnp.tile(q_gain, HEADS), jnp.tile(k_gain, HEADS)])
    x = patches.reshape(images, length, width)
    groups = jnp.pad(onehot.T, ((0, 0), (0, LANES - images)))
    band = jnp.broadcast_to(band_order.astype(jnp.float32)[:, None], (1, LANES))
    common = (groups, gains, band, cols)
    if fits:
        shards = [w_qp, w_gu, w_down]
        cuts = [half_cuts(0, 1, 0, 4 * width, 1, 1), half_cuts(1, 1, 0, 2 * ff, 4, 1)]
        cuts += [half_cuts(2, 0, 0, w_down.shape[0], 4, 1)]
    else:
        qp_all, gu_all, down_all = (lax.all_gather(w, "grp", axis=0, tiled=True) for w in (w_qp, w_gu, w_down))
        mod_part = lax.psum(mod_part, "grp")
        shards, cuts = [qp_all], []
    outs = forward(x, mod_part, *common, shards, cuts)
    normed_one, query, nq, nk, rq, rk, attended, inv, mod = outs[:9]
    tables, kv_all, rest = outs[9:12], outs[12], outs[13:]
    if fits:
        qp_all, gu_all, down_all = (full(w) for w in rest)
    live = jnp.broadcast_to(live_mask[:, None], (images, LANES))
    flat = lambda a: a.reshape(images * length, a.shape[-1])
    patches_out, d_middle, d_proj, d_attended, mid_sums, d_w_gu, d_w_down = mlp_block(
        x, grad_out.reshape(images, length, width), attended, mod, live, qp_all, gu_all, down_all
    )
    patches_out = patches_out.reshape(images, rows, cols, width)
    mod = mod.reshape(images, 6, width)
    d_query, d_kv, *rest = attention_backward(
        query,
        d_attended,
        jnp.swapaxes(inv, 1, 2),
        kv_all,
        [d_w_gu.reshape(2, -1, w_gate.shape[0], ff)] if fits else [],
        [half_cuts(0, 1, None, 2 * ff, 4, 1)] if fits else [],
        (2, 2, 1, 2),
    )
    d_qkv, d_x, sums = qkv_backward(
        x, mod, d_middle, d_query, d_kv, nq, nk, rq, rk, qp_all, gains, tables
    )
    d_patches = d_x.reshape(images, rows, cols, width)
    d_w_qp = weight_grads(flat(normed_one), flat(attended), flat(d_qkv), flat(d_proj))
    if fits:
        tags = jnp.repeat(onehot * (1.0 / lax.axis_size("band")), 6, axis=0)
        tags = jnp.pad(tags, ((0, 0), (0, LANES - GROUPS)))
        cuts = [half_cuts(0, 0, 0, w_down.shape[0], 2, 1), half_cuts(1, 1, 0, 4 * width, 8, 5)]
        d_gu = rest[0]
        d_down, d_qp, gathered, cond_blocks = scatter(
            [by_shard(d_w_down), by_shard(d_w_qp)], cuts, (2, 1, 0, 2), sums, mid_sums, tags, w_ada, silu_slope
        )
        d_mod_all = gathered[:, :GAIN_ROW, :width].reshape(-1, ada_cols)
        onehot_all = gathered[:, 0:GAIN_ROW:6, width : width + GROUPS].reshape(-1, GROUPS)
        gain_all = gathered[:, GAIN_ROW:, :width].astype(jnp.float32).reshape(-1, 2, 2, HEADS, HDIM)
        gain_all = jnp.sum(gain_all, axis=(0, 1, 3))
        d_cond = jnp.swapaxes(cond_blocks[:, :, :ada_rows], 0, 1).reshape(GROUPS, -1)
    else:
        d_gu, d_down, d_qp = (
            lax.psum(lax.psum_scatter(w, "grp", scatter_dimension=w.ndim - 2, tiled=True), "band")
            for w in (d_w_gu, d_w_down, d_w_qp)
        )
        d_mod_part = jnp.concatenate([sums[:, 0:2], mid_sums], axis=1)
        gain_part = jnp.sum(sums[:, 2:4].reshape(images, 2, HEADS, HDIM), axis=(0, 2))
        d_modulation = lax.psum(d_mod_part.reshape(images, ada_cols), "band").astype(bf)
        gain_all = lax.psum(gain_part, ("grp", "band"))
        payload = jnp.concatenate([d_modulation, onehot.astype(bf)], axis=1)
        payload = lax.all_gather(payload, "grp", axis=0, tiled=True)
        d_mod_all, onehot_all = payload[:, :ada_cols], payload[:, ada_cols:]
        d_silu = jnp.einsum("be,de->bd", d_mod_all, w_ada, preferred_element_type=jnp.float32)
        d_silu = jnp.dot(
            onehot_all.astype(jnp.float32).T,
            d_silu,
            precision=lax.Precision.HIGHEST,
            preferred_element_type=jnp.float32,
        )
        d_cond = lax.all_gather(d_silu * silu_slope, "grp", axis=1, tiled=True)
    silu_all = jnp.dot(onehot_all, silu_rows, preferred_element_type=jnp.float32).astype(bf)
    d_w_ada = jnp.einsum("bd,be->de", silu_all, d_mod_all, preferred_element_type=jnp.float32)
    d_b_ada = lax.dynamic_slice_in_dim(
        jnp.sum(d_mod_all.astype(jnp.float32), axis=0), grp * bias_cols, bias_cols, axis=0
    )
    wide = lambda a: a.astype(jnp.float32)
    return (
        patches_out,
        d_patches,
        d_cond,
        d_w_ada,
        d_b_ada,
        wide(d_qp[:, : 3 * width]),
        gain_all[0],
        gain_all[1],
        wide(d_qp[:, 3 * width :]),
        wide(d_gu[0]),
        wide(d_gu[1]),
        wide(d_down),
    )


def solution(mesh):
    in_specs = (
        P("grp", "band", None, None),
        P("grp", "band", None, None),
        P(),
        P("grp"),
        P("grp"),
        P("band"),
        P("grp", None),
        P("grp"),
        P("grp", None),
        P(),
        P(),
        P("grp", None),
        P("grp", None),
        P("grp", None),
        P("grp", None),
    )
    out_specs = (
        P("grp", "band", None, None),
        P("grp", "band", None, None),
        P(),
        P("grp", None),
        P("grp"),
        P("grp", None),
        P(),
        P(),
        P("grp", None),
        P("grp", None),
        P("grp", None),
        P("grp", None),
    )
    return jax.shard_map(body, mesh=mesh, in_specs=in_specs, out_specs=out_specs, check_vma=False)
```

```python
import functools
import math

import jax
import jax.numpy as jnp
from jax import lax
from jax.experimental import pallas as pl
from jax.experimental.pallas import tpu as pltpu
from jax.sharding import PartitionSpec as P

HEADS = 16
HDIM = 72
GROUPS = 8
LANES = 128
EPS = 1e-06
LOG2E = 1.4426950408889634

MESH = pl.DeviceIdType.MESH


class Place:
    def __init__(self):
        self.g, self.band = lax.axis_index("grp"), lax.axis_index("band")
        self.z, self.x = self.g // 2, self.g % 2
        self.y, self.c = self.band // 2, self.band % 2
        z = self.z
        self.far = [z, z + 1 - 2 * (z % 2), 2 - z // 2, 3 - 3 * (z // 2)]
        self.ypeer = (self.g, (1 - self.y) * 2 + self.c)
        self.cpeer = (self.g, self.y * 2 + 1 - self.c)
        self.xpeer = (z * 2 + 1 - self.x, self.band)
        self.draining = False

    def line(self, zz):
        return (zz * 2 + self.x, self.band)

    def greet(self, peers):
        bar = pltpu.get_barrier_semaphore()
        for d in peers:
            pl.semaphore_signal(bar, inc=1, device_id=d, device_id_type=MESH)
        pl.semaphore_wait(bar, len(peers))

    def greet_band(self):
        self.greet([self.ypeer, self.cpeer])

    def greet_all(self):
        self.greet([self.xpeer, self.ypeer, self.cpeer] + [self.line(zz) for zz in self.far[1:]])

    def copy(self, src, dst, ssem, rsem, dev):
        return pltpu.make_async_remote_copy(
            src_ref=src, dst_ref=dst, send_sem=ssem, recv_sem=rsem, device_id=dev, device_id_type=MESH
        )

    def send(self, src, dst, ssem, rsem, dev, cond=None):
        d = self.copy(src, dst, ssem, rsem, dev)
        act = d.wait_send if self.draining else d.start
        if cond is None:
            act()
        else:
            pl.when(cond)(act)

    def keep(self, src, dst, sem):
        d = pltpu.make_async_copy(src, dst, sem)
        d.wait() if self.draining else d.start()

    def arrived(self, ref, rsem):
        if not self.draining:
            self.copy(ref, ref, rsem, rsem, self.ypeer).wait_recv()

    def drain(self, steps):
        self.draining = True
        for step in steps:
            step()
        self.draining = False


def span(ref, axis, start, size):
    if axis == 0:
        return ref.at[pl.ds(pl.multiple_of(start, 16), size), :]
    return ref.at[:, pl.ds(pl.multiple_of(start, LANES), size)]


def gather_sems(n):
    s = pltpu.SemaphoreType.DMA
    return [s((n,)), s((n, 4)), s((n, 4)), s((n, 4)), s((n, 4)), s((n, 7)), s((n, 7)), s((n, 14)), s((n, 14)), s((n,))]


def gather_steps(at, cuts, ins, outs, sems):
    n = len(cuts)
    lsem, zs, zr, xs, xr, ys, yr, cs, cr, ds = sems
    ins, outs = ([refs[cut[5]] for cut in cuts] for refs in (ins, outs))
    soon = sum(cut[5] == 0 for cut in cuts)
    x, y, z, c, far = at.x, at.y, at.z, at.c, at.far

    def piece(i, ref, yy, cc):
        axis, half, a, b, base, _ = cuts[i]
        return span(ref, axis, base + cc * half + yy * b, a + b)

    def bpart(i, ref, yy, cc):
        axis, half, a, b, base, _ = cuts[i]
        return span(ref, axis, base + cc * half + yy * (a + b), b)

    def own(i):
        src, dst = piece(i, ins[i], y, c), piece(i, outs[i].at[at.g], y, c)
        at.send(src, dst, zs.at[i, 0], zr.at[i, z], (at.g + 2, at.band), z < 3)
        at.send(src, dst, ds.at[i], zr.at[i, z], (at.g - 2, at.band), z > 0)
        at.send(src, dst, xs.at[i, 0], xr.at[i, 0], at.xpeer)
        if cuts[i][4] == 0 and not (at.draining and cuts[i][5] == 0):
            at.keep(ins[i], outs[i].at[at.g], lsem.at[i])

    def down(i, slot, shard):
        p = bpart(i, outs[i].at[shard], y, c)
        at.send(p, p, ys.at[i, slot], yr.at[i, slot], at.ypeer)
        p = piece(i, outs[i].at[shard], y, c)
        at.send(p, p, cs.at[i, slot], cr.at[i, slot], at.cpeer)

    def zarr(i, t):
        zz = far[t]
        s = zz * 2 + x
        p = piece(i, outs[i].at[s], y, c)
        at.arrived(p, zr.at[i, zz])
        nxt = jnp.where(zz < z, z + 1, z - 1)
        at.send(p, p, zs.at[i, t], zr.at[i, zz], at.line(jnp.clip(nxt, 0, 3)), (nxt >= 0) & (nxt <= 3))
        at.send(p, p, xs.at[i, t], xr.at[i, t], at.xpeer)
        down(i, t - 1, s)

    def xarr(i, t):
        s = far[t] * 2 + 1 - x
        at.arrived(piece(i, outs[i].at[s], y, c), xr.at[i, t])
        down(i, 3 + t, s)

    def yarr(i, slot, s):
        p = bpart(i, outs[i].at[s], 1 - y, c)
        at.arrived(p, yr.at[i, slot])
        at.send(p, p, cs.at[i, 7 + slot], cr.at[i, 7 + slot], at.cpeer)

    slots = [(t - 1, far[t] * 2 + x) for t in (1, 2, 3)]
    slots += [(3 + t, far[t] * 2 + 1 - x) for t in range(4)]
    order = [slots[k] for k in (3, 0, 4, 1, 5, 2, 6)]
    steps = [lambda: own(0)]
    for i in range(n):
        mine = [lambda i=i: zarr(i, 1)]
        if 0 < i and i + 1 < n:
            mine.append(lambda i=i: own(i + 1))
        mine.append(lambda i=i: xarr(i, 0))
        for t in (2, 3):
            mine.append(lambda i=i, t=t: zarr(i, t))
            if i == 0 and t == 3 and n > 1:
                mine.append(lambda: own(1))
            mine.append(lambda i=i, t=t: xarr(i, t - 1))
        mine.append(lambda i=i: xarr(i, 3))
        if i > 0:
            late = [lambda i=i, k=k: yarr(i - 1, *order[k]) for k in range(7)]
            pace, held = 3 if i == soon else 1, list(late)
            merged = []
            while late or mine:
                merged += late[:pace] + mine[:1]
                late, mine = late[pace:], mine[1:]
            mine = merged
        if i == soon:
            first = len(steps) + max(k for k, step in enumerate(mine) if step in held) + 1
        steps += mine
    steps += [lambda k=k: yarr(n - 1, *order[k]) for k in range(7)]

    def last(i):
        for slot, s in slots:
            at.arrived(piece(i, outs[i].at[s], y, 1 - c), cr.at[i, slot])
            at.arrived(bpart(i, outs[i].at[s], 1 - y, 1 - c), cr.at[i, 7 + slot])

    return steps, first, last


def add_into(dst, src):
    def step(r, _):
        rows = pl.ds(pl.multiple_of(r * 16, 16), 16)
        dst[rows, :] = dst[rows, :] + src[rows, :]
        return 0

    lax.fori_loop(0, src.shape[0] // 16, step, 0)


def move_into(dst, src):
    def step(r, _):
        rows = pl.ds(pl.multiple_of(r * 16, 16), 16)
        dst[rows, :] = src[rows, :]
        return 0

    lax.fori_loop(0, src.shape[0] // 16, step, 0)


def scatter_scratch(grads, cuts):
    n = len(cuts)
    s = pltpu.SemaphoreType.DMA

    def buf(lead, k, size):
        rows, cols = grads[cuts[k][5]].shape[-2:]
        shape = (rows, size) if cuts[k][0] == 1 else (size, cols)
        return pltpu.VMEM(lead + shape, jnp.bfloat16)

    out = []
    for lead, pick in (
        ((8,), lambda c: c[1]),
        ((8,), lambda c: c[1]),
        ((8,), lambda c: c[3]),
        ((4,), lambda c: c[2] + c[3]),
        ((5,), lambda c: c[2] + c[3]),
        ((), lambda c: c[2] + c[3]),
    ):
        out += [buf(lead, k, pick(cuts[k])) for k in range(n)]
    out += [s((n, 8))] * 5 + [s((n, 4))] * 2 + [s((n, 3)), s((n, 5))] + [s((n,))] * 5
    return out


def scatter_steps(at, cuts, ins, outs, scratch, lags):
    n = len(cuts)
    own_half, core_buf, y_buf, x_buf, z_buf, fin_buf = (scratch[k * n : (k + 1) * n] for k in range(6))
    ls, cs, cr, ys, yr, xs, xr, zs, zr, fs, fr, es, er, ws = scratch[6 * n :]
    x, y, z, c, far = at.x, at.y, at.z, at.c, at.far
    ins, outs = ([refs[cut[5]] for cut in cuts] for refs in (ins, outs))

    def in_half(i, s, cc):
        axis, half, _, _, base, _ = cuts[i]
        if base is None:
            return ins[i].at[cc, s]
        return span(ins[i].at[s], axis, base + cc * half, half)

    def out_half(i, cc):
        axis, half, _, _, base, _ = cuts[i]
        if base is None:
            return outs[i].at[cc]
        return span(outs[i], axis, base + cc * half, half)

    def piece(i, ref):
        _, _, a, b = cuts[i][:4]
        return span(ref, cuts[i][0], y * b, a + b)

    def bpart(i, ref, yy):
        _, _, a, b = cuts[i][:4]
        return span(ref, cuts[i][0], yy * (a + b), b)

    order = [(t, j) for t in (3, 2, 1, 0) for j in (1, 0)]

    def shard(t, j):
        return far[t] * 2 + (1 - x if j else x)

    def load(i, t, j):
        s, q = shard(t, j), order.index((t, j))
        return pltpu.make_async_copy(in_half(i, s, c), own_half[i].at[s], ls.at[i, q])

    def give(i, t, j):
        s, q = shard(t, j), order.index((t, j))
        src = in_half(i, s, 1 - c)
        at.send(src, core_buf[i].at[s], cs.at[i, q], cr.at[i, s], at.cpeer)
        if not at.draining:
            load(i, t, j).start()

    def to_y(i, t, j):
        s = shard(t, j)
        src = bpart(i, own_half[i].at[s], 1 - y)
        return at.copy(src, y_buf[i].at[s], ys.at[i, order.index((t, j))], yr.at[i, s], at.ypeer)

    def to_fin(i):
        return at.copy(piece(i, own_half[i].at[at.g]), fin_buf[i], fs.at[i], fr.at[i], at.ypeer)

    def cadd(i, t, j):
        s = shard(t, j)
        if at.draining:
            if (t, j) != (0, 0):
                to_y(i, t, j).wait_send()
            return
        load(i, t, j).wait()
        at.arrived(core_buf[i].at[s], cr.at[i, s])
        add_into(own_half[i].at[s], core_buf[i].at[s])
        to_y(i, t, j).start()

    def yadd(i, t, j):
        s = shard(t, j)
        at.arrived(y_buf[i].at[s], yr.at[i, s])
        if not at.draining:
            add_into(bpart(i, own_half[i].at[s], y), y_buf[i].at[s])
        if j:
            at.send(piece(i, own_half[i].at[s]), x_buf[i].at[far[t]], xs.at[i, t], xr.at[i, far[t]], at.xpeer)

    def xadd(i, t):
        if at.draining:
            return
        at.arrived(x_buf[i].at[far[t]], xr.at[i, far[t]])
        add_into(piece(i, own_half[i].at[shard(t, 0)]), x_buf[i].at[far[t]])

    def zadd(i, t):
        zz = far[t]
        p = piece(i, own_half[i].at[shard(t, 0)])

        def join(cond, slot):
            def do():
                at.arrived(z_buf[i].at[slot], zr.at[i, slot])
                add_into(p, z_buf[i].at[slot])

            if not at.draining:
                pl.when(cond)(do)

        if t > 0:
            inc = jnp.where(zz < z, z + 1, z - 1)
            join((inc >= 0) & (inc <= 3), zz)
            nxt = jnp.where(zz < z, z - 1, z + 1)
            slot = jnp.where((zz < z) & (nxt == zz), 4, zz)
            at.send(p, z_buf[i].at[slot], zs.at[i, t - 1], zr.at[i, slot], at.line(nxt))
        else:
            join(z > 0, z)
            join(z < 3, 4)
            if not at.draining:
                to_fin(i).start()

    def fin(i):
        axis, half, a, b, base, _ = cuts[i]
        own = own_half[i].at[at.g]
        if not at.draining:
            at.arrived(fin_buf[i], fr.at[i])
            to_fin(i).wait_send()
            to_y(i, 0, 0).wait_send()
            for yy in (0, 1):

                @pl.when(y == 1 - yy)
                def _():
                    add_into(span(own, axis, b, a), span(fin_buf[i], axis, b if yy == 0 else 0, a))
                    move_into(span(own, axis, yy * (a + b), b), span(fin_buf[i], axis, 0 if yy == 0 else a, b))

        o = out_half(i, c)
        at.send(own, o, es.at[i], er.at[i], at.cpeer)
        at.keep(own, o, ws.at[i])

    seq = [(i, t, j) for i in range(n) for (t, j) in order]
    opening = [functools.partial(give, *p) for p in seq]
    ly, lx, lz, lf = lags
    todo = []
    for q, (i, t, j) in enumerate(seq):
        todo.append((q, 0, functools.partial(cadd, i, t, j)))
        todo.append((q + ly, 1, functools.partial(yadd, i, t, j)))
        if j == 0:
            todo.append((q + ly + lx, 2, functools.partial(xadd, i, t)))
            todo.append((q + ly + lx + lz, 3, functools.partial(zadd, i, t)))
            if t == 0:
                todo.append((q + ly + lx + lz + lf, 4, functools.partial(fin, i)))
    todo.sort(key=lambda p: p[:2])

    def last():
        for i in range(n):
            at.arrived(out_half(i, 1 - c), er.at[i])

    return opening, [f for _, _, f in todo], last


def head_window(h):
    first = jnp.minimum(h * HDIM // LANES, HEADS * HDIM // LANES - 2) * LANES
    lane = lax.broadcasted_iota(jnp.int32, (1, 2 * LANES), 1) + first
    inside = (lane >= h * HDIM) & (lane < h * HDIM + HDIM)
    return pl.ds(pl.multiple_of(first, LANES), 2 * LANES), inside


def dot_t(left, right):
    return lax.dot_general(left, right, (((1,), (1,)), ((), ())), preferred_element_type=jnp.float32)


def first_dot(left, right):
    return lax.dot_general(left, right, (((0,), (0,)), ((), ())), preferred_element_type=jnp.float32)


def pick_dot(values, chosen):
    high = values.astype(jnp.bfloat16)
    low = (values - high.astype(jnp.float32)).astype(jnp.bfloat16)
    return jnp.dot(high, chosen, preferred_element_type=jnp.float32) + jnp.dot(
        low, chosen, preferred_element_type=jnp.float32
    )


def head_pick(width):
    row = lax.broadcasted_iota(jnp.int32, (width, LANES), 0)
    first = lax.broadcasted_iota(jnp.int32, (width, LANES), 1) * HDIM
    return ((row >= first) & (row < first + HDIM)).astype(jnp.float32).astype(jnp.bfloat16)


def head_spread(width):
    lane = lax.broadcasted_iota(jnp.int32, (LANES, width), 1)
    first = lax.broadcasted_iota(jnp.int32, (LANES, width), 0) * HDIM
    return ((lane >= first) & (lane < first + HDIM)).astype(jnp.float32).astype(jnp.bfloat16)


def rope_tables(band, rows, cols, width):
    quarter = HDIM // 4
    shape = (rows * cols, width)
    token = lax.broadcasted_iota(jnp.int32, shape, 0)
    lane = lax.broadcasted_iota(jnp.int32, shape, 1) % HDIM
    power = (lane % quarter).astype(jnp.float32) * (-math.log(10000.0) / quarter)
    by_row = band * rows + (token // cols).astype(jnp.float32)
    index = jnp.where(lane < 2 * quarter, by_row, (token % cols).astype(jnp.float32))
    angle = index * jnp.exp(power)
    sine = jnp.sin(angle)
    low = (lane // quarter) % 2 == 0
    return jnp.cos(angle), jnp.where(low, -sine, 0.0), jnp.where(low, 0.0, sine)


def turn(values, cos, sin_next, sin_prev):
    width = values.shape[-1]
    after = pltpu.roll(values, width - HDIM // 4, 1)
    before = pltpu.roll(values, HDIM // 4, 1)
    return values * cos + after * sin_next + before * sin_prev


def turn_back(values, cos, sin_next, sin_prev):
    width = values.shape[-1]
    after = pltpu.roll(values, width - HDIM // 4, 1)
    before = pltpu.roll(values, HDIM // 4, 1)
    return values * cos - after * sin_next - before * sin_prev


def qkv_back_kernel(
    x_ref, mod_ref, mid_ref, dq_ref, dk_ref, dv_ref, nq_ref, nk_ref, rq_ref, rk_ref, w_ref,
    gains_ref, cos_ref, next_ref, prev_ref,
    dqkv_ref, dx_ref, sums_ref, w_buf, w_sem,
):
    width = x_ref.shape[-1]
    load = pltpu.make_async_copy(w_ref.at[:, pl.ds(0, 3 * width)], w_buf, w_sem)
    pl.when(pl.program_id(0) == 0)(load.start)
    tables = (cos_ref[...], next_ref[...], prev_ref[...])
    pick, spread = head_pick(width), head_spread(width)
    ins = ((dq_ref, nq_ref, rq_ref), (dk_ref, nk_ref, rk_ref))
    for part, (d_ref, n_ref, r_ref) in enumerate(ins):
        back = turn_back(d_ref[0].astype(jnp.float32) * HDIM ** (-0.5), *tables)
        unit = n_ref[0]
        sums_ref[0, 2 + part : 3 + part, :] = jnp.sum(back * unit, axis=0, keepdims=True)
        inner = back * gains_ref[part : part + 1, :]
        mean = pick_dot(inner * unit, pick) * (1.0 / HDIM)
        grad = (inner - unit * pick_dot(mean, spread)) * pick_dot(r_ref[0], spread)
        dqkv_ref[0, :, part * width : (part + 1) * width] = grad.astype(jnp.bfloat16)
    dqkv_ref[0, :, 2 * width : 3 * width] = dv_ref[0]
    pl.when(pl.program_id(0) == 0)(load.wait)
    d_normed = dot_t(dqkv_ref[0], w_buf[...])
    x = x_ref[0].astype(jnp.float32)
    root = lax.rsqrt(jnp.mean(x * x, axis=-1, keepdims=True) + EPS)
    unit = x * root
    sums_ref[0, 0:1, :] = jnp.sum(d_normed, axis=0, keepdims=True)
    sums_ref[0, 1:2, :] = jnp.sum(d_normed * unit, axis=0, keepdims=True)
    inner = d_normed * (1.0 + mod_ref[0, 1:2, :])
    dx_ref[0] = mid_ref[0] + root * (inner - unit * jnp.mean(inner * unit, axis=-1, keepdims=True))


def qkv_backward(x, mod, d_mid, dq, d_kv, nq, nk, rq, rk, qp_all, gains, tables):
    images, length, width = x.shape
    row = lambda w: pl.BlockSpec((1, length, w), lambda i: (i, 0, 0))
    whole = lambda a: pl.BlockSpec(a.shape, lambda i: (0,) * a.ndim)
    return pl.pallas_call(
        qkv_back_kernel,
        grid=(images,),
        in_specs=[row(width), pl.BlockSpec((1, 6, width), lambda i: (i, 0, 0))]
        + [row(width)] * 2
        + [pl.BlockSpec((None, 1, length, width), lambda i, s=s: (s, i, 0, 0)) for s in (0, 1)]
        + [row(width)] * 2
        + [row(LANES)] * 2
        + [pl.BlockSpec(memory_space=pl.ANY), whole(gains)]
        + [whole(t) for t in tables],
        out_shape=[
            jax.ShapeDtypeStruct((images, length, 3 * width), jnp.bfloat16),
            jax.ShapeDtypeStruct((images, length, width), jnp.float32),
            jax.ShapeDtypeStruct((images, 4, width), jnp.float32),
        ],
        out_specs=[row(3 * width), row(width), pl.BlockSpec((1, 4, width), lambda i: (i, 0, 0))],
        scratch_shapes=[pltpu.VMEM((width, 3 * width), jnp.bfloat16), pltpu.SemaphoreType.DMA],
        compiler_params=pltpu.CompilerParams(vmem_limit_bytes=60 * 2**20),
        name="qkv_backward",
    )(x, mod, d_mid, dq, d_kv, d_kv, nq, nk, rq, rk, qp_all, gains, *tables)


def weight_kernel(normed_ref, att_ref, dqkv_ref, dproj_ref, out_ref, turned):
    step = pl.program_id(0)

    @pl.when(step == 0)
    def _():
        turned[...] = normed_ref[...].T

    @pl.when(step == 3)
    def _():
        turned[...] = att_ref[...].T
        out_ref[...] = jnp.dot(turned[...], dproj_ref[...], preferred_element_type=jnp.float32).astype(jnp.bfloat16)

    @pl.when(step < 3)
    def _():
        out_ref[...] = jnp.dot(turned[...], dqkv_ref[...], preferred_element_type=jnp.float32).astype(jnp.bfloat16)


def weight_grads(normed, attended, d_qkv, d_proj):
    tokens, width = normed.shape
    whole = pl.BlockSpec((tokens, width), lambda k: (0, 0))
    return pl.pallas_call(
        weight_kernel,
        grid=(4,),
        in_specs=[whole, whole, pl.BlockSpec((tokens, width), lambda k: (0, jnp.minimum(k, 2))), whole],
        out_shape=jax.ShapeDtypeStruct((width, 4 * width), jnp.bfloat16),
        out_specs=pl.BlockSpec((width, width), lambda k: (0, k)),
        scratch_shapes=[pltpu.VMEM((width, tokens), jnp.bfloat16)],
        compiler_params=pltpu.CompilerParams(vmem_limit_bytes=60 * 2**20),
        name="weight_grads",
    )(normed, attended, d_qkv, d_proj)


def tail_scratch():
    s = pltpu.SemaphoreType.DMA
    wide = SMALL_COLS
    return [
        pltpu.VMEM((SMALL_ROWS, wide), jnp.float32),
        pltpu.VMEM((2, SMALL_ROWS, wide), jnp.float32),
        pltpu.VMEM((8, SMALL_ROWS, wide), jnp.bfloat16),
        pltpu.VMEM((8, GROUPS, 2 * LANES), jnp.float32),
        s((8,)),
        s((8,)),
    ]


def tail_steps(at, ins, outs, scratch):
    sums_ref, mid_ref, tag_ref, ada_ref, slope_ref = ins
    all_ref, cond_ref = outs
    acc, inbox, blocks, cond, ss, rs = scratch
    width = HEADS * HDIM
    z = at.z
    line = (at.xpeer, at.line(at.far[1]), at.line((z + 2) % 4))

    def copy(r):
        if r < 2:
            return at.copy(acc, inbox.at[r], ss.at[r], rs.at[r], (at.cpeer, at.ypeer)[r])
        ref, k = (blocks, r - 2) if r < 5 else (cond, r - 5)
        start, size = ((at.g, 1), (2 * z, 2), (4 * (z // 2), 4))[k]
        src = ref.at[pl.ds(start, size)]
        return at.copy(src, src, ss.at[r], rs.at[r], line[k])

    def collect():
        acc[...] = jnp.zeros_like(acc)
        for i in range(2):
            acc[6 * i : 6 * i + 2, :width] = sums_ref[i, 0:2, :]
            acc[6 * i + 2 : 6 * i + 6, :width] = mid_ref[i]
        acc[:GAIN_ROW, width:] = tag_ref[...]
        gains = sums_ref[0, 2:4, :] + sums_ref[1, 2:4, :]
        acc[GAIN_ROW : GAIN_ROW + 2, :width] = gains
        acc[GAIN_ROW + 2 :, :width] = gains

    def pack():
        row = lax.broadcasted_iota(jnp.int32, (SMALL_ROWS, 1), 0)
        value = acc[...]
        rest = value - value.astype(jnp.bfloat16).astype(jnp.float32)
        blocks[at.g] = jnp.where(row >= GAIN_ROW + 2, rest, value).astype(jnp.bfloat16)

    def cond_rows():
        flat = blocks[...].reshape(8 * SMALL_ROWS, SMALL_COLS)
        row = lax.broadcasted_iota(jnp.int32, (8 * SMALL_ROWS, 1), 0) % SMALL_ROWS
        silu = jnp.zeros((8 * SMALL_ROWS, ada_ref.shape[0]), jnp.float32)
        for k in range(6):
            product = dot_t(flat[:, :width], ada_ref[:, k * width : (k + 1) * width])
            silu = jnp.where((row % 6 == k) & (row < GAIN_ROW), product, silu)
        by_group = lax.dot_general(
            flat[:, width:].astype(jnp.float32),
            silu,
            (((0,), (0,)), ((), ())),
            precision=lax.Precision.HIGHEST,
            preferred_element_type=jnp.float32,
        )
        cond[at.g] = jnp.zeros((GROUPS, 2 * LANES), jnp.float32)
        cond[at.g, :, : ada_ref.shape[0]] = by_group[:GROUPS] * slope_ref[...]

    def step(r):
        if at.draining:
            return
        if r > 0:
            copy(r - 1).wait()
        if r == 0:
            collect()
        elif r <= 2:
            acc[...] = acc[...] + inbox[r - 1]
        if r == 2:
            pack()
        if r == 5:
            cond_rows()
        if r < 8:
            copy(r).start()
        else:
            all_ref[...] = blocks[...]
            cond_ref[...] = cond[...]

    return [functools.partial(step, r) for r in range(9)]


SMALL_ROWS, SMALL_COLS, GAIN_ROW = 16, HEADS * HDIM + LANES, 12


def scatter_kernel(n, cuts, lags, *refs):
    at = Place()
    at.greet_all()
    ins, small_in = refs[:n], refs[n : n + 5]
    outs, small_out = refs[n + 5 : 2 * n + 5], refs[2 * n + 5 : 2 * n + 7]
    small = tail_steps(at, small_in, small_out, refs[2 * n + 7 : 2 * n + 13])
    opening, steps, last = scatter_steps(at, cuts, ins, outs, refs[2 * n + 13 :], lags)
    small[0]()
    for step in opening:
        step()
    small = small[1:]
    for k, step in enumerate(steps):
        step()
        if k % 6 == 5 and small:
            small[0]()
            small = small[1:]
    for step in small:
        step()
    last()
    at.drain(opening + steps)


def scatter(grads, cuts, lags, sums, mid_sums, tags, w_ada, slope):
    n = len(grads)
    any_ref = pl.BlockSpec(memory_space=pl.ANY)
    vmem = pl.BlockSpec(memory_space=pltpu.VMEM)
    return pl.pallas_call(
        functools.partial(scatter_kernel, n, cuts, lags),
        out_shape=[jax.ShapeDtypeStruct(w.shape[1:], jnp.bfloat16) for w in grads]
        + [
            jax.ShapeDtypeStruct((8, SMALL_ROWS, SMALL_COLS), jnp.bfloat16),
            jax.ShapeDtypeStruct((8, GROUPS, 2 * LANES), jnp.float32),
        ],
        in_specs=[any_ref] * n + [vmem] * 5,
        out_specs=[any_ref] * n + [vmem] * 2,
        scratch_shapes=tail_scratch() + scatter_scratch(grads, cuts),
        compiler_params=pltpu.CompilerParams(
            collective_id=1, has_side_effects=True, vmem_limit_bytes=60 * 2**20
        ),
        name="gradient_scatter",
    )(*grads, sums, mid_sums, tags, w_ada, slope)


def forward_kernel(cuts, cols, refs):
    n = len(cuts)
    soon = sum(cut[5] == 0 for cut in cuts)
    at = Place()
    x_ref, *part_refs, group_ref, gains_ref, band_ref = refs["in"]
    normed_ref, q_ref, nq_ref, nk_ref, rq_ref, rk_ref, o_ref, inv_ref, mod_ref, *table_refs, kv_out = refs["out"]
    kv, w_buf, pick_ref, spread_ref, mod_buf, mod_in, w_sem, ms, mr, ks, kr, os = refs["scratch"]
    ins, outs = refs["shards"], refs["full"]
    images, length, width = x_ref.shape
    parts = [(i, s) for i in range(images) for s in (0, 1)]
    if n:
        at.greet_all()
        steps, first, last = gather_steps(at, cuts, ins, outs, refs["sems"])
    else:
        at.greet_band()
        steps, first, last = [], 0, None

    if n:
        silu_ref, ada_ref, bias_ref = part_refs
        silu = silu_ref[...].astype(jnp.bfloat16)
        mod_buf[...] = jnp.dot(silu, ada_ref[...], preferred_element_type=jnp.float32) + bias_ref[...]
    else:
        mod_buf[...] = part_refs[0][...]

    def mod_copy(r):
        peer = (at.xpeer, at.line(at.far[1]), at.line((at.z + 2) % 4))[r]
        return at.copy(mod_buf, mod_in.at[r], ms.at[r], mr.at[r], peer)

    def mod_step(r):
        if at.draining:
            return
        if r > 0:
            mod_copy(r - 1).wait()
            mod_buf[...] = mod_buf[...] + mod_in[r - 1]
        if r < 3:
            mod_copy(r).start()

    def rows(s, i, band):
        return kv.at[s, i, pl.ds(pl.multiple_of(band * length, 16), length), :]

    here, over = at.band, (1 - at.y) * 2 + at.c
    beside, across = at.y * 2 + 1 - at.c, (1 - at.y) * 2 + 1 - at.c

    def give(i, s):
        p = rows(s, i, here)
        at.send(p, p, ks.at[i, s, 0], kr.at[i, s, 0], at.ypeer)
        at.send(p, p, ks.at[i, s, 1], kr.at[i, s, 1], at.cpeer)

    def pass_on(i, s):
        p = rows(s, i, over)
        at.arrived(p, kr.at[i, s, 0])
        at.send(p, p, ks.at[i, s, 2], kr.at[i, s, 2], at.cpeer)

    def ready(i):
        for s in (0, 1):
            at.arrived(rows(s, i, beside), kr.at[i, s, 1])
            at.arrived(rows(s, i, across), kr.at[i, s, 2])
            at.keep(kv.at[s, i], kv_out.at[s, i], os.at[i, s])

    def norm(i):
        value = x_ref[i].astype(jnp.float32)
        root = lax.rsqrt(jnp.mean(value * value, axis=-1, keepdims=True) + EPS)
        chosen = jnp.sum(group_ref[:, i : i + 1] * mod_buf[...], axis=0, keepdims=True)
        mod_ref[i : i + 1, :] = chosen
        shift, scale = chosen[:, :width], chosen[:, width : 2 * width]
        normed_ref[i] = (value * root * (1.0 + scale) + shift).astype(jnp.bfloat16)

    def raw(i, part):
        return jnp.dot(
            normed_ref[i], w_buf[:, part * width : (part + 1) * width], preferred_element_type=jnp.float32
        )

    def project(i, part, n_ref, r_ref):
        values = raw(i, part)
        inv = lax.rsqrt(pick_dot(values * values, pick_ref[...]) * (1.0 / HDIM) + EPS)
        r_ref[i] = inv
        unit = values * pick_dot(inv, spread_ref[...])
        n_ref[i] = unit
        scaled = unit * gains_ref[part : part + 1, :]
        return turn(scaled, *(t[...] for t in table_refs)).astype(jnp.bfloat16)

    def key_part(i):
        norm(i)
        kv[0, i, pl.ds(pl.multiple_of(here * length, 16), length), :] = project(i, 1, nk_ref, rk_ref)
        give(i, 0)

    def value_part(i):
        kv[1, i, pl.ds(pl.multiple_of(here * length, 16), length), :] = raw(i, 2).astype(jnp.bfloat16)
        give(i, 1)

    def query_part(i):
        q_ref[i] = project(i, 0, nq_ref, rq_ref)

    def head(i, h):
        win, inside = head_window(h)
        query = q_ref[i, :, win]
        query = jnp.where(inside, query, jnp.zeros_like(query))
        power = jnp.exp2(dot_t(query, kv[0, i, :, win]) * (HDIM ** (-0.5) * LOG2E))
        inv = 1.0 / jnp.sum(power, axis=-1, keepdims=True)
        out = jnp.dot(
            (power * inv).astype(jnp.bfloat16), kv[1, i, :, win], preferred_element_type=jnp.float32
        )
        o_ref[i, :, win] = jnp.where(inside, out.astype(jnp.bfloat16), o_ref[i, :, win])
        lane = lax.broadcasted_iota(jnp.int32, (1, LANES), 1)
        inv_ref[i] = jnp.where(lane == h, inv, inv_ref[i])

    def prepare():
        pick_ref[...] = head_pick(width)
        spread_ref[...] = head_spread(width)

        def block(r, _):
            rows_of = pl.ds(pl.multiple_of(r * cols, cols), cols)
            row = band_ref[0:1, 0:1] * (length // cols) + r.astype(jnp.float32)
            for ref, value in zip(table_refs, rope_tables(row, 1, cols, width)):
                ref[rows_of, :] = value
            return 0

        lax.fori_loop(0, length // cols, block, 0)

    if not n:
        prepare()
    if n:
        for k in range(3):
            mod_step(k)
            for step in steps[2 * k : 2 * k + 2]:
                step()
                if k == 0 and step is steps[0]:
                    prepare()
        mod_step(3)
        for step in steps[6:first]:
            step()
        for i in range(soon):
            last(i)
        pltpu.make_async_copy(ins[0], outs[0].at[at.g], refs["sems"][0].at[0]).wait()
        loads = [
            pltpu.make_async_copy(
                outs[0].at[k, :, pl.ds(0, 3 * width)],
                w_buf.at[pl.ds(k * (width // 8), width // 8), :],
                w_sem.at[k],
            )
            for k in range(8)
        ]
    else:
        loads = [pltpu.make_async_copy(ins[0].at[:, pl.ds(0, 3 * width)], w_buf, w_sem.at[0])]
    for d in loads:
        d.start()
    o_ref[...] = jnp.zeros_like(o_ref)
    inv_ref[...] = jnp.zeros_like(inv_ref)
    for d in loads:
        d.wait()
    todo = steps[first:]
    for i in range(images):
        for work in (key_part, value_part):
            work(i)
            for step in todo[:2]:
                step()
            todo = todo[2:]
    for i in range(images):
        query_part(i)
        for step in todo[:2]:
            step()
        todo = todo[2:]
    for i in range(images):
        pass_on(i, 0)
        pass_on(i, 1)
        ready(i)
        mine, todo = (todo[: HEADS // 2], todo[HEADS // 2 :])

        def body(h, _, i=i, mine=mine):
            for k, step in enumerate(mine):
                pl.when(h == 2 * k)(step)
            head(i, h)
            return 0

        lax.fori_loop(0, HEADS, body, 0)
    for step in todo:
        step()
    for i in range(soon, n):
        last(i)
    at.drain(steps)
    for i, s in parts:
        at.drain([functools.partial(give, i, s), functools.partial(pass_on, i, s)])
    for i in range(images):
        at.drain([functools.partial(ready, i)])


def forward(x, mod_parts, groups, gains, band, cols, shards, cuts):
    n = len(cuts)
    images, length, width = x.shape
    bands = lax.axis_size("band")
    keys = (2, images, bands * length, width)
    s = pltpu.SemaphoreType.DMA
    bf = jnp.bfloat16
    any_ref = pl.BlockSpec(memory_space=pl.ANY)
    vmem = pl.BlockSpec(memory_space=pltpu.VMEM)
    args = [x, *mod_parts, groups, gains, band]
    table = (GROUPS, mod_parts[-1].shape[1])
    rows = lambda w, d: jax.ShapeDtypeStruct((images, length, w), d)
    outs = [rows(width, bf)] * 2 + [rows(width, jnp.float32)] * 2 + [rows(LANES, jnp.float32)] * 2
    outs += [rows(width, bf), rows(LANES, jnp.float32), jax.ShapeDtypeStruct((images, table[1]), jnp.float32)]
    outs += [jax.ShapeDtypeStruct((length, width), jnp.float32)] * 3
    scratch = [
        pltpu.VMEM(keys, bf),
        pltpu.VMEM((width, 3 * width), bf),
        pltpu.VMEM((width, LANES), bf),
        pltpu.VMEM((LANES, width), bf),
        pltpu.VMEM(table, jnp.float32),
        pltpu.VMEM((3,) + table, jnp.float32),
        s((8,)),
        s((3,)),
        s((3,)),
        s((images, 2, 3)),
        s((images, 2, 3)),
        s((images, 2)),
    ]
    whole = len(shards) if n else 0
    sizes = [len(args), len(shards), len(outs) + 1, whole, len(scratch), 10 if n else 0]

    def kernel(*refs):
        groups_of, start = [], 0
        for size in sizes:
            groups_of.append(refs[start : start + size])
            start += size
        names = ("in", "shards", "out", "full", "scratch", "sems")
        forward_kernel(cuts, cols, dict(zip(names, groups_of)))

    return pl.pallas_call(
        kernel,
        out_shape=outs
        + [jax.ShapeDtypeStruct(keys, bf)]
        + [jax.ShapeDtypeStruct((8,) + w.shape, w.dtype) for w in shards[:whole]],
        in_specs=[vmem] * len(args) + [any_ref] * len(shards),
        out_specs=[vmem] * len(outs) + [any_ref] * (1 + whole),
        scratch_shapes=scratch + (gather_sems(n) if n else []),
        compiler_params=pltpu.CompilerParams(
            collective_id=2, has_side_effects=True, vmem_limit_bytes=60 * 2**20
        ),
        name="forward",
    )(*args, *shards)


EACH = 9


def attention_back_kernel(n, cuts, lags, q_ref, do_ref, inv_ref, kv_ref, *refs):
    ins, (dq_ref, d_out), outs = refs[:n], refs[n : n + 2], refs[n + 2 : 2 * n + 2]
    kv, dkv, core_buf, y_buf, load_sem, ks, kr, ys, yr, ws = refs[2 * n + 2 : 2 * n + 12]
    images, length, width = q_ref.shape
    at = Place()
    loads = [pltpu.make_async_copy(kv_ref.at[:, i], kv.at[i], load_sem.at[i]) for i in range(images)]
    for d in loads:
        d.start()
    at.greet_all() if n else at.greet_band()
    opening, todo, last = [], [], lambda: None
    if n:
        opening, todo, last = scatter_steps(at, cuts, ins, outs, refs[2 * n + 12 :], lags)
    for step in opening:
        step()
    steps = opening + todo

    def rows(s, i, band):
        return dkv.at[s, i, pl.ds(pl.multiple_of(band * length, 16), length), :]

    def to_core(i):
        for s in (0, 1):
            for yy in (0, 1):
                at.send(rows(s, i, yy * 2 + 1 - at.c), core_buf.at[i, s, yy], ks.at[i, s, yy], kr.at[i, s, yy], at.cpeer)

    def core_add(i):
        for s in (0, 1):
            p = rows(s, i, (1 - at.y) * 2 + at.c)
            at.arrived(core_buf.at[i, s, 1 - at.y], kr.at[i, s, 1 - at.y])
            if not at.draining:
                add_into(p, core_buf.at[i, s, 1 - at.y])
            at.send(p, y_buf.at[i, s], ys.at[i, s], yr.at[i, s], at.ypeer)
        for s in (0, 1):
            at.arrived(core_buf.at[i, s, at.y], kr.at[i, s, at.y])
            if not at.draining:
                add_into(rows(s, i, at.band), core_buf.at[i, s, at.y])

    def y_add(i):
        for s in (0, 1):
            p = rows(s, i, at.band)
            at.arrived(y_buf.at[i, s], yr.at[i, s])
            if not at.draining:
                add_into(p, y_buf.at[i, s])
            at.keep(p, d_out.at[s, i], ws.at[i, s])

    def head(i, h):
        win, inside = head_window(h)
        query, grad = q_ref[i, :, win], do_ref[i, :, win]
        query = jnp.where(inside, query, jnp.zeros_like(query))
        grad = jnp.where(inside, grad, jnp.zeros_like(grad))
        keys, values = kv[i, 0, :, win], kv[i, 1, :, win]
        inv = inv_ref[i, pl.ds(h, 1), :]
        probs = jnp.exp2(dot_t(keys, query) * (HDIM ** (-0.5) * LOG2E)) * inv
        d_probs = dot_t(values, grad)
        delta = jnp.sum(probs * d_probs, axis=0, keepdims=True)
        d_scores = (probs * (d_probs - delta)).astype(jnp.bfloat16)
        d_key = jnp.dot(d_scores, query, preferred_element_type=jnp.float32).astype(jnp.bfloat16)
        d_value = jnp.dot(
            probs.astype(jnp.bfloat16), grad, preferred_element_type=jnp.float32
        ).astype(jnp.bfloat16)
        dkv[0, i, :, win] = jnp.where(inside, d_key, dkv[0, i, :, win])
        dkv[1, i, :, win] = jnp.where(inside, d_value, dkv[1, i, :, win])
        dq_ref[i, :, win] = jnp.where(inside, first_dot(d_scores, keys), dq_ref[i, :, win])

    dq_ref[...] = jnp.zeros_like(dq_ref)
    for s in (0, 1):
        for i in range(images):

            def clear(r, _, s=s, i=i):
                dkv[s, i, pl.ds(pl.multiple_of(r * 16, 16), 16), :] = jnp.zeros((16, width), jnp.bfloat16)
                return 0

            lax.fori_loop(0, kv.shape[2] // 16, clear, 0)
    exchange = []
    for i in range(images):
        loads[i].wait()
        mine, todo = (todo[:EACH], todo[EACH:])
        due = exchange
        exchange = [functools.partial(f, i) for f in (core_add, y_add)]

        def body(h, _, i=i, mine=mine, due=due):
            for k, step in enumerate(due):
                pl.when(h == 1 + 12 * k)(step)
            for k, step in enumerate(mine):
                pl.when(h == k * HEADS // EACH)(step)
            head(i, h)
            return 0

        lax.fori_loop(0, HEADS, body, 0, unroll=4)
        to_core(i)
        steps += [functools.partial(to_core, i)] + exchange
    exchange[0]()
    part = min(6, len(todo))
    for step in todo[:part] + [exchange[1]] + todo[part:]:
        step()
    last()
    at.drain(steps)


def attention_backward(q, d_att, inv_rows, kv_all, grads, cuts, lags):
    n = len(grads)
    images, length, width = q.shape
    s = pltpu.SemaphoreType.DMA
    any_ref = pl.BlockSpec(memory_space=pl.ANY)
    vmem = pl.BlockSpec(memory_space=pltpu.VMEM)
    bf = jnp.bfloat16
    return pl.pallas_call(
        functools.partial(attention_back_kernel, n, cuts, lags),
        out_shape=[
            jax.ShapeDtypeStruct(q.shape, jnp.float32),
            jax.ShapeDtypeStruct((2, images, length, width), bf),
        ]
        + [jax.ShapeDtypeStruct(w.shape[:-3] + w.shape[-2:], bf) for w in grads],
        in_specs=[vmem, vmem, vmem, any_ref] + [any_ref] * n,
        out_specs=[vmem, any_ref] + [any_ref] * n,
        scratch_shapes=[
            pltpu.VMEM((images, 2) + kv_all.shape[2:], bf),
            pltpu.VMEM(kv_all.shape, bf),
            pltpu.VMEM((images, 2, 2, length, width), bf),
            pltpu.VMEM((images, 2, length, width), bf),
            s((images,)),
            s((images, 2, 2)),
            s((images, 2, 2)),
            s((images, 2)),
            s((images, 2)),
            s((images, 2)),
        ]
        + (scatter_scratch(grads, cuts) if n else []),
        compiler_params=pltpu.CompilerParams(
            collective_id=3, has_side_effects=True, vmem_limit_bytes=63 * 2**20
        ),
        name="attention_backward",
    )(q, d_att, inv_rows, kv_all, *grads)
def mlp_kernel(
    x_ref, gout_ref, att_ref, mod_ref, live_ref, proj_ref, gate_ref, up_ref, down_ref,
    out_ref, dmid_ref, dproj_ref, datt_ref, sums_ref, dgu_ref, ddown_ref,
    mid, proj, mlp, dnorm, normed, normed_t, dmlp,
):
    step, steps = pl.program_id(0), pl.num_programs(0)
    images, length, width = x_ref.shape

    def piece(i, k):
        return mod_ref[i : i + 1, k * width : (k + 1) * width]

    def rows(i):
        return pl.ds(i * length, length)

    def live(i):
        return live_ref[i : i + 1, 0:1]

    def unit(i):
        value = mid[rows(i), :]
        root = lax.rsqrt(jnp.mean(value * value, axis=-1, keepdims=True) + EPS)
        return value * root, root

    @pl.when(step == 0)
    def _():
        for i in range(images):
            proj[rows(i), :] = jnp.dot(att_ref[i], proj_ref[...], preferred_element_type=jnp.float32)
            mid[rows(i), :] = x_ref[i].astype(jnp.float32) + piece(i, 2) * proj[rows(i), :]
            value = (unit(i)[0] * (1.0 + piece(i, 4)) + piece(i, 3)).astype(jnp.bfloat16)
            normed[rows(i), :] = value
            normed_t[:, rows(i)] = value.T
            dmlp[rows(i), :] = (piece(i, 5) * (gout_ref[i].astype(jnp.float32) * live(i))).astype(jnp.bfloat16)
        mlp[...] = jnp.zeros_like(mlp)
        dnorm[...] = jnp.zeros_like(dnorm)

    gate = jnp.dot(normed[...], gate_ref[...], preferred_element_type=jnp.float32)
    up = jnp.dot(normed[...], up_ref[...], preferred_element_type=jnp.float32)
    dhidden = dot_t(dmlp[...], down_ref[...])
    sigmoid = 1.0 / (1.0 + jnp.exp(-gate))
    silu = gate * sigmoid
    hidden = (silu * up).astype(jnp.bfloat16)
    dgate = (dhidden * up * (sigmoid * (1.0 + gate * (1.0 - sigmoid)))).astype(jnp.bfloat16)
    dup = (dhidden * silu).astype(jnp.bfloat16)
    mlp[...] += jnp.dot(hidden, down_ref[...], preferred_element_type=jnp.float32)
    dnorm[...] += dot_t(dgate, gate_ref[...]) + dot_t(dup, up_ref[...])
    ddown_ref[...] = first_dot(hidden, dmlp[...]).astype(jnp.bfloat16)
    dgu_ref[0] = jnp.dot(normed_t[...], dgate, preferred_element_type=jnp.float32).astype(jnp.bfloat16)
    dgu_ref[1] = jnp.dot(normed_t[...], dup, preferred_element_type=jnp.float32).astype(jnp.bfloat16)

    @pl.when(step == steps - 1)
    def _():
        total = lambda v: jnp.sum(v, axis=0, keepdims=True)
        for i in range(images):
            gy = gout_ref[i].astype(jnp.float32) * live(i)
            value = mlp[rows(i), :]
            out_ref[i] = ((mid[rows(i), :] + piece(i, 5) * value) * live(i)).astype(jnp.bfloat16)
            sums_ref[i, 3:4, :] = total(gy * value)
            n, root = unit(i)
            dn = dnorm[rows(i), :]
            sums_ref[i, 1:2, :] = total(dn)
            sums_ref[i, 2:3, :] = total(dn * n)
            e = dn * (1.0 + piece(i, 4))
            d_mid = gy + root * (e - n * jnp.mean(e * n, axis=-1, keepdims=True))
            dmid_ref[i] = d_mid
            sums_ref[i, 0:1, :] = total(d_mid * proj[rows(i), :])
            d_proj = (piece(i, 2) * d_mid).astype(jnp.bfloat16)
            dproj_ref[i] = d_proj
            datt_ref[i] = dot_t(d_proj, proj_ref[...]).astype(jnp.bfloat16)


def mlp_block(x, grad_out, attended, mod, live, qp_all, gu_all, down_all):
    images, length, width = x.shape
    ff = down_all.shape[0]
    chunk = 512 if ff % 512 == 0 else LANES
    steps = ff // chunk
    bf = jnp.bfloat16
    whole = lambda s: pl.BlockSpec(s, lambda k: (0,) * len(s))
    rows = lambda d: jax.ShapeDtypeStruct(x.shape, d)
    tokens = images * length
    return pl.pallas_call(
        mlp_kernel,
        grid=(steps,),
        in_specs=[whole(x.shape)] * 3
        + [whole(mod.shape), whole(live.shape), pl.BlockSpec((width, width), lambda k: (0, 3))]
        + [
            pl.BlockSpec((width, chunk), lambda k: (0, k)),
            pl.BlockSpec((width, chunk), lambda k: (0, steps + k)),
            pl.BlockSpec((chunk, width), lambda k: (k, 0)),
        ],
        out_shape=[rows(bf), rows(jnp.float32), rows(bf), rows(bf)]
        + [
            jax.ShapeDtypeStruct((images, 4, width), jnp.float32),
            jax.ShapeDtypeStruct((2, width, ff), bf),
            jax.ShapeDtypeStruct((ff, width), bf),
        ],
        out_specs=[whole(x.shape)] * 4
        + [
            whole((images, 4, width)),
            pl.BlockSpec((2, width, chunk), lambda k: (0, 0, k)),
            pl.BlockSpec((chunk, width), lambda k: (k, 0)),
        ],
        scratch_shapes=[pltpu.VMEM((tokens, width), jnp.float32)] * 4
        + [pltpu.VMEM((tokens, width), bf), pltpu.VMEM((width, tokens), bf), pltpu.VMEM((tokens, width), bf)],
        compiler_params=pltpu.CompilerParams(vmem_limit_bytes=60 * 2**20),
        name="mlp_block",
    )(x, grad_out, attended, mod, live, qp_all, gu_all, gu_all, down_all)


def half_cuts(ref, axis, base, size, own_parts, shared_parts):
    unit = size // 2 // (own_parts + 2 * shared_parts)
    return (axis, size // 2, own_parts * unit, shared_parts * unit, base, ref)


def by_shard(grad):
    parts = lax.axis_size("grp")
    return grad.reshape(parts, grad.shape[0] // parts, grad.shape[1])


def body(
    patches,
    grad_out,
    cond_table,
    group_ids,
    live_count,
    band_order,
    w_ada,
    b_ada,
    w_qkv,
    q_gain,
    k_gain,
    w_proj,
    w_gate,
    w_up,
    w_down,
):
    images, rows, cols, width = patches.shape
    length = rows * cols
    ff = w_gate.shape[1]
    bf = jnp.bfloat16
    grp = lax.axis_index("grp")
    ada_rows, ada_cols, bias_cols = w_ada.shape[0], w_ada.shape[1], b_ada.shape[0]
    fits = (
        lax.axis_size("grp") == 8
        and images == 2
        and width == HEADS * HDIM
        and w_qkv.shape[0] % 16 == 0
        and 4 * width % 4608 == 0
        and 2 * ff % 3072 == 0
        and w_down.shape[0] % 384 == 0
    )
    w_qp = jnp.concatenate([w_qkv, w_proj], axis=1)
    w_gu = jnp.concatenate([w_gate, w_up], axis=1)
    full = lambda w: w.reshape(-1, w.shape[-1])
    onehot = (group_ids[:, None] == jnp.arange(GROUPS, dtype=jnp.int32)[None, :]).astype(jnp.float32)
    cond_rows = lax.dynamic_slice_in_dim(cond_table, grp * ada_rows, ada_rows, axis=1)
    sigmoid = jax.nn.sigmoid(cond_rows)
    silu_rows = (cond_rows * sigmoid).astype(bf)
    silu_slope = sigmoid * (1.0 + cond_rows * (1.0 - sigmoid))
    bias_part = lax.dynamic_update_slice_in_dim(
        jnp.zeros((ada_cols,), jnp.float32), b_ada.astype(jnp.float32), grp * bias_cols, axis=0
    )
    mod_parts = (silu_rows.astype(jnp.float32), w_ada, bias_part[None, :])
    live_mask = (jnp.arange(images, dtype=jnp.int32) < live_count[0]).astype(jnp.float32)

    gains = jnp.stack([jnp.tile(q_gain, HEADS), jnp.tile(k_gain, HEADS)])
    x = patches.reshape(images, length, width)
    groups = jnp.pad(onehot.T, ((0, 0), (0, LANES - images)))
    band = jnp.broadcast_to(band_order.astype(jnp.float32)[:, None], (1, LANES))
    common = (groups, gains, band, cols)
    if fits:
        shards = [w_qp, w_gu, w_down]
        cuts = [half_cuts(0, 1, 0, 4 * width, 1, 1), half_cuts(1, 1, 0, 2 * ff, 4, 1)]
        cuts += [half_cuts(2, 0, 0, w_down.shape[0], 4, 1)]
    else:
        qp_all, gu_all, down_all = (lax.all_gather(w, "grp", axis=0, tiled=True) for w in (w_qp, w_gu, w_down))
        mod_part = jnp.dot(silu_rows, w_ada, preferred_element_type=jnp.float32) + bias_part[None, :]
        mod_parts = (lax.psum(mod_part, "grp"),)
        shards, cuts = [qp_all], []
    outs = forward(x, mod_parts, *common, shards, cuts)
    normed_one, query, nq, nk, rq, rk, attended, inv, mod = outs[:9]
    tables, kv_all, rest = outs[9:12], outs[12], outs[13:]
    if fits:
        qp_all, gu_all, down_all = (full(w) for w in rest)
    live = jnp.broadcast_to(live_mask[:, None], (images, LANES))
    flat = lambda a: a.reshape(images * length, a.shape[-1])
    patches_out, d_middle, d_proj, d_attended, mid_sums, d_w_gu, d_w_down = mlp_block(
        x, grad_out.reshape(images, length, width), attended, mod, live, qp_all, gu_all, down_all
    )
    patches_out = patches_out.reshape(images, rows, cols, width)
    mod = mod.reshape(images, 6, width)
    d_query, d_kv, *rest = attention_backward(
        query,
        d_attended,
        jnp.swapaxes(inv, 1, 2),
        kv_all,
        [d_w_gu.reshape(2, -1, w_gate.shape[0], ff)] if fits else [],
        [half_cuts(0, 1, None, 2 * ff, 6, 1)] if fits else [],
        (2, 2, 1, 2),
    )
    d_qkv, d_x, sums = qkv_backward(
        x, mod, d_middle, d_query, d_kv, nq, nk, rq, rk, qp_all, gains, tables
    )
    d_patches = d_x.reshape(images, rows, cols, width)
    d_w_qp = weight_grads(flat(normed_one), flat(attended), flat(d_qkv), flat(d_proj))
    if fits:
        tags = jnp.repeat(onehot * (1.0 / lax.axis_size("band")), 6, axis=0)
        tags = jnp.pad(tags, ((0, 0), (0, LANES - GROUPS)))
        cuts = [half_cuts(0, 0, 0, w_down.shape[0], 2, 1), half_cuts(1, 1, 0, 4 * width, 8, 5)]
        d_gu = rest[0]
        d_down, d_qp, gathered, cond_blocks = scatter(
            [by_shard(d_w_down), by_shard(d_w_qp)], cuts, (2, 1, 0, 2), sums, mid_sums, tags, w_ada, silu_slope
        )
        d_mod_all = gathered[:, :GAIN_ROW, :width].reshape(-1, ada_cols)
        onehot_all = gathered[:, 0:GAIN_ROW:6, width : width + GROUPS].reshape(-1, GROUPS)
        gain_all = gathered[:, GAIN_ROW:, :width].astype(jnp.float32).reshape(-1, 2, 2, HEADS, HDIM)
        gain_all = jnp.sum(gain_all, axis=(0, 1, 3))
        d_cond = jnp.swapaxes(cond_blocks[:, :, :ada_rows], 0, 1).reshape(GROUPS, -1)
    else:
        d_gu, d_down, d_qp = (
            lax.psum(lax.psum_scatter(w, "grp", scatter_dimension=w.ndim - 2, tiled=True), "band")
            for w in (d_w_gu, d_w_down, d_w_qp)
        )
        d_mod_part = jnp.concatenate([sums[:, 0:2], mid_sums], axis=1)
        gain_part = jnp.sum(sums[:, 2:4].reshape(images, 2, HEADS, HDIM), axis=(0, 2))
        d_modulation = lax.psum(d_mod_part.reshape(images, ada_cols), "band").astype(bf)
        gain_all = lax.psum(gain_part, ("grp", "band"))
        payload = jnp.concatenate([d_modulation, onehot.astype(bf)], axis=1)
        payload = lax.all_gather(payload, "grp", axis=0, tiled=True)
        d_mod_all, onehot_all = payload[:, :ada_cols], payload[:, ada_cols:]
        d_silu = jnp.einsum("be,de->bd", d_mod_all, w_ada, preferred_element_type=jnp.float32)
        d_silu = jnp.dot(
            onehot_all.astype(jnp.float32).T,
            d_silu,
            precision=lax.Precision.HIGHEST,
            preferred_element_type=jnp.float32,
        )
        d_cond = lax.all_gather(d_silu * silu_slope, "grp", axis=1, tiled=True)
    silu_all = jnp.dot(onehot_all, silu_rows, preferred_element_type=jnp.float32).astype(bf)
    d_w_ada = jnp.einsum("bd,be->de", silu_all, d_mod_all, preferred_element_type=jnp.float32)
    d_b_ada = lax.dynamic_slice_in_dim(
        jnp.sum(d_mod_all.astype(jnp.float32), axis=0), grp * bias_cols, bias_cols, axis=0
    )
    wide = lambda a: a.astype(jnp.float32)
    return (
        patches_out,
        d_patches,
        d_cond,
        d_w_ada,
        d_b_ada,
        wide(d_qp[:, : 3 * width]),
        gain_all[0],
        gain_all[1],
        wide(d_qp[:, 3 * width :]),
        wide(d_gu[0]),
        wide(d_gu[1]),
        wide(d_down),
    )


def solution(mesh):
    in_specs = (
        P("grp", "band", None, None),
        P("grp", "band", None, None),
        P(),
        P("grp"),
        P("grp"),
        P("band"),
        P("grp", None),
        P("grp"),
        P("grp", None),
        P(),
        P(),
        P("grp", None),
        P("grp", None),
        P("grp", None),
        P("grp", None),
    )
    out_specs = (
        P("grp", "band", None, None),
        P("grp", "band", None, None),
        P(),
        P("grp", None),
        P("grp"),
        P("grp", None),
        P(),
        P(),
        P("grp", None),
        P("grp", None),
        P("grp", None),
        P("grp", None),
    )
    return jax.shard_map(body, mesh=mesh, in_specs=in_specs, out_specs=out_specs, check_vma=False)
```

```python
import functools
import math

import jax
import jax.numpy as jnp
from jax import lax
from jax.experimental import pallas as pl
from jax.experimental.pallas import tpu as pltpu
from jax.sharding import PartitionSpec as P

HEADS = 16
HDIM = 72
GROUPS = 8
LANES = 128
EPS = 1e-06
LOG2E = 1.4426950408889634

MESH = pl.DeviceIdType.MESH


class Place:
    def __init__(self):
        self.g, self.band = lax.axis_index("grp"), lax.axis_index("band")
        self.z, self.x = self.g // 2, self.g % 2
        self.y, self.c = self.band // 2, self.band % 2
        z = self.z
        self.far = [z, z + 1 - 2 * (z % 2), 2 - z // 2, 3 - 3 * (z // 2)]
        self.ypeer = (self.g, (1 - self.y) * 2 + self.c)
        self.cpeer = (self.g, self.y * 2 + 1 - self.c)
        self.xpeer = (z * 2 + 1 - self.x, self.band)
        self.draining = False

    def line(self, zz):
        return (zz * 2 + self.x, self.band)

    def greet(self, peers):
        bar = pltpu.get_barrier_semaphore()
        for d in peers:
            pl.semaphore_signal(bar, inc=1, device_id=d, device_id_type=MESH)
        pl.semaphore_wait(bar, len(peers))

    def greet_band(self):
        self.greet([self.ypeer, self.cpeer])

    def greet_all(self):
        self.greet([self.xpeer, self.ypeer, self.cpeer] + [self.line(zz) for zz in self.far[1:]])

    def copy(self, src, dst, ssem, rsem, dev):
        return pltpu.make_async_remote_copy(
            src_ref=src, dst_ref=dst, send_sem=ssem, recv_sem=rsem, device_id=dev, device_id_type=MESH
        )

    def send(self, src, dst, ssem, rsem, dev, cond=None):
        d = self.copy(src, dst, ssem, rsem, dev)
        act = d.wait_send if self.draining else d.start
        if cond is None:
            act()
        else:
            pl.when(cond)(act)

    def keep(self, src, dst, sem):
        d = pltpu.make_async_copy(src, dst, sem)
        d.wait() if self.draining else d.start()

    def arrived(self, ref, rsem):
        if not self.draining:
            self.copy(ref, ref, rsem, rsem, self.ypeer).wait_recv()

    def drain(self, steps):
        self.draining = True
        for step in steps:
            step()
        self.draining = False


def span(ref, axis, start, size):
    if axis == 0:
        return ref.at[pl.ds(pl.multiple_of(start, 16), size), :]
    return ref.at[:, pl.ds(pl.multiple_of(start, LANES), size)]


def gather_sems(n):
    s = pltpu.SemaphoreType.DMA
    return [s((n,)), s((n, 4)), s((n, 4)), s((n, 4)), s((n, 4)), s((n, 7)), s((n, 7)), s((n, 14)), s((n, 14)), s((n,))]


def gather_steps(at, cuts, ins, outs, sems):
    n = len(cuts)
    lsem, zs, zr, xs, xr, ys, yr, cs, cr, ds = sems
    ins, outs = ([refs[cut[5]] for cut in cuts] for refs in (ins, outs))
    soon = sum(cut[5] == 0 for cut in cuts)
    x, y, z, c, far = at.x, at.y, at.z, at.c, at.far

    def piece(i, ref, yy, cc):
        axis, half, a, b, base, _ = cuts[i]
        return span(ref, axis, base + cc * half + yy * b, a + b)

    def bpart(i, ref, yy, cc):
        axis, half, a, b, base, _ = cuts[i]
        return span(ref, axis, base + cc * half + yy * (a + b), b)

    def own(i):
        src, dst = piece(i, ins[i], y, c), piece(i, outs[i].at[at.g], y, c)
        at.send(src, dst, zs.at[i, 0], zr.at[i, z], (at.g + 2, at.band), z < 3)
        at.send(src, dst, ds.at[i], zr.at[i, z], (at.g - 2, at.band), z > 0)
        at.send(src, dst, xs.at[i, 0], xr.at[i, 0], at.xpeer)
        if cuts[i][4] == 0 and not (at.draining and cuts[i][5] == 0):
            at.keep(ins[i], outs[i].at[at.g], lsem.at[i])

    def down(i, slot, shard):
        p = bpart(i, outs[i].at[shard], y, c)
        at.send(p, p, ys.at[i, slot], yr.at[i, slot], at.ypeer)
        p = piece(i, outs[i].at[shard], y, c)
        at.send(p, p, cs.at[i, slot], cr.at[i, slot], at.cpeer)

    def zarr(i, t):
        zz = far[t]
        s = zz * 2 + x
        p = piece(i, outs[i].at[s], y, c)
        at.arrived(p, zr.at[i, zz])
        nxt = jnp.where(zz < z, z + 1, z - 1)
        at.send(p, p, zs.at[i, t], zr.at[i, zz], at.line(jnp.clip(nxt, 0, 3)), (nxt >= 0) & (nxt <= 3))
        at.send(p, p, xs.at[i, t], xr.at[i, t], at.xpeer)
        down(i, t - 1, s)

    def xarr(i, t):
        s = far[t] * 2 + 1 - x
        at.arrived(piece(i, outs[i].at[s], y, c), xr.at[i, t])
        down(i, 3 + t, s)

    def yarr(i, slot, s):
        p = bpart(i, outs[i].at[s], 1 - y, c)
        at.arrived(p, yr.at[i, slot])
        at.send(p, p, cs.at[i, 7 + slot], cr.at[i, 7 + slot], at.cpeer)

    slots = [(t - 1, far[t] * 2 + x) for t in (1, 2, 3)]
    slots += [(3 + t, far[t] * 2 + 1 - x) for t in range(4)]
    order = [slots[k] for k in (3, 0, 4, 1, 5, 2, 6)]
    steps = [lambda: own(0)]
    for i in range(n):
        mine = [lambda i=i: zarr(i, 1)]
        if 0 < i and i + 1 < n:
            mine.append(lambda i=i: own(i + 1))
        mine.append(lambda i=i: xarr(i, 0))
        for t in (2, 3):
            mine.append(lambda i=i, t=t: zarr(i, t))
            if i == 0 and t == 3 and n > 1:
                mine.append(lambda: own(1))
            mine.append(lambda i=i, t=t: xarr(i, t - 1))
        mine.append(lambda i=i: xarr(i, 3))
        if i > 0:
            late = [lambda i=i, k=k: yarr(i - 1, *order[k]) for k in range(7)]
            pace, held = 3 if i == soon else 1, list(late)
            merged = []
            while late or mine:
                merged += late[:pace] + mine[:1]
                late, mine = late[pace:], mine[1:]
            mine = merged
        if i == soon:
            first = len(steps) + max(k for k, step in enumerate(mine) if step in held) + 1
        steps += mine
    steps += [lambda k=k: yarr(n - 1, *order[k]) for k in range(7)]

    def last(i):
        for slot, s in slots:
            at.arrived(piece(i, outs[i].at[s], y, 1 - c), cr.at[i, slot])
            at.arrived(bpart(i, outs[i].at[s], 1 - y, 1 - c), cr.at[i, 7 + slot])

    return steps, first, last


def add_into(dst, src):
    def step(r, _):
        rows = pl.ds(pl.multiple_of(r * 16, 16), 16)
        dst[rows, :] = dst[rows, :] + src[rows, :]
        return 0

    lax.fori_loop(0, src.shape[0] // 16, step, 0)


def move_into(dst, src):
    def step(r, _):
        rows = pl.ds(pl.multiple_of(r * 16, 16), 16)
        dst[rows, :] = src[rows, :]
        return 0

    lax.fori_loop(0, src.shape[0] // 16, step, 0)


def scatter_scratch(grads, cuts):
    n = len(cuts)
    s = pltpu.SemaphoreType.DMA

    def buf(lead, k, size):
        rows, cols = grads[cuts[k][5]].shape[-2:]
        shape = (rows, size) if cuts[k][0] == 1 else (size, cols)
        return pltpu.VMEM(lead + shape, jnp.bfloat16)

    out = []
    for lead, pick in (
        ((8,), lambda c: c[1]),
        ((8,), lambda c: c[1]),
        ((8,), lambda c: c[3]),
        ((4,), lambda c: c[2] + c[3]),
        ((5,), lambda c: c[2] + c[3]),
        ((), lambda c: c[2] + c[3]),
    ):
        out += [buf(lead, k, pick(cuts[k])) for k in range(n)]
    out += [s((n, 8))] * 5 + [s((n, 4))] * 2 + [s((n, 3)), s((n, 5))] + [s((n,))] * 5
    return out


def scatter_steps(at, cuts, ins, outs, scratch, lags):
    n = len(cuts)
    own_half, core_buf, y_buf, x_buf, z_buf, fin_buf = (scratch[k * n : (k + 1) * n] for k in range(6))
    ls, cs, cr, ys, yr, xs, xr, zs, zr, fs, fr, es, er, ws = scratch[6 * n :]
    x, y, z, c, far = at.x, at.y, at.z, at.c, at.far
    ins, outs = ([refs[cut[5]] for cut in cuts] for refs in (ins, outs))

    def in_half(i, s, cc):
        axis, half, _, _, base, _ = cuts[i]
        if base is None:
            return ins[i].at[cc, s]
        return span(ins[i].at[s], axis, base + cc * half, half)

    def out_half(i, cc):
        axis, half, _, _, base, _ = cuts[i]
        if base is None:
            return outs[i].at[cc]
        return span(outs[i], axis, base + cc * half, half)

    def piece(i, ref):
        _, _, a, b = cuts[i][:4]
        return span(ref, cuts[i][0], y * b, a + b)

    def bpart(i, ref, yy):
        _, _, a, b = cuts[i][:4]
        return span(ref, cuts[i][0], yy * (a + b), b)

    order = [(t, j) for t in (3, 2, 1, 0) for j in (1, 0)]

    def shard(t, j):
        return far[t] * 2 + (1 - x if j else x)

    def load(i, t, j):
        s, q = shard(t, j), order.index((t, j))
        return pltpu.make_async_copy(in_half(i, s, c), own_half[i].at[s], ls.at[i, q])

    def give(i, t, j):
        s, q = shard(t, j), order.index((t, j))
        src = in_half(i, s, 1 - c)
        at.send(src, core_buf[i].at[s], cs.at[i, q], cr.at[i, s], at.cpeer)
        if not at.draining:
            load(i, t, j).start()

    def to_y(i, t, j):
        s = shard(t, j)
        src = bpart(i, own_half[i].at[s], 1 - y)
        return at.copy(src, y_buf[i].at[s], ys.at[i, order.index((t, j))], yr.at[i, s], at.ypeer)

    def to_fin(i):
        return at.copy(piece(i, own_half[i].at[at.g]), fin_buf[i], fs.at[i], fr.at[i], at.ypeer)

    def cadd(i, t, j):
        s = shard(t, j)
        if at.draining:
            if (t, j) != (0, 0):
                to_y(i, t, j).wait_send()
            return
        load(i, t, j).wait()
        at.arrived(core_buf[i].at[s], cr.at[i, s])
        add_into(own_half[i].at[s], core_buf[i].at[s])
        to_y(i, t, j).start()

    def yadd(i, t, j):
        s = shard(t, j)
        at.arrived(y_buf[i].at[s], yr.at[i, s])
        if not at.draining:
            add_into(bpart(i, own_half[i].at[s], y), y_buf[i].at[s])
        if j:
            at.send(piece(i, own_half[i].at[s]), x_buf[i].at[far[t]], xs.at[i, t], xr.at[i, far[t]], at.xpeer)

    def xadd(i, t):
        if at.draining:
            return
        at.arrived(x_buf[i].at[far[t]], xr.at[i, far[t]])
        add_into(piece(i, own_half[i].at[shard(t, 0)]), x_buf[i].at[far[t]])

    def zadd(i, t):
        zz = far[t]
        p = piece(i, own_half[i].at[shard(t, 0)])

        def join(cond, slot):
            def do():
                at.arrived(z_buf[i].at[slot], zr.at[i, slot])
                add_into(p, z_buf[i].at[slot])

            if not at.draining:
                pl.when(cond)(do)

        if t > 0:
            inc = jnp.where(zz < z, z + 1, z - 1)
            join((inc >= 0) & (inc <= 3), zz)
            nxt = jnp.where(zz < z, z - 1, z + 1)
            slot = jnp.where((zz < z) & (nxt == zz), 4, zz)
            at.send(p, z_buf[i].at[slot], zs.at[i, t - 1], zr.at[i, slot], at.line(nxt))
        else:
            join(z > 0, z)
            join(z < 3, 4)
            if not at.draining:
                to_fin(i).start()

    def fin(i):
        axis, half, a, b, base, _ = cuts[i]
        own = own_half[i].at[at.g]
        if not at.draining:
            at.arrived(fin_buf[i], fr.at[i])
            to_fin(i).wait_send()
            to_y(i, 0, 0).wait_send()
            for yy in (0, 1):

                @pl.when(y == 1 - yy)
                def _():
                    add_into(span(own, axis, b, a), span(fin_buf[i], axis, b if yy == 0 else 0, a))
                    move_into(span(own, axis, yy * (a + b), b), span(fin_buf[i], axis, 0 if yy == 0 else a, b))

        o = out_half(i, c)
        at.send(own, o, es.at[i], er.at[i], at.cpeer)
        at.keep(own, o, ws.at[i])

    seq = [(i, t, j) for i in range(n) for (t, j) in order]
    opening = [functools.partial(give, *p) for p in seq]
    ly, lx, lz, lf = lags
    todo = []
    for q, (i, t, j) in enumerate(seq):
        todo.append((q, 0, functools.partial(cadd, i, t, j)))
        todo.append((q + ly, 1, functools.partial(yadd, i, t, j)))
        if j == 0:
            todo.append((q + ly + lx, 2, functools.partial(xadd, i, t)))
            todo.append((q + ly + lx + lz, 3, functools.partial(zadd, i, t)))
            if t == 0:
                todo.append((q + ly + lx + lz + lf, 4, functools.partial(fin, i)))
    todo.sort(key=lambda p: p[:2])

    def last():
        for i in range(n):
            at.arrived(out_half(i, 1 - c), er.at[i])

    return opening, [f for _, _, f in todo], last


def head_window(h):
    first = jnp.minimum(h * HDIM // LANES, HEADS * HDIM // LANES - 2) * LANES
    lane = lax.broadcasted_iota(jnp.int32, (1, 2 * LANES), 1) + first
    inside = (lane >= h * HDIM) & (lane < h * HDIM + HDIM)
    return pl.ds(pl.multiple_of(first, LANES), 2 * LANES), inside


def dot_t(left, right):
    return lax.dot_general(left, right, (((1,), (1,)), ((), ())), preferred_element_type=jnp.float32)


def first_dot(left, right):
    return lax.dot_general(left, right, (((0,), (0,)), ((), ())), preferred_element_type=jnp.float32)


def pick_dot(values, chosen):
    high = values.astype(jnp.bfloat16)
    low = (values - high.astype(jnp.float32)).astype(jnp.bfloat16)
    return jnp.dot(high, chosen, preferred_element_type=jnp.float32) + jnp.dot(
        low, chosen, preferred_element_type=jnp.float32
    )


def head_pick(width):
    row = lax.broadcasted_iota(jnp.int32, (width, LANES), 0)
    first = lax.broadcasted_iota(jnp.int32, (width, LANES), 1) * HDIM
    return ((row >= first) & (row < first + HDIM)).astype(jnp.float32).astype(jnp.bfloat16)


def head_spread(width):
    lane = lax.broadcasted_iota(jnp.int32, (LANES, width), 1)
    first = lax.broadcasted_iota(jnp.int32, (LANES, width), 0) * HDIM
    return ((lane >= first) & (lane < first + HDIM)).astype(jnp.float32).astype(jnp.bfloat16)


def rope_tables(band, rows, cols, width):
    quarter = HDIM // 4
    shape = (rows * cols, width)
    token = lax.broadcasted_iota(jnp.int32, shape, 0)
    lane = lax.broadcasted_iota(jnp.int32, shape, 1) % HDIM
    power = (lane % quarter).astype(jnp.float32) * (-math.log(10000.0) / quarter)
    by_row = band * rows + (token // cols).astype(jnp.float32)
    index = jnp.where(lane < 2 * quarter, by_row, (token % cols).astype(jnp.float32))
    angle = index * jnp.exp(power)
    sine = jnp.sin(angle)
    low = (lane // quarter) % 2 == 0
    return jnp.cos(angle), jnp.where(low, -sine, 0.0), jnp.where(low, 0.0, sine)


def turn(values, cos, sin_next, sin_prev):
    width = values.shape[-1]
    after = pltpu.roll(values, width - HDIM // 4, 1)
    before = pltpu.roll(values, HDIM // 4, 1)
    return values * cos + after * sin_next + before * sin_prev


def turn_back(values, cos, sin_next, sin_prev):
    width = values.shape[-1]
    after = pltpu.roll(values, width - HDIM // 4, 1)
    before = pltpu.roll(values, HDIM // 4, 1)
    return values * cos - after * sin_next - before * sin_prev


def qkv_back_kernel(
    x_ref, mod_ref, mid_ref, dq_ref, dk_ref, dv_ref, nq_ref, nk_ref, rq_ref, rk_ref, w_ref,
    gains_ref, cos_ref, next_ref, prev_ref,
    dqkv_ref, dx_ref, sums_ref, w_buf, w_sem,
):
    width = x_ref.shape[-1]
    load = pltpu.make_async_copy(w_ref.at[:, pl.ds(0, 3 * width)], w_buf, w_sem)
    pl.when(pl.program_id(0) == 0)(load.start)
    tables = (cos_ref[...], next_ref[...], prev_ref[...])
    pick, spread = head_pick(width), head_spread(width)
    ins = ((dq_ref, nq_ref, rq_ref), (dk_ref, nk_ref, rk_ref))
    for part, (d_ref, n_ref, r_ref) in enumerate(ins):
        back = turn_back(d_ref[0].astype(jnp.float32) * HDIM ** (-0.5), *tables)
        unit = n_ref[0]
        sums_ref[0, 2 + part : 3 + part, :] = jnp.sum(back * unit, axis=0, keepdims=True)
        inner = back * gains_ref[part : part + 1, :]
        mean = pick_dot(inner * unit, pick) * (1.0 / HDIM)
        grad = (inner - unit * pick_dot(mean, spread)) * pick_dot(r_ref[0], spread)
        dqkv_ref[0, :, part * width : (part + 1) * width] = grad.astype(jnp.bfloat16)
    dqkv_ref[0, :, 2 * width : 3 * width] = dv_ref[0]
    pl.when(pl.program_id(0) == 0)(load.wait)
    d_normed = dot_t(dqkv_ref[0], w_buf[...])
    x = x_ref[0].astype(jnp.float32)
    root = lax.rsqrt(jnp.mean(x * x, axis=-1, keepdims=True) + EPS)
    unit = x * root
    sums_ref[0, 0:1, :] = jnp.sum(d_normed, axis=0, keepdims=True)
    sums_ref[0, 1:2, :] = jnp.sum(d_normed * unit, axis=0, keepdims=True)
    inner = d_normed * (1.0 + mod_ref[0, 1:2, :])
    dx_ref[0] = mid_ref[0] + root * (inner - unit * jnp.mean(inner * unit, axis=-1, keepdims=True))


def qkv_backward(x, mod, d_mid, dq, d_kv, nq, nk, rq, rk, qp_all, gains, tables):
    images, length, width = x.shape
    row = lambda w: pl.BlockSpec((1, length, w), lambda i: (i, 0, 0))
    whole = lambda a: pl.BlockSpec(a.shape, lambda i: (0,) * a.ndim)
    return pl.pallas_call(
        qkv_back_kernel,
        grid=(images,),
        in_specs=[row(width), pl.BlockSpec((1, 6, width), lambda i: (i, 0, 0))]
        + [row(width)] * 2
        + [pl.BlockSpec((None, 1, length, width), lambda i, s=s: (s, i, 0, 0)) for s in (0, 1)]
        + [row(width)] * 2
        + [row(LANES)] * 2
        + [pl.BlockSpec(memory_space=pl.ANY), whole(gains)]
        + [whole(t) for t in tables],
        out_shape=[
            jax.ShapeDtypeStruct((images, length, 3 * width), jnp.bfloat16),
            jax.ShapeDtypeStruct((images, length, width), jnp.float32),
            jax.ShapeDtypeStruct((images, 4, width), jnp.float32),
        ],
        out_specs=[row(3 * width), row(width), pl.BlockSpec((1, 4, width), lambda i: (i, 0, 0))],
        scratch_shapes=[pltpu.VMEM((width, 3 * width), jnp.bfloat16), pltpu.SemaphoreType.DMA],
        compiler_params=pltpu.CompilerParams(vmem_limit_bytes=60 * 2**20),
        name="qkv_backward",
    )(x, mod, d_mid, dq, d_kv, d_kv, nq, nk, rq, rk, qp_all, gains, *tables)


def weight_kernel(normed_ref, att_ref, dqkv_ref, dproj_ref, out_ref, turned):
    step = pl.program_id(0)

    @pl.when(step == 0)
    def _():
        turned[...] = normed_ref[...].T

    @pl.when(step == 3)
    def _():
        turned[...] = att_ref[...].T
        out_ref[...] = jnp.dot(turned[...], dproj_ref[...], preferred_element_type=jnp.float32).astype(jnp.bfloat16)

    @pl.when(step < 3)
    def _():
        out_ref[...] = jnp.dot(turned[...], dqkv_ref[...], preferred_element_type=jnp.float32).astype(jnp.bfloat16)


def weight_grads(normed, attended, d_qkv, d_proj):
    tokens, width = normed.shape
    whole = pl.BlockSpec((tokens, width), lambda k: (0, 0))
    return pl.pallas_call(
        weight_kernel,
        grid=(4,),
        in_specs=[whole, whole, pl.BlockSpec((tokens, width), lambda k: (0, jnp.minimum(k, 2))), whole],
        out_shape=jax.ShapeDtypeStruct((width, 4 * width), jnp.bfloat16),
        out_specs=pl.BlockSpec((width, width), lambda k: (0, k)),
        scratch_shapes=[pltpu.VMEM((width, tokens), jnp.bfloat16)],
        compiler_params=pltpu.CompilerParams(vmem_limit_bytes=60 * 2**20),
        name="weight_grads",
    )(normed, attended, d_qkv, d_proj)


def tail_scratch():
    s = pltpu.SemaphoreType.DMA
    wide = SMALL_COLS
    return [
        pltpu.VMEM((SMALL_ROWS, wide), jnp.float32),
        pltpu.VMEM((2, SMALL_ROWS, wide), jnp.float32),
        pltpu.VMEM((8, SMALL_ROWS, wide), jnp.bfloat16),
        pltpu.VMEM((8, GROUPS, 2 * LANES), jnp.float32),
        s((8,)),
        s((8,)),
    ]


def tail_steps(at, ins, outs, scratch):
    sums_ref, mid_ref, tag_ref, ada_ref, slope_ref = ins
    all_ref, cond_ref = outs
    acc, inbox, blocks, cond, ss, rs = scratch
    width = HEADS * HDIM
    z = at.z
    line = (at.xpeer, at.line(at.far[1]), at.line((z + 2) % 4))

    def copy(r):
        if r < 2:
            return at.copy(acc, inbox.at[r], ss.at[r], rs.at[r], (at.cpeer, at.ypeer)[r])
        ref, k = (blocks, r - 2) if r < 5 else (cond, r - 5)
        start, size = ((at.g, 1), (2 * z, 2), (4 * (z // 2), 4))[k]
        src = ref.at[pl.ds(start, size)]
        return at.copy(src, src, ss.at[r], rs.at[r], line[k])

    def collect():
        acc[...] = jnp.zeros_like(acc)
        for i in range(2):
            acc[6 * i : 6 * i + 2, :width] = sums_ref[i, 0:2, :]
            acc[6 * i + 2 : 6 * i + 6, :width] = mid_ref[i]
        acc[:GAIN_ROW, width:] = tag_ref[...]
        gains = sums_ref[0, 2:4, :] + sums_ref[1, 2:4, :]
        acc[GAIN_ROW : GAIN_ROW + 2, :width] = gains
        acc[GAIN_ROW + 2 :, :width] = gains

    def pack():
        row = lax.broadcasted_iota(jnp.int32, (SMALL_ROWS, 1), 0)
        value = acc[...]
        rest = value - value.astype(jnp.bfloat16).astype(jnp.float32)
        blocks[at.g] = jnp.where(row >= GAIN_ROW + 2, rest, value).astype(jnp.bfloat16)

    def cond_rows():
        flat = blocks[...].reshape(8 * SMALL_ROWS, SMALL_COLS)
        row = lax.broadcasted_iota(jnp.int32, (8 * SMALL_ROWS, 1), 0) % SMALL_ROWS
        silu = jnp.zeros((8 * SMALL_ROWS, ada_ref.shape[0]), jnp.float32)
        for k in range(6):
            product = dot_t(flat[:, :width], ada_ref[:, k * width : (k + 1) * width])
            silu = jnp.where((row % 6 == k) & (row < GAIN_ROW), product, silu)
        by_group = lax.dot_general(
            flat[:, width:].astype(jnp.float32),
            silu,
            (((0,), (0,)), ((), ())),
            precision=lax.Precision.HIGHEST,
            preferred_element_type=jnp.float32,
        )
        cond[at.g] = jnp.zeros((GROUPS, 2 * LANES), jnp.float32)
        cond[at.g, :, : ada_ref.shape[0]] = by_group[:GROUPS] * slope_ref[...]

    def step(r):
        if at.draining:
            return
        if r > 0:
            copy(r - 1).wait()
        if r == 0:
            collect()
        elif r <= 2:
            acc[...] = acc[...] + inbox[r - 1]
        if r == 2:
            pack()
        if r == 5:
            cond_rows()
        if r < 8:
            copy(r).start()
        else:
            all_ref[...] = blocks[...]
            cond_ref[...] = cond[...]

    return [functools.partial(step, r) for r in range(9)]


SMALL_ROWS, SMALL_COLS, GAIN_ROW = 16, HEADS * HDIM + LANES, 12


def scatter_kernel(n, cuts, lags, *refs):
    at = Place()
    at.greet_all()
    ins, small_in = refs[:n], refs[n : n + 5]
    outs, small_out = refs[n + 5 : 2 * n + 5], refs[2 * n + 5 : 2 * n + 7]
    small = tail_steps(at, small_in, small_out, refs[2 * n + 7 : 2 * n + 13])
    opening, steps, last = scatter_steps(at, cuts, ins, outs, refs[2 * n + 13 :], lags)
    small[0]()
    for step in opening:
        step()
    small = small[1:]
    for k, step in enumerate(steps):
        step()
        if k % 6 == 5 and small:
            small[0]()
            small = small[1:]
    for step in small:
        step()
    last()
    at.drain(opening + steps)


def scatter(grads, cuts, lags, sums, mid_sums, tags, w_ada, slope):
    n = len(grads)
    any_ref = pl.BlockSpec(memory_space=pl.ANY)
    vmem = pl.BlockSpec(memory_space=pltpu.VMEM)
    return pl.pallas_call(
        functools.partial(scatter_kernel, n, cuts, lags),
        out_shape=[jax.ShapeDtypeStruct(w.shape[1:], jnp.bfloat16) for w in grads]
        + [
            jax.ShapeDtypeStruct((8, SMALL_ROWS, SMALL_COLS), jnp.bfloat16),
            jax.ShapeDtypeStruct((8, GROUPS, 2 * LANES), jnp.float32),
        ],
        in_specs=[any_ref] * n + [vmem] * 5,
        out_specs=[any_ref] * n + [vmem] * 2,
        scratch_shapes=tail_scratch() + scatter_scratch(grads, cuts),
        compiler_params=pltpu.CompilerParams(
            collective_id=1, has_side_effects=True, vmem_limit_bytes=60 * 2**20
        ),
        name="gradient_scatter",
    )(*grads, sums, mid_sums, tags, w_ada, slope)


def forward_kernel(cuts, cols, refs):
    n = len(cuts)
    soon = sum(cut[5] == 0 for cut in cuts)
    at = Place()
    x_ref, part_ref, group_ref, gains_ref, band_ref = refs["in"]
    normed_ref, q_ref, nq_ref, nk_ref, rq_ref, rk_ref, o_ref, inv_ref, mod_ref, *table_refs, kv_out = refs["out"]
    kv, w_buf, pick_ref, spread_ref, mod_buf, mod_in, w_sem, ms, mr, ks, kr, os = refs["scratch"]
    ins, outs = refs["shards"], refs["full"]
    images, length, width = x_ref.shape
    parts = [(i, s) for i in range(images) for s in (0, 1)]
    if n:
        at.greet_all()
        steps, first, last = gather_steps(at, cuts, ins, outs, refs["sems"])
    else:
        at.greet_band()
        steps, first, last = [], 0, None

    mod_buf[...] = part_ref[...]

    def mod_copy(r):
        peer = (at.xpeer, at.line(at.far[1]), at.line((at.z + 2) % 4))[r]
        return at.copy(mod_buf, mod_in.at[r], ms.at[r], mr.at[r], peer)

    def mod_step(r):
        if at.draining:
            return
        if r > 0:
            mod_copy(r - 1).wait()
            mod_buf[...] = mod_buf[...] + mod_in[r - 1]
        if r < 3:
            mod_copy(r).start()

    def rows(s, i, band):
        return kv.at[s, i, pl.ds(pl.multiple_of(band * length, 16), length), :]

    here, over = at.band, (1 - at.y) * 2 + at.c
    beside, across = at.y * 2 + 1 - at.c, (1 - at.y) * 2 + 1 - at.c

    def give(i, s):
        p = rows(s, i, here)
        at.send(p, p, ks.at[i, s, 0], kr.at[i, s, 0], at.ypeer)
        at.send(p, p, ks.at[i, s, 1], kr.at[i, s, 1], at.cpeer)

    def pass_on(i, s):
        p = rows(s, i, over)
        at.arrived(p, kr.at[i, s, 0])
        at.send(p, p, ks.at[i, s, 2], kr.at[i, s, 2], at.cpeer)

    def ready(i):
        for s in (0, 1):
            at.arrived(rows(s, i, beside), kr.at[i, s, 1])
            at.arrived(rows(s, i, across), kr.at[i, s, 2])
            at.keep(kv.at[s, i], kv_out.at[s, i], os.at[i, s])

    def norm(i):
        value = x_ref[i].astype(jnp.float32)
        root = lax.rsqrt(jnp.mean(value * value, axis=-1, keepdims=True) + EPS)
        chosen = jnp.sum(group_ref[:, i : i + 1] * mod_buf[...], axis=0, keepdims=True)
        mod_ref[i : i + 1, :] = chosen
        shift, scale = chosen[:, :width], chosen[:, width : 2 * width]
        normed_ref[i] = (value * root * (1.0 + scale) + shift).astype(jnp.bfloat16)

    def raw(i, part):
        return jnp.dot(
            normed_ref[i], w_buf[:, part * width : (part + 1) * width], preferred_element_type=jnp.float32
        )

    def project(i, part, n_ref, r_ref):
        values = raw(i, part)
        inv = lax.rsqrt(pick_dot(values * values, pick_ref[...]) * (1.0 / HDIM) + EPS)
        r_ref[i] = inv
        unit = values * pick_dot(inv, spread_ref[...])
        n_ref[i] = unit
        scaled = unit * gains_ref[part : part + 1, :]
        return turn(scaled, *(t[...] for t in table_refs)).astype(jnp.bfloat16)

    def key_part(i):
        norm(i)
        kv[0, i, pl.ds(pl.multiple_of(here * length, 16), length), :] = project(i, 1, nk_ref, rk_ref)
        give(i, 0)

    def value_part(i):
        kv[1, i, pl.ds(pl.multiple_of(here * length, 16), length), :] = raw(i, 2).astype(jnp.bfloat16)
        give(i, 1)

    def query_part(i):
        q_ref[i] = project(i, 0, nq_ref, rq_ref)

    def head(i, h):
        win, inside = head_window(h)
        query = q_ref[i, :, win]
        query = jnp.where(inside, query, jnp.zeros_like(query))
        power = jnp.exp2(dot_t(query, kv[0, i, :, win]) * (HDIM ** (-0.5) * LOG2E))
        inv = 1.0 / jnp.sum(power, axis=-1, keepdims=True)
        out = jnp.dot(
            (power * inv).astype(jnp.bfloat16), kv[1, i, :, win], preferred_element_type=jnp.float32
        )
        o_ref[i, :, win] = jnp.where(inside, out.astype(jnp.bfloat16), o_ref[i, :, win])
        lane = lax.broadcasted_iota(jnp.int32, (1, LANES), 1)
        inv_ref[i] = jnp.where(lane == h, inv, inv_ref[i])

    def prepare():
        pick_ref[...] = head_pick(width)
        spread_ref[...] = head_spread(width)

        def block(r, _):
            rows_of = pl.ds(pl.multiple_of(r * cols, cols), cols)
            row = band_ref[0:1, 0:1] * (length // cols) + r.astype(jnp.float32)
            for ref, value in zip(table_refs, rope_tables(row, 1, cols, width)):
                ref[rows_of, :] = value
            return 0

        lax.fori_loop(0, length // cols, block, 0)

    if not n:
        prepare()
    if n:
        for k in range(3):
            mod_step(k)
            for step in steps[2 * k : 2 * k + 2]:
                step()
                if k == 0 and step is steps[0]:
                    prepare()
        mod_step(3)
        for step in steps[6:first]:
            step()
        for i in range(soon):
            last(i)
        pltpu.make_async_copy(ins[0], outs[0].at[at.g], refs["sems"][0].at[0]).wait()
        loads = [
            pltpu.make_async_copy(
                outs[0].at[k, :, pl.ds(0, 3 * width)],
                w_buf.at[pl.ds(k * (width // 8), width // 8), :],
                w_sem.at[k],
            )
            for k in range(8)
        ]
    else:
        loads = [pltpu.make_async_copy(ins[0].at[:, pl.ds(0, 3 * width)], w_buf, w_sem.at[0])]
    for d in loads:
        d.start()
    o_ref[...] = jnp.zeros_like(o_ref)
    inv_ref[...] = jnp.zeros_like(inv_ref)
    for d in loads:
        d.wait()
    todo = steps[first:]
    for i in range(images):
        for work in (key_part, value_part):
            work(i)
            for step in todo[:2]:
                step()
            todo = todo[2:]
    for i in range(images):
        query_part(i)
        for step in todo[:2]:
            step()
        todo = todo[2:]
    for i in range(images):
        pass_on(i, 0)
        pass_on(i, 1)
        ready(i)
        mine, todo = (todo[: HEADS // 2], todo[HEADS // 2 :])

        def body(h, _, i=i, mine=mine):
            for k, step in enumerate(mine):
                pl.when(h == 2 * k)(step)
            head(i, h)
            return 0

        lax.fori_loop(0, HEADS, body, 0)
    for step in todo:
        step()
    for i in range(soon, n):
        last(i)
    at.drain(steps)
    for i, s in parts:
        at.drain([functools.partial(give, i, s), functools.partial(pass_on, i, s)])
    for i in range(images):
        at.drain([functools.partial(ready, i)])


def forward(x, mod_part, groups, gains, band, cols, shards, cuts):
    n = len(cuts)
    images, length, width = x.shape
    bands = lax.axis_size("band")
    keys = (2, images, bands * length, width)
    s = pltpu.SemaphoreType.DMA
    bf = jnp.bfloat16
    any_ref = pl.BlockSpec(memory_space=pl.ANY)
    vmem = pl.BlockSpec(memory_space=pltpu.VMEM)
    args = [x, mod_part, groups, gains, band]
    rows = lambda w, d: jax.ShapeDtypeStruct((images, length, w), d)
    outs = [rows(width, bf)] * 2 + [rows(width, jnp.float32)] * 2 + [rows(LANES, jnp.float32)] * 2
    outs += [rows(width, bf), rows(LANES, jnp.float32), jax.ShapeDtypeStruct((images, mod_part.shape[1]), jnp.float32)]
    outs += [jax.ShapeDtypeStruct((length, width), jnp.float32)] * 3
    scratch = [
        pltpu.VMEM(keys, bf),
        pltpu.VMEM((width, 3 * width), bf),
        pltpu.VMEM((width, LANES), bf),
        pltpu.VMEM((LANES, width), bf),
        pltpu.VMEM(mod_part.shape, jnp.float32),
        pltpu.VMEM((3,) + mod_part.shape, jnp.float32),
        s((8,)),
        s((3,)),
        s((3,)),
        s((images, 2, 3)),
        s((images, 2, 3)),
        s((images, 2)),
    ]
    whole = len(shards) if n else 0
    sizes = [len(args), len(shards), len(outs) + 1, whole, len(scratch), 10 if n else 0]

    def kernel(*refs):
        groups_of, start = [], 0
        for size in sizes:
            groups_of.append(refs[start : start + size])
            start += size
        names = ("in", "shards", "out", "full", "scratch", "sems")
        forward_kernel(cuts, cols, dict(zip(names, groups_of)))

    return pl.pallas_call(
        kernel,
        out_shape=outs
        + [jax.ShapeDtypeStruct(keys, bf)]
        + [jax.ShapeDtypeStruct((8,) + w.shape, w.dtype) for w in shards[:whole]],
        in_specs=[vmem] * len(args) + [any_ref] * len(shards),
        out_specs=[vmem] * len(outs) + [any_ref] * (1 + whole),
        scratch_shapes=scratch + (gather_sems(n) if n else []),
        compiler_params=pltpu.CompilerParams(
            collective_id=2, has_side_effects=True, vmem_limit_bytes=60 * 2**20
        ),
        name="forward",
    )(*args, *shards)


EACH = 9


def attention_back_kernel(n, cuts, lags, q_ref, do_ref, inv_ref, kv_ref, *refs):
    ins, (dq_ref, d_out), outs = refs[:n], refs[n : n + 2], refs[n + 2 : 2 * n + 2]
    kv, dkv, core_buf, y_buf, load_sem, ks, kr, ys, yr, ws = refs[2 * n + 2 : 2 * n + 12]
    images, length, width = q_ref.shape
    at = Place()
    loads = [pltpu.make_async_copy(kv_ref.at[:, i], kv.at[i], load_sem.at[i]) for i in range(images)]
    for d in loads:
        d.start()
    at.greet_all() if n else at.greet_band()
    opening, todo, last = [], [], lambda: None
    if n:
        opening, todo, last = scatter_steps(at, cuts, ins, outs, refs[2 * n + 12 :], lags)
    for step in opening:
        step()
    steps = opening + todo

    def rows(s, i, band):
        return dkv.at[s, i, pl.ds(pl.multiple_of(band * length, 16), length), :]

    def to_core(i):
        for s in (0, 1):
            for yy in (0, 1):
                at.send(rows(s, i, yy * 2 + 1 - at.c), core_buf.at[i, s, yy], ks.at[i, s, yy], kr.at[i, s, yy], at.cpeer)

    def core_add(i):
        for s in (0, 1):
            p = rows(s, i, (1 - at.y) * 2 + at.c)
            at.arrived(core_buf.at[i, s, 1 - at.y], kr.at[i, s, 1 - at.y])
            if not at.draining:
                add_into(p, core_buf.at[i, s, 1 - at.y])
            at.send(p, y_buf.at[i, s], ys.at[i, s], yr.at[i, s], at.ypeer)
        for s in (0, 1):
            at.arrived(core_buf.at[i, s, at.y], kr.at[i, s, at.y])
            if not at.draining:
                add_into(rows(s, i, at.band), core_buf.at[i, s, at.y])

    def y_add(i):
        for s in (0, 1):
            p = rows(s, i, at.band)
            at.arrived(y_buf.at[i, s], yr.at[i, s])
            if not at.draining:
                add_into(p, y_buf.at[i, s])
            at.keep(p, d_out.at[s, i], ws.at[i, s])

    def head(i, h):
        win, inside = head_window(h)
        query, grad = q_ref[i, :, win], do_ref[i, :, win]
        query = jnp.where(inside, query, jnp.zeros_like(query))
        grad = jnp.where(inside, grad, jnp.zeros_like(grad))
        keys, values = kv[i, 0, :, win], kv[i, 1, :, win]
        inv = inv_ref[i, pl.ds(h, 1), :]
        probs = jnp.exp2(dot_t(keys, query) * (HDIM ** (-0.5) * LOG2E)) * inv
        d_probs = dot_t(values, grad)
        delta = jnp.sum(probs * d_probs, axis=0, keepdims=True)
        d_scores = (probs * (d_probs - delta)).astype(jnp.bfloat16)
        d_key = jnp.dot(d_scores, query, preferred_element_type=jnp.float32).astype(jnp.bfloat16)
        d_value = jnp.dot(
            probs.astype(jnp.bfloat16), grad, preferred_element_type=jnp.float32
        ).astype(jnp.bfloat16)
        dkv[0, i, :, win] = jnp.where(inside, d_key, dkv[0, i, :, win])
        dkv[1, i, :, win] = jnp.where(inside, d_value, dkv[1, i, :, win])
        dq_ref[i, :, win] = jnp.where(inside, first_dot(d_scores, keys), dq_ref[i, :, win])

    dq_ref[...] = jnp.zeros_like(dq_ref)
    for s in (0, 1):
        for i in range(images):

            def clear(r, _, s=s, i=i):
                dkv[s, i, pl.ds(pl.multiple_of(r * 16, 16), 16), :] = jnp.zeros((16, width), jnp.bfloat16)
                return 0

            lax.fori_loop(0, kv.shape[2] // 16, clear, 0)
    exchange = []
    for i in range(images):
        loads[i].wait()
        mine, todo = (todo[:EACH], todo[EACH:])
        due = exchange
        exchange = [functools.partial(f, i) for f in (core_add, y_add)]

        def body(h, _, i=i, mine=mine, due=due):
            for k, step in enumerate(due):
                pl.when(h == 1 + 12 * k)(step)
            for k, step in enumerate(mine):
                pl.when(h == k * HEADS // EACH)(step)
            head(i, h)
            return 0

        lax.fori_loop(0, HEADS, body, 0, unroll=4)
        to_core(i)
        steps += [functools.partial(to_core, i)] + exchange
    exchange[0]()
    part = min(6, len(todo))
    for step in todo[:part] + [exchange[1]] + todo[part:]:
        step()
    last()
    at.drain(steps)


def attention_backward(q, d_att, inv_rows, kv_all, grads, cuts, lags):
    n = len(grads)
    images, length, width = q.shape
    s = pltpu.SemaphoreType.DMA
    any_ref = pl.BlockSpec(memory_space=pl.ANY)
    vmem = pl.BlockSpec(memory_space=pltpu.VMEM)
    bf = jnp.bfloat16
    return pl.pallas_call(
        functools.partial(attention_back_kernel, n, cuts, lags),
        out_shape=[
            jax.ShapeDtypeStruct(q.shape, jnp.float32),
            jax.ShapeDtypeStruct((2, images, length, width), bf),
        ]
        + [jax.ShapeDtypeStruct(w.shape[:-3] + w.shape[-2:], bf) for w in grads],
        in_specs=[vmem, vmem, vmem, any_ref] + [any_ref] * n,
        out_specs=[vmem, any_ref] + [any_ref] * n,
        scratch_shapes=[
            pltpu.VMEM((images, 2) + kv_all.shape[2:], bf),
            pltpu.VMEM(kv_all.shape, bf),
            pltpu.VMEM((images, 2, 2, length, width), bf),
            pltpu.VMEM((images, 2, length, width), bf),
            s((images,)),
            s((images, 2, 2)),
            s((images, 2, 2)),
            s((images, 2)),
            s((images, 2)),
            s((images, 2)),
        ]
        + (scatter_scratch(grads, cuts) if n else []),
        compiler_params=pltpu.CompilerParams(
            collective_id=3, has_side_effects=True, vmem_limit_bytes=63 * 2**20
        ),
        name="attention_backward",
    )(q, d_att, inv_rows, kv_all, *grads)
def mlp_kernel(
    x_ref, gout_ref, att_ref, mod_ref, live_ref, proj_ref, gate_ref, up_ref, down_ref,
    out_ref, dmid_ref, dproj_ref, datt_ref, sums_ref, dgu_ref, ddown_ref,
    mid, proj, mlp, dnorm, normed, normed_t, dmlp,
):
    step, steps = pl.program_id(0), pl.num_programs(0)
    images, length, width = x_ref.shape

    def piece(i, k):
        return mod_ref[i : i + 1, k * width : (k + 1) * width]

    def rows(i):
        return pl.ds(i * length, length)

    def live(i):
        return live_ref[i : i + 1, 0:1]

    def unit(i):
        value = mid[rows(i), :]
        root = lax.rsqrt(jnp.mean(value * value, axis=-1, keepdims=True) + EPS)
        return value * root, root

    @pl.when(step == 0)
    def _():
        for i in range(images):
            proj[rows(i), :] = jnp.dot(att_ref[i], proj_ref[...], preferred_element_type=jnp.float32)
            mid[rows(i), :] = x_ref[i].astype(jnp.float32) + piece(i, 2) * proj[rows(i), :]
            value = (unit(i)[0] * (1.0 + piece(i, 4)) + piece(i, 3)).astype(jnp.bfloat16)
            normed[rows(i), :] = value
            normed_t[:, rows(i)] = value.T
            dmlp[rows(i), :] = (piece(i, 5) * (gout_ref[i].astype(jnp.float32) * live(i))).astype(jnp.bfloat16)
        mlp[...] = jnp.zeros_like(mlp)
        dnorm[...] = jnp.zeros_like(dnorm)

    gate = jnp.dot(normed[...], gate_ref[...], preferred_element_type=jnp.float32)
    up = jnp.dot(normed[...], up_ref[...], preferred_element_type=jnp.float32)
    dhidden = dot_t(dmlp[...], down_ref[...])
    sigmoid = 1.0 / (1.0 + jnp.exp(-gate))
    silu = gate * sigmoid
    hidden = (silu * up).astype(jnp.bfloat16)
    dgate = (dhidden * up * (sigmoid * (1.0 + gate * (1.0 - sigmoid)))).astype(jnp.bfloat16)
    dup = (dhidden * silu).astype(jnp.bfloat16)
    mlp[...] += jnp.dot(hidden, down_ref[...], preferred_element_type=jnp.float32)
    dnorm[...] += dot_t(dgate, gate_ref[...]) + dot_t(dup, up_ref[...])
    ddown_ref[...] = first_dot(hidden, dmlp[...]).astype(jnp.bfloat16)
    dgu_ref[0] = jnp.dot(normed_t[...], dgate, preferred_element_type=jnp.float32).astype(jnp.bfloat16)
    dgu_ref[1] = jnp.dot(normed_t[...], dup, preferred_element_type=jnp.float32).astype(jnp.bfloat16)

    @pl.when(step == steps - 1)
    def _():
        total = lambda v: jnp.sum(v, axis=0, keepdims=True)
        for i in range(images):
            gy = gout_ref[i].astype(jnp.float32) * live(i)
            value = mlp[rows(i), :]
            out_ref[i] = ((mid[rows(i), :] + piece(i, 5) * value) * live(i)).astype(jnp.bfloat16)
            sums_ref[i, 3:4, :] = total(gy * value)
            n, root = unit(i)
            dn = dnorm[rows(i), :]
            sums_ref[i, 1:2, :] = total(dn)
            sums_ref[i, 2:3, :] = total(dn * n)
            e = dn * (1.0 + piece(i, 4))
            d_mid = gy + root * (e - n * jnp.mean(e * n, axis=-1, keepdims=True))
            dmid_ref[i] = d_mid
            sums_ref[i, 0:1, :] = total(d_mid * proj[rows(i), :])
            d_proj = (piece(i, 2) * d_mid).astype(jnp.bfloat16)
            dproj_ref[i] = d_proj
            datt_ref[i] = dot_t(d_proj, proj_ref[...]).astype(jnp.bfloat16)


def mlp_block(x, grad_out, attended, mod, live, qp_all, gu_all, down_all):
    images, length, width = x.shape
    ff = down_all.shape[0]
    chunk = 512 if ff % 512 == 0 else LANES
    steps = ff // chunk
    bf = jnp.bfloat16
    whole = lambda s: pl.BlockSpec(s, lambda k: (0,) * len(s))
    rows = lambda d: jax.ShapeDtypeStruct(x.shape, d)
    tokens = images * length
    return pl.pallas_call(
        mlp_kernel,
        grid=(steps,),
        in_specs=[whole(x.shape)] * 3
        + [whole(mod.shape), whole(live.shape), pl.BlockSpec((width, width), lambda k: (0, 3))]
        + [
            pl.BlockSpec((width, chunk), lambda k: (0, k)),
            pl.BlockSpec((width, chunk), lambda k: (0, steps + k)),
            pl.BlockSpec((chunk, width), lambda k: (k, 0)),
        ],
        out_shape=[rows(bf), rows(jnp.float32), rows(bf), rows(bf)]
        + [
            jax.ShapeDtypeStruct((images, 4, width), jnp.float32),
            jax.ShapeDtypeStruct((2, width, ff), bf),
            jax.ShapeDtypeStruct((ff, width), bf),
        ],
        out_specs=[whole(x.shape)] * 4
        + [
            whole((images, 4, width)),
            pl.BlockSpec((2, width, chunk), lambda k: (0, 0, k)),
            pl.BlockSpec((chunk, width), lambda k: (k, 0)),
        ],
        scratch_shapes=[pltpu.VMEM((tokens, width), jnp.float32)] * 4
        + [pltpu.VMEM((tokens, width), bf), pltpu.VMEM((width, tokens), bf), pltpu.VMEM((tokens, width), bf)],
        compiler_params=pltpu.CompilerParams(vmem_limit_bytes=60 * 2**20),
        name="mlp_block",
    )(x, grad_out, attended, mod, live, qp_all, gu_all, gu_all, down_all)


def half_cuts(ref, axis, base, size, own_parts, shared_parts):
    unit = size // 2 // (own_parts + 2 * shared_parts)
    return (axis, size // 2, own_parts * unit, shared_parts * unit, base, ref)


def by_shard(grad):
    parts = lax.axis_size("grp")
    return grad.reshape(parts, grad.shape[0] // parts, grad.shape[1])


def body(
    patches,
    grad_out,
    cond_table,
    group_ids,
    live_count,
    band_order,
    w_ada,
    b_ada,
    w_qkv,
    q_gain,
    k_gain,
    w_proj,
    w_gate,
    w_up,
    w_down,
):
    images, rows, cols, width = patches.shape
    length = rows * cols
    ff = w_gate.shape[1]
    bf = jnp.bfloat16
    grp = lax.axis_index("grp")
    ada_rows, ada_cols, bias_cols = w_ada.shape[0], w_ada.shape[1], b_ada.shape[0]
    fits = (
        lax.axis_size("grp") == 8
        and images == 2
        and width == HEADS * HDIM
        and w_qkv.shape[0] % 16 == 0
        and 4 * width % 4608 == 0
        and 2 * ff % 3072 == 0
        and w_down.shape[0] % 384 == 0
    )
    w_qp = jnp.concatenate([w_qkv, w_proj], axis=1)
    w_gu = jnp.concatenate([w_gate, w_up], axis=1)
    full = lambda w: w.reshape(-1, w.shape[-1])
    onehot = (group_ids[:, None] == jnp.arange(GROUPS, dtype=jnp.int32)[None, :]).astype(jnp.float32)
    cond_rows = lax.dynamic_slice_in_dim(cond_table, grp * ada_rows, ada_rows, axis=1)
    sigmoid = jax.nn.sigmoid(cond_rows)
    silu_rows = (cond_rows * sigmoid).astype(bf)
    silu_slope = sigmoid * (1.0 + cond_rows * (1.0 - sigmoid))
    mod_part = jnp.dot(silu_rows, w_ada, preferred_element_type=jnp.float32)
    bias_part = lax.dynamic_update_slice_in_dim(
        jnp.zeros((ada_cols,), jnp.float32), b_ada.astype(jnp.float32), grp * bias_cols, axis=0
    )
    mod_part = mod_part + bias_part[None, :]
    live_mask = (jnp.arange(images, dtype=jnp.int32) < live_count[0]).astype(jnp.float32)

    gains = jnp.stack([jnp.tile(q_gain, HEADS), jnp.tile(k_gain, HEADS)])
    x = patches.reshape(images, length, width)
    groups = jnp.pad(onehot.T, ((0, 0), (0, LANES - images)))
    band = jnp.broadcast_to(band_order.astype(jnp.float32)[:, None], (1, LANES))
    common = (groups, gains, band, cols)
    if fits:
        shards = [w_qp, w_gu, w_down]
        cuts = [half_cuts(0, 1, 0, 4 * width, 1, 1), half_cuts(1, 1, 0, 2 * ff, 4, 1)]
        cuts += [half_cuts(2, 0, 0, w_down.shape[0], 4, 1)]
    else:
        qp_all, gu_all, down_all = (lax.all_gather(w, "grp", axis=0, tiled=True) for w in (w_qp, w_gu, w_down))
        mod_part = lax.psum(mod_part, "grp")
        shards, cuts = [qp_all], []
    outs = forward(x, mod_part, *common, shards, cuts)
    normed_one, query, nq, nk, rq, rk, attended, inv, mod = outs[:9]
    tables, kv_all, rest = outs[9:12], outs[12], outs[13:]
    if fits:
        qp_all, gu_all, down_all = (full(w) for w in rest)
    live = jnp.broadcast_to(live_mask[:, None], (images, LANES))
    flat = lambda a: a.reshape(images * length, a.shape[-1])
    patches_out, d_middle, d_proj, d_attended, mid_sums, d_w_gu, d_w_down = mlp_block(
        x, grad_out.reshape(images, length, width), attended, mod, live, qp_all, gu_all, down_all
    )
    patches_out = patches_out.reshape(images, rows, cols, width)
    mod = mod.reshape(images, 6, width)
    d_query, d_kv, *rest = attention_backward(
        query,
        d_attended,
        jnp.swapaxes(inv, 1, 2),
        kv_all,
        [d_w_gu.reshape(2, -1, w_gate.shape[0], ff)] if fits else [],
        [half_cuts(0, 1, None, 2 * ff, 6, 1)] if fits else [],
        (2, 2, 1, 2),
    )
    d_qkv, d_x, sums = qkv_backward(
        x, mod, d_middle, d_query, d_kv, nq, nk, rq, rk, qp_all, gains, tables
    )
    d_patches = d_x.reshape(images, rows, cols, width)
    d_w_qp = weight_grads(flat(normed_one), flat(attended), flat(d_qkv), flat(d_proj))
    if fits:
        tags = jnp.repeat(onehot * (1.0 / lax.axis_size("band")), 6, axis=0)
        tags = jnp.pad(tags, ((0, 0), (0, LANES - GROUPS)))
        cuts = [half_cuts(0, 0, 0, w_down.shape[0], 2, 1), half_cuts(1, 1, 0, 4 * width, 8, 5)]
        d_gu = rest[0]
        d_down, d_qp, gathered, cond_blocks = scatter(
            [by_shard(d_w_down), by_shard(d_w_qp)], cuts, (2, 1, 0, 2), sums, mid_sums, tags, w_ada, silu_slope
        )
        d_mod_all = gathered[:, :GAIN_ROW, :width].reshape(-1, ada_cols)
        onehot_all = gathered[:, 0:GAIN_ROW:6, width : width + GROUPS].reshape(-1, GROUPS)
        gain_all = gathered[:, GAIN_ROW:, :width].astype(jnp.float32).reshape(-1, 2, 2, HEADS, HDIM)
        gain_all = jnp.sum(gain_all, axis=(0, 1, 3))
        d_cond = jnp.swapaxes(cond_blocks[:, :, :ada_rows], 0, 1).reshape(GROUPS, -1)
    else:
        d_gu, d_down, d_qp = (
            lax.psum(lax.psum_scatter(w, "grp", scatter_dimension=w.ndim - 2, tiled=True), "band")
            for w in (d_w_gu, d_w_down, d_w_qp)
        )
        d_mod_part = jnp.concatenate([sums[:, 0:2], mid_sums], axis=1)
        gain_part = jnp.sum(sums[:, 2:4].reshape(images, 2, HEADS, HDIM), axis=(0, 2))
        d_modulation = lax.psum(d_mod_part.reshape(images, ada_cols), "band").astype(bf)
        gain_all = lax.psum(gain_part, ("grp", "band"))
        payload = jnp.concatenate([d_modulation, onehot.astype(bf)], axis=1)
        payload = lax.all_gather(payload, "grp", axis=0, tiled=True)
        d_mod_all, onehot_all = payload[:, :ada_cols], payload[:, ada_cols:]
        d_silu = jnp.einsum("be,de->bd", d_mod_all, w_ada, preferred_element_type=jnp.float32)
        d_silu = jnp.dot(
            onehot_all.astype(jnp.float32).T,
            d_silu,
            precision=lax.Precision.HIGHEST,
            preferred_element_type=jnp.float32,
        )
        d_cond = lax.all_gather(d_silu * silu_slope, "grp", axis=1, tiled=True)
    silu_all = jnp.dot(onehot_all, silu_rows, preferred_element_type=jnp.float32).astype(bf)
    d_w_ada = jnp.einsum("bd,be->de", silu_all, d_mod_all, preferred_element_type=jnp.float32)
    d_b_ada = lax.dynamic_slice_in_dim(
        jnp.sum(d_mod_all.astype(jnp.float32), axis=0), grp * bias_cols, bias_cols, axis=0
    )
    wide = lambda a: a.astype(jnp.float32)
    return (
        patches_out,
        d_patches,
        d_cond,
        d_w_ada,
        d_b_ada,
        wide(d_qp[:, : 3 * width]),
        gain_all[0],
        gain_all[1],
        wide(d_qp[:, 3 * width :]),
        wide(d_gu[0]),
        wide(d_gu[1]),
        wide(d_down),
    )


def solution(mesh):
    in_specs = (
        P("grp", "band", None, None),
        P("grp", "band", None, None),
        P(),
        P("grp"),
        P("grp"),
        P("band"),
        P("grp", None),
        P("grp"),
        P("grp", None),
        P(),
        P(),
        P("grp", None),
        P("grp", None),
        P("grp", None),
        P("grp", None),
    )
    out_specs = (
        P("grp", "band", None, None),
        P("grp", "band", None, None),
        P(),
        P("grp", None),
        P("grp"),
        P("grp", None),
        P(),
        P(),
        P("grp", None),
        P("grp", None),
        P("grp", None),
        P("grp", None),
    )
    return jax.shard_map(body, mesh=mesh, in_specs=in_specs, out_specs=out_specs, check_vma=False)
```
